128 devices in a mesh: group: 2 (over core), gx: 8 (over z_lo, x), gy: 8 (over z_hi, y).
Axes of the slice: x: 4, y: 4, z: 4 (z_hi: 2, z_lo: 2; z = z_hi * 2 + z_lo), core: 2. Of those that a mesh axis runs over, the one named last changes fastest.
Arguments:
- state: float32 [2, 3, 128, 256, 128], P('group', None, 'gx', 'gy'), may hold values from -6 to 6
- conduct: float32 [2, 3, 3, 128, 256, 128], P('group', None, None, 'gx', 'gy'), may hold values from 0.1 to 10
- capacity: float32 [2, 128, 256, 128], P('group', 'gx', 'gy'), may hold values from 0.3 to 3
- supply: float32 [2, 3, 128, 256, 128], P('group', None, 'gx', 'gy'), may hold values from -10.5 to 13.5
- flags: int32 [128, 256], P('gx', 'gy'), may hold values 0 or 1
- layer_map: int32 [384], replicated, may hold values from 0 to 127, never falling along the last dimension, each value on 1 to 6 neighbouring positions
Outputs:
- new_state: float32 [2, 3, 128, 256, 128], P('group', None, 'gx', 'gy')
- balance: float32 [2], replicated
The draws below stay inside these ranges and needn't reach their ends.
Inputs may be any that keep to these rules, and one draw needn't show every extreme that they name: `layer_map`: never falls; every brick layer holds 1 to 6 fine layers, one exactly 6.
All inputs are finite; a program needn't handle non-finite values. No bound on the sum of `flags` on one device may be relied on, other than what follows from the above.
Results may differ from the reference program's by a relative error of at most 0.0001.
Values sent between devices are 32-bit elements; how exact they have to be, the bound alone decides.
No kernel may reach another device: no remote copies, remote signals or barrier semaphores. Data moves between devices by JAX's collectives and lax.ppermute only.
A program may use at most 128 MiB of HBM per device.

```python
import math
import jax
import jax.numpy as jnp
import numpy as np
from jax import lax

NZ = 128
MOST = 6
ITERS = 2
NX = 128
NY = 256
NZF = 384


def draw_supply(key, part):
    key = jax.random.fold_in(key, 11)
    row_ramp = jnp.arange(NX, dtype=jnp.float32) / max(NX - 1, 1)
    column_ramp = jnp.arange(NY, dtype=jnp.float32) / max(NY - 1, 1)
    growth_ramp = 3.0 ** (row_ramp[:, None, None] + 0.0 * column_ramp[None, :, None])
    rough_part = jnp.clip(jax.random.normal(key, (2, 3, NX, NY, NZ), jnp.float32), -4.0, 4.0)
    offset = 0.5
    return growth_ramp * (offset + rough_part)


def set_ends(values, rng, smallest, largest):
    shape = values.shape
    index_at = [jax.random.randint(jax.random.fold_in(rng, axis), (), 0, shape[axis]) for axis in range(len(shape))]
    values = values.at[tuple(index_at)].set(smallest)
    longest = shape.index(max(shape))
    index_at[longest] = (index_at[longest] + 1) % shape[longest]
    return values.at[tuple(index_at)].set(largest)


def levels(key, shape, pieces, low, high):
    def one(axis_at, parts):
        heights = jax.random.uniform(jax.random.fold_in(jax.random.fold_in(key, 6), axis_at), (parts,), jnp.float32, low / len(pieces), high / len(pieces))
        return jnp.repeat(jnp.exp(heights), shape[axis_at] // parts).reshape((-1,) + (1,) * (len(shape) - axis_at - 1))

    gain = one(*pieces[0])
    for cut in pieces[1:]:
        gain = gain * one(*cut)
    return gain


def profile(amount, total, bound, skew):
    loads = [(1 << 20) // math.isqrt(rank ** skew) + 1 for rank in range(2, amount + 1)]
    rest, given = total - bound - (amount - 1), [1] * (amount - 1)
    while rest > 0:
        free = [i for i in range(amount - 1) if given[i] < bound]
        mass, budget = sum([loads[i] for i in free]), rest
        for i in free:
            addition = min(bound - given[i], max(1, budget * loads[i] // mass), rest)
            given[i] = given[i] + addition
            rest = rest - addition
    return np.array([bound] + given)


def ragged_sizes(stream_key, count, total, bound, slope):
    if count == 2:
        one = jax.random.randint(stream_key, (), max(1, total - bound), min(bound, total - 1) + 1)
        return jnp.stack([one, total - one])
    lengths = jnp.asarray(profile(count, total, bound, slope), jnp.int32)
    pairs = (count - 1) // 2
    giver, receiver = lengths[1:1 + 2 * pairs:2], lengths[2:2 + 2 * pairs:2]
    room = jnp.minimum(giver - 1, bound - receiver)
    shifted = jax.random.randint(jax.random.fold_in(stream_key, 1), (pairs,), 0, 1 << 20) % (room + 1)
    lengths = lengths.at[1:1 + 2 * pairs:2].set(giver - shifted).at[2:2 + 2 * pairs:2].set(receiver + shifted)
    return lengths[jax.random.permutation(jax.random.fold_in(stream_key, 2), count)]


def bell_draw(own_key, dims, deviation, bound, split=(), kind=jnp.bfloat16):
    entries = jax.random.normal(own_key, dims, jnp.float32) * deviation
    if len(split) > 0:
        entries = levels(own_key, dims, split, -0.22, 0.18) * entries
    return jnp.clip(entries, min=-bound, max=bound).astype(kind)


def setup_inputs(seed: int = 0) -> dict:
    splits = jax.random.split(jax.random.key(seed), 7)
    state = bell_draw(splits[0], (2, 3, NX, NY, NZ), 1.0, 6.0, ((0, 2), (2, 8), (3, 8)), jnp.float32)
    conduct = jnp.clip(jnp.exp(math.log(10.0) - 4.6051702 * jax.random.uniform(splits[1], (2, 3, 3, NX, NY, NZ), jnp.float32) ** levels(splits[1], (2, 3, 3, NX, NY, NZ), ((0, 2), (3, 8), (4, 8)), -0.2, 0.2)), 0.1, 10.0)
    capacity = jnp.clip(jnp.exp(math.log(3.0) - 2.3025851 * jax.random.uniform(splits[2], (2, NX, NY, NZ), jnp.float32) ** levels(splits[2], (2, NX, NY, NZ), ((0, 2), (1, 8), (2, 8)), -0.2, 0.2)), 0.3, 3.0)
    supply = draw_supply(jax.random.fold_in(splits[6], 71), 0)
    flags = set_ends((jax.random.randint(splits[4], (NX, NY), 0, 2) < 1).astype(jnp.int32), jax.random.fold_in(splits[4], 1), 0, 1)
    layer_map = jnp.searchsorted(jnp.cumsum(ragged_sizes(splits[5], NZ, NZF, MOST, 1)), jnp.arange(NZF), side="right").astype(jnp.int32)
    return {"state": state, "conduct": conduct, "capacity": capacity, "supply": supply, "flags": flags, "layer_map": layer_map}


fixed_beta = 0.5
biot_weight = 0.8
precise = lax.Precision.HIGHEST


def harmonic(first_value, second_value):
    return 2.0 * first_value * second_value / (first_value + second_value)


def forward(values, dimension):
    padding = [(0, 0)] * values.ndim
    padding[dimension] = (0, 1)
    return lax.slice_in_dim(jnp.pad(values, padding), 1, values.shape[dimension] + 1, axis=dimension)


def backward(values, dimension):
    padding = [(0, 0)] * values.ndim
    padding[dimension] = (1, 0)
    return lax.slice_in_dim(jnp.pad(values, padding), 0, values.shape[dimension], axis=dimension)


def to_layers(triple):
    return jnp.moveaxis(triple, 0, 2).reshape(NX, NY, NZF)


def from_layers(layered):
    return jnp.moveaxis(layered.reshape(NX, NY, 3, NZ), 2, 0)


def conjugate(operator, iterate, right_side):
    residual = right_side - operator(iterate)
    direction = residual
    current = jnp.sum(residual * residual)
    for iteration in range(ITERS):
        image_vec = operator(direction)
        step_size = current / jnp.sum(direction * image_vec)
        iterate = iterate + step_size * direction
        residual = residual - step_size * image_vec
        if iteration + 1 < ITERS:
            following = jnp.sum(residual * residual)
            direction = residual + (following / current) * direction
            current = following
    return iterate


def reference(state, conduct, capacity, supply, flags, layer_map):
    mapping = (layer_map[:, None] == jnp.arange(NZ, dtype=jnp.int32)[None, :]).astype(jnp.float32)
    counts = jnp.sum(mapping, axis=0)
    pressure = to_layers(state[0])
    moving = state[1]
    open_bottom = flags.astype(jnp.float32)

    perm_x = to_layers(conduct[0, 0])
    perm_y = to_layers(conduct[0, 1])
    perm_z = to_layers(conduct[0, 2])
    face_x = harmonic(perm_x, forward(perm_x, 0))
    face_y = harmonic(perm_y, forward(perm_y, 1))
    vertical_next = jnp.concatenate([perm_z[:, :, 1:], (open_bottom * perm_z[:, :, -1])[:, :, None]], axis=2)
    face_z = harmonic(perm_z, vertical_next)
    storage = jnp.einsum("xyw,lw->xyl", capacity[0], mapping, precision=precise) + fixed_beta

    def flow_apply(field_now):
        result = storage * field_now
        result = result + face_x * (field_now - forward(field_now, 0)) + backward(face_x, 0) * (field_now - backward(field_now, 0))
        result = result + face_y * (field_now - forward(field_now, 1)) + backward(face_y, 1) * (field_now - backward(field_now, 1))
        result = result + face_z * (field_now - forward(field_now, 2)) + backward(face_z, 2) * (field_now - backward(field_now, 2))
        return result

    stiff_x = conduct[1, 0]
    stiff_y = conduct[1, 1]
    stiff_z = conduct[1, 2]
    shear_x = harmonic(stiff_x, forward(stiff_x, 1))
    shear_y = harmonic(stiff_y, forward(stiff_y, 2))
    shear_z = harmonic(stiff_z, jnp.concatenate([stiff_z[..., 1:], stiff_z[..., -1:]], axis=3))
    bulk_modulus = capacity[1]

    def strain(displaced):
        return (forward(displaced[0], 0) - displaced[0]) + (forward(displaced[1], 1) - displaced[1]) + (forward(displaced[2], 2) - displaced[2])

    def mech_apply(displaced):
        result = shear_x * (displaced - forward(displaced, 1)) + backward(shear_x, 1) * (displaced - backward(displaced, 1))
        result = result + shear_y * (displaced - forward(displaced, 2)) + backward(shear_y, 2) * (displaced - backward(displaced, 2))
        result = result + shear_z * (displaced - forward(displaced, 3)) + backward(shear_z, 3) * (displaced - backward(displaced, 3))
        stress = bulk_modulus * strain(displaced)
        gradient = jnp.stack([backward(stress, 0) - stress, backward(stress, 1) - stress, backward(stress, 2) - stress])
        return result + gradient

    strain_old = strain(moving)
    rhs_flow = to_layers(supply[0]) + fixed_beta * pressure - biot_weight * jnp.einsum("xyw,lw->xyl", strain_old, mapping, precision=precise)
    pressure_new = conjugate(flow_apply, pressure, rhs_flow)
    unit_pressure = jnp.einsum("xyl,lw->xyw", pressure_new, mapping, precision=precise) / counts
    coupling_force = jnp.stack([backward(unit_pressure, 0) - unit_pressure, backward(unit_pressure, 1) - unit_pressure, backward(unit_pressure, 2) - unit_pressure])
    rhs_mech = supply[1] + biot_weight * coupling_force
    moving_new = conjugate(mech_apply, moving, rhs_mech)
    new_state = jnp.stack([from_layers(pressure_new), moving_new])
    bottom_flux = jnp.sum(open_bottom * perm_z[:, :, -1] * pressure_new[:, :, -1]) / (NX * NY)
    change = jnp.sum(storage * (pressure_new - pressure)) / (NX * NY * NZF)
    return new_state, jnp.stack([bottom_flux, change])
```

```python
import jax
import jax.numpy as jnp
from jax import lax
from jax.experimental import pallas as pl
from jax.experimental.pallas import tpu as pltpu
from jax.sharding import PartitionSpec as P

AXES = ("group", "gx", "gy")
X, Y, Z = 16, 32, 128
OX, OY = 3, 4
EX, EY = X + 2 * OX, Y + 2 * OY
BETA = 0.5
BIOT = 0.8
F32 = jnp.float32

X_ROWS = [(f, r) for f in range(13) for r in range(1, (3 if f < 3 else 2) + 1)]
Y_ROWS = [(f, r) for f in range(13) for r in range(1, (3 if 3 <= f < 6 else 2) + 1)]
CORNER = [(1, 1), (1, 2), (2, 1), (2, 2), (1, 3), (3, 1)]
CORNERS = [(f, i, j) for f in range(13) for i, j in CORNER]
R_ROWS = [(f, r) for f in range(3) for r in range(1, 4)]
R_CORNERS = [(f, i, j) for f in range(3) for i, j in CORNER]


def padded(count):
    return -(-count // 8) * 8


def struct(*shape):
    return jax.ShapeDtypeStruct(shape, F32)


def call(kernel, outs, scratch=(), limit=56):
    return pl.pallas_call(
        kernel,
        out_shape=outs,
        scratch_shapes=list(scratch),
        compiler_params=pltpu.CompilerParams(vmem_limit_bytes=limit << 20),
    )


def up_y(v):
    return pltpu.roll(v, v.shape[0] - 1, 0)


def down_y(v):
    return pltpu.roll(v, 1, 0)


def up_z(v):
    return pltpu.roll(v, Z - 1, 1)


def down_z(v):
    return pltpu.roll(v, 1, 1)


def lanes(rows):
    return lax.broadcasted_iota(jnp.int32, (rows, Z), 1)


def rows_of(rows):
    return lax.broadcasted_iota(jnp.int32, (rows, Z), 0)


def to_tile(v):
    return pltpu.roll(v, EY - OY, 0)[:Y]


def harmonic(a, b):
    return 2.0 * a * b / jnp.maximum(a + b, 1e-30)


def one_hot(map_ref):
    brick = lax.broadcasted_iota(jnp.int32, (Z, 3 * Z), 0)
    return jnp.where(brick == map_ref[...], 1.0, 0.0).astype(jnp.bfloat16)


def dot_split(v, hot, contract):
    high = v.astype(jnp.bfloat16)
    low = (v - high.astype(F32)).astype(jnp.bfloat16)
    dims = (((1,), (contract,)), ((), ()))
    return lax.dot_general(high, hot, dims, preferred_element_type=F32) + lax.dot_general(
        low, hot, dims, preferred_element_type=F32
    )


def spread(v, hot, k):
    return dot_split(v, hot[:, k * Z : (k + 1) * Z], 0)


def gather_up(ref, first, last, hot):
    total = None
    count = (last - first) * EY
    for k in range(3):
        v = ref[k, first:last].reshape(count, Z)
        part = dot_split(v, hot[:, k * Z : (k + 1) * Z], 1)
        total = part if total is None else total + part
    ones = jnp.ones((8, 3 * Z), jnp.bfloat16)
    counts = lax.dot_general(ones, hot, (((1,), (1,)), ((), ())), preferred_element_type=F32)
    return (total * (1.0 / counts[:1])).reshape(last - first, EY, Z)


def pack(source, x_rows, y_rows, corners, outs):
    xt, xh, yt, yh, ctt, cth, cht, chh = outs
    for n, (f, r) in enumerate(x_rows):
        xt[n] = source(f)[X - r]
        xh[n] = source(f)[r - 1]
    for n, (f, r) in enumerate(y_rows):
        yt[n] = source(f)[:, Y - r, :]
        yh[n] = source(f)[:, r - 1, :]
    for n, (f, i, j) in enumerate(corners):
        ctt[n : n + 1] = source(f)[X - i, Y - j : Y - j + 1]
        cth[n : n + 1] = source(f)[X - i, j - 1 : j]
        cht[n : n + 1] = source(f)[i - 1, Y - j : Y - j + 1]
        chh[n : n + 1] = source(f)[i - 1, j - 1 : j]


def unpack(target, x_rows, y_rows, corners, halos):
    xl, xu, yl, yu, cll, clu, cul, cuu = halos
    for n, (f, r) in enumerate(x_rows):
        target(f)[OX - r, OY : OY + Y] = xl[n]
        target(f)[OX + X - 1 + r, OY : OY + Y] = xu[n]
    for n, (f, r) in enumerate(y_rows):
        target(f)[OX : OX + X, OY - r, :] = yl[n]
        target(f)[OX : OX + X, OY + Y - 1 + r, :] = yu[n]
    for n, (f, i, j) in enumerate(corners):
        x_low, x_up = OX - i, OX + X - 1 + i
        y_low, y_up = OY - j, OY + Y - 1 + j
        target(f)[x_low, y_low : y_low + 1] = cll[n : n + 1]
        target(f)[x_low, y_up : y_up + 1] = clu[n : n + 1]
        target(f)[x_up, y_low : y_low + 1] = cul[n : n + 1]
        target(f)[x_up, y_up : y_up + 1] = cuu[n : n + 1]


def pack_shapes(x_rows, y_rows, corners):
    corner = struct(padded(len(corners)), Z)
    x_face = struct(len(x_rows), Y, Z)
    y_face = struct(len(y_rows), X, Z)
    return [x_face, x_face, y_face, y_face, corner, corner, corner, corner]


def loop(first, last, body, init=0):
    return lax.fori_loop(first, last, body, init)


def pack_kernel(state, conduct, capacity, bottom, tz, *outs):
    flow = lax.axis_index("group") == 0
    last = lanes(Y) == Z - 1

    def faces(x, carry):
        kz = [conduct[2, k, x] for k in range(3)]
        rolled = [up_z(v) for v in kz]
        ends = [rolled[1], rolled[2], bottom[x] * kz[2]]
        for k in range(3):
            end = jnp.where(flow, ends[k], kz[k])
            tz[k, x] = harmonic(kz[k], jnp.where(last, end, rolled[k]))
        return carry

    loop(0, X, faces)

    def source(f):
        if f < 6:
            return conduct.at[f // 3, f % 3]
        if f < 9:
            return tz.at[f - 6]
        return capacity if f == 9 else state.at[f - 10]

    pack(source, X_ROWS, Y_ROWS, CORNERS, outs)


def lateral(faces, v_ref, c, i, v, fx_before):
    fx = faces[c, i] * (v - v_ref[c, i + 1])
    fy = faces[3 + c, i] * (v - up_y(v))
    return (fx - fx_before) + (fy - down_y(fy)), fx


def x_flux(faces, v_ref, i):
    return tuple(faces[c, i] * (v_ref[c, i] - v_ref[c, i + 1]) for c in range(3))


def flow_below(vs, last):
    rolled = [up_z(v) for v in vs]
    ends = [rolled[1], rolled[2], 0.0]
    return [jnp.where(last, ends[k], rolled[k]) for k in range(3)]


def flow_row(faces, v_ref, i, fx_before):
    last, first = lanes(EY) == Z - 1, lanes(EY) == 0
    vs = [v_ref[k, i] for k in range(3)]
    below = flow_below(vs, last)
    fz = [faces[6 + k, i] * (vs[k] - below[k]) for k in range(3)]
    moved = [down_z(v) for v in fz]
    ends = [0.0, moved[0], moved[1]]
    out, fx_now = [], []
    for k in range(3):
        side, fx = lateral(faces, v_ref, k, i, vs[k], fx_before[k])
        above = jnp.where(first, ends[k], moved[k])
        out.append(faces[9 + k, i] * vs[k] + side + (fz[k] - above))
        fx_now.append(fx)
    return out, tuple(fx_now)


def strain_row(v_ref, i):
    v0, v1, v2 = v_ref[0, i], v_ref[1, i], v_ref[2, i]
    low = jnp.where(lanes(EY) == Z - 1, 0.0, up_z(v2))
    return (v_ref[0, i + 1] - v0) + (up_y(v1) - v1) + (low - v2)


def solid_row(faces, v_ref, i, s_before, fx_before):
    last, first = lanes(EY) == Z - 1, lanes(EY) == 0
    e = strain_row(v_ref, i)
    s = faces[9, i] * e
    grad = [s_before - s, down_y(s) - s, jnp.where(first, 0.0, down_z(s)) - s]
    out, fx_now = [], []
    for c in range(3):
        v = v_ref[c, i]
        side, fx = lateral(faces, v_ref, c, i, v, fx_before[c])
        fz = faces[6 + c, i] * (v - jnp.where(last, 0.0, up_z(v)))
        above = jnp.where(first, 0.0, down_z(fz))
        out.append((side + (fz - above)) + grad[c])
        fx_now.append(fx)
    return out, e, s, tuple(fx_now)


def first_kernel(state, conduct, capacity, supply, tz, layer_map, *refs):
    halos, (faces, base, strain, unit, keep, caps, field) = refs[:8], refs[8:]
    flow = lax.axis_index("group") == 0

    def target(f):
        if f < 6:
            return keep.at[f]
        if f < 9:
            return faces.at[f]
        return caps if f == 9 else field.at[f - 10]

    def place(x, carry):
        at = slice(OY, OY + Y)
        for f in range(6):
            keep[f, OX + x, at] = conduct[f // 3, f % 3, x]
        for k in range(3):
            faces[6 + k, OX + x, at] = tz[k, x]
            field[k, OX + x, at] = state[k, x]
        caps[OX + x, at] = capacity[x]
        return carry

    loop(0, X, place)
    unpack(target, X_ROWS, Y_ROWS, CORNERS, halos)

    def lateral_faces(i, carry):
        for c in range(3):
            faces[c, i] = harmonic(keep[c, i], keep[c, i + 1])
            here = keep[3 + c, i]
            faces[3 + c, i] = harmonic(here, up_y(here))
        return carry

    loop(0, EX - 1, lateral_faces)

    @pl.when(flow)
    def _():
        hot = one_hot(layer_map)
        bricks = caps[1 : EX - 1].reshape((EX - 2) * EY, Z)
        for k in range(3):
            faces[9 + k, 1 : EX - 1] = (spread(bricks, hot, k) + BETA).reshape(EX - 2, EY, Z)

        def row(i, fx_before):
            image, fx = flow_row(faces, field, i, fx_before)
            for k in range(3):
                base[k, i - OX] = (
                    supply[k, i - OX] + BETA * state[k, i - OX] - to_tile(image[k])
                )
            return fx

        loop(OX, OX + X, row, x_flux(faces, field, OX - 1))
        unit[...] = gather_up(field, 1, EX - 1, hot)

    @pl.when(jnp.logical_not(flow))
    def _():
        faces[9] = caps[...]

        def row(i, carry):
            image, e, s, fx = solid_row(faces, field, i, carry[0], carry[1])
            for c in range(3):
                base[c, i - OX] = supply[c, i - OX] - to_tile(image[c])
            strain[i - OX] = to_tile(e)
            return s, fx

        before = faces[9, OX - 1] * strain_row(field, OX - 1)
        loop(OX, OX + X, row, (before, x_flux(faces, field, OX - 1)))


def residual_kernel(base, strain, layer_map, residual, *outs):
    flow = lax.axis_index("group") == 0

    @pl.when(flow)
    def _():
        hot = one_hot(layer_map)
        e = strain[...].reshape(X * Y, Z)
        for k in range(3):
            residual[k] = base[k] - BIOT * spread(e, hot, k).reshape(X, Y, Z)

    @pl.when(jnp.logical_not(flow))
    def _():
        residual[...] = base[...]

    pack(lambda f: residual.at[f], R_ROWS, R_ROWS, R_CORNERS, outs)


def fold(v):
    return jnp.sum(v.reshape(v.shape[0] // 8, 8, Z), axis=0)


def spread_sums(totals, start):
    lane = lanes(8)
    row = jnp.zeros((8, Z), F32)
    first = rows_of(8) == 0
    for n, total in enumerate(totals):
        row = jnp.where(first & (lane == start + n), jnp.sum(total), row)
    return row


def tile_rows():
    at = rows_of(EY)
    return (at >= OY) & (at < OY + Y)


def fill(residual, target, halos):
    def place(x, carry):
        for k in range(3):
            target[k, OX + x, OY : OY + Y] = residual[k, x]
        return carry

    loop(0, X, place)
    unpack(lambda f: target.at[f], R_ROWS, R_ROWS, R_CORNERS, halos)


def flow_kernel(residual, state, faces, layer_map, *refs):
    halos, (image, unit, sums, field, product) = refs[:8], refs[8:]
    flow = lax.axis_index("group") == 0
    sums[...] = jnp.zeros((8, Z), F32)

    @pl.when(flow)
    def _():
        hot = one_hot(layer_map)
        fill(residual, field, halos)

        def row(i, fx_before):
            out, fx = flow_row(faces, field, i, fx_before)
            for k in range(3):
                product[k, i] = out[k]
            return fx

        loop(1, EX - 1, row, x_flux(faces, field, 0))
        unit[0] = gather_up(field, 1, EX - 1, hot)
        unit[1] = gather_up(product, 1, EX - 1, hot)

        def dots(i, acc):
            acc = list(acc)
            inside, last = tile_rows(), lanes(EY) == Z - 1

            def add(n, v):
                acc[n] = acc[n] + fold(jnp.where(inside, v, 0.0))

            ws = [product[k, i] for k in range(3)]
            below = flow_below(ws, last)
            g = m1 = m2 = m3 = cr = cw = 0.0
            for k in range(3):
                r, w = field[k, i], ws[k]
                image[k, i - OX] = to_tile(w)
                dx, dy, dz = w - product[k, i + 1], w - up_y(w), w - below[k]
                cf = faces[9 + k, i]
                g = g + r * r
                m1 = m1 + r * w
                m2 = m2 + w * w
                cr = cr + cf * r
                cw = cw + cf * w
                m3 = m3 + (
                    faces[k, i] * dx * dx
                    + faces[3 + k, i] * dy * dy
                    + faces[6 + k, i] * dz * dz
                    + cf * w * w
                )
            for n, v in enumerate((g, m1, m2, m3, cr, cw)):
                add(n, v)
            weight = jnp.where(last, faces[8, i], 0.0)
            add(6, weight * field[2, i])
            add(7, weight * ws[2])
            acc[8] = acc[8] + fold(to_tile(weight) * state[2, i - OX])
            return tuple(acc)

        zero = jnp.zeros((8, Z), F32)
        sums[...] = spread_sums(loop(OX, OX + X, dots, (zero,) * 9), 0)


PAIRS = [(0, 0), (0, 1), (0, 2), (1, 1), (1, 2), (2, 2)]


def solid_kernel(residual, faces, unit0, unit12, sums_in, *refs):
    halos, (res_out, image, sums, field, product, acc) = refs[:8], refs[8:]
    flow = lax.axis_index("group") == 0
    sums[...] = sums_in[...]
    gx, gy = lax.axis_index("gx"), lax.axis_index("gy")
    gx_last, gy_last = lax.axis_size("gx") - 1, lax.axis_size("gy") - 1

    @pl.when(jnp.logical_not(flow))
    def _():
        fill(residual, field.at[0], halos)
        at = rows_of(EY)
        in_y = ((at >= OY) | (gy > 0)) & ((at < OY + Y) | (gy < gy_last))

        def in_grid(i):
            in_x = ((i >= OX) | (gx > 0)) & ((i < OX + X) | (gx < gx_last))
            return in_y & in_x

        def loads(i, carry):
            first, ok = lanes(EY) == 0, in_grid(i)
            for a in range(3):
                q_ref = unit0 if a == 0 else unit12.at[a - 1]
                q = q_ref[i - 1]
                push = [
                    BIOT * (q_ref[i - 2] - q),
                    BIOT * (down_y(q) - q),
                    BIOT * (jnp.where(first, 0.0, down_z(q)) - q),
                ]
                for c in range(3):
                    v = push[c] + field[a, c, i] if a == 0 else push[c]
                    field[a, c, i] = jnp.where(ok, v, 0.0)
            return carry

        loop(OX - 1, OX + X + 2, loads)

        for a in range(3):
            f_ref = field.at[a]

            def row(i, carry):
                out, e, s, fx = solid_row(faces, f_ref, i, carry[0], carry[1])
                ok = in_grid(i)
                for c in range(3):
                    product[a, c, i] = jnp.where(ok, out[c], 0.0)
                return s, fx

            before = faces[9, OX - 1] * strain_row(f_ref, OX - 1)
            loop(OX, OX + X + 1, row, (before, x_flux(faces, f_ref, OX - 1)))

        acc[...] = jnp.zeros(acc.shape, F32)

        def dots(i, carry):
            inside, last = tile_rows(), lanes(EY) == Z - 1

            def add(n, v):
                acc[n] = acc[n] + fold(jnp.where(inside, v, 0.0))

            strains = [strain_row(product.at[a], i) for a in range(3)]
            modulus = faces[9, i]
            for n, (a, b) in enumerate(PAIRS):
                add(18 + n, modulus * strains[a] * strains[b])
            for c in range(3):
                rs = [field[a, c, i] for a in range(3)]
                ws = [product[a, c, i] for a in range(3)]
                for a in range(3):
                    res_out[a, c, i - OX] = to_tile(rs[a])
                    image[a, c, i - OX] = to_tile(ws[a])
                dx = [ws[a] - product[a, c, i + 1] for a in range(3)]
                dy = [w - up_y(w) for w in ws]
                dz = [w - jnp.where(last, 0.0, up_z(w)) for w in ws]
                fx = [faces[c, i] * d for d in dx]
                fy = [faces[3 + c, i] * d for d in dy]
                fz = [faces[6 + c, i] * d for d in dz]
                for n, (a, b) in enumerate(PAIRS):
                    add(n, rs[a] * rs[b])
                    add(6 + n, rs[a] * ws[b])
                    add(12 + n, ws[a] * ws[b])
                    add(18 + n, fx[a] * dx[b] + fy[a] * dy[b] + fz[a] * dz[b])
            return carry

        loop(OX, OX + X, dots)
        sums[...] = spread_sums([acc[n] for n in range(24)], 9)


def two_sum(a, b):
    s = a + b
    t = s - a
    return s, (a - (s - t)) + (b - t)


def quick(a, b):
    s = a + b
    return s, b - (s - a)


def halves(a):
    t = 4097.0 * a
    high = t - (t - a)
    return high, a - high


def two_product(a, b):
    p = a * b
    ah, al = halves(a)
    bh, bl = halves(b)
    return p, ((ah * bh - p) + ah * bl + al * bh) + al * bl


def pair_add(a, b):
    s, e = two_sum(a[0], b[0])
    return quick(s, e + (a[1] + b[1]))


def pair_less(a, b):
    return pair_add(a, (-b[0], -b[1]))


def pair_times(a, b):
    p, e = two_product(a[0], b[0])
    return quick(p, e + (a[0] * b[1] + a[1] * b[0]))


def pair_over(a, b):
    q = a[0] / b[0]
    rest = pair_less(a, pair_times(b, (q, jnp.zeros_like(q))))
    return quick(q, rest[0] / b[0])


def krylov(g, m1, m2, m3):
    a0 = pair_over(g, m1)
    h = pair_times(a0, pair_over(m2, m1))
    one = (jnp.ones_like(a0[0]), jnp.zeros_like(a0[0]))
    rho = pair_less(h, one)[0]
    third = pair_times(pair_times(a0, a0), pair_over(m3, m1))
    sigma = pair_less(third, pair_times(h, h))[0]
    more = (rho > 1e-9) & (sigma > 1e-9)
    a1 = jnp.where(more, a0[0] * rho / jnp.where(more, sigma, 1.0), 0.0)
    return a0[0] + a1 * h[0], -a0[0] * a1


def final_kernel(sums, state, res_flow, image_flow, res_solid, image_solid, out, balance, *, cells):
    flow = lax.axis_index("group") == 0

    def number(n):
        return (jnp.full((8, Z), sums[0, n], F32), jnp.full((8, Z), sums[1, n], F32))

    c0, c1 = krylov(number(0), number(1), number(2), number(3))
    columns = cells // (3 * Z)
    outflow = (number(8)[0] + c0 * number(6)[0] + c1 * number(7)[0]) / columns
    stored = (c0 * number(4)[0] + c1 * number(5)[0]) / cells
    balance[...] = jnp.where(lanes(8) == 0, outflow, stored)

    def tall(v):
        return jnp.concatenate([v] * (Y // 8), axis=0)

    @pl.when(flow)
    def _():
        s0, s1 = tall(c0), tall(c1)

        def row(x, carry):
            for k in range(3):
                out[k, x] = state[k, x] + s0 * res_flow[k, x] + s1 * image_flow[k, x]
            return carry

        loop(0, X, row)

    @pl.when(jnp.logical_not(flow))
    def _():
        zero = jnp.zeros((8, Z), F32)
        weights = [
            (jnp.ones((8, Z), F32), zero),
            (2.0 * c0, zero),
            (2.0 * c1, zero),
            two_product(c0, c0),
            two_product(2.0 * c0, c1),
            two_product(c1, c1),
        ]
        moments = []
        for start in (9, 15, 21, 27):
            total = number(start)
            for n in range(1, 6):
                total = pair_add(total, pair_times(weights[n], number(start + n)))
            moments.append(total)
        d0, d1 = krylov(*moments)
        scale_r = [tall(d0), tall(d0 * c0), tall(d0 * c1)]
        scale_w = [tall(d1), tall(d1 * c0), tall(d1 * c1)]

        def row(x, carry):
            for c in range(3):
                v = state[c, x]
                for a in range(3):
                    v = v + scale_r[a] * res_solid[a, c, x] + scale_w[a] * image_solid[a, c, x]
                out[c, x] = v
            return carry

        loop(0, X, row)


def grid_shift(value, dx, dy):
    groups, rows, columns = (lax.axis_size(a) for a in AXES)
    pairs = []
    for g in range(groups):
        for i in range(rows):
            for j in range(columns):
                if 0 <= i + dx < rows and 0 <= j + dy < columns:
                    here = (g * rows + i) * columns + j
                    pairs.append((here, here + dx * columns + dy))
    return lax.ppermute(value, AXES, pairs)


def exchange(packs):
    steps = [(1, 0), (-1, 0), (0, 1), (0, -1), (1, 1), (1, -1), (-1, 1), (-1, -1)]
    return [grid_shift(v, dx, dy) for v, (dx, dy) in zip(packs, steps)]


def partner_steps(rows, columns):
    def ring(a):
        return [(a ^ 1), (a + 1 if a % 2 else a - 1) % 4]

    steps = []
    for half in range(2):
        steps.append([lambda g, i, j, h=half: (g, i, (j & 4) | ring(j & 3)[h])][0])
        steps.append([lambda g, i, j, h=half: (g, (i & 4) | ring(i & 3)[h], j)][0])

        def deep(g, i, j, h=half):
            z = ring((j >> 2) * 2 + (i >> 2))[h]
            return (g, (z & 1) * 4 + (i & 3), (z >> 1) * 4 + (j & 3))

        steps.append(deep)
    steps.append(lambda g, i, j: (1 - g, i, j))
    return steps


def total_over_devices(part):
    groups, rows, columns = (lax.axis_size(a) for a in AXES)
    if (groups, rows, columns) != (2, 8, 8):
        return lax.psum(part, AXES)
    for step in partner_steps(rows, columns):
        pairs = []
        for g in range(groups):
            for i in range(rows):
                for j in range(columns):
                    a, b, c = step(g, i, j)
                    pairs.append(((g * 8 + i) * 8 + j, (a * 8 + b) * 8 + c))
        other = lax.ppermute(part, AXES, pairs)
        high, rest = two_sum(part[:1], other[:1])
        low = (part[1:2] + other[1:2]) + rest
        part = jnp.concatenate([high, low, jnp.zeros((6, Z), F32)], axis=0)
    return part


def to_group(value, source):
    rows, columns = lax.axis_size("gx"), lax.axis_size("gy")
    count = rows * columns
    pairs = [(source * count + n, (1 - source) * count + n) for n in range(count)]
    return lax.ppermute(value, AXES, pairs)


def body(state, conduct, capacity, supply, flags, layer_map):
    state, conduct, capacity, supply = state[0], conduct[0], capacity[0], supply[0]
    layer_map = layer_map.reshape(1, 3 * Z)
    cells = X * Y * 3 * Z * lax.axis_size("gx") * lax.axis_size("gy")
    bottom = jnp.broadcast_to(flags.astype(F32)[:, :, None], (X, Y, Z))
    tile = struct(3, X, Y, Z)
    wide = (EX, EY, Z)

    tz, *packs = call(pack_kernel, [tile] + pack_shapes(X_ROWS, Y_ROWS, CORNERS))(
        state, conduct, capacity, bottom
    )
    halos = exchange(packs)
    faces, base, strain, unit0 = call(
        first_kernel,
        [struct(12, *wide), tile, struct(X, Y, Z), struct(EX - 2, EY, Z)],
        [pltpu.VMEM((6, *wide), F32), pltpu.VMEM(wide, F32), pltpu.VMEM((3, *wide), F32)],
    )(state, conduct, capacity, supply, tz, layer_map, *halos)
    strain = to_group(strain, 1)
    unit0 = to_group(unit0, 0)
    residual, *packs = call(
        residual_kernel, [tile] + pack_shapes(R_ROWS, R_ROWS, R_CORNERS)
    )(base, strain, layer_map)
    halos = exchange(packs)
    image, unit12, sums = call(
        flow_kernel,
        [tile, struct(2, EX - 2, EY, Z), struct(8, Z)],
        [pltpu.VMEM((3, *wide), F32), pltpu.VMEM((3, *wide), F32)],
    )(residual, state, faces, layer_map, *halos)
    unit12 = to_group(unit12, 0)
    res_solid, image_solid, sums = call(
        solid_kernel,
        [struct(3, 3, X, Y, Z), struct(3, 3, X, Y, Z), struct(8, Z)],
        [
            pltpu.VMEM((3, 3, *wide), F32),
            pltpu.VMEM((3, 3, *wide), F32),
            pltpu.VMEM((24, 8, Z), F32),
        ],
    )(residual, faces, unit0, unit12, sums, *halos)
    sums = total_over_devices(sums)
    vmem = pl.BlockSpec(memory_space=pltpu.VMEM)

    def finish(*refs):
        final_kernel(*refs, cells=cells)

    new_state, balance = pl.pallas_call(
        finish,
        out_shape=[tile, struct(8, Z)],
        in_specs=[pl.BlockSpec(memory_space=pltpu.SMEM)] + [vmem] * 5,
        out_specs=[vmem, vmem],
        compiler_params=pltpu.CompilerParams(vmem_limit_bytes=56 << 20),
    )(sums, state, residual, image, res_solid, image_solid)
    return new_state[None], balance[0, :2]


def solution(mesh):
    placed = (
        P("group", None, "gx", "gy", None),
        P("group", None, None, "gx", "gy", None),
        P("group", "gx", "gy", None),
        P("group", None, "gx", "gy", None),
        P("gx", "gy"),
        P(),
    )
    return jax.shard_map(
        body,
        mesh=mesh,
        in_specs=placed,
        out_specs=(P("group", None, "gx", "gy", None), P()),
        check_vma=False,
    )
```

```python
import jax
import jax.numpy as jnp
from jax import lax
from jax.experimental import pallas as pl
from jax.experimental.pallas import tpu as pltpu
from jax.sharding import PartitionSpec as P

AXES = ("group", "gx", "gy")
X, Y, Z = 16, 32, 128
OX, OY = 3, 4
EX, EY = X + 2 * OX, Y + 2 * OY
BETA = 0.5
BIOT = 0.8
F32 = jnp.float32

X_ROWS = [(f, r) for f in range(13) for r in range(1, (3 if f < 3 else 2) + 1)]
Y_ROWS = [(f, r) for f in range(13) for r in range(1, (3 if 3 <= f < 6 else 2) + 1)]
CORNER = [(1, 1), (1, 2), (2, 1), (2, 2), (1, 3), (3, 1)]
K_CORNERS = (
    [(f, i, j) for f in range(3) for i, j in CORNER[:4] + [(3, 1)]]
    + [(f, i, j) for f in range(3, 6) for i, j in CORNER[:4] + [(1, 3)]]
    + [(f, i, j) for f in range(6, 10) for i, j in CORNER[:3]]
)
R_ROWS = [(f, r) for f in range(3) for r in range(1, 4)]
R_CORNERS = [(f, i, j) for f in range(3) for i, j in CORNER]
AT_R = [len(R_ROWS) * X, len(R_ROWS) * X + len(R_CORNERS)]
AT_K = [AT_R[1] + len(R_CORNERS), AT_R[1] + len(R_CORNERS) + len(K_CORNERS)]
AT_Q = [AT_K[1] + len(K_CORNERS), AT_K[1] + len(K_CORNERS) + 3]
AT_U = AT_Q[1] + 3
Y_PACK = -(-(AT_U + 4) // 8) * 8
RIM = [0, 1, 2, 3, EX - 4, EX - 3, EX - 2, EX - 1]


def struct(*shape):
    return jax.ShapeDtypeStruct(shape, F32)


def call(kernel, outs, scratch=(), inputs=(), limit=26):
    count, left = inputs if inputs else (0, ())
    specs = [pl.BlockSpec(memory_space=pl.ANY if n in left else pltpu.VMEM) for n in range(count)]
    return pl.pallas_call(
        kernel,
        out_shape=outs,
        **({"in_specs": specs} if specs else {}),
        scratch_shapes=list(scratch),
        compiler_params=pltpu.CompilerParams(vmem_limit_bytes=limit << 20),
    )


def up_y(v):
    return pltpu.roll(v, v.shape[0] - 1, 0)


def down_y(v):
    return pltpu.roll(v, 1, 0)


def up_z(v):
    return pltpu.roll(v, Z - 1, 1)


def down_z(v):
    return pltpu.roll(v, 1, 1)


def lanes(rows):
    return lax.broadcasted_iota(jnp.int32, (rows, Z), 1)


def rows_of(rows):
    return lax.broadcasted_iota(jnp.int32, (rows, Z), 0)


def to_tile(v):
    return pltpu.roll(v, EY - OY, 0)[:Y]


def harmonic(a, b):
    return 2.0 * a * b / jnp.maximum(a + b, 1e-30)


def one_hot(map_ref):
    brick = lax.broadcasted_iota(jnp.int32, (Z, 3 * Z), 0)
    return jnp.where(brick == map_ref[...], 1.0, 0.0).astype(jnp.bfloat16)


def dot_split(v, hot, contract):
    high = v.astype(jnp.bfloat16)
    low = (v - high.astype(F32)).astype(jnp.bfloat16)
    dims = (((1,), (contract,)), ((), ()))
    return lax.dot_general(high, hot, dims, preferred_element_type=F32) + lax.dot_general(
        low, hot, dims, preferred_element_type=F32
    )


def spread(v, hot, k):
    return dot_split(v, hot[:, k * Z : (k + 1) * Z], 0)


def gather_up(ref, first, last, hot):
    total = None
    count = (last - first) * EY
    for k in range(3):
        v = ref[k, first:last].reshape(count, Z)
        part = dot_split(v, hot[:, k * Z : (k + 1) * Z], 1)
        total = part if total is None else total + part
    ones = jnp.ones((8, 3 * Z), jnp.bfloat16)
    counts = lax.dot_general(ones, hot, (((1,), (1,)), ((), ())), preferred_element_type=F32)
    return (total * (1.0 / counts[:1])).reshape(last - first, EY, Z)


def pack_x(source, rows, tails, heads):
    for n, (f, r) in enumerate(rows):
        tails[n] = source(f)[X - r]
        heads[n] = source(f)[r - 1]


def unpack_x(target, rows, low, up):
    for n, (f, r) in enumerate(rows):
        target(f)[OX - r, OY : OY + Y] = low[n]
        target(f)[OX + X - 1 + r, OY : OY + Y] = up[n]


def corner_at(side, i, j):
    row = OX - i if side[0] == 0 else OX + X - 1 + i
    column = OY - j if side[1] == 0 else OY + Y - 1 + j
    return row, slice(column, column + 1)


def x_faces(rows):
    return [struct(len(rows), Y, Z)] * 2


def loop(first, last, body, init=0):
    return lax.fori_loop(first, last, body, init)


def pack_kernel(state, conduct, capacity, bottom, tz, xt, xh, yt, yh):
    flow = lax.axis_index("group") == 0
    last = lanes(Y) == Z - 1

    def faces(x, carry):
        kz = [conduct[2, k, x] for k in range(3)]
        rolled = [up_z(v) for v in kz]
        ends = [rolled[1], rolled[2], bottom[x] * kz[2]]
        for k in range(3):
            end = jnp.where(flow, ends[k], kz[k])
            tz[k, x] = harmonic(kz[k], jnp.where(last, end, rolled[k]))
        return carry

    loop(0, X, faces)

    def source(f):
        if f < 6:
            return conduct.at[f // 3, f % 3]
        if f < 9:
            return tz.at[f - 6]
        return capacity if f == 9 else state.at[f - 10]

    pack_x(source, X_ROWS, xt, xh)
    for n, (f, r) in enumerate(Y_ROWS):
        yt[n] = source(f)[:, Y - r, :]
        yh[n] = source(f)[:, r - 1, :]


def lateral(faces, v_ref, c, i, v, fx_before):
    fx = faces[c, i] * (v - v_ref[c, i + 1])
    fy = faces[3 + c, i] * (v - up_y(v))
    return (fx - fx_before) + (fy - down_y(fy)), fx


def x_flux(faces, v_ref, i):
    return tuple(faces[c, i] * (v_ref[c, i] - v_ref[c, i + 1]) for c in range(3))


def flow_below(vs, last):
    rolled = [up_z(v) for v in vs]
    ends = [rolled[1], rolled[2], 0.0]
    return [jnp.where(last, ends[k], rolled[k]) for k in range(3)]


def flow_row(faces, v_ref, i, fx_before):
    last, first = lanes(EY) == Z - 1, lanes(EY) == 0
    vs = [v_ref[k, i] for k in range(3)]
    below = flow_below(vs, last)
    fz = [faces[6 + k, i] * (vs[k] - below[k]) for k in range(3)]
    moved = [down_z(v) for v in fz]
    ends = [0.0, moved[0], moved[1]]
    out, fx_now = [], []
    for k in range(3):
        side, fx = lateral(faces, v_ref, k, i, vs[k], fx_before[k])
        above = jnp.where(first, ends[k], moved[k])
        out.append(faces[9 + k, i] * vs[k] + side + (fz[k] - above))
        fx_now.append(fx)
    return out, tuple(fx_now)


def strain_row(v_ref, i):
    v0, v1, v2 = v_ref[0, i], v_ref[1, i], v_ref[2, i]
    low = jnp.where(lanes(EY) == Z - 1, 0.0, up_z(v2))
    return (v_ref[0, i + 1] - v0) + (up_y(v1) - v1) + (low - v2)


def solid_row(faces, v_ref, i, s_before, fx_before):
    last, first = lanes(EY) == Z - 1, lanes(EY) == 0
    e = strain_row(v_ref, i)
    s = faces[9, i] * e
    grad = [s_before - s, down_y(s) - s, jnp.where(first, 0.0, down_z(s)) - s]
    out, fx_now = [], []
    for c in range(3):
        v = v_ref[c, i]
        side, fx = lateral(faces, v_ref, c, i, v, fx_before[c])
        fz = faces[6 + c, i] * (v - jnp.where(last, 0.0, up_z(v)))
        above = jnp.where(first, 0.0, down_z(fz))
        out.append((side + (fz - above)) + grad[c])
        fx_now.append(fx)
    return out, e, s, tuple(fx_now)


BESIDE = [(1, -1, Y), (1, X - 1, Y), (1, -1, 0), (1, X - 1, 0)]
BESIDE += [(0, X, -1), (0, 0, -1), (0, X, Y - 1), (0, 0, Y - 1)]


def first_kernel(state, conduct, capacity, supply, tz, layer_map, *refs):
    xl, xu, yl, yu, faces, base, strain, unit, rim, beside, keep, caps, field = refs
    flow = lax.axis_index("group") == 0

    def target(f):
        if f < 6:
            return keep.at[f]
        if f < 9:
            return faces.at[f]
        return caps if f == 9 else field.at[f - 10]

    def place(x, carry):
        at = slice(OY, OY + Y)
        for f in range(6):
            keep[f, OX + x, at] = conduct[f // 3, f % 3, x]
        for k in range(3):
            faces[6 + k, OX + x, at] = tz[k, x]
            field[k, OX + x, at] = state[k, x]
        caps[OX + x, at] = capacity[x]
        return carry

    loop(0, X, place)
    unpack_x(target, X_ROWS, xl, xu)
    for n, (f, r) in enumerate(Y_ROWS):
        target(f)[OX : OX + X, OY - r, :] = yl[n]
        target(f)[OX : OX + X, OY + Y - 1 + r, :] = yu[n]
    field[1, OX - 1, OY + Y : OY + Y + 1] = jnp.zeros((1, Z), F32)
    field[0, OX + X, OY - 1 : OY] = jnp.zeros((1, Z), F32)
    for n, i in enumerate(RIM):
        rim[:, n] = keep[:, i]
    for n, (c, x, y) in enumerate(BESIDE):
        beside[n : n + 1] = field[c, OX + x, OY + y : OY + y + 1]

    def lateral_faces(i, carry):
        for c in range(3):
            faces[c, i] = harmonic(keep[c, i], keep[c, i + 1])
            here = keep[3 + c, i]
            faces[3 + c, i] = harmonic(here, up_y(here))
        return carry

    loop(0, EX - 1, lateral_faces)

    @pl.when(flow)
    def _():
        hot = one_hot(layer_map)
        bricks = caps[1 : EX - 1].reshape((EX - 2) * EY, Z)
        for k in range(3):
            faces[9 + k, 1 : EX - 1] = (spread(bricks, hot, k) + BETA).reshape(EX - 2, EY, Z)

        def row(i, fx_before):
            image, fx = flow_row(faces, field, i, fx_before)
            for k in range(3):
                base[k, i - OX] = (
                    supply[k, i - OX] + BETA * state[k, i - OX] - to_tile(image[k])
                )
            return fx

        loop(OX, OX + X, row, x_flux(faces, field, OX - 1))
        unit[...] = gather_up(field, 1, EX - 1, hot)

    @pl.when(jnp.logical_not(flow))
    def _():
        faces[9] = caps[...]

        def row(i, carry):
            image, e, s, fx = solid_row(faces, field, i, carry[0], carry[1])
            for c in range(3):
                base[c, i - OX] = supply[c, i - OX] - to_tile(image[c])
            strain[i - OX] = to_tile(e)
            return s, fx

        before = faces[9, OX - 1] * strain_row(field, OX - 1)
        loop(OX, OX + X, row, (before, x_flux(faces, field, OX - 1)))


def residual_kernel(base, strain, layer_map, residual, xt, xh):
    flow = lax.axis_index("group") == 0

    @pl.when(flow)
    def _():
        hot = one_hot(layer_map)
        e = strain[...].reshape(X * Y, Z)
        for k in range(3):
            residual[k] = base[k] - BIOT * spread(e, hot, k).reshape(X, Y, Z)

    @pl.when(jnp.logical_not(flow))
    def _():
        residual[...] = base[...]

    pack_x(lambda f: residual.at[f], R_ROWS, xt, xh)


def relay_kernel(residual, xl, xu, kl, ku, unit, yt, yh):
    for out, edge in ((yt, lambda j: Y - j), (yh, lambda j: j - 1)):
        for n, (f, r) in enumerate(R_ROWS):
            out[n * X : (n + 1) * X] = residual[f, :, edge(r), :]
        for side, (r_halo, k_halo) in enumerate(((xl, kl), (xu, ku))):
            for n, (f, i, j) in enumerate(R_CORNERS):
                at = AT_R[side] + n
                out[at : at + 1] = r_halo[R_ROWS.index((f, i)), edge(j) : edge(j) + 1]
            for n, (f, i, j) in enumerate(K_CORNERS):
                at = AT_K[side] + n
                out[at : at + 1] = k_halo[X_ROWS.index((f, i)), edge(j) : edge(j) + 1]
            for n, (i, j) in enumerate(CORNER[:3]):
                at, row = AT_Q[side] + n, (OX - i if side == 0 else OX + X - 1 + i) - 1
                out[at : at + 1] = unit[row, OY + edge(j) : OY + edge(j) + 1]
            for c in range(2):
                at = AT_U + 2 * side + c
                out[at : at + 1] = k_halo[X_ROWS.index((10 + c, 1)), edge(1) : edge(1) + 1]


def fetch(pairs, sem):
    copies = [pltpu.make_async_copy(a, b, sem.at[n]) for n, (a, b) in enumerate(pairs)]
    for copy in copies:
        copy.start()
    return copies


def fold(v):
    return jnp.sum(v.reshape(v.shape[0] // 8, 8, Z), axis=0)


def spread_sums(totals, start):
    lane = lanes(8)
    row = jnp.zeros((8, Z), F32)
    first = rows_of(8) == 0
    for n, total in enumerate(totals):
        row = jnp.where(first & (lane == start + n), jnp.sum(total), row)
    return row


def tile_rows():
    at = rows_of(EY)
    return (at >= OY) & (at < OY + Y)


def fill(residual, target, halos):
    xl, xu, yl, yu = halos

    def place(x, carry):
        for k in range(3):
            target[k, OX + x, OY : OY + Y] = residual[k, x]
        return carry

    loop(0, X, place)
    unpack_x(lambda f: target.at[f], R_ROWS, xl, xu)
    for n, (f, r) in enumerate(R_ROWS):
        target[f, OX : OX + X, OY - r, :] = yl[n * X : (n + 1) * X]
        target[f, OX : OX + X, OY + Y - 1 + r, :] = yu[n * X : (n + 1) * X]
    for v, pack in enumerate((yl, yu)):
        for h in range(2):
            for n, (f, i, j) in enumerate(R_CORNERS):
                row, column = corner_at((h, v), i, j)
                target[f, row, column] = pack[AT_R[h] + n : AT_R[h] + n + 1]


def complete(faces, rim, halos, hot):
    order = []
    for v, pack in enumerate(halos[2:]):
        for h in range(2):
            for n, (f, i, j) in enumerate(K_CORNERS):
                row, column = corner_at((h, v), i, j)
                value = pack[AT_K[h] + n : AT_K[h] + n + 1]
                if f < 6:
                    rim[f, RIM.index(row), column] = value
                elif f < 9:
                    faces[f, row, column] = value
                else:
                    order.append((row, column, value))
    for c in range(3):
        for n in (0, 1, 2, 4, 5, 6):
            faces[c, RIM[n]] = harmonic(rim[c, n], rim[c, n + 1])
        for n in (1, 2, 5, 6):
            here = rim[3 + c, n]
            faces[3 + c, RIM[n]] = harmonic(here, up_y(here))
    if hot is None:
        for row, column, value in order:
            faces[9, row, column] = value
    else:
        values = [value for _, _, value in order]
        values += [jnp.zeros((1, Z), F32)] * (16 - len(values))
        caps = jnp.concatenate(values, axis=0)
        for k in range(3):
            storage = spread(caps, hot, k) + BETA
            for n, (row, column, _) in enumerate(order):
                faces[9 + k, row, column] = storage[n : n + 1]


def flow_kernel(residual, state, layer_map, faces_in, rim_in, *refs):
    halos, (image, unit, sums, faces, rim, field, product, sem) = refs[:4], refs[4:]
    flow = lax.axis_index("group") == 0
    sums[...] = jnp.zeros((8, Z), F32)

    @pl.when(flow)
    def _():
        copies = fetch(((faces_in, faces), (rim_in, rim)), sem)
        hot = one_hot(layer_map)
        fill(residual, field, halos)
        for copy in copies:
            copy.wait()
        complete(faces, rim, halos, hot)

        def row(i, fx_before):
            out, fx = flow_row(faces, field, i, fx_before)
            for k in range(3):
                product[k, i] = out[k]
            return fx

        loop(1, EX - 1, row, x_flux(faces, field, 0))
        unit[0] = gather_up(field, 1, EX - 1, hot)
        unit[1] = gather_up(product, 1, EX - 1, hot)

        def dots(i, acc):
            acc = list(acc)
            inside, last = tile_rows(), lanes(EY) == Z - 1

            def add(n, v):
                acc[n] = acc[n] + fold(jnp.where(inside, v, 0.0))

            ws = [product[k, i] for k in range(3)]
            below = flow_below(ws, last)
            g = m1 = m2 = m3 = cr = cw = 0.0
            for k in range(3):
                r, w = field[k, i], ws[k]
                image[k, i - OX] = to_tile(w)
                dx, dy, dz = w - product[k, i + 1], w - up_y(w), w - below[k]
                cf = faces[9 + k, i]
                g = g + r * r
                m1 = m1 + r * w
                m2 = m2 + w * w
                cr = cr + cf * r
                cw = cw + cf * w
                m3 = m3 + (
                    faces[k, i] * dx * dx
                    + faces[3 + k, i] * dy * dy
                    + faces[6 + k, i] * dz * dz
                    + cf * w * w
                )
            for n, v in enumerate((g, m1, m2, m3, cr, cw)):
                add(n, v)
            weight = jnp.where(last, faces[8, i], 0.0)
            add(6, weight * field[2, i])
            add(7, weight * ws[2])
            acc[8] = acc[8] + fold(to_tile(weight) * state[2, i - OX])
            return tuple(acc)

        zero = jnp.zeros((8, Z), F32)
        sums[...] = spread_sums(loop(OX, OX + X, dots, (zero,) * 9), 0)


PAIRS = [(0, 0), (0, 1), (0, 2), (1, 1), (1, 2), (2, 2)]


def solid_kernel(residual, beside, sums_in, faces_in, rim_in, unit0_in, unit12, *refs):
    halos, refs = refs[:4], refs[4:]
    res_out, image, sums, faces, rim, unit0, field, product, acc, sem = refs
    flow = lax.axis_index("group") == 0
    everyone = sums.shape[0]
    sums[...] = jnp.broadcast_to(sums_in[:1], (everyone, Z))
    gx, gy = lax.axis_index("gx"), lax.axis_index("gy")
    gx_last, gy_last = lax.axis_size("gx") - 1, lax.axis_size("gy") - 1

    @pl.when(jnp.logical_not(flow))
    def _():
        copies = fetch(((faces_in, faces), (rim_in, rim), (unit0_in, unit0)), sem)
        fill(residual, field.at[0], halos)
        for copy in copies:
            copy.wait()
        complete(faces, rim, halos, None)
        yl, yu = halos[2:]
        for v, pack in enumerate((yl, yu)):
            for h in range(2):
                for n, (i, j) in enumerate(CORNER[:3]):
                    row, column = corner_at((h, v), i, j)
                    unit0[row - 1, column] = pack[AT_Q[h] + n : AT_Q[h] + n + 1]
        u1 = [yu[AT_U + 1 : AT_U + 2]] + [beside[n : n + 1] for n in (1, 2, 3)]
        u0 = [yl[AT_U + 2 : AT_U + 3]] + [beside[n : n + 1] for n in (5, 6, 7)]
        for u, (x, y) in zip(u1, ((0, Y - 1), (X, Y - 1), (0, -1), (X, -1))):
            row, column = OX + x, slice(OY + y, OY + y + 1)
            field[0, 0, row, column] = field[0, 0, row, column] - faces[9, row - 1, column] * u
        for u, (x, y) in zip(u0, ((X - 1, 0), (-1, 0), (X - 1, Y), (-1, Y))):
            row, column = OX + x, slice(OY + y, OY + y + 1)
            before = slice(OY + y - 1, OY + y)
            field[0, 1, row, column] = field[0, 1, row, column] - faces[9, row, before] * u
        at = rows_of(EY)
        in_y = ((at >= OY) | (gy > 0)) & ((at < OY + Y) | (gy < gy_last))

        def in_grid(i):
            in_x = ((i >= OX) | (gx > 0)) & ((i < OX + X) | (gx < gx_last))
            return in_y & in_x

        def loads(i, carry):
            first, ok = lanes(EY) == 0, in_grid(i)
            for a in range(3):
                q_ref = unit0 if a == 0 else unit12.at[a - 1]
                q = q_ref[i - 1]
                push = [
                    BIOT * (q_ref[i - 2] - q),
                    BIOT * (down_y(q) - q),
                    BIOT * (jnp.where(first, 0.0, down_z(q)) - q),
                ]
                for c in range(3):
                    v = push[c] + field[a, c, i] if a == 0 else push[c]
                    field[a, c, i] = jnp.where(ok, v, 0.0)
            return carry

        loop(OX - 1, OX + X + 2, loads)

        for a in range(3):
            f_ref = field.at[a]

            def row(i, carry):
                out, e, s, fx = solid_row(faces, f_ref, i, carry[0], carry[1])
                ok = in_grid(i)
                for c in range(3):
                    product[a, c, i] = jnp.where(ok, out[c], 0.0)
                return s, fx

            before = faces[9, OX - 1] * strain_row(f_ref, OX - 1)
            loop(OX, OX + X + 1, row, (before, x_flux(faces, f_ref, OX - 1)))

        acc[...] = jnp.zeros(acc.shape, F32)

        def dots(i, carry):
            inside, last = tile_rows(), lanes(EY) == Z - 1

            def add(n, v):
                acc[n] = acc[n] + fold(jnp.where(inside, v, 0.0))

            strains = [strain_row(product.at[a], i) for a in range(3)]
            modulus = faces[9, i]
            for n, (a, b) in enumerate(PAIRS):
                add(18 + n, modulus * strains[a] * strains[b])
            for c in range(3):
                rs = [field[a, c, i] for a in range(3)]
                ws = [product[a, c, i] for a in range(3)]
                for a in range(3):
                    res_out[a, c, i - OX] = to_tile(rs[a])
                    image[a, c, i - OX] = to_tile(ws[a])
                dx = [ws[a] - product[a, c, i + 1] for a in range(3)]
                dy = [w - up_y(w) for w in ws]
                dz = [w - jnp.where(last, 0.0, up_z(w)) for w in ws]
                fx = [faces[c, i] * d for d in dx]
                fy = [faces[3 + c, i] * d for d in dy]
                fz = [faces[6 + c, i] * d for d in dz]
                for n, (a, b) in enumerate(PAIRS):
                    add(n, rs[a] * rs[b])
                    add(6 + n, rs[a] * ws[b])
                    add(12 + n, ws[a] * ws[b])
                    add(18 + n, fx[a] * dx[b] + fy[a] * dy[b] + fz[a] * dz[b])
            return carry

        loop(OX, OX + X, dots)
        own = spread_sums([acc[n] for n in range(24)], 9)
        sums[...] = jnp.broadcast_to(own[:1], (everyone, Z))


def two_sum(a, b):
    s = a + b
    t = s - a
    return s, (a - (s - t)) + (b - t)


def quick(a, b):
    s = a + b
    return s, b - (s - a)


def halves(a):
    t = 4097.0 * a
    high = t - (t - a)
    return high, a - high


def two_product(a, b):
    p = a * b
    ah, al = halves(a)
    bh, bl = halves(b)
    return p, ((ah * bh - p) + ah * bl + al * bh) + al * bl


def pair_add(a, b):
    s, e = two_sum(a[0], b[0])
    return quick(s, e + (a[1] + b[1]))


def pair_less(a, b):
    return pair_add(a, (-b[0], -b[1]))


def pair_times(a, b):
    p, e = two_product(a[0], b[0])
    return quick(p, e + (a[0] * b[1] + a[1] * b[0]))


def pair_over(a, b):
    q = a[0] / b[0]
    rest = pair_less(a, pair_times(b, (q, jnp.zeros_like(q))))
    return quick(q, rest[0] / b[0])


def krylov(g, m1, m2, m3):
    a0 = pair_over(g, m1)
    h = pair_times(a0, pair_over(m2, m1))
    one = (jnp.ones_like(a0[0]), jnp.zeros_like(a0[0]))
    rho = pair_less(h, one)[0]
    third = pair_times(pair_times(a0, a0), pair_over(m3, m1))
    sigma = pair_less(third, pair_times(h, h))[0]
    more = (rho > 1e-9) & (sigma > 1e-9)
    a1 = jnp.where(more, a0[0] * rho / jnp.where(more, sigma, 1.0), 0.0)
    return a0[0] + a1 * h[0], -a0[0] * a1


def final_kernel(sums, state, res_flow, image_flow, res_solid, image_solid, out, balance, *, cells):
    flow = lax.axis_index("group") == 0
    total = (sums[...], jnp.zeros(sums.shape, F32))
    while total[0].shape[0] > 8:
        half = total[0].shape[0] // 2
        total = pair_add([v[:half] for v in total], [v[half:] for v in total])
    for step in (4, 2, 1):
        total = pair_add(total, [pltpu.roll(v, step, 0) for v in total])

    def number(n):
        return tuple(jnp.broadcast_to(v[:1, n : n + 1], (8, Z)) for v in total)

    c0, c1 = krylov(number(0), number(1), number(2), number(3))
    columns = cells // (3 * Z)
    outflow = (number(8)[0] + c0 * number(6)[0] + c1 * number(7)[0]) / columns
    stored = (c0 * number(4)[0] + c1 * number(5)[0]) / cells
    balance[...] = jnp.where(lanes(8) == 0, outflow, stored)

    def tall(v):
        return jnp.concatenate([v] * (Y // 8), axis=0)

    @pl.when(flow)
    def _():
        s0, s1 = tall(c0), tall(c1)

        def row(x, carry):
            for k in range(3):
                out[k, x] = state[k, x] + s0 * res_flow[k, x] + s1 * image_flow[k, x]
            return carry

        loop(0, X, row)

    @pl.when(jnp.logical_not(flow))
    def _():
        zero = jnp.zeros((8, Z), F32)
        weights = [
            (jnp.ones((8, Z), F32), zero),
            (2.0 * c0, zero),
            (2.0 * c1, zero),
            two_product(c0, c0),
            two_product(2.0 * c0, c1),
            two_product(c1, c1),
        ]
        moments = []
        for start in (9, 15, 21, 27):
            total = number(start)
            for n in range(1, 6):
                total = pair_add(total, pair_times(weights[n], number(start + n)))
            moments.append(total)
        d0, d1 = krylov(*moments)
        scale_r = [tall(d0), tall(d0 * c0), tall(d0 * c1)]
        scale_w = [tall(d1), tall(d1 * c0), tall(d1 * c1)]

        def row(x, carry):
            for c in range(3):
                v = state[c, x]
                for a in range(3):
                    v = v + scale_r[a] * res_solid[a, c, x] + scale_w[a] * image_solid[a, c, x]
                out[c, x] = v
            return carry

        loop(0, X, row)


def grid_shift(value, dx, dy):
    groups, rows, columns = (lax.axis_size(a) for a in AXES)
    pairs = []
    for g in range(groups):
        for i in range(rows):
            for j in range(columns):
                if 0 <= i + dx < rows and 0 <= j + dy < columns:
                    here = (g * rows + i) * columns + j
                    pairs.append((here, here + dx * columns + dy))
    return lax.ppermute(value, AXES, pairs)


def exchange_x(tails, heads):
    return [grid_shift(tails, 1, 0), grid_shift(heads, -1, 0)]


def exchange_y(tails, heads):
    return [grid_shift(tails, 0, 1), grid_shift(heads, 0, -1)]


def to_group(value, source):
    rows, columns = lax.axis_size("gx"), lax.axis_size("gy")
    count = rows * columns
    pairs = [(source * count + n, (1 - source) * count + n) for n in range(count)]
    return lax.ppermute(value, AXES, pairs)


def body(state, conduct, capacity, supply, flags, layer_map):
    state, conduct, capacity, supply = state[0], conduct[0], capacity[0], supply[0]
    layer_map = layer_map.reshape(1, 3 * Z)
    cells = X * Y * 3 * Z * lax.axis_size("gx") * lax.axis_size("gy")
    bottom = jnp.broadcast_to(flags.astype(F32)[:, :, None], (X, Y, Z))
    tile = struct(3, X, Y, Z)
    wide = (EX, EY, Z)

    y_face = struct(len(Y_ROWS), X, Z)
    tz, xt, xh, yt, yh = call(pack_kernel, [tile] + x_faces(X_ROWS) + [y_face] * 2)(
        state, conduct, capacity, bottom
    )
    k_halos = exchange_x(xt, xh) + exchange_y(yt, yh)
    faces, base, strain, unit0, rim, beside = call(
        first_kernel,
        [
            struct(12, *wide),
            tile,
            struct(X, Y, Z),
            struct(EX - 2, EY, Z),
            struct(6, len(RIM), EY, Z),
            struct(8, Z),
        ],
        [pltpu.VMEM((6, *wide), F32), pltpu.VMEM(wide, F32), pltpu.VMEM((3, *wide), F32)],
    )(state, conduct, capacity, supply, tz, layer_map, *k_halos)
    strain = to_group(strain, 1)
    unit0 = to_group(unit0, 0)
    residual, xt, xh = call(residual_kernel, [tile] + x_faces(R_ROWS))(base, strain, layer_map)
    halos = exchange_x(xt, xh)
    yt, yh = call(relay_kernel, [struct(Y_PACK, Z)] * 2)(
        residual, *halos, k_halos[0], k_halos[1], unit0
    )
    halos = halos + exchange_y(yt, yh)
    field = pltpu.VMEM((3, *wide), F32)
    full_faces = [pltpu.VMEM((12, *wide), F32), pltpu.VMEM((6, len(RIM), EY, Z), F32)]
    image, unit12, sums = call(
        flow_kernel,
        [tile, struct(2, EX - 2, EY, Z), struct(8, Z)],
        full_faces + [field, field, pltpu.SemaphoreType.DMA((2,))],
        (9, (3, 4)),
    )(residual, state, layer_map, faces, rim, *halos)
    unit12 = to_group(unit12, 0)
    devices = lax.axis_size("group") * lax.axis_size("gx") * lax.axis_size("gy")
    res_solid, image_solid, sums = call(
        solid_kernel,
        [struct(3, 3, X, Y, Z), struct(3, 3, X, Y, Z), struct(devices, Z)],
        full_faces
        + [
            pltpu.VMEM((EX - 2, EY, Z), F32),
            pltpu.VMEM((3, 3, *wide), F32),
            pltpu.VMEM((3, 3, *wide), F32),
            pltpu.VMEM((24, 8, Z), F32),
            pltpu.SemaphoreType.DMA((3,)),
        ],
        (11, (3, 4, 5)),
    )(residual, beside, sums, faces, rim, unit0, unit12, *halos)
    sums = lax.all_to_all(sums, AXES, 0, 0, tiled=True)

    def finish(*refs):
        final_kernel(*refs, cells=cells)

    new_state, balance = call(finish, [tile, struct(8, Z)])(sums, state, residual, image, res_solid, image_solid)
    return new_state[None], balance[0, :2]


def solution(mesh):
    placed = (
        P("group", None, "gx", "gy", None),
        P("group", None, None, "gx", "gy", None),
        P("group", "gx", "gy", None),
        P("group", None, "gx", "gy", None),
        P("gx", "gy"),
        P(),
    )
    return jax.shard_map(
        body,
        mesh=mesh,
        in_specs=placed,
        out_specs=(P("group", None, "gx", "gy", None), P()),
        check_vma=False,
    )
```

```python
import jax
import jax.numpy as jnp
from jax import lax
from jax.experimental import pallas as pl
from jax.experimental.pallas import tpu as pltpu
from jax.sharding import PartitionSpec as P

AXES = ("group", "gx", "gy")
X, Y, Z = 16, 32, 128
OX, OY = 3, 4
EX, EY = X + 2 * OX, Y + 2 * OY
BETA = 0.5
BIOT = 0.8
F32 = jnp.float32

X_ROWS = [(f, r) for f in range(13) for r in range(1, (3 if f < 3 else 2 if f < 10 else 1) + 1)]
Y_ROWS = [
    (f, r) for f in range(13) for r in range(1, (3 if 3 <= f < 6 else 2 if f < 10 else 1) + 1)
]
CORNER = [(1, 1), (1, 2), (2, 1), (2, 2), (1, 3), (3, 1)]
K_CORNERS = (
    [(f, i, j) for f in range(3) for i, j in CORNER[:4] + [(3, 1)]]
    + [(f, i, j) for f in range(3, 6) for i, j in CORNER[:4] + [(1, 3)]]
    + [(f, i, j) for f in range(6, 10) for i, j in CORNER[:3]]
)
R_ROWS = [(f, r) for f in range(3) for r in range(1, 4)]
R_CORNERS = [(f, i, j) for f in range(3) for i, j in CORNER]
AT_R = [len(R_ROWS) * X, len(R_ROWS) * X + len(R_CORNERS)]
AT_K = [AT_R[1] + len(R_CORNERS), AT_R[1] + len(R_CORNERS) + len(K_CORNERS)]
AT_Q = [AT_K[1] + len(K_CORNERS), AT_K[1] + len(K_CORNERS) + 3]
AT_U = AT_Q[1] + 3
Y_PACK = -(-(AT_U + 4) // 8) * 8
Q_SLOT = [R_ROWS.index((0, 3)), R_ROWS.index((1, 3))]


def struct(*shape):
    return jax.ShapeDtypeStruct(shape, F32)


def call(kernel, outs, scratch=(), left=(), count=0, cost=None, limit=20):
    extra = {}
    if left:
        extra["in_specs"] = [
            pl.BlockSpec(memory_space=pltpu.HBM if n in left else pltpu.VMEM) for n in range(count)
        ]
    if cost:
        extra["cost_estimate"] = pl.CostEstimate(
            flops=cost, bytes_accessed=cost, transcendentals=0
        )
    return pl.pallas_call(
        kernel,
        out_shape=outs,
        scratch_shapes=list(scratch),
        compiler_params=pltpu.CompilerParams(vmem_limit_bytes=limit << 20),
        **extra,
    )


def up_y(v):
    return pltpu.roll(v, v.shape[0] - 1, 0)


def down_y(v):
    return pltpu.roll(v, 1, 0)


def up_z(v):
    return pltpu.roll(v, Z - 1, 1)


def down_z(v):
    return pltpu.roll(v, 1, 1)


def lanes(rows):
    return lax.broadcasted_iota(jnp.int32, (rows, Z), 1)


def rows_of(rows):
    return lax.broadcasted_iota(jnp.int32, (rows, Z), 0)


def to_tile(v):
    return pltpu.roll(v, EY - OY, 0)[:Y]


def harmonic(a, b):
    return 2.0 * a * b / jnp.maximum(a + b, 1e-30)


def one_hot(map_ref):
    brick = lax.broadcasted_iota(jnp.int32, (Z, 3 * Z), 0)
    return jnp.where(brick == map_ref[...], 1.0, 0.0).astype(jnp.bfloat16)


def dot_split(v, hot, contract):
    high = v.astype(jnp.bfloat16)
    low = (v - high.astype(F32)).astype(jnp.bfloat16)
    dims = (((1,), (contract,)), ((), ()))
    return lax.dot_general(high, hot, dims, preferred_element_type=F32) + lax.dot_general(
        low, hot, dims, preferred_element_type=F32
    )


def spread(v, hot, k):
    return dot_split(v, hot[:, k * Z : (k + 1) * Z], 0)


def gather_up(parts, hot):
    total = None
    for k, v in enumerate(parts):
        part = dot_split(v, hot[:, k * Z : (k + 1) * Z], 1)
        total = part if total is None else total + part
    ones = jnp.ones((8, 3 * Z), jnp.bfloat16)
    counts = lax.dot_general(ones, hot, (((1,), (1,)), ((), ())), preferred_element_type=F32)
    return total * (1.0 / counts[:1])


def gather_wide(ref, hot):
    rows = EX - 2
    parts = [ref[k, 1 : EX - 1].reshape(rows * EY, Z) for k in range(3)]
    return gather_up(parts, hot).reshape(rows, EY, Z)


def fetch(pairs, sem, start=0):
    copies = [pltpu.make_async_copy(a, b, sem.at[start + n]) for n, (a, b) in enumerate(pairs)]
    for copy in copies:
        copy.start()
    return copies


def pack_x(source, rows, tails, heads):
    for n, (f, r) in enumerate(rows):
        tails[n] = source(f)[X - r]
        heads[n] = source(f)[r - 1]


def unpack_x(target, rows, low, up):
    for n, (f, r) in enumerate(rows):
        target(f)[OX - r, OY : OY + Y] = low[n]
        target(f)[OX + X - 1 + r, OY : OY + Y] = up[n]


def corner_at(side, i, j):
    row = OX - i if side[0] == 0 else OX + X - 1 + i
    column = OY - j if side[1] == 0 else OY + Y - 1 + j
    return row, slice(column, column + 1)


def x_faces(rows):
    return [struct(len(rows), Y, Z)] * 2


def loop(first, last, body, init=0):
    return lax.fori_loop(first, last, body, init)


def pack_kernel(flags_in, state_in, conduct_in, capacity_in, tz, xt, xh, yt, yh, *scratch):
    flags, state, conduct, capacity, bottom, sem = scratch
    flow = lax.axis_index("group") == 0
    last = lanes(Y) == Z - 1
    early = [(flags_in, flags)] + [(conduct_in.at[2, k], conduct.at[2, k]) for k in range(3)]
    late = [(conduct_in.at[d, k], conduct.at[d, k]) for d in range(2) for k in range(3)]
    late += [(state_in.at[k], state.at[k]) for k in range(3)] + [(capacity_in, capacity)]
    early = fetch(early, sem)
    late = fetch(late, sem, len(early))
    for copy in early:
        copy.wait()
    eye = jnp.where(
        lax.broadcasted_iota(jnp.int32, (Y, Y), 0) == lax.broadcasted_iota(jnp.int32, (Y, Y), 1),
        1.0,
        0.0,
    ).astype(jnp.bfloat16)
    columns = lax.dot_general(
        eye,
        flags[...].astype(F32).astype(jnp.bfloat16),
        (((1,), (1,)), ((), ())),
        preferred_element_type=F32,
    )
    for x in range(X):
        bottom[x] = jnp.broadcast_to(columns[:, x : x + 1], (Y, Z))

    def faces(x, carry):
        kz = [conduct[2, k, x] for k in range(3)]
        rolled = [up_z(v) for v in kz]
        ends = [rolled[1], rolled[2], bottom[x] * kz[2]]
        for k in range(3):
            end = jnp.where(flow, ends[k], kz[k])
            tz[k, x] = harmonic(kz[k], jnp.where(last, end, rolled[k]))
        return carry

    loop(0, X, faces)
    for copy in late:
        copy.wait()

    def source(f):
        if f < 6:
            return conduct.at[f // 3, f % 3]
        if f < 9:
            return tz.at[f - 6]
        return capacity if f == 9 else state.at[f - 10]

    pack_x(source, X_ROWS, xt, xh)
    for n, (f, r) in enumerate(Y_ROWS):
        yt[n] = source(f)[:, Y - r, :]
        yh[n] = source(f)[:, r - 1, :]


class Faces:
    def __init__(self, x, y, z, own):
        self.x, self.y, self.z, self.own = x, y, z, own


def faces_in(ref, shift=0):
    return Faces(*[lambda c, i, d=d: ref[3 * d + c, i - shift] for d in range(4)])


def lateral(faces, v_ref, c, i, v, fx_before):
    fx = faces.x(c, i) * (v - v_ref[c, i + 1])
    fy = faces.y(c, i) * (v - up_y(v))
    return (fx - fx_before) + (fy - down_y(fy)), fx


def x_flux(faces, v_ref, i):
    return tuple(faces.x(c, i) * (v_ref[c, i] - v_ref[c, i + 1]) for c in range(3))


def flow_below(vs, last):
    rolled = [up_z(v) for v in vs]
    ends = [rolled[1], rolled[2], 0.0]
    return [jnp.where(last, ends[k], rolled[k]) for k in range(3)]


def flow_row(faces, v_ref, i, fx_before):
    last, first = lanes(EY) == Z - 1, lanes(EY) == 0
    vs = [v_ref[k, i] for k in range(3)]
    below = flow_below(vs, last)
    fz = [faces.z(k, i) * (vs[k] - below[k]) for k in range(3)]
    moved = [down_z(v) for v in fz]
    ends = [0.0, moved[0], moved[1]]
    out, fx_now = [], []
    for k in range(3):
        side, fx = lateral(faces, v_ref, k, i, vs[k], fx_before[k])
        above = jnp.where(first, ends[k], moved[k])
        out.append(faces.own(k, i) * vs[k] + side + (fz[k] - above))
        fx_now.append(fx)
    return out, tuple(fx_now)


def strain_row(v_ref, i):
    v0, v1, v2 = v_ref[0, i], v_ref[1, i], v_ref[2, i]
    low = jnp.where(lanes(EY) == Z - 1, 0.0, up_z(v2))
    return (v_ref[0, i + 1] - v0) + (up_y(v1) - v1) + (low - v2)


def solid_row(faces, v_ref, i, s_before, fx_before):
    last, first = lanes(EY) == Z - 1, lanes(EY) == 0
    e = strain_row(v_ref, i)
    s = faces.own(0, i) * e
    grad = [s_before - s, down_y(s) - s, jnp.where(first, 0.0, down_z(s)) - s]
    out, fx_now = [], []
    for c in range(3):
        v = v_ref[c, i]
        side, fx = lateral(faces, v_ref, c, i, v, fx_before[c])
        fz = faces.z(c, i) * (v - jnp.where(last, 0.0, up_z(v)))
        above = jnp.where(first, 0.0, down_z(fz))
        out.append((side + (fz - above)) + grad[c])
        fx_now.append(fx)
    return out, e, s, tuple(fx_now)


BESIDE = [(1, -1, Y), (1, X - 1, Y), (1, -1, 0), (1, X - 1, 0)]
BESIDE += [(0, X, -1), (0, 0, -1), (0, X, Y - 1), (0, 0, Y - 1)]


def place_tile(conduct, capacity, keep, caps):
    at = slice(OY, OY + Y)

    def row(x, carry):
        for f in range(6):
            keep[f, OX + x, at] = conduct[f // 3, f % 3, x]
        caps[OX + x, at] = capacity[x]
        return carry

    loop(0, X, row)


def interior_kernel(state, conduct, capacity, tz, layer_map, faces, unit, keep, caps):
    flow = lax.axis_index("group") == 0
    place_tile(conduct, capacity, keep, caps)

    def row(i, carry):
        lateral_faces(keep, faces, i)
        for k in range(3):
            faces[6 + k, i, OY : OY + Y] = tz[k, i - OX]
        return carry

    loop(OX, OX + X, row)

    @pl.when(flow)
    def _():
        hot = one_hot(layer_map)
        bricks = caps[OX : OX + X].reshape(X * EY, Z)
        for k in range(3):
            faces[9 + k, OX : OX + X] = (spread(bricks, hot, k) + BETA).reshape(X, EY, Z)
        parts = [state[k].reshape(X * Y, Z) for k in range(3)]
        unit[...] = gather_up(parts, hot).reshape(X, Y, Z)


def lateral_faces(keep, faces, i):
    for c in range(3):
        faces[c, i] = harmonic(keep[c, i], keep[c, i + 1])
        here = keep[3 + c, i]
        faces[3 + c, i] = harmonic(here, up_y(here))
    return 0


def first_kernel(state, conduct, capacity, supply, faces_ref, xl, xu, yl, yu, *refs):
    base, strain, beside, sides, own, field = refs
    flow = lax.axis_index("group") == 0

    def place(x, carry):
        for c in range(3):
            field[c, OX + x, OY : OY + Y] = state[c, x]
        for f in range(6):
            sides[f, OX + x] = faces_ref[f, OX + x]
        return carry

    loop(0, X, place)
    for c in range(3):
        n = X_ROWS.index((10 + c, 1))
        field[c, OX - 1, OY : OY + Y] = xl[n]
        field[c, OX + X, OY : OY + Y] = xu[n]
        n = Y_ROWS.index((10 + c, 1))
        field[c, OX : OX + X, OY - 1, :] = yl[n]
        field[c, OX : OX + X, OY + Y, :] = yu[n]
        n = X_ROWS.index((c, 1))
        at = slice(OY, OY + Y)
        sides[c, OX - 1, at] = harmonic(xl[n], conduct[0, c, 0])
        sides[c, OX + X - 1, at] = harmonic(conduct[0, c, X - 1], xu[n])
        n = Y_ROWS.index((3 + c, 1))
        sides[3 + c, OX : OX + X, OY - 1, :] = harmonic(yl[n], conduct[1, c, :, 0, :])
        sides[3 + c, OX : OX + X, OY + Y - 1, :] = harmonic(conduct[1, c, :, Y - 1, :], yu[n])
    field[1, OX - 1, OY + Y : OY + Y + 1] = jnp.zeros((1, Z), F32)
    field[0, OX + X, OY - 1 : OY] = jnp.zeros((1, Z), F32)
    for n, (c, x, y) in enumerate(BESIDE):
        beside[n : n + 1] = field[c, OX + x, OY + y : OY + y + 1]
    inner = faces_in(faces_ref)
    outer = faces_in(sides)

    @pl.when(flow)
    def _():
        faces = Faces(outer.x, outer.y, inner.z, inner.own)

        def row(i, fx_before):
            image, fx = flow_row(faces, field, i, fx_before)
            for k in range(3):
                base[k, i - OX] = (
                    supply[k, i - OX] + BETA * state[k, i - OX] - to_tile(image[k])
                )
            return fx

        loop(OX, OX + X, row, x_flux(faces, field, OX - 1))

    @pl.when(jnp.logical_not(flow))
    def _():
        def place(x, carry):
            own[OX + x, OY : OY + Y] = capacity[x]
            return carry

        loop(0, X, place)
        own[OX - 1, OY : OY + Y] = xl[X_ROWS.index((9, 1))]
        own[OX : OX + X, OY - 1, :] = yl[Y_ROWS.index((9, 1))]
        faces = Faces(outer.x, outer.y, inner.z, lambda c, i: own[i])

        def row(i, carry):
            image, e, s, fx = solid_row(faces, field, i, carry[0], carry[1])
            for c in range(3):
                base[c, i - OX] = supply[c, i - OX] - to_tile(image[c])
            strain[i - OX] = to_tile(e)
            return s, fx

        before = faces.own(0, OX - 1) * strain_row(field, OX - 1)
        loop(OX, OX + X, row, (before, x_flux(faces, field, OX - 1)))


def halo_kernel(conduct, capacity, tz, layer_map, xl, xu, yl, yu, faces, rim, keep, caps):
    flow = lax.axis_index("group") == 0

    def target(f):
        if f < 6:
            return keep.at[f]
        return faces.at[f] if f < 9 else caps

    place_tile(conduct, capacity, keep, caps)

    def place(x, carry):
        for k in range(3):
            faces[6 + k, OX + x, OY : OY + Y] = tz[k, x]
        return carry

    loop(0, X, place)
    for n, (f, r) in enumerate(X_ROWS):
        if f < 10:
            target(f)[OX - r, OY : OY + Y] = xl[n]
            target(f)[OX + X - 1 + r, OY : OY + Y] = xu[n]
    for n, (f, r) in enumerate(Y_ROWS):
        if f < 10:
            target(f)[OX : OX + X, OY - r, :] = yl[n]
            target(f)[OX : OX + X, OY + Y - 1 + r, :] = yu[n]
    loop(0, EX - 1, lambda i, carry: lateral_faces(keep, faces, i))
    for n, i in enumerate(K_RIM):
        for f in range(6):
            rim[f, n] = keep[f, i]

    @pl.when(flow)
    def _():
        hot = one_hot(layer_map)
        bricks = caps[1 : EX - 1].reshape((EX - 2) * EY, Z)
        for k in range(3):
            faces[9 + k, 1 : EX - 1] = (spread(bricks, hot, k) + BETA).reshape(EX - 2, EY, Z)

    @pl.when(jnp.logical_not(flow))
    def _():
        faces[9] = caps[...]


BESIDE = [(1, -1, Y), (1, X - 1, Y), (1, -1, 0), (1, X - 1, 0)]
BESIDE += [(0, X, -1), (0, 0, -1), (0, X, Y - 1), (0, 0, Y - 1)]
RIM = [0, 1, 2, EX - 4, EX - 3, EX - 2]
K_RIM = [0, 1, 2, 3, EX - 4, EX - 3, EX - 2, EX - 1]


def residual_kernel(base, strain, unit, layer_map, residual, xt, xh):
    flow = lax.axis_index("group") == 0

    @pl.when(flow)
    def _():
        hot = one_hot(layer_map)
        e = strain[...].reshape(X * Y, Z)
        for k in range(3):
            residual[k] = base[k] - BIOT * spread(e, hot, k).reshape(X, Y, Z)

    @pl.when(jnp.logical_not(flow))
    def _():
        residual[...] = base[...]

    pack_x(lambda f: residual.at[f], R_ROWS, xt, xh)

    @pl.when(jnp.logical_not(flow))
    def _():
        for depth, n in enumerate(Q_SLOT):
            xt[n] = unit[X - 1 - depth]
            xh[n] = unit[depth]


def relay_kernel(residual, unit, xl, xu, kl, ku, yt, yh):
    flow = lax.axis_index("group") == 0
    for out, edge in ((yt, lambda j: Y - j), (yh, lambda j: j - 1)):
        for n, (f, r) in enumerate(R_ROWS):
            out[n * X : (n + 1) * X] = residual[f, :, edge(r), :]
        for side, (r_halo, k_halo) in enumerate(((xl, kl), (xu, ku))):
            for n, (f, i, j) in enumerate(R_CORNERS):
                at = AT_R[side] + n
                out[at : at + 1] = r_halo[R_ROWS.index((f, i)), edge(j) : edge(j) + 1]
            for n, (f, i, j) in enumerate(K_CORNERS):
                at = AT_K[side] + n
                out[at : at + 1] = k_halo[X_ROWS.index((f, i)), edge(j) : edge(j) + 1]
            for n, (i, j) in enumerate(CORNER[:3]):
                at = AT_Q[side] + n
                out[at : at + 1] = r_halo[Q_SLOT[i - 1], edge(j) : edge(j) + 1]
            for c in range(2):
                at = AT_U + 2 * side + c
                out[at : at + 1] = k_halo[X_ROWS.index((10 + c, 1)), edge(1) : edge(1) + 1]

    @pl.when(jnp.logical_not(flow))
    def _():
        for out, edge in ((yt, lambda j: Y - j), (yh, lambda j: j - 1)):
            for depth, n in enumerate(Q_SLOT):
                out[n * X : (n + 1) * X] = unit[:, edge(depth + 1), :]


def fold(v):
    return jnp.sum(v.reshape(v.shape[0] // 8, 8, Z), axis=0)


def spread_sums(found):
    lane = lanes(8)
    row = jnp.zeros((8, Z), F32)
    first = rows_of(8) == 0
    for n, total in found.items():
        row = jnp.where(first & (lane == n), jnp.sum(total), row)
    return row


def tile_rows():
    at = rows_of(EY)
    return (at >= OY) & (at < OY + Y)


def fill(residual, target, halos):
    xl, xu, yl, yu = halos

    def place(x, carry):
        for k in range(3):
            target[k, OX + x, OY : OY + Y] = residual[k, x]
        return carry

    loop(0, X, place)
    unpack_x(lambda f: target.at[f], R_ROWS, xl, xu)
    for n, (f, r) in enumerate(R_ROWS):
        target[f, OX : OX + X, OY - r, :] = yl[n * X : (n + 1) * X]
        target[f, OX : OX + X, OY + Y - 1 + r, :] = yu[n * X : (n + 1) * X]
    for v, pack in enumerate((yl, yu)):
        for h in range(2):
            for n, (f, i, j) in enumerate(R_CORNERS):
                row, column = corner_at((h, v), i, j)
                target[f, row, column] = pack[AT_R[h] + n : AT_R[h] + n + 1]


def complete(faces, rim, k_rim_in, k_rim, halos, hot):
    for n, i in enumerate(RIM):
        for f in range(6, 12):
            rim[f, n] = faces[f, i]
    k_rim[...] = k_rim_in[...]
    order = []
    for v, pack in enumerate(halos[2:]):
        for h in range(2):
            for n, (f, i, j) in enumerate(K_CORNERS):
                row, column = corner_at((h, v), i, j)
                value = pack[AT_K[h] + n : AT_K[h] + n + 1]
                if f < 6:
                    k_rim[f, K_RIM.index(row), column] = value
                elif f < 9:
                    rim[f, RIM.index(row), column] = value
                else:
                    order.append((RIM.index(row), column, value))
    for n, i in enumerate(RIM):
        m = K_RIM.index(i)
        for c in range(3):
            rim[c, n] = harmonic(k_rim[c, m], k_rim[c, m + 1])
            here = k_rim[3 + c, m]
            rim[3 + c, n] = harmonic(here, up_y(here))
    if hot is None:
        for row, column, value in order:
            rim[9, row, column] = value
    else:
        values = [value for _, _, value in order]
        values += [jnp.zeros((1, Z), F32)] * (16 - len(values))
        caps = jnp.concatenate(values, axis=0)
        for k in range(3):
            storage = spread(caps, hot, k) + BETA
            for n, (row, column, _) in enumerate(order):
                rim[9 + k, row, column] = storage[n : n + 1]


def row_parts(faces, rim):
    return faces_in(rim), faces_in(faces), faces_in(rim, EX - 7)


def run_rows(parts, first, last, body, init):
    low, middle, high = parts
    for i in range(first, OX):
        init = body(low, i, init)
    init = loop(max(first, OX), EX - 4, lambda i, carry: body(middle, i, carry), init)
    for i in range(EX - 4, last):
        init = body(high, i, init)
    return init


PAIRS = [(0, 0), (0, 1), (0, 2), (1, 1), (1, 2), (2, 2)]
FIRST_SUM = 9


def grid_mask(before, after):
    gx, gy = lax.axis_index("gx"), lax.axis_index("gy")
    gx_last, gy_last = lax.axis_size("gx") - 1, lax.axis_size("gy") - 1
    at = rows_of(EY)
    in_y = (at >= OY - jnp.where(gy > 0, before, 0)) & (
        at < OY + Y + jnp.where(gy < gy_last, after, 0)
    )

    def in_grid(i):
        in_x = ((i >= OX) | (gx > 0)) & ((i < OX + X) | (gx < gx_last))
        return in_y & in_x

    return in_grid


def load_rows(q_ref, target, added):
    in_grid = grid_mask(1, 2)

    def row(i, carry):
        first, ok = lanes(EY) == 0, in_grid(i)
        q = q_ref[i - 1]
        push = [
            BIOT * (q_ref[i - 2] - q),
            BIOT * (down_y(q) - q),
            BIOT * (jnp.where(first, 0.0, down_z(q)) - q),
        ]
        for c in range(3):
            v = push[c] + target[c, i] if added else push[c]
            target[c, i] = jnp.where(ok, v, 0.0)
        return carry

    loop(OX - 1, OX + X + 2, row)


def solid_image(parts, f_ref, p_ref):
    in_grid = grid_mask(0, 1)

    def row(faces, i, carry):
        out, _, s, fx = solid_row(faces, f_ref, i, carry[0], carry[1])
        ok = in_grid(i)
        for c in range(3):
            p_ref[c, i] = jnp.where(ok, out[c], 0.0)
        return s, fx

    before = parts[0].own(0, OX - 1) * strain_row(f_ref, OX - 1)
    run_rows(parts, OX, OX + X + 1, row, (before, x_flux(parts[0], f_ref, OX - 1)))


def gram_sums(faces, fields, products, pairs, acc):
    acc[...] = jnp.zeros(acc.shape, F32)
    vectors = range(len(fields))

    def row(i, carry):
        inside, last = tile_rows(), lanes(EY) == Z - 1

        def only(v):
            return jnp.where(inside, v, 0.0)

        def add(n, v):
            acc[n] = acc[n] + fold(v)

        strains = [strain_row(p, i) for p in products]
        modulus = only(faces[9, i])
        pushes = [modulus * e for e in strains]
        for n, (a, b) in enumerate(pairs):
            add(4 * n + 3, pushes[a] * strains[b])
        for c in range(3):
            ws = [p[c, i] for p in products]
            dx = [ws[a] - products[a][c, i + 1] for a in vectors]
            dy = [w - up_y(w) for w in ws]
            dz = [w - jnp.where(last, 0.0, up_z(w)) for w in ws]
            sx, sy, sz = (only(faces[3 * d + c, i]) for d in range(3))
            fx = [sx * d for d in dx]
            fy = [sy * d for d in dy]
            fz = [sz * d for d in dz]
            for n, (a, b) in enumerate(pairs):
                add(4 * n + 3, fx[a] * dx[b] + fy[a] * dy[b] + fz[a] * dz[b])
            rs = [only(f[c, i]) for f in fields]
            ws = [only(w) for w in ws]
            for n, (a, b) in enumerate(pairs):
                add(4 * n, rs[a] * rs[b])
                add(4 * n + 1, rs[a] * ws[b])
                add(4 * n + 2, ws[a] * ws[b])
        return carry

    loop(OX, OX + X, row)
    found = {}
    for n, pair in enumerate(pairs):
        for m in range(4):
            found[FIRST_SUM + 6 * m + PAIRS.index(pair)] = acc[4 * n + m]
    return found


def unit_surroundings(unit, halos, q):
    xl, xu, yl, yu = halos

    def place(x, carry):
        q[OX - 1 + x, OY : OY + Y] = unit[x]
        return carry

    loop(0, X, place)
    for depth, n in enumerate(Q_SLOT):
        q[OX - 2 - depth, OY : OY + Y] = xl[n]
        q[OX + X - 1 + depth, OY : OY + Y] = xu[n]
        rows = slice(n * X, (n + 1) * X)
        q[OX - 1 : OX - 1 + X, OY - 1 - depth, :] = yl[rows]
        q[OX - 1 : OX - 1 + X, OY + Y + depth, :] = yu[rows]
    for v, pack in enumerate((yl, yu)):
        for h in range(2):
            for n, (i, j) in enumerate(CORNER[:3]):
                row, column = corner_at((h, v), i, j)
                q[row - 1, column] = pack[AT_Q[h] + n : AT_Q[h] + n + 1]


def late_terms(faces, rim, field, beside, halos):
    yl, yu = halos[2:]

    def modulus(x, y):
        i, column = OX + x, slice(OY + y, OY + y + 1)
        return rim[9, RIM.index(i), column] if i in RIM else faces[9, i, column]

    u1 = [yu[AT_U + 1 : AT_U + 2]] + [beside[n : n + 1] for n in (1, 2, 3)]
    u0 = [yl[AT_U + 2 : AT_U + 3]] + [beside[n : n + 1] for n in (5, 6, 7)]
    for u, (x, y) in zip(u1, ((0, Y - 1), (X, Y - 1), (0, -1), (X, -1))):
        row, column = OX + x, slice(OY + y, OY + y + 1)
        field[0, row, column] = field[0, row, column] - modulus(x - 1, y) * u
    for u, (x, y) in zip(u0, ((X - 1, 0), (-1, 0), (X - 1, Y), (-1, Y))):
        row, column = OX + x, slice(OY + y, OY + y + 1)
        field[1, row, column] = field[1, row, column] - modulus(x, y - 1) * u


def image_kernel(residual, unit_old, beside, layer_map, *refs):
    halos, (faces, k_rim_in, rim, field, product, unit, sums, k_rim, q, acc) = refs[:4], refs[4:]
    flow = lax.axis_index("group") == 0
    fill(residual, field, halos)

    @pl.when(flow)
    def _():
        hot = one_hot(layer_map)
        complete(faces, rim, k_rim_in, k_rim, halos, hot)
        parts = row_parts(faces, rim)

        def row(view, i, fx_before):
            out, fx = flow_row(view, field, i, fx_before)
            for k in range(3):
                product[k, i] = out[k]
            return fx

        run_rows(parts, 1, EX - 1, row, x_flux(parts[0], field, 0))
        unit[0] = gather_wide(field, hot)
        unit[1] = gather_wide(product, hot)

    @pl.when(jnp.logical_not(flow))
    def _():
        complete(faces, rim, k_rim_in, k_rim, halos, None)
        late_terms(faces, rim, field, beside, halos)
        unit_surroundings(unit_old, halos, q)
        load_rows(q, field, True)
        solid_image(row_parts(faces, rim), field, product)
        sums[...] = spread_sums(gram_sums(faces, [field], [product], PAIRS[:1], acc))


def sums_kernel(field, product, faces, rim, unit, state, sums_in, *refs):
    sums, field12, product12, acc = refs
    flow = lax.axis_index("group") == 0
    everyone = sums.shape[0]

    @pl.when(flow)
    def _():
        def dots(i, acc):
            acc = list(acc)
            inside, last = tile_rows(), lanes(EY) == Z - 1

            def add(n, v):
                acc[n] = acc[n] + fold(jnp.where(inside, v, 0.0))

            ws = [product[k, i] for k in range(3)]
            below = flow_below(ws, last)
            g = m1 = m2 = m3 = cr = cw = 0.0
            for k in range(3):
                r, w = field[k, i], ws[k]
                dx, dy, dz = w - product[k, i + 1], w - up_y(w), w - below[k]
                cf = faces[9 + k, i]
                g = g + r * r
                m1 = m1 + r * w
                m2 = m2 + w * w
                cr = cr + cf * r
                cw = cw + cf * w
                m3 = m3 + (
                    faces[k, i] * dx * dx
                    + faces[3 + k, i] * dy * dy
                    + faces[6 + k, i] * dz * dz
                    + cf * w * w
                )
            for n, v in enumerate((g, m1, m2, m3, cr, cw)):
                add(n, v)
            weight = jnp.where(last, faces[8, i], 0.0)
            add(6, weight * field[2, i])
            add(7, weight * ws[2])
            acc[8] = acc[8] + fold(to_tile(weight) * state[2, i - OX])
            return tuple(acc)

        zero = jnp.zeros((8, Z), F32)
        found = dict(enumerate(loop(OX, OX + X, dots, (zero,) * FIRST_SUM)))
        sums[...] = jnp.broadcast_to(spread_sums(found)[:1], (everyone, Z))

    @pl.when(jnp.logical_not(flow))
    def _():
        fields = [field] + [field12.at[a] for a in range(2)]
        products = [product] + [product12.at[a] for a in range(2)]
        for a in range(2):
            load_rows(unit.at[a], fields[a + 1], False)
            solid_image(row_parts(faces, rim), fields[a + 1], products[a + 1])
        found = gram_sums(faces, fields, products, PAIRS[1:], acc)
        own = sums_in[:1] + spread_sums(found)[:1]
        sums[...] = jnp.broadcast_to(own, (everyone, Z))


def two_sum(a, b):
    s = a + b
    t = s - a
    return s, (a - (s - t)) + (b - t)


def quick(a, b):
    s = a + b
    return s, b - (s - a)


def halves(a):
    t = 4097.0 * a
    high = t - (t - a)
    return high, a - high


def two_product(a, b):
    p = a * b
    ah, al = halves(a)
    bh, bl = halves(b)
    return p, ((ah * bh - p) + ah * bl + al * bh) + al * bl


def pair_add(a, b):
    s, e = two_sum(a[0], b[0])
    return quick(s, e + (a[1] + b[1]))


def pair_less(a, b):
    return pair_add(a, (-b[0], -b[1]))


def pair_times(a, b):
    p, e = two_product(a[0], b[0])
    return quick(p, e + (a[0] * b[1] + a[1] * b[0]))


def pair_over(a, b):
    q = a[0] / b[0]
    rest = pair_less(a, pair_times(b, (q, jnp.zeros_like(q))))
    return quick(q, rest[0] / b[0])


def krylov(g, m1, m2, m3):
    a0 = pair_over(g, m1)
    h = pair_times(a0, pair_over(m2, m1))
    one = (jnp.ones_like(a0[0]), jnp.zeros_like(a0[0]))
    rho = pair_less(h, one)[0]
    third = pair_times(pair_times(a0, a0), pair_over(m3, m1))
    sigma = pair_less(third, pair_times(h, h))[0]
    more = (rho > 1e-9) & (sigma > 1e-9)
    a1 = jnp.where(more, a0[0] * rho / jnp.where(more, sigma, 1.0), 0.0)
    return a0[0] + a1 * h[0], -a0[0] * a1


def final_kernel(sums, state, field, product, field12, product12, out, balance, *, cells):
    flow = lax.axis_index("group") == 0
    total = (sums[...], jnp.zeros(sums.shape, F32))
    while total[0].shape[0] > 8:
        half = total[0].shape[0] // 2
        total = pair_add([v[:half] for v in total], [v[half:] for v in total])
    for step in (4, 2, 1):
        total = pair_add(total, [pltpu.roll(v, step, 0) for v in total])

    def number(n):
        return tuple(jnp.broadcast_to(v[:1, n : n + 1], (8, Z)) for v in total)

    c0, c1 = krylov(number(0), number(1), number(2), number(3))
    columns = cells // (3 * Z)
    outflow = (number(8)[0] + c0 * number(6)[0] + c1 * number(7)[0]) / columns
    stored = (c0 * number(4)[0] + c1 * number(5)[0]) / cells
    balance[...] = jnp.where(lanes(8) == 0, outflow, stored)

    def tall(v):
        return jnp.concatenate([v] * (EY // 8), axis=0)

    @pl.when(flow)
    def _():
        s0, s1 = tall(c0), tall(c1)

        def row(x, carry):
            for k in range(3):
                step = s0 * field[k, OX + x] + s1 * product[k, OX + x]
                out[k, x] = state[k, x] + to_tile(step)
            return carry

        loop(0, X, row)

    @pl.when(jnp.logical_not(flow))
    def _():
        zero = jnp.zeros((8, Z), F32)
        weights = [
            (jnp.ones((8, Z), F32), zero),
            (2.0 * c0, zero),
            (2.0 * c1, zero),
            two_product(c0, c0),
            two_product(2.0 * c0, c1),
            two_product(c1, c1),
        ]
        moments = []
        for m in range(4):
            start = FIRST_SUM + 6 * m
            total = number(start)
            for n in range(1, 6):
                total = pair_add(total, pair_times(weights[n], number(start + n)))
            moments.append(total)
        d0, d1 = krylov(*moments)
        scale_r = [tall(d0), tall(d0 * c0), tall(d0 * c1)]
        scale_w = [tall(d1), tall(d1 * c0), tall(d1 * c1)]

        def row(x, carry):
            for c in range(3):
                step = scale_r[0] * field[c, OX + x] + scale_w[0] * product[c, OX + x]
                for a in range(2):
                    step = step + scale_r[a + 1] * field12[a, c, OX + x]
                    step = step + scale_w[a + 1] * product12[a, c, OX + x]
                out[c, x] = state[c, x] + to_tile(step)
            return carry

        loop(0, X, row)


def grid_shift(value, dx, dy):
    groups, rows, columns = (lax.axis_size(a) for a in AXES)
    pairs = []
    for g in range(groups):
        for i in range(rows):
            for j in range(columns):
                if 0 <= i + dx < rows and 0 <= j + dy < columns:
                    here = (g * rows + i) * columns + j
                    pairs.append((here, here + dx * columns + dy))
    return lax.ppermute(value, AXES, pairs)


def exchange_x(tails, heads):
    return [grid_shift(tails, 1, 0), grid_shift(heads, -1, 0)]


def exchange_y(tails, heads):
    return [grid_shift(tails, 0, 1), grid_shift(heads, 0, -1)]


def to_group(value, source):
    rows, columns = lax.axis_size("gx"), lax.axis_size("gy")
    count = rows * columns
    pairs = [(source * count + n, (1 - source) * count + n) for n in range(count)]
    return lax.ppermute(value, AXES, pairs)


def body(state, conduct, capacity, supply, flags, layer_map):
    state, conduct, capacity, supply = state[0], conduct[0], capacity[0], supply[0]
    layer_map = layer_map.reshape(1, 3 * Z)
    cells = X * Y * 3 * Z * lax.axis_size("gx") * lax.axis_size("gy")
    devices = lax.axis_size("group") * lax.axis_size("gx") * lax.axis_size("gy")
    tile = struct(3, X, Y, Z)
    brick = struct(X, Y, Z)
    wide = (EX, EY, Z)
    full = struct(3, *wide)

    y_face = struct(len(Y_ROWS), X, Z)
    tz, xt, xh, yt, yh = call(
        pack_kernel,
        [tile] + x_faces(X_ROWS) + [y_face] * 2,
        [
            pltpu.VMEM((X, Y), jnp.int32),
            pltpu.VMEM((3, X, Y, Z), F32),
            pltpu.VMEM((3, 3, X, Y, Z), F32),
            pltpu.VMEM((X, Y, Z), F32),
            pltpu.VMEM((X, Y, Z), F32),
            pltpu.SemaphoreType.DMA((14,)),
        ],
        left=(0, 1, 2, 3),
        limit=58,
        count=4,
    )(flags, state, conduct, capacity)
    k_halos = exchange_x(xt, xh) + exchange_y(yt, yh)
    wide_faces = struct(12, *wide)
    tables = [pltpu.VMEM((6, *wide), F32), pltpu.VMEM(wide, F32)]
    inner, unit0 = call(interior_kernel, [wide_faces, brick], tables, cost=30_000_000)(
        state, conduct, capacity, tz, layer_map
    )
    unit0 = to_group(unit0, 0)
    base, strain, beside = call(
        first_kernel,
        [tile, brick, struct(8, Z)],
        tables + [pltpu.VMEM((3, *wide), F32)],
    )(state, conduct, capacity, supply, inner, *k_halos)
    strain = to_group(strain, 1)
    faces, k_rim = call(
        halo_kernel, [wide_faces, struct(6, len(K_RIM), EY, Z)], tables, cost=30_000_000
    )(conduct, capacity, tz, layer_map, *k_halos)
    residual, xt, xh = call(residual_kernel, [tile] + x_faces(R_ROWS))(
        base, strain, unit0, layer_map
    )
    halos = exchange_x(xt, xh)
    yt, yh = call(relay_kernel, [struct(Y_PACK, Z)] * 2)(
        residual, unit0, *halos, k_halos[0], k_halos[1]
    )
    halos = halos + exchange_y(yt, yh)
    rim, field, product, unit12, sums = call(
        image_kernel,
        [struct(12, len(RIM), EY, Z), full, full, struct(2, EX - 2, EY, Z), struct(8, Z)],
        [
            pltpu.VMEM((6, len(K_RIM), EY, Z), F32),
            pltpu.VMEM((EX - 2, EY, Z), F32),
            pltpu.VMEM((4, 8, Z), F32),
        ],
    )(residual, unit0, beside, layer_map, *halos, faces, k_rim)
    unit12 = to_group(unit12, 0)
    sums, field12, product12 = call(
        sums_kernel,
        [struct(devices, Z), struct(2, 3, *wide), struct(2, 3, *wide)],
        [pltpu.VMEM((20, 8, Z), F32)],
    )(field, product, faces, rim, unit12, state, sums)
    sums = lax.all_to_all(sums, AXES, 0, 0, tiled=True)

    def finish(*refs):
        final_kernel(*refs, cells=cells)

    new_state, balance = call(finish, [tile, struct(8, Z)])(
        sums, state, field, product, field12, product12
    )
    return new_state[None], balance[0, :2]


def solution(mesh):
    placed = (
        P("group", None, "gx", "gy", None),
        P("group", None, None, "gx", "gy", None),
        P("group", "gx", "gy", None),
        P("group", None, "gx", "gy", None),
        P("gx", "gy"),
        P(),
    )
    return jax.shard_map(
        body,
        mesh=mesh,
        in_specs=placed,
        out_specs=(P("group", None, "gx", "gy", None), P()),
        check_vma=False,
    )
```

```python
import jax
import jax.numpy as jnp
from jax import lax
from jax.experimental import pallas as pl
from jax.experimental.pallas import tpu as pltpu
from jax.sharding import PartitionSpec as P

AXES = ("group", "gx", "gy")
X, Y, Z = 16, 32, 128
OX, OY = 3, 4
EX, EY = X + 2 * OX, Y + 2 * OY
BETA = 0.5
BIOT = 0.8
F32 = jnp.float32

X_ROWS = [(f, r) for f in range(13) for r in range(1, (3 if f < 3 else 2 if f < 10 else 1) + 1)]
Y_ROWS = [
    (f, r) for f in range(13) for r in range(1, (3 if 3 <= f < 6 else 2 if f < 10 else 1) + 1)
]
CORNER = [(1, 1), (1, 2), (2, 1), (2, 2), (1, 3), (3, 1)]
K_CORNERS = (
    [(f, i, j) for f in range(3) for i, j in CORNER[:4] + [(3, 1)]]
    + [(f, i, j) for f in range(3, 6) for i, j in CORNER[:4] + [(1, 3)]]
    + [(f, i, j) for f in range(6, 10) for i, j in CORNER[:3]]
)
R_ROWS = [(f, r) for f in range(3) for r in range(1, 4)]
R_CORNERS = [(f, i, j) for f in range(3) for i, j in CORNER]
AT_R = [len(R_ROWS) * X, len(R_ROWS) * X + len(R_CORNERS)]
AT_K = [AT_R[1] + len(R_CORNERS), AT_R[1] + len(R_CORNERS) + len(K_CORNERS)]
AT_Q = [AT_K[1] + len(K_CORNERS), AT_K[1] + len(K_CORNERS) + 3]
AT_U = AT_Q[1] + 3
Y_PACK = -(-(AT_U + 4) // 8) * 8
Q_SLOT = [R_ROWS.index((0, 3)), R_ROWS.index((1, 3))]


def struct(*shape):
    return jax.ShapeDtypeStruct(shape, F32)


def call(kernel, outs, scratch=(), left=(), count=0, cost=None, limit=20, scalars=()):
    extra = {}
    if left:
        extra["in_specs"] = [
            pl.BlockSpec(memory_space=pltpu.HBM if n in left else pltpu.VMEM) for n in range(count)
        ]
    if scalars:
        extra["out_specs"] = [
            pl.BlockSpec(memory_space=pltpu.SMEM if n in scalars else pltpu.VMEM)
            for n in range(len(outs))
        ]
    if cost:
        extra["cost_estimate"] = pl.CostEstimate(
            flops=cost, bytes_accessed=cost, transcendentals=0
        )
    return pl.pallas_call(
        kernel,
        out_shape=outs,
        scratch_shapes=list(scratch),
        compiler_params=pltpu.CompilerParams(vmem_limit_bytes=limit << 20),
        **extra,
    )


def up_y(v):
    return pltpu.roll(v, v.shape[0] - 1, 0)


def down_y(v):
    return pltpu.roll(v, 1, 0)


def up_z(v):
    return pltpu.roll(v, Z - 1, 1)


def down_z(v):
    return pltpu.roll(v, 1, 1)


def lanes(rows):
    return lax.broadcasted_iota(jnp.int32, (rows, Z), 1)


def rows_of(rows):
    return lax.broadcasted_iota(jnp.int32, (rows, Z), 0)


def to_tile(v):
    return pltpu.roll(v, EY - OY, 0)[:Y]


def harmonic(a, b):
    return 2.0 * a * b / jnp.maximum(a + b, 1e-30)


def one_hot(map_ref):
    brick = lax.broadcasted_iota(jnp.int32, (Z, 3 * Z), 0)
    return jnp.where(brick == map_ref[...], 1.0, 0.0).astype(jnp.bfloat16)


def dot_split(v, hot, contract):
    high = v.astype(jnp.bfloat16)
    low = (v - high.astype(F32)).astype(jnp.bfloat16)
    dims = (((1,), (contract,)), ((), ()))
    return lax.dot_general(high, hot, dims, preferred_element_type=F32) + lax.dot_general(
        low, hot, dims, preferred_element_type=F32
    )


def spread(v, hot, k):
    return dot_split(v, hot[:, k * Z : (k + 1) * Z], 0)


def gather_up(parts, hot):
    total = None
    for k, v in enumerate(parts):
        part = dot_split(v, hot[:, k * Z : (k + 1) * Z], 1)
        total = part if total is None else total + part
    ones = jnp.ones((8, 3 * Z), jnp.bfloat16)
    counts = lax.dot_general(ones, hot, (((1,), (1,)), ((), ())), preferred_element_type=F32)
    return total * (1.0 / counts[:1])


def gather_wide(ref, hot):
    rows = EX - 2
    parts = [ref[k, 1 : EX - 1].reshape(rows * EY, Z) for k in range(3)]
    return gather_up(parts, hot).reshape(rows, EY, Z)


def fetch(pairs, sem, start=0):
    copies = [pltpu.make_async_copy(a, b, sem.at[start + n]) for n, (a, b) in enumerate(pairs)]
    for copy in copies:
        copy.start()
    return copies


def pack_x(source, rows, tails, heads):
    for n, (f, r) in enumerate(rows):
        tails[n] = source(f)[X - r]
        heads[n] = source(f)[r - 1]


def unpack_x(target, rows, low, up):
    for n, (f, r) in enumerate(rows):
        target(f)[OX - r, OY : OY + Y] = low[n]
        target(f)[OX + X - 1 + r, OY : OY + Y] = up[n]


def corner_at(side, i, j):
    row = OX - i if side[0] == 0 else OX + X - 1 + i
    column = OY - j if side[1] == 0 else OY + Y - 1 + j
    return row, slice(column, column + 1)


def x_faces(rows):
    return [struct(len(rows), Y, Z)] * 2


def loop(first, last, body, init=0, unroll=4):
    steps = (last - first) // unroll

    def step(n, carry):
        for m in range(unroll):
            carry = body(first + n * unroll + m, carry)
        return carry

    init = lax.fori_loop(0, steps, step, init)
    for i in range(first + steps * unroll, last):
        init = body(i, init)
    return init


def pack_kernel(flags_in, state_in, conduct_in, capacity_in, tz, xt, xh, yt, yh, *scratch):
    flags, state, conduct, capacity, bottom, sem = scratch
    flow = lax.axis_index("group") == 0
    last = lanes(Y) == Z - 1
    early = [(flags_in, flags)] + [(conduct_in.at[2, k], conduct.at[2, k]) for k in range(3)]
    late = [(conduct_in.at[d, k], conduct.at[d, k]) for d in range(2) for k in range(3)]
    late += [(state_in.at[k], state.at[k]) for k in range(3)] + [(capacity_in, capacity)]
    early = fetch(early, sem)
    late = fetch(late, sem, len(early))
    for copy in early:
        copy.wait()
    eye = jnp.where(
        lax.broadcasted_iota(jnp.int32, (Y, Y), 0) == lax.broadcasted_iota(jnp.int32, (Y, Y), 1),
        1.0,
        0.0,
    ).astype(jnp.bfloat16)
    columns = lax.dot_general(
        eye,
        flags[...].astype(F32).astype(jnp.bfloat16),
        (((1,), (1,)), ((), ())),
        preferred_element_type=F32,
    )
    for x in range(X):
        bottom[x] = jnp.broadcast_to(columns[:, x : x + 1], (Y, Z))

    def faces(x, carry):
        kz = [conduct[2, k, x] for k in range(3)]
        rolled = [up_z(v) for v in kz]
        ends = [rolled[1], rolled[2], bottom[x] * kz[2]]
        for k in range(3):
            end = jnp.where(flow, ends[k], kz[k])
            tz[k, x] = harmonic(kz[k], jnp.where(last, end, rolled[k]))
        return carry

    loop(0, X, faces)
    for copy in late:
        copy.wait()

    def source(f):
        if f < 6:
            return conduct.at[f // 3, f % 3]
        if f < 9:
            return tz.at[f - 6]
        return capacity if f == 9 else state.at[f - 10]

    pack_x(source, X_ROWS, xt, xh)
    for n, (f, r) in enumerate(Y_ROWS):
        yt[n] = source(f)[:, Y - r, :]
        yh[n] = source(f)[:, r - 1, :]


class Faces:
    def __init__(self, x, y, z, own):
        self.x, self.y, self.z, self.own = x, y, z, own


def faces_in(ref, shift=0):
    return Faces(*[lambda c, i, d=d: ref[3 * d + c, i - shift] for d in range(4)])


def lateral(faces, v_ref, c, i, v, fx_before):
    fx = faces.x(c, i) * (v - v_ref[c, i + 1])
    fy = faces.y(c, i) * (v - up_y(v))
    return (fx - fx_before) + (fy - down_y(fy)), fx


def x_flux(faces, v_ref, i):
    return tuple(faces.x(c, i) * (v_ref[c, i] - v_ref[c, i + 1]) for c in range(3))


def flow_below(vs, last):
    rolled = [up_z(v) for v in vs]
    ends = [rolled[1], rolled[2], 0.0]
    return [jnp.where(last, ends[k], rolled[k]) for k in range(3)]


def flow_row(faces, v_ref, i, fx_before):
    last, first = lanes(EY) == Z - 1, lanes(EY) == 0
    vs = [v_ref[k, i] for k in range(3)]
    below = flow_below(vs, last)
    fz = [faces.z(k, i) * (vs[k] - below[k]) for k in range(3)]
    moved = [down_z(v) for v in fz]
    ends = [0.0, moved[0], moved[1]]
    out, fx_now = [], []
    for k in range(3):
        side, fx = lateral(faces, v_ref, k, i, vs[k], fx_before[k])
        above = jnp.where(first, ends[k], moved[k])
        out.append(faces.own(k, i) * vs[k] + side + (fz[k] - above))
        fx_now.append(fx)
    return out, tuple(fx_now)


def strain_row(v_ref, i):
    v0, v1, v2 = v_ref[0, i], v_ref[1, i], v_ref[2, i]
    low = jnp.where(lanes(EY) == Z - 1, 0.0, up_z(v2))
    return (v_ref[0, i + 1] - v0) + (up_y(v1) - v1) + (low - v2)


def solid_row(faces, v_ref, i, s_before, fx_before):
    last, first = lanes(EY) == Z - 1, lanes(EY) == 0
    e = strain_row(v_ref, i)
    s = faces.own(0, i) * e
    grad = [s_before - s, down_y(s) - s, jnp.where(first, 0.0, down_z(s)) - s]
    out, fx_now = [], []
    for c in range(3):
        v = v_ref[c, i]
        side, fx = lateral(faces, v_ref, c, i, v, fx_before[c])
        fz = faces.z(c, i) * (v - jnp.where(last, 0.0, up_z(v)))
        above = jnp.where(first, 0.0, down_z(fz))
        out.append((side + (fz - above)) + grad[c])
        fx_now.append(fx)
    return out, e, s, tuple(fx_now)


BESIDE = [(1, -1, Y), (1, X - 1, Y), (1, -1, 0), (1, X - 1, 0)]
BESIDE += [(0, X, -1), (0, 0, -1), (0, X, Y - 1), (0, 0, Y - 1)]


def place_tile(conduct, capacity, keep, caps):
    at = slice(OY, OY + Y)

    def row(x, carry):
        for f in range(6):
            keep[f, OX + x, at] = conduct[f // 3, f % 3, x]
        caps[OX + x, at] = capacity[x]
        return carry

    loop(0, X, row)


def interior_kernel(state, conduct, capacity, tz, layer_map, faces, unit, keep, caps):
    flow = lax.axis_index("group") == 0
    place_tile(conduct, capacity, keep, caps)

    def row(i, carry):
        lateral_faces(keep, faces, i)
        for k in range(3):
            faces[6 + k, i, OY : OY + Y] = tz[k, i - OX]
        return carry

    loop(OX, OX + X, row)

    @pl.when(flow)
    def _():
        hot = one_hot(layer_map)
        bricks = caps[OX : OX + X].reshape(X * EY, Z)
        for k in range(3):
            faces[9 + k, OX : OX + X] = (spread(bricks, hot, k) + BETA).reshape(X, EY, Z)
        parts = [state[k].reshape(X * Y, Z) for k in range(3)]
        unit[...] = gather_up(parts, hot).reshape(X, Y, Z)


def lateral_faces(keep, faces, i):
    for c in range(3):
        faces[c, i] = harmonic(keep[c, i], keep[c, i + 1])
        here = keep[3 + c, i]
        faces[3 + c, i] = harmonic(here, up_y(here))
    return 0


def first_kernel(state, conduct, capacity, supply, faces_ref, xl, xu, yl, yu, *refs):
    base, strain, beside, sides, own, field = refs
    flow = lax.axis_index("group") == 0

    def place(x, carry):
        for c in range(3):
            field[c, OX + x, OY : OY + Y] = state[c, x]
        for f in range(6):
            sides[f, OX + x] = faces_ref[f, OX + x]
        return carry

    loop(0, X, place)
    for c in range(3):
        n = X_ROWS.index((10 + c, 1))
        field[c, OX - 1, OY : OY + Y] = xl[n]
        field[c, OX + X, OY : OY + Y] = xu[n]
        n = Y_ROWS.index((10 + c, 1))
        field[c, OX : OX + X, OY - 1, :] = yl[n]
        field[c, OX : OX + X, OY + Y, :] = yu[n]
        n = X_ROWS.index((c, 1))
        at = slice(OY, OY + Y)
        sides[c, OX - 1, at] = harmonic(xl[n], conduct[0, c, 0])
        sides[c, OX + X - 1, at] = harmonic(conduct[0, c, X - 1], xu[n])
        n = Y_ROWS.index((3 + c, 1))
        sides[3 + c, OX : OX + X, OY - 1, :] = harmonic(yl[n], conduct[1, c, :, 0, :])
        sides[3 + c, OX : OX + X, OY + Y - 1, :] = harmonic(conduct[1, c, :, Y - 1, :], yu[n])
    field[1, OX - 1, OY + Y : OY + Y + 1] = jnp.zeros((1, Z), F32)
    field[0, OX + X, OY - 1 : OY] = jnp.zeros((1, Z), F32)
    for n, (c, x, y) in enumerate(BESIDE):
        beside[n : n + 1] = field[c, OX + x, OY + y : OY + y + 1]
    inner = faces_in(faces_ref)
    outer = faces_in(sides)

    @pl.when(flow)
    def _():
        faces = Faces(outer.x, outer.y, inner.z, inner.own)

        def row(i, fx_before):
            image, fx = flow_row(faces, field, i, fx_before)
            for k in range(3):
                base[k, i - OX] = (
                    supply[k, i - OX] + BETA * state[k, i - OX] - to_tile(image[k])
                )
            return fx

        loop(OX, OX + X, row, x_flux(faces, field, OX - 1))

    @pl.when(jnp.logical_not(flow))
    def _():
        def place(x, carry):
            own[OX + x, OY : OY + Y] = capacity[x]
            return carry

        loop(0, X, place)
        own[OX - 1, OY : OY + Y] = xl[X_ROWS.index((9, 1))]
        own[OX : OX + X, OY - 1, :] = yl[Y_ROWS.index((9, 1))]
        faces = Faces(outer.x, outer.y, inner.z, lambda c, i: own[i])

        def row(i, carry):
            image, e, s, fx = solid_row(faces, field, i, carry[0], carry[1])
            for c in range(3):
                base[c, i - OX] = supply[c, i - OX] - to_tile(image[c])
            strain[i - OX] = to_tile(e)
            return s, fx

        before = faces.own(0, OX - 1) * strain_row(field, OX - 1)
        loop(OX, OX + X, row, (before, x_flux(faces, field, OX - 1)))


def halo_kernel(conduct, capacity, tz, layer_map, xl, xu, yl, yu, faces, rim, keep, caps):
    flow = lax.axis_index("group") == 0

    def target(f):
        if f < 6:
            return keep.at[f]
        return faces.at[f] if f < 9 else caps

    place_tile(conduct, capacity, keep, caps)

    def place(x, carry):
        for k in range(3):
            faces[6 + k, OX + x, OY : OY + Y] = tz[k, x]
        return carry

    loop(0, X, place)
    for n, (f, r) in enumerate(X_ROWS):
        if f < 10:
            target(f)[OX - r, OY : OY + Y] = xl[n]
            target(f)[OX + X - 1 + r, OY : OY + Y] = xu[n]
    for n, (f, r) in enumerate(Y_ROWS):
        if f < 10:
            target(f)[OX : OX + X, OY - r, :] = yl[n]
            target(f)[OX : OX + X, OY + Y - 1 + r, :] = yu[n]
    loop(0, EX - 1, lambda i, carry: lateral_faces(keep, faces, i))
    for n, i in enumerate(K_RIM):
        for f in range(6):
            rim[f, n] = keep[f, i]

    @pl.when(flow)
    def _():
        hot = one_hot(layer_map)
        bricks = caps[1 : EX - 1].reshape((EX - 2) * EY, Z)
        for k in range(3):
            faces[9 + k, 1 : EX - 1] = (spread(bricks, hot, k) + BETA).reshape(EX - 2, EY, Z)

    @pl.when(jnp.logical_not(flow))
    def _():
        faces[9] = caps[...]


BESIDE = [(1, -1, Y), (1, X - 1, Y), (1, -1, 0), (1, X - 1, 0)]
BESIDE += [(0, X, -1), (0, 0, -1), (0, X, Y - 1), (0, 0, Y - 1)]
RIM = [0, 1, 2, EX - 4, EX - 3, EX - 2]
K_RIM = [0, 1, 2, 3, EX - 4, EX - 3, EX - 2, EX - 1]


def residual_kernel(base, strain, unit, layer_map, residual, xt, xh):
    flow = lax.axis_index("group") == 0

    @pl.when(flow)
    def _():
        hot = one_hot(layer_map)
        e = strain[...].reshape(X * Y, Z)
        for k in range(3):
            residual[k] = base[k] - BIOT * spread(e, hot, k).reshape(X, Y, Z)

    @pl.when(jnp.logical_not(flow))
    def _():
        residual[...] = base[...]

    pack_x(lambda f: residual.at[f], R_ROWS, xt, xh)

    @pl.when(jnp.logical_not(flow))
    def _():
        for depth, n in enumerate(Q_SLOT):
            xt[n] = unit[X - 1 - depth]
            xh[n] = unit[depth]


def relay_kernel(residual, unit, xl, xu, kl, ku, yt, yh):
    flow = lax.axis_index("group") == 0
    for out, edge in ((yt, lambda j: Y - j), (yh, lambda j: j - 1)):
        for n, (f, r) in enumerate(R_ROWS):
            out[n * X : (n + 1) * X] = residual[f, :, edge(r), :]
        for side, (r_halo, k_halo) in enumerate(((xl, kl), (xu, ku))):
            for n, (f, i, j) in enumerate(R_CORNERS):
                at = AT_R[side] + n
                out[at : at + 1] = r_halo[R_ROWS.index((f, i)), edge(j) : edge(j) + 1]
            for n, (f, i, j) in enumerate(K_CORNERS):
                at = AT_K[side] + n
                out[at : at + 1] = k_halo[X_ROWS.index((f, i)), edge(j) : edge(j) + 1]
            for n, (i, j) in enumerate(CORNER[:3]):
                at = AT_Q[side] + n
                out[at : at + 1] = r_halo[Q_SLOT[i - 1], edge(j) : edge(j) + 1]
            for c in range(2):
                at = AT_U + 2 * side + c
                out[at : at + 1] = k_halo[X_ROWS.index((10 + c, 1)), edge(1) : edge(1) + 1]

    @pl.when(jnp.logical_not(flow))
    def _():
        for out, edge in ((yt, lambda j: Y - j), (yh, lambda j: j - 1)):
            for depth, n in enumerate(Q_SLOT):
                out[n * X : (n + 1) * X] = unit[:, edge(depth + 1), :]


def fold(v):
    return jnp.sum(v.reshape(v.shape[0] // 8, 8, Z), axis=0)


def spread_sums(found):
    lane = lanes(8)
    row = jnp.zeros((8, Z), F32)
    first = rows_of(8) == 0
    for n, total in found.items():
        row = jnp.where(first & (lane == n), jnp.sum(total), row)
    return row


def tile_rows():
    at = rows_of(EY)
    return (at >= OY) & (at < OY + Y)


def fill(residual, target, halos):
    xl, xu, yl, yu = halos

    def place(x, carry):
        for k in range(3):
            target[k, OX + x, OY : OY + Y] = residual[k, x]
        return carry

    loop(0, X, place)
    unpack_x(lambda f: target.at[f], R_ROWS, xl, xu)
    for n, (f, r) in enumerate(R_ROWS):
        target[f, OX : OX + X, OY - r, :] = yl[n * X : (n + 1) * X]
        target[f, OX : OX + X, OY + Y - 1 + r, :] = yu[n * X : (n + 1) * X]
    for v, pack in enumerate((yl, yu)):
        for h in range(2):
            for n, (f, i, j) in enumerate(R_CORNERS):
                row, column = corner_at((h, v), i, j)
                target[f, row, column] = pack[AT_R[h] + n : AT_R[h] + n + 1]


def complete(faces, rim, k_rim_in, k_rim, halos, hot):
    for n, i in enumerate(RIM):
        for f in range(6, 12):
            rim[f, n] = faces[f, i]
    k_rim[...] = k_rim_in[...]
    order = []
    for v, pack in enumerate(halos[2:]):
        for h in range(2):
            for n, (f, i, j) in enumerate(K_CORNERS):
                row, column = corner_at((h, v), i, j)
                value = pack[AT_K[h] + n : AT_K[h] + n + 1]
                if f < 6:
                    k_rim[f, K_RIM.index(row), column] = value
                elif f < 9:
                    rim[f, RIM.index(row), column] = value
                else:
                    order.append((RIM.index(row), column, value))
    for n, i in enumerate(RIM):
        m = K_RIM.index(i)
        for c in range(3):
            rim[c, n] = harmonic(k_rim[c, m], k_rim[c, m + 1])
            here = k_rim[3 + c, m]
            rim[3 + c, n] = harmonic(here, up_y(here))
    if hot is None:
        for row, column, value in order:
            rim[9, row, column] = value
    else:
        values = [value for _, _, value in order]
        values += [jnp.zeros((1, Z), F32)] * (16 - len(values))
        caps = jnp.concatenate(values, axis=0)
        for k in range(3):
            storage = spread(caps, hot, k) + BETA
            for n, (row, column, _) in enumerate(order):
                rim[9 + k, row, column] = storage[n : n + 1]


def row_parts(faces, rim):
    return faces_in(rim), faces_in(faces), faces_in(rim, EX - 7)


def run_rows(parts, first, last, body, init, unroll=3):
    low, middle, high = parts
    for i in range(first, OX):
        init = body(low, i, init)
    init = loop(max(first, OX), EX - 4, lambda i, carry: body(middle, i, carry), init, unroll)
    for i in range(EX - 4, last):
        init = body(high, i, init)
    return init


PAIRS = [(0, 0), (0, 1), (0, 2), (1, 1), (1, 2), (2, 2)]
FIRST_SUM = 9


def grid_mask(before, after):
    gx, gy = lax.axis_index("gx"), lax.axis_index("gy")
    gx_last, gy_last = lax.axis_size("gx") - 1, lax.axis_size("gy") - 1
    at = rows_of(EY)
    in_y = (at >= OY - jnp.where(gy > 0, before, 0)) & (
        at < OY + Y + jnp.where(gy < gy_last, after, 0)
    )

    def in_grid(i):
        in_x = ((i >= OX) | (gx > 0)) & ((i < OX + X) | (gx < gx_last))
        return in_y & in_x

    return in_grid


def load_rows(q_refs, targets, added):
    in_grid = grid_mask(1, 2)

    def row(i, carry):
        for q_ref, target in zip(q_refs, targets):
            load_row(q_ref, target, i, in_grid(i))
        return carry

    def load_row(q_ref, target, i, ok):
        first = lanes(EY) == 0
        q = q_ref[i - 1]
        push = [
            BIOT * (q_ref[i - 2] - q),
            BIOT * (down_y(q) - q),
            BIOT * (jnp.where(first, 0.0, down_z(q)) - q),
        ]
        for c in range(3):
            v = push[c] + target[c, i] if added else push[c]
            target[c, i] = jnp.where(ok, v, 0.0)

    loop(OX - 1, OX + X + 2, row)


def solid_image(parts, f_refs, p_refs, unroll):
    in_grid = grid_mask(0, 1)

    def row(faces, i, carry):
        ok, after = in_grid(i), []
        for f_ref, p_ref, (s, fx) in zip(f_refs, p_refs, carry):
            out, _, s, fx = solid_row(faces, f_ref, i, s, fx)
            for c in range(3):
                p_ref[c, i] = jnp.where(ok, out[c], 0.0)
            after.append((s, fx))
        return tuple(after)

    view = parts[0]
    start = [
        (view.own(0, OX - 1) * strain_row(f, OX - 1), x_flux(view, f, OX - 1)) for f in f_refs
    ]
    run_rows(parts, OX, OX + X + 1, row, tuple(start), unroll)


def gram_sums(faces, fields, products, pairs, acc):
    acc[...] = jnp.zeros(acc.shape, F32)
    vectors = range(len(fields))

    def row(i, carry):
        inside, last = tile_rows(), lanes(EY) == Z - 1

        def only(v):
            return jnp.where(inside, v, 0.0)

        def add(n, v):
            acc[n] = acc[n] + fold(v)

        strains = [strain_row(p, i) for p in products]
        modulus = only(faces[9, i])
        pushes = [modulus * e for e in strains]
        for n, (a, b) in enumerate(pairs):
            add(4 * n + 3, pushes[a] * strains[b])
        for c in range(3):
            ws = [p[c, i] for p in products]
            dx = [ws[a] - products[a][c, i + 1] for a in vectors]
            dy = [w - up_y(w) for w in ws]
            dz = [w - jnp.where(last, 0.0, up_z(w)) for w in ws]
            sx, sy, sz = (only(faces[3 * d + c, i]) for d in range(3))
            fx = [sx * d for d in dx]
            fy = [sy * d for d in dy]
            fz = [sz * d for d in dz]
            for n, (a, b) in enumerate(pairs):
                add(4 * n + 3, fx[a] * dx[b] + fy[a] * dy[b] + fz[a] * dz[b])
            rs = [only(f[c, i]) for f in fields]
            ws = [only(w) for w in ws]
            for n, (a, b) in enumerate(pairs):
                add(4 * n, rs[a] * rs[b])
                add(4 * n + 1, rs[a] * ws[b])
                add(4 * n + 2, ws[a] * ws[b])
        return carry

    loop(OX, OX + X, row, 0, 2)
    found = {}
    for n, pair in enumerate(pairs):
        for m in range(4):
            found[FIRST_SUM + 6 * m + PAIRS.index(pair)] = acc[4 * n + m]
    return found


def unit_surroundings(unit, halos, q):
    xl, xu, yl, yu = halos

    def place(x, carry):
        q[OX - 1 + x, OY : OY + Y] = unit[x]
        return carry

    loop(0, X, place)
    for depth, n in enumerate(Q_SLOT):
        q[OX - 2 - depth, OY : OY + Y] = xl[n]
        q[OX + X - 1 + depth, OY : OY + Y] = xu[n]
        rows = slice(n * X, (n + 1) * X)
        q[OX - 1 : OX - 1 + X, OY - 1 - depth, :] = yl[rows]
        q[OX - 1 : OX - 1 + X, OY + Y + depth, :] = yu[rows]
    for v, pack in enumerate((yl, yu)):
        for h in range(2):
            for n, (i, j) in enumerate(CORNER[:3]):
                row, column = corner_at((h, v), i, j)
                q[row - 1, column] = pack[AT_Q[h] + n : AT_Q[h] + n + 1]


def late_terms(faces, rim, field, beside, halos):
    yl, yu = halos[2:]

    def modulus(x, y):
        i, column = OX + x, slice(OY + y, OY + y + 1)
        return rim[9, RIM.index(i), column] if i in RIM else faces[9, i, column]

    u1 = [yu[AT_U + 1 : AT_U + 2]] + [beside[n : n + 1] for n in (1, 2, 3)]
    u0 = [yl[AT_U + 2 : AT_U + 3]] + [beside[n : n + 1] for n in (5, 6, 7)]
    for u, (x, y) in zip(u1, ((0, Y - 1), (X, Y - 1), (0, -1), (X, -1))):
        row, column = OX + x, slice(OY + y, OY + y + 1)
        field[0, row, column] = field[0, row, column] - modulus(x - 1, y) * u
    for u, (x, y) in zip(u0, ((X - 1, 0), (-1, 0), (X - 1, Y), (-1, Y))):
        row, column = OX + x, slice(OY + y, OY + y + 1)
        field[1, row, column] = field[1, row, column] - modulus(x, y - 1) * u


def image_kernel(residual, unit_old, beside, layer_map, *refs):
    halos, (faces, k_rim_in, rim, field, product, unit, sums, k_rim, q, acc) = refs[:4], refs[4:]
    flow = lax.axis_index("group") == 0
    fill(residual, field, halos)

    @pl.when(flow)
    def _():
        hot = one_hot(layer_map)
        complete(faces, rim, k_rim_in, k_rim, halos, hot)
        parts = row_parts(faces, rim)

        def row(view, i, fx_before):
            out, fx = flow_row(view, field, i, fx_before)
            for k in range(3):
                product[k, i] = out[k]
            return fx

        run_rows(parts, 1, EX - 1, row, x_flux(parts[0], field, 0))
        unit[0] = gather_wide(field, hot)
        unit[1] = gather_wide(product, hot)

    @pl.when(jnp.logical_not(flow))
    def _():
        complete(faces, rim, k_rim_in, k_rim, halos, None)
        late_terms(faces, rim, field, beside, halos)
        unit_surroundings(unit_old, halos, q)
        load_rows([q], [field], True)
        solid_image(row_parts(faces, rim), [field], [product], 3)
        sums[...] = spread_sums(gram_sums(faces, [field], [product], PAIRS[:1], acc))


def sums_kernel(field, product, faces, rim, unit, state, sums_in, *refs):
    sums, field12, product12, acc = refs
    flow = lax.axis_index("group") == 0
    everyone = sums.shape[0]

    @pl.when(flow)
    def _():
        def dots(i, acc):
            acc = list(acc)
            inside, last = tile_rows(), lanes(EY) == Z - 1

            def add(n, v):
                acc[n] = acc[n] + fold(jnp.where(inside, v, 0.0))

            ws = [product[k, i] for k in range(3)]
            below = flow_below(ws, last)
            g = m1 = m2 = m3 = cr = cw = 0.0
            for k in range(3):
                r, w = field[k, i], ws[k]
                dx, dy, dz = w - product[k, i + 1], w - up_y(w), w - below[k]
                cf = faces[9 + k, i]
                g = g + r * r
                m1 = m1 + r * w
                m2 = m2 + w * w
                cr = cr + cf * r
                cw = cw + cf * w
                m3 = m3 + (
                    faces[k, i] * dx * dx
                    + faces[3 + k, i] * dy * dy
                    + faces[6 + k, i] * dz * dz
                    + cf * w * w
                )
            for n, v in enumerate((g, m1, m2, m3, cr, cw)):
                add(n, v)
            weight = jnp.where(last, faces[8, i], 0.0)
            add(6, weight * field[2, i])
            add(7, weight * ws[2])
            acc[8] = acc[8] + fold(to_tile(weight) * state[2, i - OX])
            return tuple(acc)

        zero = jnp.zeros((8, Z), F32)
        found = dict(enumerate(loop(OX, OX + X, dots, (zero,) * FIRST_SUM, 2)))
        sums[...] = jnp.broadcast_to(spread_sums(found)[:1], (everyone, Z))

    @pl.when(jnp.logical_not(flow))
    def _():
        fields = [field] + [field12.at[a] for a in range(2)]
        products = [product] + [product12.at[a] for a in range(2)]
        load_rows([unit.at[a] for a in range(2)], fields[1:], False)
        solid_image(row_parts(faces, rim), fields[1:], products[1:], 2)
        found = gram_sums(faces, fields, products, PAIRS[1:], acc)
        own = sums_in[:1] + spread_sums(found)[:1]
        sums[...] = jnp.broadcast_to(own, (everyone, Z))


def two_sum(a, b):
    s = a + b
    t = s - a
    return s, (a - (s - t)) + (b - t)


def quick(a, b):
    s = a + b
    return s, b - (s - a)


def halves(a):
    t = 4097.0 * a
    high = t - (t - a)
    return high, a - high


def two_product(a, b):
    p = a * b
    ah, al = halves(a)
    bh, bl = halves(b)
    return p, ((ah * bh - p) + ah * bl + al * bh) + al * bl


def pair_add(a, b):
    s, e = two_sum(a[0], b[0])
    return quick(s, e + (a[1] + b[1]))


def pair_less(a, b):
    return pair_add(a, (-b[0], -b[1]))


def pair_times(a, b):
    p, e = two_product(a[0], b[0])
    return quick(p, e + (a[0] * b[1] + a[1] * b[0]))


def pair_over(a, b):
    q = a[0] / b[0]
    rest = pair_less(a, pair_times(b, (q, jnp.zeros_like(q))))
    return quick(q, rest[0] / b[0])


def krylov(g, m1, m2, m3):
    a0 = pair_over(g, m1)
    h = pair_times(a0, pair_over(m2, m1))
    one = (jnp.ones_like(a0[0]), jnp.zeros_like(a0[0]))
    rho = pair_less(h, one)[0]
    third = pair_times(pair_times(a0, a0), pair_over(m3, m1))
    sigma = pair_less(third, pair_times(h, h))[0]
    more = (rho > 1e-9) & (sigma > 1e-9)
    a1 = jnp.where(more, a0[0] * rho / jnp.where(more, sigma, 1.0), 0.0)
    return a0[0] + a1 * h[0], -a0[0] * a1


def final_kernel(sums, state, field, product, field12, product12, out, balance, *, cells):
    flow = lax.axis_index("group") == 0
    total = (sums[...], jnp.zeros(sums.shape, F32))
    while total[0].shape[0] > 8:
        half = total[0].shape[0] // 2
        total = pair_add([v[:half] for v in total], [v[half:] for v in total])
    for step in (4, 2, 1):
        total = pair_add(total, [pltpu.roll(v, step, 0) for v in total])

    def number(n):
        return tuple(jnp.broadcast_to(v[:1, n : n + 1], (8, Z)) for v in total)

    c0, c1 = krylov(number(0), number(1), number(2), number(3))
    columns = cells // (3 * Z)
    outflow = (number(8)[0] + c0 * number(6)[0] + c1 * number(7)[0]) / columns
    stored = (c0 * number(4)[0] + c1 * number(5)[0]) / cells
    balance[0] = outflow[0, 0]
    balance[1] = stored[0, 0]

    def tall(v):
        return jnp.concatenate([v] * (EY // 8), axis=0)

    @pl.when(flow)
    def _():
        s0, s1 = tall(c0), tall(c1)

        def row(x, carry):
            for k in range(3):
                step = s0 * field[k, OX + x] + s1 * product[k, OX + x]
                out[k, x] = state[k, x] + to_tile(step)
            return carry

        loop(0, X, row)

    @pl.when(jnp.logical_not(flow))
    def _():
        zero = jnp.zeros((8, Z), F32)
        weights = [
            (jnp.ones((8, Z), F32), zero),
            (2.0 * c0, zero),
            (2.0 * c1, zero),
            two_product(c0, c0),
            two_product(2.0 * c0, c1),
            two_product(c1, c1),
        ]
        moments = []
        for m in range(4):
            start = FIRST_SUM + 6 * m
            total = number(start)
            for n in range(1, 6):
                total = pair_add(total, pair_times(weights[n], number(start + n)))
            moments.append(total)
        d0, d1 = krylov(*moments)
        scale_r = [tall(d0), tall(d0 * c0), tall(d0 * c1)]
        scale_w = [tall(d1), tall(d1 * c0), tall(d1 * c1)]

        def row(x, carry):
            for c in range(3):
                step = scale_r[0] * field[c, OX + x] + scale_w[0] * product[c, OX + x]
                for a in range(2):
                    step = step + scale_r[a + 1] * field12[a, c, OX + x]
                    step = step + scale_w[a + 1] * product12[a, c, OX + x]
                out[c, x] = state[c, x] + to_tile(step)
            return carry

        loop(0, X, row)


def grid_shift(value, dx, dy):
    groups, rows, columns = (lax.axis_size(a) for a in AXES)
    pairs = []
    for g in range(groups):
        for i in range(rows):
            for j in range(columns):
                if 0 <= i + dx < rows and 0 <= j + dy < columns:
                    here = (g * rows + i) * columns + j
                    pairs.append((here, here + dx * columns + dy))
    return lax.ppermute(value, AXES, pairs)


def exchange_x(tails, heads):
    return [grid_shift(tails, 1, 0), grid_shift(heads, -1, 0)]


def exchange_y(tails, heads):
    return [grid_shift(tails, 0, 1), grid_shift(heads, 0, -1)]


def to_group(value, source):
    rows, columns = lax.axis_size("gx"), lax.axis_size("gy")
    count = rows * columns
    pairs = [(source * count + n, (1 - source) * count + n) for n in range(count)]
    return lax.ppermute(value, AXES, pairs)


def body(state, conduct, capacity, supply, flags, layer_map):
    state, conduct, capacity, supply = state[0], conduct[0], capacity[0], supply[0]
    layer_map = layer_map.reshape(1, 3 * Z)
    cells = X * Y * 3 * Z * lax.axis_size("gx") * lax.axis_size("gy")
    devices = lax.axis_size("group") * lax.axis_size("gx") * lax.axis_size("gy")
    tile = struct(3, X, Y, Z)
    brick = struct(X, Y, Z)
    wide = (EX, EY, Z)
    full = struct(3, *wide)

    y_face = struct(len(Y_ROWS), X, Z)
    tz, xt, xh, yt, yh = call(
        pack_kernel,
        [tile] + x_faces(X_ROWS) + [y_face] * 2,
        [
            pltpu.VMEM((X, Y), jnp.int32),
            pltpu.VMEM((3, X, Y, Z), F32),
            pltpu.VMEM((3, 3, X, Y, Z), F32),
            pltpu.VMEM((X, Y, Z), F32),
            pltpu.VMEM((X, Y, Z), F32),
            pltpu.SemaphoreType.DMA((14,)),
        ],
        left=(0, 1, 2, 3),
        limit=58,
        count=4,
    )(flags, state, conduct, capacity)
    k_halos = exchange_x(xt, xh) + exchange_y(yt, yh)
    wide_faces = struct(12, *wide)
    tables = [pltpu.VMEM((6, *wide), F32), pltpu.VMEM(wide, F32)]
    inner, unit0 = call(interior_kernel, [wide_faces, brick], tables, cost=30_000_000)(
        state, conduct, capacity, tz, layer_map
    )
    unit0 = to_group(unit0, 0)
    base, strain, beside = call(
        first_kernel,
        [tile, brick, struct(8, Z)],
        tables + [pltpu.VMEM((3, *wide), F32)],
    )(state, conduct, capacity, supply, inner, *k_halos)
    strain = to_group(strain, 1)
    faces, k_rim = call(
        halo_kernel, [wide_faces, struct(6, len(K_RIM), EY, Z)], tables, cost=30_000_000
    )(conduct, capacity, tz, layer_map, *k_halos)
    residual, xt, xh = call(residual_kernel, [tile] + x_faces(R_ROWS))(
        base, strain, unit0, layer_map
    )
    halos = exchange_x(xt, xh)
    yt, yh = call(relay_kernel, [struct(Y_PACK, Z)] * 2)(
        residual, unit0, *halos, k_halos[0], k_halos[1]
    )
    halos = halos + exchange_y(yt, yh)
    rim, field, product, unit12, sums = call(
        image_kernel,
        [struct(12, len(RIM), EY, Z), full, full, struct(2, EX - 2, EY, Z), struct(8, Z)],
        [
            pltpu.VMEM((6, len(K_RIM), EY, Z), F32),
            pltpu.VMEM((EX - 2, EY, Z), F32),
            pltpu.VMEM((4, 8, Z), F32),
        ],
    )(residual, unit0, beside, layer_map, *halos, faces, k_rim)
    unit12 = to_group(unit12, 0)
    sums, field12, product12 = call(
        sums_kernel,
        [struct(devices, Z), struct(2, 3, *wide), struct(2, 3, *wide)],
        [pltpu.VMEM((20, 8, Z), F32)],
    )(field, product, faces, rim, unit12, state, sums)
    sums = lax.all_to_all(sums, AXES, 0, 0, tiled=True)

    def finish(*refs):
        final_kernel(*refs, cells=cells)

    new_state, balance = call(finish, [tile, struct(2)], scalars=(1,))(
        sums, state, field, product, field12, product12
    )
    return new_state[None], balance


def solution(mesh):
    placed = (
        P("group", None, "gx", "gy", None),
        P("group", None, None, "gx", "gy", None),
        P("group", "gx", "gy", None),
        P("group", None, "gx", "gy", None),
        P("gx", "gy"),
        P(),
    )
    return jax.shard_map(
        body,
        mesh=mesh,
        in_specs=placed,
        out_specs=(P("group", None, "gx", "gy", None), P()),
        check_vma=False,
    )
```

```python
import jax
import jax.numpy as jnp
from jax import lax
from jax.experimental import pallas as pl
from jax.experimental.pallas import tpu as pltpu
from jax.sharding import PartitionSpec as P

AXES = ("group", "gx", "gy")
X, Y, Z = 16, 32, 128
OX, OY = 3, 4
EX, EY = X + 2 * OX, Y + 2 * OY
BETA = 0.5
BIOT = 0.8
F32 = jnp.float32

X_ROWS = [(f, r) for f in range(13) for r in range(1, (3 if f < 3 else 2 if f < 10 else 1) + 1)]
Y_ROWS = [
    (f, r) for f in range(13) for r in range(1, (3 if 3 <= f < 6 else 2 if f < 10 else 1) + 1)
]
CORNER = [(1, 1), (1, 2), (2, 1), (2, 2), (1, 3), (3, 1)]
K_CORNERS = (
    [(f, i, j) for f in range(3) for i, j in CORNER[:4] + [(3, 1)]]
    + [(f, i, j) for f in range(3, 6) for i, j in CORNER[:4] + [(1, 3)]]
    + [(f, i, j) for f in range(6, 10) for i, j in CORNER[:3]]
)
R_ROWS = [(f, r) for f in range(3) for r in range(1, 4)]
R_CORNERS = [(f, i, j) for f in range(3) for i, j in CORNER]
AT_R = [len(R_ROWS) * X, len(R_ROWS) * X + len(R_CORNERS)]
AT_K = [AT_R[1] + len(R_CORNERS), AT_R[1] + len(R_CORNERS) + len(K_CORNERS)]
AT_Q = [AT_K[1] + len(K_CORNERS), AT_K[1] + len(K_CORNERS) + 3]
AT_U = AT_Q[1] + 3
Y_PACK = -(-(AT_U + 4) // 8) * 8
Q_SLOT = [R_ROWS.index((0, 3)), R_ROWS.index((1, 3))]


def struct(*shape):
    return jax.ShapeDtypeStruct(shape, F32)


def call(kernel, outs, scratch=(), left=(), count=0, cost=None, limit=20, scalars=()):
    extra = {}
    if left:
        extra["in_specs"] = [
            pl.BlockSpec(memory_space=pltpu.HBM if n in left else pltpu.VMEM) for n in range(count)
        ]
    if scalars:
        extra["out_specs"] = [
            pl.BlockSpec(memory_space=pltpu.SMEM if n in scalars else pltpu.VMEM)
            for n in range(len(outs))
        ]
    if cost:
        extra["cost_estimate"] = pl.CostEstimate(
            flops=cost, bytes_accessed=cost, transcendentals=0
        )
    return pl.pallas_call(
        kernel,
        out_shape=outs,
        scratch_shapes=list(scratch),
        compiler_params=pltpu.CompilerParams(vmem_limit_bytes=limit << 20),
        **extra,
    )


def up_y(v):
    return pltpu.roll(v, v.shape[0] - 1, 0)


def down_y(v):
    return pltpu.roll(v, 1, 0)


def up_z(v):
    return pltpu.roll(v, Z - 1, 1)


def down_z(v):
    return pltpu.roll(v, 1, 1)


def lanes(rows):
    return lax.broadcasted_iota(jnp.int32, (rows, Z), 1)


def rows_of(rows):
    return lax.broadcasted_iota(jnp.int32, (rows, Z), 0)


def to_tile(v):
    return pltpu.roll(v, EY - OY, 0)[:Y]


def harmonic(a, b):
    return 2.0 * a * b / jnp.maximum(a + b, 1e-30)


def one_hot(map_ref):
    brick = lax.broadcasted_iota(jnp.int32, (Z, 3 * Z), 0)
    return jnp.where(brick == map_ref[...], 1.0, 0.0).astype(jnp.bfloat16)


def dot_split(v, hot, contract):
    high = v.astype(jnp.bfloat16)
    low = (v - high.astype(F32)).astype(jnp.bfloat16)
    dims = (((1,), (contract,)), ((), ()))
    return lax.dot_general(high, hot, dims, preferred_element_type=F32) + lax.dot_general(
        low, hot, dims, preferred_element_type=F32
    )


def spread(v, hot, k):
    return dot_split(v, hot[:, k * Z : (k + 1) * Z], 0)


def gather_up(parts, hot):
    total = None
    for k, v in enumerate(parts):
        part = dot_split(v, hot[:, k * Z : (k + 1) * Z], 1)
        total = part if total is None else total + part
    ones = jnp.ones((8, 3 * Z), jnp.bfloat16)
    counts = lax.dot_general(ones, hot, (((1,), (1,)), ((), ())), preferred_element_type=F32)
    return total * (1.0 / counts[:1])


def gather_wide(ref, hot):
    rows = EX - 2
    parts = [ref[k, 1 : EX - 1].reshape(rows * EY, Z) for k in range(3)]
    return gather_up(parts, hot).reshape(rows, EY, Z)


def fetch(pairs, sem, start=0):
    copies = [pltpu.make_async_copy(a, b, sem.at[start + n]) for n, (a, b) in enumerate(pairs)]
    for copy in copies:
        copy.start()
    return copies


def pack_x(source, rows, tails, heads):
    for n, (f, r) in enumerate(rows):
        tails[n] = source(f)[X - r]
        heads[n] = source(f)[r - 1]


def unpack_x(target, rows, low, up):
    for n, (f, r) in enumerate(rows):
        target(f)[OX - r, OY : OY + Y] = low[n]
        target(f)[OX + X - 1 + r, OY : OY + Y] = up[n]


def corner_at(side, i, j):
    row = OX - i if side[0] == 0 else OX + X - 1 + i
    column = OY - j if side[1] == 0 else OY + Y - 1 + j
    return row, slice(column, column + 1)


def x_faces(rows):
    return [struct(len(rows), Y, Z)] * 2


def loop(first, last, body, init=0, unroll=4):
    steps = (last - first) // unroll

    def step(n, carry):
        for m in range(unroll):
            carry = body(first + n * unroll + m, carry)
        return carry

    init = lax.fori_loop(0, steps, step, init)
    for i in range(first + steps * unroll, last):
        init = body(i, init)
    return init


def pack_kernel(flags_in, state_in, conduct_in, capacity_in, tz, xt, xh, yt, yh, *scratch):
    flags, state, conduct, capacity, bottom, sem = scratch
    flow = lax.axis_index("group") == 0
    last = lanes(Y) == Z - 1
    early = [(flags_in, flags)] + [(conduct_in.at[2, k], conduct.at[2, k]) for k in range(3)]
    late = [(conduct_in.at[d, k], conduct.at[d, k]) for d in range(2) for k in range(3)]
    late += [(state_in.at[k], state.at[k]) for k in range(3)] + [(capacity_in, capacity)]
    early = fetch(early, sem)
    late = fetch(late, sem, len(early))
    for copy in early:
        copy.wait()
    eye = jnp.where(
        lax.broadcasted_iota(jnp.int32, (Y, Y), 0) == lax.broadcasted_iota(jnp.int32, (Y, Y), 1),
        1.0,
        0.0,
    ).astype(jnp.bfloat16)
    columns = lax.dot_general(
        eye,
        flags[...].astype(F32).astype(jnp.bfloat16),
        (((1,), (1,)), ((), ())),
        preferred_element_type=F32,
    )
    for x in range(X):
        bottom[x] = jnp.broadcast_to(columns[:, x : x + 1], (Y, Z))

    def faces(x, carry):
        kz = [conduct[2, k, x] for k in range(3)]
        rolled = [up_z(v) for v in kz]
        ends = [rolled[1], rolled[2], bottom[x] * kz[2]]
        for k in range(3):
            end = jnp.where(flow, ends[k], kz[k])
            tz[k, x] = harmonic(kz[k], jnp.where(last, end, rolled[k]))
        return carry

    loop(0, X, faces)
    for copy in late:
        copy.wait()

    def source(f):
        if f < 6:
            return conduct.at[f // 3, f % 3]
        if f < 9:
            return tz.at[f - 6]
        return capacity if f == 9 else state.at[f - 10]

    pack_x(source, X_ROWS, xt, xh)
    for n, (f, r) in enumerate(Y_ROWS):
        yt[n] = source(f)[:, Y - r, :]
        yh[n] = source(f)[:, r - 1, :]


class Faces:
    def __init__(self, x, y, z, own):
        self.x, self.y, self.z, self.own = x, y, z, own


def faces_in(ref, shift=0):
    return Faces(*[lambda c, i, d=d: ref[3 * d + c, i - shift] for d in range(4)])


def lateral(faces, v_ref, c, i, v, fx_before):
    fx = faces.x(c, i) * (v - v_ref[c, i + 1])
    fy = faces.y(c, i) * (v - up_y(v))
    return (fx - fx_before) + (fy - down_y(fy)), fx


def x_flux(faces, v_ref, i):
    return tuple(faces.x(c, i) * (v_ref[c, i] - v_ref[c, i + 1]) for c in range(3))


def flow_below(vs, last):
    rolled = [up_z(v) for v in vs]
    ends = [rolled[1], rolled[2], 0.0]
    return [jnp.where(last, ends[k], rolled[k]) for k in range(3)]


def flow_row(faces, v_ref, i, fx_before):
    last, first = lanes(EY) == Z - 1, lanes(EY) == 0
    vs = [v_ref[k, i] for k in range(3)]
    below = flow_below(vs, last)
    fz = [faces.z(k, i) * (vs[k] - below[k]) for k in range(3)]
    moved = [down_z(v) for v in fz]
    ends = [0.0, moved[0], moved[1]]
    out, fx_now = [], []
    for k in range(3):
        side, fx = lateral(faces, v_ref, k, i, vs[k], fx_before[k])
        above = jnp.where(first, ends[k], moved[k])
        out.append(faces.own(k, i) * vs[k] + side + (fz[k] - above))
        fx_now.append(fx)
    return out, tuple(fx_now)


def strain_row(v_ref, i):
    v0, v1, v2 = v_ref[0, i], v_ref[1, i], v_ref[2, i]
    low = jnp.where(lanes(EY) == Z - 1, 0.0, up_z(v2))
    return (v_ref[0, i + 1] - v0) + (up_y(v1) - v1) + (low - v2)


def solid_row(faces, v_ref, i, s_before, fx_before):
    last, first = lanes(EY) == Z - 1, lanes(EY) == 0
    e = strain_row(v_ref, i)
    s = faces.own(0, i) * e
    grad = [s_before - s, down_y(s) - s, jnp.where(first, 0.0, down_z(s)) - s]
    out, fx_now = [], []
    for c in range(3):
        v = v_ref[c, i]
        side, fx = lateral(faces, v_ref, c, i, v, fx_before[c])
        fz = faces.z(c, i) * (v - jnp.where(last, 0.0, up_z(v)))
        above = jnp.where(first, 0.0, down_z(fz))
        out.append((side + (fz - above)) + grad[c])
        fx_now.append(fx)
    return out, s, tuple(fx_now)


BESIDE = [(1, -1, Y), (1, X - 1, Y), (1, -1, 0), (1, X - 1, 0)]
BESIDE += [(0, X, -1), (0, 0, -1), (0, X, Y - 1), (0, 0, Y - 1)]


def place_tile(conduct, capacity, keep, caps):
    at = slice(OY, OY + Y)

    def row(x, carry):
        for f in range(6):
            keep[f, OX + x, at] = conduct[f // 3, f % 3, x]
        caps[OX + x, at] = capacity[x]
        return carry

    loop(0, X, row)


def interior_kernel(state, conduct, capacity, tz, layer_map, faces, unit, keep, caps):
    flow = lax.axis_index("group") == 0
    place_tile(conduct, capacity, keep, caps)

    def row(i, carry):
        lateral_faces(keep, faces, i)
        for k in range(3):
            faces[6 + k, i, OY : OY + Y] = tz[k, i - OX]
        return carry

    loop(OX, OX + X, row)

    @pl.when(flow)
    def _():
        hot = one_hot(layer_map)
        bricks = caps[OX : OX + X].reshape(X * EY, Z)
        for k in range(3):
            faces[9 + k, OX : OX + X] = (spread(bricks, hot, k) + BETA).reshape(X, EY, Z)
        parts = [state[k].reshape(X * Y, Z) for k in range(3)]
        unit[...] = gather_up(parts, hot).reshape(X, Y, Z)


def lateral_faces(keep, faces, i):
    for c in range(3):
        faces[c, i] = harmonic(keep[c, i], keep[c, i + 1])
        here = keep[3 + c, i]
        faces[3 + c, i] = harmonic(here, up_y(here))
    return 0


def strain_kernel(state, xu, yu, strain):
    flow = lax.axis_index("group") == 0

    @pl.when(jnp.logical_not(flow))
    def _():
        last = lanes(Y) == Z - 1
        edge = rows_of(Y) == Y - 1
        n_x, n_y = X_ROWS.index((10, 1)), Y_ROWS.index((11, 1))
        for x in range(X):
            v0, v1, v2 = (state[c, x] for c in range(3))
            east = state[0, x + 1] if x + 1 < X else xu[n_x]
            north = jnp.where(edge, yu[n_y, x : x + 1], up_y(v1))
            low = jnp.where(last, 0.0, up_z(v2))
            strain[x] = (east - v0) + (north - v1) + (low - v2)


def first_kernel(state, conduct, capacity, supply, faces_ref, xl, xu, yl, yu, *refs):
    base, beside, sides, own, field = refs
    flow = lax.axis_index("group") == 0

    def place(x, carry):
        for c in range(3):
            field[c, OX + x, OY : OY + Y] = state[c, x]
        for f in range(6):
            sides[f, OX + x] = faces_ref[f, OX + x]
        return carry

    loop(0, X, place)
    for c in range(3):
        n = X_ROWS.index((10 + c, 1))
        field[c, OX - 1, OY : OY + Y] = xl[n]
        field[c, OX + X, OY : OY + Y] = xu[n]
        n = Y_ROWS.index((10 + c, 1))
        field[c, OX : OX + X, OY - 1, :] = yl[n]
        field[c, OX : OX + X, OY + Y, :] = yu[n]
        n = X_ROWS.index((c, 1))
        at = slice(OY, OY + Y)
        sides[c, OX - 1, at] = harmonic(xl[n], conduct[0, c, 0])
        sides[c, OX + X - 1, at] = harmonic(conduct[0, c, X - 1], xu[n])
        n = Y_ROWS.index((3 + c, 1))
        sides[3 + c, OX : OX + X, OY - 1, :] = harmonic(yl[n], conduct[1, c, :, 0, :])
        sides[3 + c, OX : OX + X, OY + Y - 1, :] = harmonic(conduct[1, c, :, Y - 1, :], yu[n])
    field[1, OX - 1, OY + Y : OY + Y + 1] = jnp.zeros((1, Z), F32)
    field[0, OX + X, OY - 1 : OY] = jnp.zeros((1, Z), F32)
    for n, (c, x, y) in enumerate(BESIDE):
        beside[n : n + 1] = field[c, OX + x, OY + y : OY + y + 1]
    inner = faces_in(faces_ref)
    outer = faces_in(sides)

    @pl.when(flow)
    def _():
        faces = Faces(outer.x, outer.y, inner.z, inner.own)

        def row(i, fx_before):
            image, fx = flow_row(faces, field, i, fx_before)
            for k in range(3):
                base[k, i - OX] = (
                    supply[k, i - OX] + BETA * state[k, i - OX] - to_tile(image[k])
                )
            return fx

        loop(OX, OX + X, row, x_flux(faces, field, OX - 1))

    @pl.when(jnp.logical_not(flow))
    def _():
        def place(x, carry):
            own[OX + x, OY : OY + Y] = capacity[x]
            return carry

        loop(0, X, place)
        own[OX - 1, OY : OY + Y] = xl[X_ROWS.index((9, 1))]
        own[OX : OX + X, OY - 1, :] = yl[Y_ROWS.index((9, 1))]
        faces = Faces(outer.x, outer.y, inner.z, lambda c, i: own[i])

        def row(i, carry):
            image, s, fx = solid_row(faces, field, i, carry[0], carry[1])
            for c in range(3):
                base[c, i - OX] = supply[c, i - OX] - to_tile(image[c])
            return s, fx

        before = faces.own(0, OX - 1) * strain_row(field, OX - 1)
        loop(OX, OX + X, row, (before, x_flux(faces, field, OX - 1)))


def halo_kernel(conduct, capacity, tz, layer_map, xl, xu, yl, yu, faces, rim, keep, caps):
    flow = lax.axis_index("group") == 0

    def target(f):
        if f < 6:
            return keep.at[f]
        return faces.at[f] if f < 9 else caps

    place_tile(conduct, capacity, keep, caps)

    def place(x, carry):
        for k in range(3):
            faces[6 + k, OX + x, OY : OY + Y] = tz[k, x]
        return carry

    loop(0, X, place)
    for n, (f, r) in enumerate(X_ROWS):
        if f < 10:
            target(f)[OX - r, OY : OY + Y] = xl[n]
            target(f)[OX + X - 1 + r, OY : OY + Y] = xu[n]
    for n, (f, r) in enumerate(Y_ROWS):
        if f < 10:
            target(f)[OX : OX + X, OY - r, :] = yl[n]
            target(f)[OX : OX + X, OY + Y - 1 + r, :] = yu[n]
    loop(0, EX - 1, lambda i, carry: lateral_faces(keep, faces, i))
    for n, i in enumerate(K_RIM):
        for f in range(6):
            rim[f, n] = keep[f, i]

    @pl.when(flow)
    def _():
        hot = one_hot(layer_map)
        bricks = caps[1 : EX - 1].reshape((EX - 2) * EY, Z)
        for k in range(3):
            faces[9 + k, 1 : EX - 1] = (spread(bricks, hot, k) + BETA).reshape(EX - 2, EY, Z)

    @pl.when(jnp.logical_not(flow))
    def _():
        faces[9] = caps[...]


BESIDE = [(1, -1, Y), (1, X - 1, Y), (1, -1, 0), (1, X - 1, 0)]
BESIDE += [(0, X, -1), (0, 0, -1), (0, X, Y - 1), (0, 0, Y - 1)]
RIM = [0, 1, 2, EX - 4, EX - 3, EX - 2]
K_RIM = [0, 1, 2, 3, EX - 4, EX - 3, EX - 2, EX - 1]


def residual_kernel(base, strain, unit, layer_map, residual, xt, xh):
    flow = lax.axis_index("group") == 0

    @pl.when(flow)
    def _():
        hot = one_hot(layer_map)
        e = strain[...].reshape(X * Y, Z)
        for k in range(3):
            residual[k] = base[k] - BIOT * spread(e, hot, k).reshape(X, Y, Z)

    @pl.when(jnp.logical_not(flow))
    def _():
        residual[...] = base[...]

    pack_x(lambda f: residual.at[f], R_ROWS, xt, xh)

    @pl.when(jnp.logical_not(flow))
    def _():
        for depth, n in enumerate(Q_SLOT):
            xt[n] = unit[X - 1 - depth]
            xh[n] = unit[depth]


def relay_kernel(residual, unit, xl, xu, kl, ku, yt, yh):
    flow = lax.axis_index("group") == 0
    for out, edge in ((yt, lambda j: Y - j), (yh, lambda j: j - 1)):
        for n, (f, r) in enumerate(R_ROWS):
            out[n * X : (n + 1) * X] = residual[f, :, edge(r), :]
        for side, (r_halo, k_halo) in enumerate(((xl, kl), (xu, ku))):
            for n, (f, i, j) in enumerate(R_CORNERS):
                at = AT_R[side] + n
                out[at : at + 1] = r_halo[R_ROWS.index((f, i)), edge(j) : edge(j) + 1]
            for n, (f, i, j) in enumerate(K_CORNERS):
                at = AT_K[side] + n
                out[at : at + 1] = k_halo[X_ROWS.index((f, i)), edge(j) : edge(j) + 1]
            for n, (i, j) in enumerate(CORNER[:3]):
                at = AT_Q[side] + n
                out[at : at + 1] = r_halo[Q_SLOT[i - 1], edge(j) : edge(j) + 1]
            for c in range(2):
                at = AT_U + 2 * side + c
                out[at : at + 1] = k_halo[X_ROWS.index((10 + c, 1)), edge(1) : edge(1) + 1]

    @pl.when(jnp.logical_not(flow))
    def _():
        for out, edge in ((yt, lambda j: Y - j), (yh, lambda j: j - 1)):
            for depth, n in enumerate(Q_SLOT):
                out[n * X : (n + 1) * X] = unit[:, edge(depth + 1), :]


def fold(v):
    return jnp.sum(v.reshape(v.shape[0] // 8, 8, Z), axis=0)


def spread_sums(found):
    lane = lanes(8)
    row = jnp.zeros((8, Z), F32)
    first = rows_of(8) == 0
    for n, total in found.items():
        row = jnp.where(first & (lane == n), jnp.sum(total), row)
    return row


def tile_rows():
    at = rows_of(EY)
    return (at >= OY) & (at < OY + Y)


def fill(residual, target, halos):
    xl, xu, yl, yu = halos

    def place(x, carry):
        for k in range(3):
            target[k, OX + x, OY : OY + Y] = residual[k, x]
        return carry

    loop(0, X, place)
    unpack_x(lambda f: target.at[f], R_ROWS, xl, xu)
    for n, (f, r) in enumerate(R_ROWS):
        target[f, OX : OX + X, OY - r, :] = yl[n * X : (n + 1) * X]
        target[f, OX : OX + X, OY + Y - 1 + r, :] = yu[n * X : (n + 1) * X]
    for v, pack in enumerate((yl, yu)):
        for h in range(2):
            for n, (f, i, j) in enumerate(R_CORNERS):
                row, column = corner_at((h, v), i, j)
                target[f, row, column] = pack[AT_R[h] + n : AT_R[h] + n + 1]


def complete(faces, rim, k_rim_in, k_rim, halos, hot):
    for n, i in enumerate(RIM):
        for f in range(6, 12):
            rim[f, n] = faces[f, i]
    k_rim[...] = k_rim_in[...]
    order = []
    for v, pack in enumerate(halos[2:]):
        for h in range(2):
            for n, (f, i, j) in enumerate(K_CORNERS):
                row, column = corner_at((h, v), i, j)
                value = pack[AT_K[h] + n : AT_K[h] + n + 1]
                if f < 6:
                    k_rim[f, K_RIM.index(row), column] = value
                elif f < 9:
                    rim[f, RIM.index(row), column] = value
                else:
                    order.append((RIM.index(row), column, value))
    for n, i in enumerate(RIM):
        m = K_RIM.index(i)
        for c in range(3):
            rim[c, n] = harmonic(k_rim[c, m], k_rim[c, m + 1])
            here = k_rim[3 + c, m]
            rim[3 + c, n] = harmonic(here, up_y(here))
    if hot is None:
        for row, column, value in order:
            rim[9, row, column] = value
    else:
        values = [value for _, _, value in order]
        values += [jnp.zeros((1, Z), F32)] * (16 - len(values))
        caps = jnp.concatenate(values, axis=0)
        for k in range(3):
            storage = spread(caps, hot, k) + BETA
            for n, (row, column, _) in enumerate(order):
                rim[9 + k, row, column] = storage[n : n + 1]


def row_parts(faces, rim):
    return faces_in(rim), faces_in(faces), faces_in(rim, EX - 7)


def run_rows(parts, first, last, body, init, unroll=3):
    low, middle, high = parts
    for i in range(first, OX):
        init = body(low, i, init)
    init = loop(max(first, OX), EX - 4, lambda i, carry: body(middle, i, carry), init, unroll)
    for i in range(EX - 4, last):
        init = body(high, i, init)
    return init


PAIRS = [(0, 0), (0, 1), (0, 2), (1, 1), (1, 2), (2, 2)]
FIRST_SUM = 9


def grid_mask(before, after):
    gx, gy = lax.axis_index("gx"), lax.axis_index("gy")
    gx_last, gy_last = lax.axis_size("gx") - 1, lax.axis_size("gy") - 1
    at = rows_of(EY)
    in_y = (at >= OY - jnp.where(gy > 0, before, 0)) & (
        at < OY + Y + jnp.where(gy < gy_last, after, 0)
    )

    def in_grid(i):
        in_x = ((i >= OX) | (gx > 0)) & ((i < OX + X) | (gx < gx_last))
        return in_y & in_x

    return in_grid


def load_rows(q_refs, targets, added):
    in_grid = grid_mask(1, 2)

    def row(i, carry):
        for q_ref, target in zip(q_refs, targets):
            load_row(q_ref, target, i, in_grid(i))
        return carry

    def load_row(q_ref, target, i, ok):
        first = lanes(EY) == 0
        q = q_ref[i - 1]
        push = [
            BIOT * (q_ref[i - 2] - q),
            BIOT * (down_y(q) - q),
            BIOT * (jnp.where(first, 0.0, down_z(q)) - q),
        ]
        for c in range(3):
            v = push[c] + target[c, i] if added else push[c]
            target[c, i] = jnp.where(ok, v, 0.0)

    loop(OX - 1, OX + X + 2, row)


def solid_image(parts, f_refs, p_refs, unroll):
    in_grid = grid_mask(0, 1)

    def row(faces, i, carry):
        ok, after = in_grid(i), []
        for f_ref, p_ref, (s, fx) in zip(f_refs, p_refs, carry):
            out, s, fx = solid_row(faces, f_ref, i, s, fx)
            for c in range(3):
                p_ref[c, i] = jnp.where(ok, out[c], 0.0)
            after.append((s, fx))
        return tuple(after)

    view = parts[0]
    start = [
        (view.own(0, OX - 1) * strain_row(f, OX - 1), x_flux(view, f, OX - 1)) for f in f_refs
    ]
    run_rows(parts, OX, OX + X + 1, row, tuple(start), unroll)


def gram_sums(faces, fields, products, pairs, acc):
    acc[...] = jnp.zeros(acc.shape, F32)
    vectors = range(len(fields))

    def row(i, carry):
        inside, last = tile_rows(), lanes(EY) == Z - 1

        def only(v):
            return jnp.where(inside, v, 0.0)

        def add(n, v):
            acc[n] = acc[n] + fold(v)

        strains = [strain_row(p, i) for p in products]
        modulus = only(faces[9, i])
        pushes = [modulus * e for e in strains]
        for n, (a, b) in enumerate(pairs):
            add(4 * n + 3, pushes[a] * strains[b])
        for c in range(3):
            ws = [p[c, i] for p in products]
            dx = [ws[a] - products[a][c, i + 1] for a in vectors]
            dy = [w - up_y(w) for w in ws]
            dz = [w - jnp.where(last, 0.0, up_z(w)) for w in ws]
            sx, sy, sz = (only(faces[3 * d + c, i]) for d in range(3))
            fx = [sx * d for d in dx]
            fy = [sy * d for d in dy]
            fz = [sz * d for d in dz]
            for n, (a, b) in enumerate(pairs):
                add(4 * n + 3, fx[a] * dx[b] + fy[a] * dy[b] + fz[a] * dz[b])
            rs = [only(f[c, i]) for f in fields]
            ws = [only(w) for w in ws]
            for n, (a, b) in enumerate(pairs):
                add(4 * n, rs[a] * rs[b])
                add(4 * n + 1, rs[a] * ws[b])
                add(4 * n + 2, ws[a] * ws[b])
        return carry

    loop(OX, OX + X, row, 0, 2)
    found = {}
    for n, pair in enumerate(pairs):
        for m in range(4):
            found[FIRST_SUM + 6 * m + PAIRS.index(pair)] = acc[4 * n + m]
    return found


def unit_surroundings(unit, halos, q):
    xl, xu, yl, yu = halos

    def place(x, carry):
        q[OX - 1 + x, OY : OY + Y] = unit[x]
        return carry

    loop(0, X, place)
    for depth, n in enumerate(Q_SLOT):
        q[OX - 2 - depth, OY : OY + Y] = xl[n]
        q[OX + X - 1 + depth, OY : OY + Y] = xu[n]
        rows = slice(n * X, (n + 1) * X)
        q[OX - 1 : OX - 1 + X, OY - 1 - depth, :] = yl[rows]
        q[OX - 1 : OX - 1 + X, OY + Y + depth, :] = yu[rows]
    for v, pack in enumerate((yl, yu)):
        for h in range(2):
            for n, (i, j) in enumerate(CORNER[:3]):
                row, column = corner_at((h, v), i, j)
                q[row - 1, column] = pack[AT_Q[h] + n : AT_Q[h] + n + 1]


def late_terms(faces, rim, field, beside, halos):
    yl, yu = halos[2:]

    def modulus(x, y):
        i, column = OX + x, slice(OY + y, OY + y + 1)
        return rim[9, RIM.index(i), column] if i in RIM else faces[9, i, column]

    u1 = [yu[AT_U + 1 : AT_U + 2]] + [beside[n : n + 1] for n in (1, 2, 3)]
    u0 = [yl[AT_U + 2 : AT_U + 3]] + [beside[n : n + 1] for n in (5, 6, 7)]
    for u, (x, y) in zip(u1, ((0, Y - 1), (X, Y - 1), (0, -1), (X, -1))):
        row, column = OX + x, slice(OY + y, OY + y + 1)
        field[0, row, column] = field[0, row, column] - modulus(x - 1, y) * u
    for u, (x, y) in zip(u0, ((X - 1, 0), (-1, 0), (X - 1, Y), (-1, Y))):
        row, column = OX + x, slice(OY + y, OY + y + 1)
        field[1, row, column] = field[1, row, column] - modulus(x, y - 1) * u


def image_kernel(residual, unit_old, beside, layer_map, *refs):
    halos, (faces, k_rim_in, rim, field, product, unit, k_rim, q) = refs[:4], refs[4:]
    flow = lax.axis_index("group") == 0
    fill(residual, field, halos)

    @pl.when(flow)
    def _():
        hot = one_hot(layer_map)
        complete(faces, rim, k_rim_in, k_rim, halos, hot)
        parts = row_parts(faces, rim)

        def row(view, i, fx_before):
            out, fx = flow_row(view, field, i, fx_before)
            for k in range(3):
                product[k, i] = out[k]
            return fx

        run_rows(parts, 1, EX - 1, row, x_flux(parts[0], field, 0))
        unit[0] = gather_wide(field, hot)
        unit[1] = gather_wide(product, hot)

    @pl.when(jnp.logical_not(flow))
    def _():
        complete(faces, rim, k_rim_in, k_rim, halos, None)
        late_terms(faces, rim, field, beside, halos)
        unit_surroundings(unit_old, halos, q)
        load_rows([q], [field], True)
        solid_image(row_parts(faces, rim), [field], [product], 3)


def early_kernel(field, product, faces, state, sums, acc):
    flow = lax.axis_index("group") == 0

    @pl.when(flow)
    def _():
        def dots(i, acc):
            acc = list(acc)
            inside, last = tile_rows(), lanes(EY) == Z - 1

            def add(n, v):
                acc[n] = acc[n] + fold(jnp.where(inside, v, 0.0))

            ws = [product[k, i] for k in range(3)]
            below = flow_below(ws, last)
            g = m1 = m2 = m3 = cr = cw = 0.0
            for k in range(3):
                r, w = field[k, i], ws[k]
                dx, dy, dz = w - product[k, i + 1], w - up_y(w), w - below[k]
                cf = faces[9 + k, i]
                g = g + r * r
                m1 = m1 + r * w
                m2 = m2 + w * w
                cr = cr + cf * r
                cw = cw + cf * w
                m3 = m3 + (
                    faces[k, i] * dx * dx
                    + faces[3 + k, i] * dy * dy
                    + faces[6 + k, i] * dz * dz
                    + cf * w * w
                )
            for n, v in enumerate((g, m1, m2, m3, cr, cw)):
                add(n, v)
            weight = jnp.where(last, faces[8, i], 0.0)
            add(6, weight * field[2, i])
            add(7, weight * ws[2])
            acc[8] = acc[8] + fold(to_tile(weight) * state[2, i - OX])
            return tuple(acc)

        zero = jnp.zeros((8, Z), F32)
        found = dict(enumerate(loop(OX, OX + X, dots, (zero,) * FIRST_SUM, 2)))
        sums[...] = spread_sums(found)

    @pl.when(jnp.logical_not(flow))
    def _():
        sums[...] = spread_sums(gram_sums(faces, [field], [product], PAIRS[:1], acc))


def sums_kernel(field, product, faces, rim, unit, sums_in, sums, field12, product12, acc):
    flow = lax.axis_index("group") == 0
    everyone = sums.shape[0]

    @pl.when(flow)
    def _():
        sums[...] = jnp.broadcast_to(sums_in[:1], (everyone, Z))

    @pl.when(jnp.logical_not(flow))
    def _():
        fields = [field] + [field12.at[a] for a in range(2)]
        products = [product] + [product12.at[a] for a in range(2)]
        load_rows([unit.at[a] for a in range(2)], fields[1:], False)
        solid_image(row_parts(faces, rim), fields[1:], products[1:], 2)
        found = gram_sums(faces, fields, products, PAIRS[1:], acc)
        own = sums_in[:1] + spread_sums(found)[:1]
        sums[...] = jnp.broadcast_to(own, (everyone, Z))


def two_sum(a, b):
    s = a + b
    t = s - a
    return s, (a - (s - t)) + (b - t)


def quick(a, b):
    s = a + b
    return s, b - (s - a)


def halves(a):
    t = 4097.0 * a
    high = t - (t - a)
    return high, a - high


def two_product(a, b):
    p = a * b
    ah, al = halves(a)
    bh, bl = halves(b)
    return p, ((ah * bh - p) + ah * bl + al * bh) + al * bl


def pair_add(a, b):
    s, e = two_sum(a[0], b[0])
    return quick(s, e + (a[1] + b[1]))


def pair_less(a, b):
    return pair_add(a, (-b[0], -b[1]))


def pair_times(a, b):
    p, e = two_product(a[0], b[0])
    return quick(p, e + (a[0] * b[1] + a[1] * b[0]))


def pair_over(a, b):
    q = a[0] / b[0]
    rest = pair_less(a, pair_times(b, (q, jnp.zeros_like(q))))
    return quick(q, rest[0] / b[0])


def krylov(g, m1, m2, m3):
    a0 = pair_over(g, m1)
    h = pair_times(a0, pair_over(m2, m1))
    one = (jnp.ones_like(a0[0]), jnp.zeros_like(a0[0]))
    rho = pair_less(h, one)[0]
    third = pair_times(pair_times(a0, a0), pair_over(m3, m1))
    sigma = pair_less(third, pair_times(h, h))[0]
    more = (rho > 1e-9) & (sigma > 1e-9)
    a1 = jnp.where(more, a0[0] * rho / jnp.where(more, sigma, 1.0), 0.0)
    return a0[0] + a1 * h[0], -a0[0] * a1


def final_kernel(sums, state, field, product, field12, product12, out, balance, *, cells):
    flow = lax.axis_index("group") == 0
    total = (sums[...], jnp.zeros(sums.shape, F32))
    while total[0].shape[0] > 8:
        half = total[0].shape[0] // 2
        total = pair_add([v[:half] for v in total], [v[half:] for v in total])
    for step in (4, 2, 1):
        total = pair_add(total, [pltpu.roll(v, step, 0) for v in total])

    def number(n):
        return tuple(jnp.broadcast_to(v[:1, n : n + 1], (8, Z)) for v in total)

    c0, c1 = krylov(number(0), number(1), number(2), number(3))
    columns = cells // (3 * Z)
    outflow = (number(8)[0] + c0 * number(6)[0] + c1 * number(7)[0]) / columns
    stored = (c0 * number(4)[0] + c1 * number(5)[0]) / cells
    balance[0] = outflow[0, 0]
    balance[1] = stored[0, 0]

    def tall(v):
        return jnp.concatenate([v] * (EY // 8), axis=0)

    @pl.when(flow)
    def _():
        s0, s1 = tall(c0), tall(c1)

        def row(x, carry):
            for k in range(3):
                step = s0 * field[k, OX + x] + s1 * product[k, OX + x]
                out[k, x] = state[k, x] + to_tile(step)
            return carry

        loop(0, X, row)

    @pl.when(jnp.logical_not(flow))
    def _():
        zero = jnp.zeros((8, Z), F32)
        weights = [
            (jnp.ones((8, Z), F32), zero),
            (2.0 * c0, zero),
            (2.0 * c1, zero),
            two_product(c0, c0),
            two_product(2.0 * c0, c1),
            two_product(c1, c1),
        ]
        moments = []
        for m in range(4):
            start = FIRST_SUM + 6 * m
            total = number(start)
            for n in range(1, 6):
                total = pair_add(total, pair_times(weights[n], number(start + n)))
            moments.append(total)
        d0, d1 = krylov(*moments)
        scale_r = [tall(d0), tall(d0 * c0), tall(d0 * c1)]
        scale_w = [tall(d1), tall(d1 * c0), tall(d1 * c1)]

        def row(x, carry):
            for c in range(3):
                step = scale_r[0] * field[c, OX + x] + scale_w[0] * product[c, OX + x]
                for a in range(2):
                    step = step + scale_r[a + 1] * field12[a, c, OX + x]
                    step = step + scale_w[a + 1] * product12[a, c, OX + x]
                out[c, x] = state[c, x] + to_tile(step)
            return carry

        loop(0, X, row)


def grid_shift(value, dx, dy):
    groups, rows, columns = (lax.axis_size(a) for a in AXES)
    pairs = []
    for g in range(groups):
        for i in range(rows):
            for j in range(columns):
                if 0 <= i + dx < rows and 0 <= j + dy < columns:
                    here = (g * rows + i) * columns + j
                    pairs.append((here, here + dx * columns + dy))
    return lax.ppermute(value, AXES, pairs)


def exchange_x(tails, heads):
    return [grid_shift(tails, 1, 0), grid_shift(heads, -1, 0)]


def exchange_y(tails, heads):
    return [grid_shift(tails, 0, 1), grid_shift(heads, 0, -1)]


def to_group(value, source):
    rows, columns = lax.axis_size("gx"), lax.axis_size("gy")
    count = rows * columns
    pairs = [(source * count + n, (1 - source) * count + n) for n in range(count)]
    return lax.ppermute(value, AXES, pairs)


def body(state, conduct, capacity, supply, flags, layer_map):
    state, conduct, capacity, supply = state[0], conduct[0], capacity[0], supply[0]
    layer_map = layer_map.reshape(1, 3 * Z)
    cells = X * Y * 3 * Z * lax.axis_size("gx") * lax.axis_size("gy")
    devices = lax.axis_size("group") * lax.axis_size("gx") * lax.axis_size("gy")
    tile = struct(3, X, Y, Z)
    brick = struct(X, Y, Z)
    wide = (EX, EY, Z)
    full = struct(3, *wide)

    y_face = struct(len(Y_ROWS), X, Z)
    tz, xt, xh, yt, yh = call(
        pack_kernel,
        [tile] + x_faces(X_ROWS) + [y_face] * 2,
        [
            pltpu.VMEM((X, Y), jnp.int32),
            pltpu.VMEM((3, X, Y, Z), F32),
            pltpu.VMEM((3, 3, X, Y, Z), F32),
            pltpu.VMEM((X, Y, Z), F32),
            pltpu.VMEM((X, Y, Z), F32),
            pltpu.SemaphoreType.DMA((14,)),
        ],
        left=(0, 1, 2, 3),
        limit=58,
        count=4,
    )(flags, state, conduct, capacity)
    k_halos = lax.optimization_barrier(exchange_x(xt, xh) + exchange_y(yt, yh))
    wide_faces = struct(12, *wide)
    tables = [pltpu.VMEM((6, *wide), F32), pltpu.VMEM(wide, F32)]
    inner, unit0 = call(interior_kernel, [wide_faces, brick], tables, cost=30_000_000)(
        state, conduct, capacity, tz, layer_map
    )
    unit0 = to_group(unit0, 0)
    strain = call(strain_kernel, brick)(state, k_halos[1], k_halos[3])
    strain = to_group(strain, 1)
    base, beside = call(
        first_kernel,
        [tile, struct(8, Z)],
        tables + [pltpu.VMEM((3, *wide), F32)],
        cost=20_000_000,
    )(state, conduct, capacity, supply, inner, *k_halos)
    faces, k_rim = call(
        halo_kernel, [wide_faces, struct(6, len(K_RIM), EY, Z)], tables, cost=30_000_000
    )(conduct, capacity, tz, layer_map, *k_halos)
    residual, xt, xh = call(residual_kernel, [tile] + x_faces(R_ROWS))(
        base, strain, unit0, layer_map
    )
    halos = exchange_x(xt, xh)
    yt, yh = call(relay_kernel, [struct(Y_PACK, Z)] * 2)(
        residual, unit0, *halos, k_halos[0], k_halos[1]
    )
    halos = halos + exchange_y(yt, yh)
    rim, field, product, unit12 = call(
        image_kernel,
        [struct(12, len(RIM), EY, Z), full, full, struct(2, EX - 2, EY, Z)],
        [pltpu.VMEM((6, len(K_RIM), EY, Z), F32), pltpu.VMEM((EX - 2, EY, Z), F32)],
    )(residual, unit0, beside, layer_map, *halos, faces, k_rim)
    unit12 = to_group(unit12, 0)
    sums = call(early_kernel, struct(8, Z), [pltpu.VMEM((4, 8, Z), F32)], cost=20_000_000)(
        field, product, faces, state
    )
    sums, field12, product12 = call(
        sums_kernel,
        [struct(devices, Z), struct(2, 3, *wide), struct(2, 3, *wide)],
        [pltpu.VMEM((20, 8, Z), F32)],
    )(field, product, faces, rim, unit12, sums)
    sums = lax.all_to_all(sums, AXES, 0, 0, tiled=True)

    def finish(*refs):
        final_kernel(*refs, cells=cells)

    new_state, balance = call(finish, [tile, struct(2)], scalars=(1,))(
        sums, state, field, product, field12, product12
    )
    return new_state[None], balance


def solution(mesh):
    placed = (
        P("group", None, "gx", "gy", None),
        P("group", None, None, "gx", "gy", None),
        P("group", "gx", "gy", None),
        P("group", None, "gx", "gy", None),
        P("gx", "gy"),
        P(),
    )
    return jax.shard_map(
        body,
        mesh=mesh,
        in_specs=placed,
        out_specs=(P("group", None, "gx", "gy", None), P()),
        check_vma=False,
    )
```

```python
import jax
import jax.numpy as jnp
from jax import lax
from jax.experimental import pallas as pl
from jax.experimental.pallas import tpu as pltpu
from jax.sharding import PartitionSpec as P

AXES = ("group", "gx", "gy")
X, Y, Z = 16, 32, 128
OX, OY = 3, 4
EX, EY = X + 2 * OX, Y + 2 * OY
BETA = 0.5
BIOT = 0.8
F32 = jnp.float32

X_ROWS = [(f, r) for f in range(13) for r in range(1, (3 if f < 3 else 2 if f < 10 else 1) + 1)]
Y_ROWS = [
    (f, r) for f in range(13) for r in range(1, (3 if 3 <= f < 6 else 2 if f < 10 else 1) + 1)
]
CORNER = [(1, 1), (1, 2), (2, 1), (2, 2), (1, 3), (3, 1)]
K_CORNERS = (
    [(f, i, j) for f in range(3) for i, j in CORNER[:4] + [(3, 1)]]
    + [(f, i, j) for f in range(3, 6) for i, j in CORNER[:4] + [(1, 3)]]
    + [(f, i, j) for f in range(6, 10) for i, j in CORNER[:3]]
)
R_ROWS = [(f, r) for f in range(3) for r in range(1, 4)]
R_CORNERS = [(f, i, j) for f in range(3) for i, j in CORNER]
AT_R = [len(R_ROWS) * X, len(R_ROWS) * X + len(R_CORNERS)]
AT_K = [AT_R[1] + len(R_CORNERS), AT_R[1] + len(R_CORNERS) + len(K_CORNERS)]
AT_Q = [AT_K[1] + len(K_CORNERS), AT_K[1] + len(K_CORNERS) + 3]
AT_U = AT_Q[1] + 3
Y_PACK = -(-(AT_U + 4) // 8) * 8
Q_SLOT = [R_ROWS.index((0, 3)), R_ROWS.index((1, 3))]


def struct(*shape):
    return jax.ShapeDtypeStruct(shape, F32)


def call(kernel, outs, scratch=(), left=(), count=0, cost=None, limit=20, scalars=()):
    extra = {}
    if left:
        extra["in_specs"] = [
            pl.BlockSpec(memory_space=pltpu.HBM if n in left else pltpu.VMEM) for n in range(count)
        ]
    if scalars:
        extra["out_specs"] = [
            pl.BlockSpec(memory_space=pltpu.SMEM if n in scalars else pltpu.VMEM)
            for n in range(len(outs))
        ]
    if cost:
        extra["cost_estimate"] = pl.CostEstimate(
            flops=cost, bytes_accessed=cost, transcendentals=0
        )
    return pl.pallas_call(
        kernel,
        out_shape=outs,
        scratch_shapes=list(scratch),
        compiler_params=pltpu.CompilerParams(vmem_limit_bytes=limit << 20),
        **extra,
    )


def up_y(v):
    return pltpu.roll(v, v.shape[0] - 1, 0)


def down_y(v):
    return pltpu.roll(v, 1, 0)


def up_z(v):
    return pltpu.roll(v, Z - 1, 1)


def down_z(v):
    return pltpu.roll(v, 1, 1)


def lanes(rows):
    return lax.broadcasted_iota(jnp.int32, (rows, Z), 1)


def rows_of(rows):
    return lax.broadcasted_iota(jnp.int32, (rows, Z), 0)


def to_tile(v):
    return pltpu.roll(v, EY - OY, 0)[:Y]


def harmonic(a, b):
    return 2.0 * a * b / jnp.maximum(a + b, 1e-30)


def one_hot(map_ref):
    brick = lax.broadcasted_iota(jnp.int32, (Z, 3 * Z), 0)
    return jnp.where(brick == map_ref[...], 1.0, 0.0).astype(jnp.bfloat16)


def dot_split(v, hot, contract):
    high = v.astype(jnp.bfloat16)
    low = (v - high.astype(F32)).astype(jnp.bfloat16)
    dims = (((1,), (contract,)), ((), ()))
    return lax.dot_general(high, hot, dims, preferred_element_type=F32) + lax.dot_general(
        low, hot, dims, preferred_element_type=F32
    )


def spread(v, hot, k):
    return dot_split(v, hot[:, k * Z : (k + 1) * Z], 0)


def gather_up(parts, hot):
    total = None
    for k, v in enumerate(parts):
        part = dot_split(v, hot[:, k * Z : (k + 1) * Z], 1)
        total = part if total is None else total + part
    ones = jnp.ones((8, 3 * Z), jnp.bfloat16)
    counts = lax.dot_general(ones, hot, (((1,), (1,)), ((), ())), preferred_element_type=F32)
    return total * (1.0 / counts[:1])


def gather_wide(ref, hot):
    rows = EX - 2
    parts = [ref[k, 1 : EX - 1].reshape(rows * EY, Z) for k in range(3)]
    return gather_up(parts, hot).reshape(rows, EY, Z)


def fetch(pairs, sem, start=0):
    copies = [pltpu.make_async_copy(a, b, sem.at[start + n]) for n, (a, b) in enumerate(pairs)]
    for copy in copies:
        copy.start()
    return copies


class Either:
    def __init__(self, odd, at_odd, at_even):
        self.odd, self.at_odd, self.at_even = odd, at_odd, at_even

    def __getitem__(self, at):
        return jnp.where(self.odd, self.at_odd[at], self.at_even[at])


def parity(axis):
    return lax.rem(lax.axis_index(axis), 2) == 1


def lower_upper(axis, first, second):
    odd = parity(axis)
    return Either(odd, first, second), Either(odd, second, first)


def surroundings(xa, xb, ya, yb):
    return lower_upper("gx", xa, xb) + lower_upper("gy", ya, yb)


def put(first, second, at, odd, tail, head):
    first[at] = jnp.where(odd, head, tail)
    second[at] = jnp.where(odd, tail, head)


def pack_x(source, rows, first, second):
    odd = parity("gx")
    for n, (f, r) in enumerate(rows):
        put(first, second, n, odd, source(f)[X - r], source(f)[r - 1])


def unpack_x(target, rows, low, up):
    for n, (f, r) in enumerate(rows):
        target(f)[OX - r, OY : OY + Y] = low[n]
        target(f)[OX + X - 1 + r, OY : OY + Y] = up[n]


def corner_at(side, i, j):
    row = OX - i if side[0] == 0 else OX + X - 1 + i
    column = OY - j if side[1] == 0 else OY + Y - 1 + j
    return row, slice(column, column + 1)


def x_faces(rows):
    return [struct(len(rows), Y, Z)] * 2


def loop(first, last, body, init=0, unroll=4):
    steps = (last - first) // unroll

    def step(n, carry):
        for m in range(unroll):
            carry = body(first + n * unroll + m, carry)
        return carry

    init = lax.fori_loop(0, steps, step, init)
    for i in range(first + steps * unroll, last):
        init = body(i, init)
    return init


def pack_kernel(flags_in, state_in, conduct_in, capacity_in, tz, xa, xb, ya, yb, *scratch):
    flags, state, conduct, capacity, bottom, sem = scratch
    flow = lax.axis_index("group") == 0
    last = lanes(Y) == Z - 1
    early = [(flags_in, flags)] + [(conduct_in.at[2, k], conduct.at[2, k]) for k in range(3)]
    late = [(conduct_in.at[d, k], conduct.at[d, k]) for d in range(2) for k in range(3)]
    late += [(state_in.at[k], state.at[k]) for k in range(3)] + [(capacity_in, capacity)]
    early = fetch(early, sem)
    late = fetch(late, sem, len(early))
    for copy in early:
        copy.wait()
    eye = jnp.where(
        lax.broadcasted_iota(jnp.int32, (Y, Y), 0) == lax.broadcasted_iota(jnp.int32, (Y, Y), 1),
        1.0,
        0.0,
    ).astype(jnp.bfloat16)
    columns = lax.dot_general(
        eye,
        flags[...].astype(F32).astype(jnp.bfloat16),
        (((1,), (1,)), ((), ())),
        preferred_element_type=F32,
    )
    for x in range(X):
        bottom[x] = jnp.broadcast_to(columns[:, x : x + 1], (Y, Z))

    def faces(x, carry):
        kz = [conduct[2, k, x] for k in range(3)]
        rolled = [up_z(v) for v in kz]
        ends = [rolled[1], rolled[2], bottom[x] * kz[2]]
        for k in range(3):
            end = jnp.where(flow, ends[k], kz[k])
            tz[k, x] = harmonic(kz[k], jnp.where(last, end, rolled[k]))
        return carry

    loop(0, X, faces)
    for copy in late:
        copy.wait()

    def source(f):
        if f < 6:
            return conduct.at[f // 3, f % 3]
        if f < 9:
            return tz.at[f - 6]
        return capacity if f == 9 else state.at[f - 10]

    pack_x(source, X_ROWS, xa, xb)
    odd = parity("gy")
    for n, (f, r) in enumerate(Y_ROWS):
        put(ya, yb, n, odd, source(f)[:, Y - r, :], source(f)[:, r - 1, :])


class Faces:
    def __init__(self, x, y, z, own):
        self.x, self.y, self.z, self.own = x, y, z, own


def faces_in(ref, shift=0):
    return Faces(*[lambda c, i, d=d: ref[3 * d + c, i - shift] for d in range(4)])


def lateral(faces, v_ref, c, i, v, fx_before):
    fx = faces.x(c, i) * (v - v_ref[c, i + 1])
    fy = faces.y(c, i) * (v - up_y(v))
    return (fx - fx_before) + (fy - down_y(fy)), fx


def x_flux(faces, v_ref, i):
    return tuple(faces.x(c, i) * (v_ref[c, i] - v_ref[c, i + 1]) for c in range(3))


def flow_below(vs, last):
    rolled = [up_z(v) for v in vs]
    ends = [rolled[1], rolled[2], 0.0]
    return [jnp.where(last, ends[k], rolled[k]) for k in range(3)]


def flow_row(faces, v_ref, i, fx_before):
    last, first = lanes(EY) == Z - 1, lanes(EY) == 0
    vs = [v_ref[k, i] for k in range(3)]
    below = flow_below(vs, last)
    fz = [faces.z(k, i) * (vs[k] - below[k]) for k in range(3)]
    moved = [down_z(v) for v in fz]
    ends = [0.0, moved[0], moved[1]]
    out, fx_now = [], []
    for k in range(3):
        side, fx = lateral(faces, v_ref, k, i, vs[k], fx_before[k])
        above = jnp.where(first, ends[k], moved[k])
        out.append(faces.own(k, i) * vs[k] + side + (fz[k] - above))
        fx_now.append(fx)
    return out, tuple(fx_now)


def strain_row(v_ref, i):
    v0, v1, v2 = v_ref[0, i], v_ref[1, i], v_ref[2, i]
    low = jnp.where(lanes(EY) == Z - 1, 0.0, up_z(v2))
    return (v_ref[0, i + 1] - v0) + (up_y(v1) - v1) + (low - v2)


def solid_row(faces, v_ref, i, s_before, fx_before):
    last, first = lanes(EY) == Z - 1, lanes(EY) == 0
    e = strain_row(v_ref, i)
    s = faces.own(0, i) * e
    grad = [s_before - s, down_y(s) - s, jnp.where(first, 0.0, down_z(s)) - s]
    out, fx_now = [], []
    for c in range(3):
        v = v_ref[c, i]
        side, fx = lateral(faces, v_ref, c, i, v, fx_before[c])
        fz = faces.z(c, i) * (v - jnp.where(last, 0.0, up_z(v)))
        above = jnp.where(first, 0.0, down_z(fz))
        out.append((side + (fz - above)) + grad[c])
        fx_now.append(fx)
    return out, s, tuple(fx_now)


BESIDE = [(1, -1, Y), (1, X - 1, Y), (1, -1, 0), (1, X - 1, 0)]
BESIDE += [(0, X, -1), (0, 0, -1), (0, X, Y - 1), (0, 0, Y - 1)]


def place_tile(conduct, capacity, keep, caps):
    at = slice(OY, OY + Y)

    def row(x, carry):
        for f in range(6):
            keep[f, OX + x, at] = conduct[f // 3, f % 3, x]
        caps[OX + x, at] = capacity[x]
        return carry

    loop(0, X, row)


def interior_kernel(state, conduct, capacity, tz, layer_map, faces, unit, keep, caps):
    flow = lax.axis_index("group") == 0
    place_tile(conduct, capacity, keep, caps)

    def row(i, carry):
        lateral_faces(keep, faces, i)
        for k in range(3):
            faces[6 + k, i, OY : OY + Y] = tz[k, i - OX]
        return carry

    loop(OX, OX + X, row)

    @pl.when(flow)
    def _():
        hot = one_hot(layer_map)
        bricks = caps[OX : OX + X].reshape(X * EY, Z)
        for k in range(3):
            faces[9 + k, OX : OX + X] = (spread(bricks, hot, k) + BETA).reshape(X, EY, Z)
        parts = [state[k].reshape(X * Y, Z) for k in range(3)]
        unit[...] = gather_up(parts, hot).reshape(X, Y, Z)


def lateral_faces(keep, faces, i):
    for c in range(3):
        faces[c, i] = harmonic(keep[c, i], keep[c, i + 1])
        here = keep[3 + c, i]
        faces[3 + c, i] = harmonic(here, up_y(here))
    return 0


def strain_kernel(state, xa, xb, ya, yb, strain):
    flow = lax.axis_index("group") == 0
    _, xu, _, yu = surroundings(xa, xb, ya, yb)

    @pl.when(jnp.logical_not(flow))
    def _():
        last = lanes(Y) == Z - 1
        edge = rows_of(Y) == Y - 1
        n_x, n_y = X_ROWS.index((10, 1)), Y_ROWS.index((11, 1))
        for x in range(X):
            v0, v1, v2 = (state[c, x] for c in range(3))
            east = state[0, x + 1] if x + 1 < X else xu[n_x]
            north = jnp.where(edge, yu[n_y, x : x + 1], up_y(v1))
            low = jnp.where(last, 0.0, up_z(v2))
            strain[x] = (east - v0) + (north - v1) + (low - v2)


def first_kernel(state, conduct, capacity, supply, faces_ref, xa, xb, ya, yb, *refs):
    xl, xu, yl, yu = surroundings(xa, xb, ya, yb)
    base, beside, sides, own, field = refs
    flow = lax.axis_index("group") == 0

    def place(x, carry):
        for c in range(3):
            field[c, OX + x, OY : OY + Y] = state[c, x]
        for f in range(6):
            sides[f, OX + x] = faces_ref[f, OX + x]
        return carry

    loop(0, X, place)
    for c in range(3):
        n = X_ROWS.index((10 + c, 1))
        field[c, OX - 1, OY : OY + Y] = xl[n]
        field[c, OX + X, OY : OY + Y] = xu[n]
        n = Y_ROWS.index((10 + c, 1))
        field[c, OX : OX + X, OY - 1, :] = yl[n]
        field[c, OX : OX + X, OY + Y, :] = yu[n]
        n = X_ROWS.index((c, 1))
        at = slice(OY, OY + Y)
        sides[c, OX - 1, at] = harmonic(xl[n], conduct[0, c, 0])
        sides[c, OX + X - 1, at] = harmonic(conduct[0, c, X - 1], xu[n])
        n = Y_ROWS.index((3 + c, 1))
        sides[3 + c, OX : OX + X, OY - 1, :] = harmonic(yl[n], conduct[1, c, :, 0, :])
        sides[3 + c, OX : OX + X, OY + Y - 1, :] = harmonic(conduct[1, c, :, Y - 1, :], yu[n])
    field[1, OX - 1, OY + Y : OY + Y + 1] = jnp.zeros((1, Z), F32)
    field[0, OX + X, OY - 1 : OY] = jnp.zeros((1, Z), F32)
    for n, (c, x, y) in enumerate(BESIDE):
        beside[n : n + 1] = field[c, OX + x, OY + y : OY + y + 1]
    inner = faces_in(faces_ref)
    outer = faces_in(sides)

    @pl.when(flow)
    def _():
        faces = Faces(outer.x, outer.y, inner.z, inner.own)

        def row(i, fx_before):
            image, fx = flow_row(faces, field, i, fx_before)
            for k in range(3):
                base[k, i - OX] = (
                    supply[k, i - OX] + BETA * state[k, i - OX] - to_tile(image[k])
                )
            return fx

        loop(OX, OX + X, row, x_flux(faces, field, OX - 1))

    @pl.when(jnp.logical_not(flow))
    def _():
        def place(x, carry):
            own[OX + x, OY : OY + Y] = capacity[x]
            return carry

        loop(0, X, place)
        own[OX - 1, OY : OY + Y] = xl[X_ROWS.index((9, 1))]
        own[OX : OX + X, OY - 1, :] = yl[Y_ROWS.index((9, 1))]
        faces = Faces(outer.x, outer.y, inner.z, lambda c, i: own[i])

        def row(i, carry):
            image, s, fx = solid_row(faces, field, i, carry[0], carry[1])
            for c in range(3):
                base[c, i - OX] = supply[c, i - OX] - to_tile(image[c])
            return s, fx

        before = faces.own(0, OX - 1) * strain_row(field, OX - 1)
        loop(OX, OX + X, row, (before, x_flux(faces, field, OX - 1)))


def halo_kernel(conduct, capacity, tz, layer_map, xa, xb, ya, yb, faces, rim, keep, caps):
    xl, xu, yl, yu = surroundings(xa, xb, ya, yb)
    flow = lax.axis_index("group") == 0

    def target(f):
        if f < 6:
            return keep.at[f]
        return faces.at[f] if f < 9 else caps

    place_tile(conduct, capacity, keep, caps)

    def place(x, carry):
        for k in range(3):
            faces[6 + k, OX + x, OY : OY + Y] = tz[k, x]
        return carry

    loop(0, X, place)
    for n, (f, r) in enumerate(X_ROWS):
        if f < 10:
            target(f)[OX - r, OY : OY + Y] = xl[n]
            target(f)[OX + X - 1 + r, OY : OY + Y] = xu[n]
    for n, (f, r) in enumerate(Y_ROWS):
        if f < 10:
            target(f)[OX : OX + X, OY - r, :] = yl[n]
            target(f)[OX : OX + X, OY + Y - 1 + r, :] = yu[n]
    loop(0, EX - 1, lambda i, carry: lateral_faces(keep, faces, i))
    for n, i in enumerate(K_RIM):
        for f in range(6):
            rim[f, n] = keep[f, i]

    @pl.when(flow)
    def _():
        hot = one_hot(layer_map)
        bricks = caps[1 : EX - 1].reshape((EX - 2) * EY, Z)
        for k in range(3):
            faces[9 + k, 1 : EX - 1] = (spread(bricks, hot, k) + BETA).reshape(EX - 2, EY, Z)

    @pl.when(jnp.logical_not(flow))
    def _():
        faces[9] = caps[...]


BESIDE = [(1, -1, Y), (1, X - 1, Y), (1, -1, 0), (1, X - 1, 0)]
BESIDE += [(0, X, -1), (0, 0, -1), (0, X, Y - 1), (0, 0, Y - 1)]
RIM = [0, 1, 2, EX - 4, EX - 3, EX - 2]
K_RIM = [0, 1, 2, 3, EX - 4, EX - 3, EX - 2, EX - 1]


def residual_kernel(base, strain, unit, layer_map, residual, xa, xb):
    flow = lax.axis_index("group") == 0

    @pl.when(flow)
    def _():
        hot = one_hot(layer_map)
        e = strain[...].reshape(X * Y, Z)
        for k in range(3):
            residual[k] = base[k] - BIOT * spread(e, hot, k).reshape(X, Y, Z)

    @pl.when(jnp.logical_not(flow))
    def _():
        residual[...] = base[...]

    pack_x(lambda f: residual.at[f], R_ROWS, xa, xb)

    @pl.when(jnp.logical_not(flow))
    def _():
        odd = parity("gx")
        for depth, n in enumerate(Q_SLOT):
            put(xa, xb, n, odd, unit[X - 1 - depth], unit[depth])


def relay_kernel(residual, unit, xa, xb, ka, kb, ya, yb):
    flow = lax.axis_index("group") == 0
    odd = parity("gy")
    r_halos, k_halos = lower_upper("gx", xa, xb), lower_upper("gx", ka, kb)

    def give(at, count, ref, index, j):
        put(ya, yb, slice(at, at + count), odd, ref[index(Y - j)], ref[index(j - 1)])

    for n, (f, r) in enumerate(R_ROWS):
        give(n * X, X, residual, lambda y: (f, slice(None), y), r)
    for side in range(2):
        r_halo, k_halo = r_halos[side], k_halos[side]
        for n, (f, i, j) in enumerate(R_CORNERS):
            row = R_ROWS.index((f, i))
            give(AT_R[side] + n, 1, r_halo, lambda y: (row, slice(y, y + 1)), j)
        for n, (f, i, j) in enumerate(K_CORNERS):
            row = X_ROWS.index((f, i))
            give(AT_K[side] + n, 1, k_halo, lambda y: (row, slice(y, y + 1)), j)
        for n, (i, j) in enumerate(CORNER[:3]):
            row = Q_SLOT[i - 1]
            give(AT_Q[side] + n, 1, r_halo, lambda y: (row, slice(y, y + 1)), j)
        for c in range(2):
            row = X_ROWS.index((10 + c, 1))
            give(AT_U + 2 * side + c, 1, k_halo, lambda y: (row, slice(y, y + 1)), 1)

    @pl.when(jnp.logical_not(flow))
    def _():
        for depth, n in enumerate(Q_SLOT):
            give(n * X, X, unit, lambda y: (slice(None), y), depth + 1)


def fold(v):
    return jnp.sum(v.reshape(v.shape[0] // 8, 8, Z), axis=0)


def spread_sums(found):
    lane = lanes(8)
    row = jnp.zeros((8, Z), F32)
    first = rows_of(8) == 0
    for n, total in found.items():
        row = jnp.where(first & (lane == n), jnp.sum(total), row)
    return row


def tile_rows():
    at = rows_of(EY)
    return (at >= OY) & (at < OY + Y)


def fill(residual, target, halos):
    xl, xu, yl, yu = halos

    def place(x, carry):
        for k in range(3):
            target[k, OX + x, OY : OY + Y] = residual[k, x]
        return carry

    loop(0, X, place)
    unpack_x(lambda f: target.at[f], R_ROWS, xl, xu)
    for n, (f, r) in enumerate(R_ROWS):
        target[f, OX : OX + X, OY - r, :] = yl[n * X : (n + 1) * X]
        target[f, OX : OX + X, OY + Y - 1 + r, :] = yu[n * X : (n + 1) * X]
    for v, pack in enumerate((yl, yu)):
        for h in range(2):
            for n, (f, i, j) in enumerate(R_CORNERS):
                row, column = corner_at((h, v), i, j)
                target[f, row, column] = pack[AT_R[h] + n : AT_R[h] + n + 1]


def complete(faces, rim, k_rim_in, k_rim, halos, hot):
    for n, i in enumerate(RIM):
        for f in range(6, 12):
            rim[f, n] = faces[f, i]
    k_rim[...] = k_rim_in[...]
    order = []
    for v, pack in enumerate(halos[2:]):
        for h in range(2):
            for n, (f, i, j) in enumerate(K_CORNERS):
                row, column = corner_at((h, v), i, j)
                value = pack[AT_K[h] + n : AT_K[h] + n + 1]
                if f < 6:
                    k_rim[f, K_RIM.index(row), column] = value
                elif f < 9:
                    rim[f, RIM.index(row), column] = value
                else:
                    order.append((RIM.index(row), column, value))
    for n, i in enumerate(RIM):
        m = K_RIM.index(i)
        for c in range(3):
            rim[c, n] = harmonic(k_rim[c, m], k_rim[c, m + 1])
            here = k_rim[3 + c, m]
            rim[3 + c, n] = harmonic(here, up_y(here))
    if hot is None:
        for row, column, value in order:
            rim[9, row, column] = value
    else:
        values = [value for _, _, value in order]
        values += [jnp.zeros((1, Z), F32)] * (16 - len(values))
        caps = jnp.concatenate(values, axis=0)
        for k in range(3):
            storage = spread(caps, hot, k) + BETA
            for n, (row, column, _) in enumerate(order):
                rim[9 + k, row, column] = storage[n : n + 1]


def row_parts(faces, rim):
    return faces_in(rim), faces_in(faces), faces_in(rim, EX - 7)


def run_rows(parts, first, last, body, init, unroll=3):
    low, middle, high = parts
    for i in range(first, OX):
        init = body(low, i, init)
    init = loop(max(first, OX), EX - 4, lambda i, carry: body(middle, i, carry), init, unroll)
    for i in range(EX - 4, last):
        init = body(high, i, init)
    return init


PAIRS = [(0, 0), (0, 1), (0, 2), (1, 1), (1, 2), (2, 2)]
FIRST_SUM = 9


def grid_mask(before, after):
    gx, gy = lax.axis_index("gx"), lax.axis_index("gy")
    gx_last, gy_last = lax.axis_size("gx") - 1, lax.axis_size("gy") - 1
    at = rows_of(EY)
    in_y = (at >= OY - jnp.where(gy > 0, before, 0)) & (
        at < OY + Y + jnp.where(gy < gy_last, after, 0)
    )

    def in_grid(i):
        in_x = ((i >= OX) | (gx > 0)) & ((i < OX + X) | (gx < gx_last))
        return in_y & in_x

    return in_grid


def load_rows(q_refs, targets, added):
    in_grid = grid_mask(1, 2)

    def row(i, carry):
        for q_ref, target in zip(q_refs, targets):
            load_row(q_ref, target, i, in_grid(i))
        return carry

    def load_row(q_ref, target, i, ok):
        first = lanes(EY) == 0
        q = q_ref[i - 1]
        push = [
            BIOT * (q_ref[i - 2] - q),
            BIOT * (down_y(q) - q),
            BIOT * (jnp.where(first, 0.0, down_z(q)) - q),
        ]
        for c in range(3):
            v = push[c] + target[c, i] if added else push[c]
            target[c, i] = jnp.where(ok, v, 0.0)

    loop(OX - 1, OX + X + 2, row)


def solid_image(parts, f_refs, p_refs, unroll):
    in_grid = grid_mask(0, 1)

    def row(faces, i, carry):
        ok, after = in_grid(i), []
        for f_ref, p_ref, (s, fx) in zip(f_refs, p_refs, carry):
            out, s, fx = solid_row(faces, f_ref, i, s, fx)
            for c in range(3):
                p_ref[c, i] = jnp.where(ok, out[c], 0.0)
            after.append((s, fx))
        return tuple(after)

    view = parts[0]
    start = [
        (view.own(0, OX - 1) * strain_row(f, OX - 1), x_flux(view, f, OX - 1)) for f in f_refs
    ]
    run_rows(parts, OX, OX + X + 1, row, tuple(start), unroll)


def gram_sums(faces, fields, products, pairs, acc):
    acc[...] = jnp.zeros(acc.shape, F32)
    vectors = range(len(fields))

    def row(i, carry):
        inside, last = tile_rows(), lanes(EY) == Z - 1

        def only(v):
            return jnp.where(inside, v, 0.0)

        def add(n, v):
            acc[n] = acc[n] + fold(v)

        strains = [strain_row(p, i) for p in products]
        modulus = only(faces[9, i])
        pushes = [modulus * e for e in strains]
        for n, (a, b) in enumerate(pairs):
            add(4 * n + 3, pushes[a] * strains[b])
        for c in range(3):
            ws = [p[c, i] for p in products]
            dx = [ws[a] - products[a][c, i + 1] for a in vectors]
            dy = [w - up_y(w) for w in ws]
            dz = [w - jnp.where(last, 0.0, up_z(w)) for w in ws]
            sx, sy, sz = (only(faces[3 * d + c, i]) for d in range(3))
            fx = [sx * d for d in dx]
            fy = [sy * d for d in dy]
            fz = [sz * d for d in dz]
            for n, (a, b) in enumerate(pairs):
                add(4 * n + 3, fx[a] * dx[b] + fy[a] * dy[b] + fz[a] * dz[b])
            rs = [only(f[c, i]) for f in fields]
            ws = [only(w) for w in ws]
            for n, (a, b) in enumerate(pairs):
                add(4 * n, rs[a] * rs[b])
                add(4 * n + 1, rs[a] * ws[b])
                add(4 * n + 2, ws[a] * ws[b])
        return carry

    loop(OX, OX + X, row, 0, 2)
    found = {}
    for n, pair in enumerate(pairs):
        for m in range(4):
            found[FIRST_SUM + 6 * m + PAIRS.index(pair)] = acc[4 * n + m]
    return found


def unit_surroundings(unit, halos, q):
    xl, xu, yl, yu = halos

    def place(x, carry):
        q[OX - 1 + x, OY : OY + Y] = unit[x]
        return carry

    loop(0, X, place)
    for depth, n in enumerate(Q_SLOT):
        q[OX - 2 - depth, OY : OY + Y] = xl[n]
        q[OX + X - 1 + depth, OY : OY + Y] = xu[n]
        rows = slice(n * X, (n + 1) * X)
        q[OX - 1 : OX - 1 + X, OY - 1 - depth, :] = yl[rows]
        q[OX - 1 : OX - 1 + X, OY + Y + depth, :] = yu[rows]
    for v, pack in enumerate((yl, yu)):
        for h in range(2):
            for n, (i, j) in enumerate(CORNER[:3]):
                row, column = corner_at((h, v), i, j)
                q[row - 1, column] = pack[AT_Q[h] + n : AT_Q[h] + n + 1]


def late_terms(faces, rim, field, beside, halos):
    yl, yu = halos[2:]

    def modulus(x, y):
        i, column = OX + x, slice(OY + y, OY + y + 1)
        return rim[9, RIM.index(i), column] if i in RIM else faces[9, i, column]

    u1 = [yu[AT_U + 1 : AT_U + 2]] + [beside[n : n + 1] for n in (1, 2, 3)]
    u0 = [yl[AT_U + 2 : AT_U + 3]] + [beside[n : n + 1] for n in (5, 6, 7)]
    for u, (x, y) in zip(u1, ((0, Y - 1), (X, Y - 1), (0, -1), (X, -1))):
        row, column = OX + x, slice(OY + y, OY + y + 1)
        field[0, row, column] = field[0, row, column] - modulus(x - 1, y) * u
    for u, (x, y) in zip(u0, ((X - 1, 0), (-1, 0), (X - 1, Y), (-1, Y))):
        row, column = OX + x, slice(OY + y, OY + y + 1)
        field[1, row, column] = field[1, row, column] - modulus(x, y - 1) * u


def image_kernel(residual, unit_old, beside, layer_map, *refs):
    halos, (faces, k_rim_in, rim, field, product, unit, k_rim, q) = refs[:4], refs[4:]
    halos = surroundings(*halos)
    flow = lax.axis_index("group") == 0
    fill(residual, field, halos)

    @pl.when(flow)
    def _():
        hot = one_hot(layer_map)
        complete(faces, rim, k_rim_in, k_rim, halos, hot)
        parts = row_parts(faces, rim)

        def row(view, i, fx_before):
            out, fx = flow_row(view, field, i, fx_before)
            for k in range(3):
                product[k, i] = out[k]
            return fx

        run_rows(parts, 1, EX - 1, row, x_flux(parts[0], field, 0))
        unit[0] = gather_wide(field, hot)
        unit[1] = gather_wide(product, hot)

    @pl.when(jnp.logical_not(flow))
    def _():
        complete(faces, rim, k_rim_in, k_rim, halos, None)
        late_terms(faces, rim, field, beside, halos)
        unit_surroundings(unit_old, halos, q)
        load_rows([q], [field], True)
        solid_image(row_parts(faces, rim), [field], [product], 3)


def early_kernel(field, product, faces, state, sums, acc):
    flow = lax.axis_index("group") == 0

    @pl.when(flow)
    def _():
        def dots(i, acc):
            acc = list(acc)
            inside, last = tile_rows(), lanes(EY) == Z - 1

            def add(n, v):
                acc[n] = acc[n] + fold(jnp.where(inside, v, 0.0))

            ws = [product[k, i] for k in range(3)]
            below = flow_below(ws, last)
            g = m1 = m2 = m3 = cr = cw = 0.0
            for k in range(3):
                r, w = field[k, i], ws[k]
                dx, dy, dz = w - product[k, i + 1], w - up_y(w), w - below[k]
                cf = faces[9 + k, i]
                g = g + r * r
                m1 = m1 + r * w
                m2 = m2 + w * w
                cr = cr + cf * r
                cw = cw + cf * w
                m3 = m3 + (
                    faces[k, i] * dx * dx
                    + faces[3 + k, i] * dy * dy
                    + faces[6 + k, i] * dz * dz
                    + cf * w * w
                )
            for n, v in enumerate((g, m1, m2, m3, cr, cw)):
                add(n, v)
            weight = jnp.where(last, faces[8, i], 0.0)
            add(6, weight * field[2, i])
            add(7, weight * ws[2])
            acc[8] = acc[8] + fold(to_tile(weight) * state[2, i - OX])
            return tuple(acc)

        zero = jnp.zeros((8, Z), F32)
        found = dict(enumerate(loop(OX, OX + X, dots, (zero,) * FIRST_SUM, 2)))
        sums[...] = spread_sums(found)

    @pl.when(jnp.logical_not(flow))
    def _():
        sums[...] = spread_sums(gram_sums(faces, [field], [product], PAIRS[:1], acc))


def sums_kernel(field, product, faces, rim, unit, sums_in, sums, field12, product12, acc):
    flow = lax.axis_index("group") == 0
    everyone = sums.shape[0]

    @pl.when(flow)
    def _():
        sums[...] = jnp.broadcast_to(sums_in[:1], (everyone, Z))

    @pl.when(jnp.logical_not(flow))
    def _():
        fields = [field] + [field12.at[a] for a in range(2)]
        products = [product] + [product12.at[a] for a in range(2)]
        load_rows([unit.at[a] for a in range(2)], fields[1:], False)
        solid_image(row_parts(faces, rim), fields[1:], products[1:], 2)
        found = gram_sums(faces, fields, products, PAIRS[1:], acc)
        own = sums_in[:1] + spread_sums(found)[:1]
        sums[...] = jnp.broadcast_to(own, (everyone, Z))


def two_sum(a, b):
    s = a + b
    t = s - a
    return s, (a - (s - t)) + (b - t)


def quick(a, b):
    s = a + b
    return s, b - (s - a)


def halves(a):
    t = 4097.0 * a
    high = t - (t - a)
    return high, a - high


def two_product(a, b):
    p = a * b
    ah, al = halves(a)
    bh, bl = halves(b)
    return p, ((ah * bh - p) + ah * bl + al * bh) + al * bl


def pair_add(a, b):
    s, e = two_sum(a[0], b[0])
    return quick(s, e + (a[1] + b[1]))


def pair_less(a, b):
    return pair_add(a, (-b[0], -b[1]))


def pair_times(a, b):
    p, e = two_product(a[0], b[0])
    return quick(p, e + (a[0] * b[1] + a[1] * b[0]))


def pair_over(a, b):
    q = a[0] / b[0]
    rest = pair_less(a, pair_times(b, (q, jnp.zeros_like(q))))
    return quick(q, rest[0] / b[0])


def krylov(g, m1, m2, m3):
    a0 = pair_over(g, m1)
    h = pair_times(a0, pair_over(m2, m1))
    one = (jnp.ones_like(a0[0]), jnp.zeros_like(a0[0]))
    rho = pair_less(h, one)[0]
    third = pair_times(pair_times(a0, a0), pair_over(m3, m1))
    sigma = pair_less(third, pair_times(h, h))[0]
    more = (rho > 1e-9) & (sigma > 1e-9)
    a1 = jnp.where(more, a0[0] * rho / jnp.where(more, sigma, 1.0), 0.0)
    return a0[0] + a1 * h[0], -a0[0] * a1


def final_kernel(sums, state, field, product, field12, product12, out, balance, *, cells):
    flow = lax.axis_index("group") == 0
    total = (sums[...], jnp.zeros(sums.shape, F32))
    while total[0].shape[0] > 8:
        half = total[0].shape[0] // 2
        total = pair_add([v[:half] for v in total], [v[half:] for v in total])
    for step in (4, 2, 1):
        total = pair_add(total, [pltpu.roll(v, step, 0) for v in total])

    def number(n):
        return tuple(jnp.broadcast_to(v[:1, n : n + 1], (8, Z)) for v in total)

    c0, c1 = krylov(number(0), number(1), number(2), number(3))
    columns = cells // (3 * Z)
    outflow = (number(8)[0] + c0 * number(6)[0] + c1 * number(7)[0]) / columns
    stored = (c0 * number(4)[0] + c1 * number(5)[0]) / cells
    balance[0] = outflow[0, 0]
    balance[1] = stored[0, 0]

    def tall(v):
        return jnp.concatenate([v] * (EY // 8), axis=0)

    @pl.when(flow)
    def _():
        s0, s1 = tall(c0), tall(c1)

        def row(x, carry):
            for k in range(3):
                step = s0 * field[k, OX + x] + s1 * product[k, OX + x]
                out[k, x] = state[k, x] + to_tile(step)
            return carry

        loop(0, X, row)

    @pl.when(jnp.logical_not(flow))
    def _():
        zero = jnp.zeros((8, Z), F32)
        weights = [
            (jnp.ones((8, Z), F32), zero),
            (2.0 * c0, zero),
            (2.0 * c1, zero),
            two_product(c0, c0),
            two_product(2.0 * c0, c1),
            two_product(c1, c1),
        ]
        moments = []
        for m in range(4):
            start = FIRST_SUM + 6 * m
            total = number(start)
            for n in range(1, 6):
                total = pair_add(total, pair_times(weights[n], number(start + n)))
            moments.append(total)
        d0, d1 = krylov(*moments)
        scale_r = [tall(d0), tall(d0 * c0), tall(d0 * c1)]
        scale_w = [tall(d1), tall(d1 * c0), tall(d1 * c1)]

        def row(x, carry):
            for c in range(3):
                step = scale_r[0] * field[c, OX + x] + scale_w[0] * product[c, OX + x]
                for a in range(2):
                    step = step + scale_r[a + 1] * field12[a, c, OX + x]
                    step = step + scale_w[a + 1] * product12[a, c, OX + x]
                out[c, x] = state[c, x] + to_tile(step)
            return carry

        loop(0, X, row)


def swaps(first, second, axis):
    groups, rows, columns = (lax.axis_size(a) for a in AXES)
    count, found = lax.axis_size(axis), []
    for value, start in ((first, 0), (second, 1)):
        pairs = []
        for g in range(groups):
            for i in range(rows):
                for j in range(columns):
                    place = i if axis == "gx" else j
                    step = 1 if place % 2 == start else -1
                    if 0 <= place + step < count:
                        here = (g * rows + i) * columns + j
                        pairs.append((here, here + step * (columns if axis == "gx" else 1)))
        found.append(lax.ppermute(value, AXES, pairs))
    return found


def to_group(value, source):
    rows, columns = lax.axis_size("gx"), lax.axis_size("gy")
    count = rows * columns
    pairs = [(source * count + n, (1 - source) * count + n) for n in range(count)]
    return lax.ppermute(value, AXES, pairs)


def body(state, conduct, capacity, supply, flags, layer_map):
    state, conduct, capacity, supply = state[0], conduct[0], capacity[0], supply[0]
    layer_map = layer_map.reshape(1, 3 * Z)
    cells = X * Y * 3 * Z * lax.axis_size("gx") * lax.axis_size("gy")
    devices = lax.axis_size("group") * lax.axis_size("gx") * lax.axis_size("gy")
    tile = struct(3, X, Y, Z)
    brick = struct(X, Y, Z)
    wide = (EX, EY, Z)
    full = struct(3, *wide)

    y_face = struct(len(Y_ROWS), X, Z)
    tz, xa, xb, ya, yb = call(
        pack_kernel,
        [tile] + x_faces(X_ROWS) + [y_face] * 2,
        [
            pltpu.VMEM((X, Y), jnp.int32),
            pltpu.VMEM((3, X, Y, Z), F32),
            pltpu.VMEM((3, 3, X, Y, Z), F32),
            pltpu.VMEM((X, Y, Z), F32),
            pltpu.VMEM((X, Y, Z), F32),
            pltpu.SemaphoreType.DMA((14,)),
        ],
        left=(0, 1, 2, 3),
        limit=58,
        count=4,
    )(flags, state, conduct, capacity)
    k_halos = lax.optimization_barrier(swaps(xa, xb, "gx") + swaps(ya, yb, "gy"))
    wide_faces = struct(12, *wide)
    tables = [pltpu.VMEM((6, *wide), F32), pltpu.VMEM(wide, F32)]
    inner, unit0 = call(interior_kernel, [wide_faces, brick], tables, cost=30_000_000)(
        state, conduct, capacity, tz, layer_map
    )
    unit0 = to_group(unit0, 0)
    strain = call(strain_kernel, brick)(state, *k_halos)
    strain = to_group(strain, 1)
    base, beside = call(
        first_kernel,
        [tile, struct(8, Z)],
        tables + [pltpu.VMEM((3, *wide), F32)],
        cost=20_000_000,
    )(state, conduct, capacity, supply, inner, *k_halos)
    faces, k_rim = call(
        halo_kernel, [wide_faces, struct(6, len(K_RIM), EY, Z)], tables, cost=30_000_000
    )(conduct, capacity, tz, layer_map, *k_halos)
    residual, xa, xb = call(residual_kernel, [tile] + x_faces(R_ROWS))(
        base, strain, unit0, layer_map
    )
    halos = swaps(xa, xb, "gx")
    ya, yb = call(relay_kernel, [struct(Y_PACK, Z)] * 2)(
        residual, unit0, *halos, k_halos[0], k_halos[1]
    )
    halos = halos + swaps(ya, yb, "gy")
    rim, field, product, unit12 = call(
        image_kernel,
        [struct(12, len(RIM), EY, Z), full, full, struct(2, EX - 2, EY, Z)],
        [pltpu.VMEM((6, len(K_RIM), EY, Z), F32), pltpu.VMEM((EX - 2, EY, Z), F32)],
    )(residual, unit0, beside, layer_map, *halos, faces, k_rim)
    unit12 = to_group(unit12, 0)
    sums = call(early_kernel, struct(8, Z), [pltpu.VMEM((4, 8, Z), F32)], cost=20_000_000)(
        field, product, faces, state
    )
    sums, field12, product12 = call(
        sums_kernel,
        [struct(devices, Z), struct(2, 3, *wide), struct(2, 3, *wide)],
        [pltpu.VMEM((20, 8, Z), F32)],
    )(field, product, faces, rim, unit12, sums)
    sums = lax.all_to_all(sums, AXES, 0, 0, tiled=True)

    def finish(*refs):
        final_kernel(*refs, cells=cells)

    new_state, balance = call(finish, [tile, struct(2)], scalars=(1,))(
        sums, state, field, product, field12, product12
    )
    return new_state[None], balance


def solution(mesh):
    placed = (
        P("group", None, "gx", "gy", None),
        P("group", None, None, "gx", "gy", None),
        P("group", "gx", "gy", None),
        P("group", None, "gx", "gy", None),
        P("gx", "gy"),
        P(),
    )
    return jax.shard_map(
        body,
        mesh=mesh,
        in_specs=placed,
        out_specs=(P("group", None, "gx", "gy", None), P()),
        check_vma=False,
    )
```

```python
import jax
import jax.numpy as jnp
from jax import lax
from jax.experimental import pallas as pl
from jax.experimental.pallas import tpu as pltpu
from jax.sharding import PartitionSpec as P

AXES = ("group", "gx", "gy")
X, Y, Z = 16, 32, 128
OX, OY = 3, 4
EX, EY = X + 2 * OX, Y + 2 * OY
BETA = 0.5
BIOT = 0.8
F32 = jnp.float32

X_ROWS = [(f, r) for f in range(13) for r in range(1, (3 if f < 3 else 2 if f < 10 else 1) + 1)]
Y_ROWS = [
    (f, r) for f in range(13) for r in range(1, (3 if 3 <= f < 6 else 2 if f < 10 else 1) + 1)
]
CORNER = [(1, 1), (1, 2), (2, 1), (2, 2), (1, 3), (3, 1)]
K_CORNERS = (
    [(f, i, j) for f in range(3) for i, j in CORNER[:4] + [(3, 1)]]
    + [(f, i, j) for f in range(3, 6) for i, j in CORNER[:4] + [(1, 3)]]
    + [(f, i, j) for f in range(6, 10) for i, j in CORNER[:3]]
)
R_ROWS = [(f, r) for f in range(3) for r in range(1, 4)]
R_CORNERS = [(f, i, j) for f in range(3) for i, j in CORNER]
AT_R = [len(R_ROWS) * X, len(R_ROWS) * X + len(R_CORNERS)]
AT_K = [AT_R[1] + len(R_CORNERS), AT_R[1] + len(R_CORNERS) + len(K_CORNERS)]
AT_Q = [AT_K[1] + len(K_CORNERS), AT_K[1] + len(K_CORNERS) + 3]
AT_U = AT_Q[1] + 3
Y_PACK = -(-(AT_U + 4) // 8) * 8
Q_SLOT = [R_ROWS.index((0, 3)), R_ROWS.index((1, 3))]


def struct(*shape):
    return jax.ShapeDtypeStruct(shape, F32)


def call(kernel, outs, scratch=(), left=(), count=0, cost=None, limit=20, scalars=()):
    extra = {}
    if left:
        extra["in_specs"] = [
            pl.BlockSpec(memory_space=pltpu.HBM if n in left else pltpu.VMEM) for n in range(count)
        ]
    if scalars:
        extra["out_specs"] = [
            pl.BlockSpec(memory_space=pltpu.SMEM if n in scalars else pltpu.VMEM)
            for n in range(len(outs))
        ]
    if cost:
        extra["cost_estimate"] = pl.CostEstimate(
            flops=cost, bytes_accessed=cost, transcendentals=0
        )
    return pl.pallas_call(
        kernel,
        out_shape=outs,
        scratch_shapes=list(scratch),
        compiler_params=pltpu.CompilerParams(vmem_limit_bytes=limit << 20),
        **extra,
    )


def up_y(v):
    return pltpu.roll(v, v.shape[0] - 1, 0)


def down_y(v):
    return pltpu.roll(v, 1, 0)


def up_z(v):
    return pltpu.roll(v, Z - 1, 1)


def down_z(v):
    return pltpu.roll(v, 1, 1)


def lanes(rows):
    return lax.broadcasted_iota(jnp.int32, (rows, Z), 1)


def rows_of(rows):
    return lax.broadcasted_iota(jnp.int32, (rows, Z), 0)


def to_tile(v):
    return pltpu.roll(v, EY - OY, 0)[:Y]


def harmonic(a, b):
    return 2.0 * a * b / jnp.maximum(a + b, 1e-30)


def one_hot(map_ref):
    brick = lax.broadcasted_iota(jnp.int32, (Z, 3 * Z), 0)
    return jnp.where(brick == map_ref[...], 1.0, 0.0).astype(jnp.bfloat16)


def dot_split(v, hot, contract):
    high = v.astype(jnp.bfloat16)
    low = (v - high.astype(F32)).astype(jnp.bfloat16)
    dims = (((1,), (contract,)), ((), ()))
    return lax.dot_general(high, hot, dims, preferred_element_type=F32) + lax.dot_general(
        low, hot, dims, preferred_element_type=F32
    )


def spread(v, hot, k):
    return dot_split(v, hot[:, k * Z : (k + 1) * Z], 0)


def gather_up(parts, hot):
    total = None
    for k, v in enumerate(parts):
        part = dot_split(v, hot[:, k * Z : (k + 1) * Z], 1)
        total = part if total is None else total + part
    ones = jnp.ones((8, 3 * Z), jnp.bfloat16)
    counts = lax.dot_general(ones, hot, (((1,), (1,)), ((), ())), preferred_element_type=F32)
    return total * (1.0 / counts[:1])


def gather_wide(ref, hot):
    rows = EX - 2
    parts = [ref[k, 1 : EX - 1].reshape(rows * EY, Z) for k in range(3)]
    return gather_up(parts, hot).reshape(rows, EY, Z)


def fetch(pairs, sem, start=0):
    copies = [pltpu.make_async_copy(a, b, sem.at[start + n]) for n, (a, b) in enumerate(pairs)]
    for copy in copies:
        copy.start()
    return copies


class Either:
    def __init__(self, odd, at_odd, at_even):
        self.odd, self.at_odd, self.at_even = odd, at_odd, at_even

    def __getitem__(self, at):
        return jnp.where(self.odd, self.at_odd[at], self.at_even[at])


def parity(axis):
    return lax.rem(lax.axis_index(axis), 2) == 1


def lower_upper(axis, first, second):
    odd = parity(axis)
    return Either(odd, first, second), Either(odd, second, first)


def surroundings(xa, xb, ya, yb):
    return lower_upper("gx", xa, xb) + lower_upper("gy", ya, yb)


def put(first, second, at, odd, tail, head):
    first[at] = jnp.where(odd, head, tail)
    second[at] = jnp.where(odd, tail, head)


def pack_x(source, rows, first, second):
    odd = parity("gx")
    for n, (f, r) in enumerate(rows):
        put(first, second, n, odd, source(f)[X - r], source(f)[r - 1])


def unpack_x(target, rows, low, up):
    for n, (f, r) in enumerate(rows):
        target(f)[OX - r, OY : OY + Y] = low[n]
        target(f)[OX + X - 1 + r, OY : OY + Y] = up[n]


def corner_at(side, i, j):
    row = OX - i if side[0] == 0 else OX + X - 1 + i
    column = OY - j if side[1] == 0 else OY + Y - 1 + j
    return row, slice(column, column + 1)


def x_faces(rows):
    return [struct(len(rows), Y, Z)] * 2


def loop(first, last, body, init=0, unroll=4):
    steps = (last - first) // unroll

    def step(n, carry):
        for m in range(unroll):
            carry = body(first + n * unroll + m, carry)
        return carry

    init = lax.fori_loop(0, steps, step, init)
    for i in range(first + steps * unroll, last):
        init = body(i, init)
    return init


def vertical_faces(conduct, flags, bottom, store):
    flow = lax.axis_index("group") == 0
    last = lanes(Y) == Z - 1
    eye = jnp.where(
        lax.broadcasted_iota(jnp.int32, (Y, Y), 0) == lax.broadcasted_iota(jnp.int32, (Y, Y), 1),
        1.0,
        0.0,
    ).astype(jnp.bfloat16)
    columns = lax.dot_general(
        eye,
        flags[...].astype(F32).astype(jnp.bfloat16),
        (((1,), (1,)), ((), ())),
        preferred_element_type=F32,
    )
    for x in range(X):
        bottom[x] = jnp.broadcast_to(columns[:, x : x + 1], (Y, Z))

    def row(x, carry):
        kz = [conduct[2, k, x] for k in range(3)]
        rolled = [up_z(v) for v in kz]
        ends = [rolled[1], rolled[2], bottom[x] * kz[2]]
        for k in range(3):
            end = jnp.where(flow, ends[k], kz[k])
            store(x, k, harmonic(kz[k], jnp.where(last, end, rolled[k])))
        return carry

    loop(0, X, row)


def pack_kernel(flags_in, state_in, conduct_in, capacity_in, xa, xb, ya, yb, *scratch):
    flags, state, conduct, capacity, bottom, tz, sem = scratch
    early = [(flags_in, flags)] + [(conduct_in.at[2, k], conduct.at[2, k]) for k in range(3)]
    late = [(conduct_in.at[d, k], conduct.at[d, k]) for d in range(2) for k in range(3)]
    late += [(state_in.at[k], state.at[k]) for k in range(3)] + [(capacity_in, capacity)]
    early = fetch(early, sem)
    late = fetch(late, sem, len(early))
    for copy in early:
        copy.wait()
    def store(x, k, value):
        tz[k, x] = value

    vertical_faces(conduct, flags, bottom, store)
    for copy in late:
        copy.wait()

    def source(f):
        if f < 6:
            return conduct.at[f // 3, f % 3]
        if f < 9:
            return tz.at[f - 6]
        return capacity if f == 9 else state.at[f - 10]

    pack_x(source, X_ROWS, xa, xb)
    odd = parity("gy")
    for n, (f, r) in enumerate(Y_ROWS):
        put(ya, yb, n, odd, source(f)[:, Y - r, :], source(f)[:, r - 1, :])


class Faces:
    def __init__(self, x, y, z, own):
        self.x, self.y, self.z, self.own = x, y, z, own


def faces_in(ref, shift=0):
    return Faces(*[lambda c, i, d=d: ref[3 * d + c, i - shift] for d in range(4)])


def lateral(faces, v_ref, c, i, v, fx_before):
    fx = faces.x(c, i) * (v - v_ref[c, i + 1])
    fy = faces.y(c, i) * (v - up_y(v))
    return (fx - fx_before) + (fy - down_y(fy)), fx


def x_flux(faces, v_ref, i):
    return tuple(faces.x(c, i) * (v_ref[c, i] - v_ref[c, i + 1]) for c in range(3))


def flow_below(vs, last):
    rolled = [up_z(v) for v in vs]
    ends = [rolled[1], rolled[2], 0.0]
    return [jnp.where(last, ends[k], rolled[k]) for k in range(3)]


def flow_row(faces, v_ref, i, fx_before):
    last, first = lanes(EY) == Z - 1, lanes(EY) == 0
    vs = [v_ref[k, i] for k in range(3)]
    below = flow_below(vs, last)
    fz = [faces.z(k, i) * (vs[k] - below[k]) for k in range(3)]
    moved = [down_z(v) for v in fz]
    ends = [0.0, moved[0], moved[1]]
    out, fx_now = [], []
    for k in range(3):
        side, fx = lateral(faces, v_ref, k, i, vs[k], fx_before[k])
        above = jnp.where(first, ends[k], moved[k])
        out.append(faces.own(k, i) * vs[k] + side + (fz[k] - above))
        fx_now.append(fx)
    return out, tuple(fx_now)


def strain_row(v_ref, i):
    v0, v1, v2 = v_ref[0, i], v_ref[1, i], v_ref[2, i]
    low = jnp.where(lanes(EY) == Z - 1, 0.0, up_z(v2))
    return (v_ref[0, i + 1] - v0) + (up_y(v1) - v1) + (low - v2)


def solid_row(faces, v_ref, i, s_before, fx_before):
    last, first = lanes(EY) == Z - 1, lanes(EY) == 0
    e = strain_row(v_ref, i)
    s = faces.own(0, i) * e
    grad = [s_before - s, down_y(s) - s, jnp.where(first, 0.0, down_z(s)) - s]
    out, fx_now = [], []
    for c in range(3):
        v = v_ref[c, i]
        side, fx = lateral(faces, v_ref, c, i, v, fx_before[c])
        fz = faces.z(c, i) * (v - jnp.where(last, 0.0, up_z(v)))
        above = jnp.where(first, 0.0, down_z(fz))
        out.append((side + (fz - above)) + grad[c])
        fx_now.append(fx)
    return out, s, tuple(fx_now)


BESIDE = [(1, -1, Y), (1, X - 1, Y), (1, -1, 0), (1, X - 1, 0)]
BESIDE += [(0, X, -1), (0, 0, -1), (0, X, Y - 1), (0, 0, Y - 1)]


def place_tile(conduct, capacity, keep, caps):
    at = slice(OY, OY + Y)

    def row(x, carry):
        for f in range(6):
            keep[f, OX + x, at] = conduct[f // 3, f % 3, x]
        caps[OX + x, at] = capacity[x]
        return carry

    loop(0, X, row)


def interior_kernel(state, conduct, capacity, flags, layer_map, faces, tz, unit, keep, caps, bottom):
    flow = lax.axis_index("group") == 0
    place_tile(conduct, capacity, keep, caps)

    def store(x, k, value):
        tz[k, x] = value
        faces[6 + k, OX + x, OY : OY + Y] = value

    vertical_faces(conduct, flags, bottom, store)
    loop(OX, OX + X, lambda i, carry: lateral_faces(keep, faces, i))

    @pl.when(flow)
    def _():
        hot = one_hot(layer_map)
        bricks = caps[OX : OX + X].reshape(X * EY, Z)
        for k in range(3):
            faces[9 + k, OX : OX + X] = (spread(bricks, hot, k) + BETA).reshape(X, EY, Z)
        parts = [state[k].reshape(X * Y, Z) for k in range(3)]
        unit[...] = gather_up(parts, hot).reshape(X, Y, Z)


def lateral_faces(keep, faces, i):
    for c in range(3):
        faces[c, i] = harmonic(keep[c, i], keep[c, i + 1])
        here = keep[3 + c, i]
        faces[3 + c, i] = harmonic(here, up_y(here))
    return 0


def strain_kernel(state, unit, xa, xb, ya, yb, strain):
    flow = lax.axis_index("group") == 0
    _, xu, _, yu = surroundings(xa, xb, ya, yb)

    @pl.when(flow)
    def _():
        strain[...] = unit[...]

    @pl.when(jnp.logical_not(flow))
    def _():
        last = lanes(Y) == Z - 1
        edge = rows_of(Y) == Y - 1
        n_x, n_y = X_ROWS.index((10, 1)), Y_ROWS.index((11, 1))
        for x in range(X):
            v0, v1, v2 = (state[c, x] for c in range(3))
            east = state[0, x + 1] if x + 1 < X else xu[n_x]
            north = jnp.where(edge, yu[n_y, x : x + 1], up_y(v1))
            low = jnp.where(last, 0.0, up_z(v2))
            strain[x] = (east - v0) + (north - v1) + (low - v2)


def first_kernel(state, conduct, capacity, supply, faces_ref, xa, xb, ya, yb, *refs):
    xl, xu, yl, yu = surroundings(xa, xb, ya, yb)
    base, beside, sides, own, field = refs
    flow = lax.axis_index("group") == 0

    def place(x, carry):
        for c in range(3):
            field[c, OX + x, OY : OY + Y] = state[c, x]
        for f in range(6):
            sides[f, OX + x] = faces_ref[f, OX + x]
        return carry

    loop(0, X, place)
    for c in range(3):
        n = X_ROWS.index((10 + c, 1))
        field[c, OX - 1, OY : OY + Y] = xl[n]
        field[c, OX + X, OY : OY + Y] = xu[n]
        n = Y_ROWS.index((10 + c, 1))
        field[c, OX : OX + X, OY - 1, :] = yl[n]
        field[c, OX : OX + X, OY + Y, :] = yu[n]
        n = X_ROWS.index((c, 1))
        at = slice(OY, OY + Y)
        sides[c, OX - 1, at] = harmonic(xl[n], conduct[0, c, 0])
        sides[c, OX + X - 1, at] = harmonic(conduct[0, c, X - 1], xu[n])
        n = Y_ROWS.index((3 + c, 1))
        sides[3 + c, OX : OX + X, OY - 1, :] = harmonic(yl[n], conduct[1, c, :, 0, :])
        sides[3 + c, OX : OX + X, OY + Y - 1, :] = harmonic(conduct[1, c, :, Y - 1, :], yu[n])
    field[1, OX - 1, OY + Y : OY + Y + 1] = jnp.zeros((1, Z), F32)
    field[0, OX + X, OY - 1 : OY] = jnp.zeros((1, Z), F32)
    for n, (c, x, y) in enumerate(BESIDE):
        beside[n : n + 1] = field[c, OX + x, OY + y : OY + y + 1]
    inner = faces_in(faces_ref)
    outer = faces_in(sides)

    @pl.when(flow)
    def _():
        faces = Faces(outer.x, outer.y, inner.z, inner.own)

        def row(i, fx_before):
            image, fx = flow_row(faces, field, i, fx_before)
            for k in range(3):
                base[k, i - OX] = (
                    supply[k, i - OX] + BETA * state[k, i - OX] - to_tile(image[k])
                )
            return fx

        loop(OX, OX + X, row, x_flux(faces, field, OX - 1))

    @pl.when(jnp.logical_not(flow))
    def _():
        def place(x, carry):
            own[OX + x, OY : OY + Y] = capacity[x]
            return carry

        loop(0, X, place)
        own[OX - 1, OY : OY + Y] = xl[X_ROWS.index((9, 1))]
        own[OX : OX + X, OY - 1, :] = yl[Y_ROWS.index((9, 1))]
        faces = Faces(outer.x, outer.y, inner.z, lambda c, i: own[i])

        def row(i, carry):
            image, s, fx = solid_row(faces, field, i, carry[0], carry[1])
            for c in range(3):
                base[c, i - OX] = supply[c, i - OX] - to_tile(image[c])
            return s, fx

        before = faces.own(0, OX - 1) * strain_row(field, OX - 1)
        loop(OX, OX + X, row, (before, x_flux(faces, field, OX - 1)))


def halo_kernel(conduct, capacity, tz, layer_map, xa, xb, ya, yb, faces, rim, keep, caps):
    xl, xu, yl, yu = surroundings(xa, xb, ya, yb)
    flow = lax.axis_index("group") == 0

    def target(f):
        if f < 6:
            return keep.at[f]
        return faces.at[f] if f < 9 else caps

    place_tile(conduct, capacity, keep, caps)

    def place(x, carry):
        for k in range(3):
            faces[6 + k, OX + x, OY : OY + Y] = tz[k, x]
        return carry

    loop(0, X, place)
    for n, (f, r) in enumerate(X_ROWS):
        if f < 10:
            target(f)[OX - r, OY : OY + Y] = xl[n]
            target(f)[OX + X - 1 + r, OY : OY + Y] = xu[n]
    for n, (f, r) in enumerate(Y_ROWS):
        if f < 10:
            target(f)[OX : OX + X, OY - r, :] = yl[n]
            target(f)[OX : OX + X, OY + Y - 1 + r, :] = yu[n]
    loop(0, EX - 1, lambda i, carry: lateral_faces(keep, faces, i))
    for n, i in enumerate(K_RIM):
        for f in range(6):
            rim[f, n] = keep[f, i]

    @pl.when(flow)
    def _():
        hot = one_hot(layer_map)
        bricks = caps[1 : EX - 1].reshape((EX - 2) * EY, Z)
        for k in range(3):
            faces[9 + k, 1 : EX - 1] = (spread(bricks, hot, k) + BETA).reshape(EX - 2, EY, Z)

    @pl.when(jnp.logical_not(flow))
    def _():
        faces[9] = caps[...]


BESIDE = [(1, -1, Y), (1, X - 1, Y), (1, -1, 0), (1, X - 1, 0)]
BESIDE += [(0, X, -1), (0, 0, -1), (0, X, Y - 1), (0, 0, Y - 1)]
RIM = [0, 1, 2, EX - 4, EX - 3, EX - 2]
K_RIM = [0, 1, 2, 3, EX - 4, EX - 3, EX - 2, EX - 1]


def residual_kernel(base, strain, unit, layer_map, residual, xa, xb):
    flow = lax.axis_index("group") == 0

    @pl.when(flow)
    def _():
        hot = one_hot(layer_map)
        e = strain[...].reshape(X * Y, Z)
        for k in range(3):
            residual[k] = base[k] - BIOT * spread(e, hot, k).reshape(X, Y, Z)

    @pl.when(jnp.logical_not(flow))
    def _():
        residual[...] = base[...]

    pack_x(lambda f: residual.at[f], R_ROWS, xa, xb)

    @pl.when(jnp.logical_not(flow))
    def _():
        odd = parity("gx")
        for depth, n in enumerate(Q_SLOT):
            put(xa, xb, n, odd, unit[X - 1 - depth], unit[depth])


def relay_kernel(residual, unit, xa, xb, ka, kb, ya, yb):
    flow = lax.axis_index("group") == 0
    odd = parity("gy")
    r_halos, k_halos = lower_upper("gx", xa, xb), lower_upper("gx", ka, kb)

    def give(at, count, ref, index, j):
        put(ya, yb, slice(at, at + count), odd, ref[index(Y - j)], ref[index(j - 1)])

    for n, (f, r) in enumerate(R_ROWS):
        give(n * X, X, residual, lambda y: (f, slice(None), y), r)
    for side in range(2):
        r_halo, k_halo = r_halos[side], k_halos[side]
        for n, (f, i, j) in enumerate(R_CORNERS):
            row = R_ROWS.index((f, i))
            give(AT_R[side] + n, 1, r_halo, lambda y: (row, slice(y, y + 1)), j)
        for n, (f, i, j) in enumerate(K_CORNERS):
            row = X_ROWS.index((f, i))
            give(AT_K[side] + n, 1, k_halo, lambda y: (row, slice(y, y + 1)), j)
        for n, (i, j) in enumerate(CORNER[:3]):
            row = Q_SLOT[i - 1]
            give(AT_Q[side] + n, 1, r_halo, lambda y: (row, slice(y, y + 1)), j)
        for c in range(2):
            row = X_ROWS.index((10 + c, 1))
            give(AT_U + 2 * side + c, 1, k_halo, lambda y: (row, slice(y, y + 1)), 1)

    @pl.when(jnp.logical_not(flow))
    def _():
        for depth, n in enumerate(Q_SLOT):
            give(n * X, X, unit, lambda y: (slice(None), y), depth + 1)


def fold(v):
    return jnp.sum(v.reshape(v.shape[0] // 8, 8, Z), axis=0)


def spread_sums(found):
    lane = lanes(8)
    row = jnp.zeros((8, Z), F32)
    first = rows_of(8) == 0
    for n, total in found.items():
        row = jnp.where(first & (lane == n), jnp.sum(total), row)
    return row


def tile_rows():
    at = rows_of(EY)
    return (at >= OY) & (at < OY + Y)


def fill(residual, target, halos):
    xl, xu, yl, yu = halos

    def place(x, carry):
        for k in range(3):
            target[k, OX + x, OY : OY + Y] = residual[k, x]
        return carry

    loop(0, X, place)
    unpack_x(lambda f: target.at[f], R_ROWS, xl, xu)
    for n, (f, r) in enumerate(R_ROWS):
        target[f, OX : OX + X, OY - r, :] = yl[n * X : (n + 1) * X]
        target[f, OX : OX + X, OY + Y - 1 + r, :] = yu[n * X : (n + 1) * X]
    for v, pack in enumerate((yl, yu)):
        for h in range(2):
            for n, (f, i, j) in enumerate(R_CORNERS):
                row, column = corner_at((h, v), i, j)
                target[f, row, column] = pack[AT_R[h] + n : AT_R[h] + n + 1]


def complete(faces, rim, k_rim_in, k_rim, halos, hot):
    for n, i in enumerate(RIM):
        for f in range(6, 12):
            rim[f, n] = faces[f, i]
    k_rim[...] = k_rim_in[...]
    order = []
    for v, pack in enumerate(halos[2:]):
        for h in range(2):
            for n, (f, i, j) in enumerate(K_CORNERS):
                row, column = corner_at((h, v), i, j)
                value = pack[AT_K[h] + n : AT_K[h] + n + 1]
                if f < 6:
                    k_rim[f, K_RIM.index(row), column] = value
                elif f < 9:
                    rim[f, RIM.index(row), column] = value
                else:
                    order.append((RIM.index(row), column, value))
    for n, i in enumerate(RIM):
        m = K_RIM.index(i)
        for c in range(3):
            rim[c, n] = harmonic(k_rim[c, m], k_rim[c, m + 1])
            here = k_rim[3 + c, m]
            rim[3 + c, n] = harmonic(here, up_y(here))
    if hot is None:
        for row, column, value in order:
            rim[9, row, column] = value
    else:
        values = [value for _, _, value in order]
        values += [jnp.zeros((1, Z), F32)] * (16 - len(values))
        caps = jnp.concatenate(values, axis=0)
        for k in range(3):
            storage = spread(caps, hot, k) + BETA
            for n, (row, column, _) in enumerate(order):
                rim[9 + k, row, column] = storage[n : n + 1]


def row_parts(faces, rim):
    return faces_in(rim), faces_in(faces), faces_in(rim, EX - 7)


def run_rows(parts, first, last, body, init, unroll=3):
    low, middle, high = parts
    for i in range(first, OX):
        init = body(low, i, init)
    init = loop(max(first, OX), EX - 4, lambda i, carry: body(middle, i, carry), init, unroll)
    for i in range(EX - 4, last):
        init = body(high, i, init)
    return init


PAIRS = [(0, 0), (0, 1), (0, 2), (1, 1), (1, 2), (2, 2)]
FIRST_SUM = 9


def grid_mask(before, after):
    gx, gy = lax.axis_index("gx"), lax.axis_index("gy")
    gx_last, gy_last = lax.axis_size("gx") - 1, lax.axis_size("gy") - 1
    at = rows_of(EY)
    in_y = (at >= OY - jnp.where(gy > 0, before, 0)) & (
        at < OY + Y + jnp.where(gy < gy_last, after, 0)
    )

    def in_grid(i):
        in_x = ((i >= OX) | (gx > 0)) & ((i < OX + X) | (gx < gx_last))
        return in_y & in_x

    return in_grid


def load_rows(q_refs, targets, added):
    in_grid = grid_mask(1, 2)

    def row(i, carry):
        for q_ref, target in zip(q_refs, targets):
            load_row(q_ref, target, i, in_grid(i))
        return carry

    def load_row(q_ref, target, i, ok):
        first = lanes(EY) == 0
        q = q_ref[i - 1]
        push = [
            BIOT * (q_ref[i - 2] - q),
            BIOT * (down_y(q) - q),
            BIOT * (jnp.where(first, 0.0, down_z(q)) - q),
        ]
        for c in range(3):
            v = push[c] + target[c, i] if added else push[c]
            target[c, i] = jnp.where(ok, v, 0.0)

    loop(OX - 1, OX + X + 2, row)


def solid_image(parts, f_refs, p_refs, unroll):
    in_grid = grid_mask(0, 1)

    def row(faces, i, carry):
        ok, after = in_grid(i), []
        for f_ref, p_ref, (s, fx) in zip(f_refs, p_refs, carry):
            out, s, fx = solid_row(faces, f_ref, i, s, fx)
            for c in range(3):
                p_ref[c, i] = jnp.where(ok, out[c], 0.0)
            after.append((s, fx))
        return tuple(after)

    view = parts[0]
    start = [
        (view.own(0, OX - 1) * strain_row(f, OX - 1), x_flux(view, f, OX - 1)) for f in f_refs
    ]
    run_rows(parts, OX, OX + X + 1, row, tuple(start), unroll)


def gram_sums(faces, fields, products, pairs, acc):
    acc[...] = jnp.zeros(acc.shape, F32)
    vectors = range(len(fields))

    def row(i, carry):
        inside, last = tile_rows(), lanes(EY) == Z - 1

        def only(v):
            return jnp.where(inside, v, 0.0)

        def add(n, v):
            acc[n] = acc[n] + fold(v)

        strains = [strain_row(p, i) for p in products]
        modulus = only(faces[9, i])
        pushes = [modulus * e for e in strains]
        for n, (a, b) in enumerate(pairs):
            add(4 * n + 3, pushes[a] * strains[b])
        for c in range(3):
            ws = [p[c, i] for p in products]
            dx = [ws[a] - products[a][c, i + 1] for a in vectors]
            dy = [w - up_y(w) for w in ws]
            dz = [w - jnp.where(last, 0.0, up_z(w)) for w in ws]
            sx, sy, sz = (only(faces[3 * d + c, i]) for d in range(3))
            fx = [sx * d for d in dx]
            fy = [sy * d for d in dy]
            fz = [sz * d for d in dz]
            for n, (a, b) in enumerate(pairs):
                add(4 * n + 3, fx[a] * dx[b] + fy[a] * dy[b] + fz[a] * dz[b])
            rs = [only(f[c, i]) for f in fields]
            ws = [only(w) for w in ws]
            for n, (a, b) in enumerate(pairs):
                add(4 * n, rs[a] * rs[b])
                add(4 * n + 1, rs[a] * ws[b])
                add(4 * n + 2, ws[a] * ws[b])
        return carry

    loop(OX, OX + X, row, 0, 2)
    found = {}
    for n, pair in enumerate(pairs):
        for m in range(4):
            found[FIRST_SUM + 6 * m + PAIRS.index(pair)] = acc[4 * n + m]
    return found


def unit_surroundings(unit, halos, q):
    xl, xu, yl, yu = halos

    def place(x, carry):
        q[OX - 1 + x, OY : OY + Y] = unit[x]
        return carry

    loop(0, X, place)
    for depth, n in enumerate(Q_SLOT):
        q[OX - 2 - depth, OY : OY + Y] = xl[n]
        q[OX + X - 1 + depth, OY : OY + Y] = xu[n]
        rows = slice(n * X, (n + 1) * X)
        q[OX - 1 : OX - 1 + X, OY - 1 - depth, :] = yl[rows]
        q[OX - 1 : OX - 1 + X, OY + Y + depth, :] = yu[rows]
    for v, pack in enumerate((yl, yu)):
        for h in range(2):
            for n, (i, j) in enumerate(CORNER[:3]):
                row, column = corner_at((h, v), i, j)
                q[row - 1, column] = pack[AT_Q[h] + n : AT_Q[h] + n + 1]


def late_terms(faces, rim, field, beside, halos):
    yl, yu = halos[2:]

    def modulus(x, y):
        i, column = OX + x, slice(OY + y, OY + y + 1)
        return rim[9, RIM.index(i), column] if i in RIM else faces[9, i, column]

    u1 = [yu[AT_U + 1 : AT_U + 2]] + [beside[n : n + 1] for n in (1, 2, 3)]
    u0 = [yl[AT_U + 2 : AT_U + 3]] + [beside[n : n + 1] for n in (5, 6, 7)]
    for u, (x, y) in zip(u1, ((0, Y - 1), (X, Y - 1), (0, -1), (X, -1))):
        row, column = OX + x, slice(OY + y, OY + y + 1)
        field[0, row, column] = field[0, row, column] - modulus(x - 1, y) * u
    for u, (x, y) in zip(u0, ((X - 1, 0), (-1, 0), (X - 1, Y), (-1, Y))):
        row, column = OX + x, slice(OY + y, OY + y + 1)
        field[1, row, column] = field[1, row, column] - modulus(x, y - 1) * u


def image_kernel(residual, unit_old, beside, layer_map, *refs):
    halos, (faces, k_rim_in, rim, field, product, unit, k_rim, q) = refs[:4], refs[4:]
    halos = surroundings(*halos)
    flow = lax.axis_index("group") == 0
    fill(residual, field, halos)

    @pl.when(flow)
    def _():
        hot = one_hot(layer_map)
        complete(faces, rim, k_rim_in, k_rim, halos, hot)
        parts = row_parts(faces, rim)

        def row(view, i, fx_before):
            out, fx = flow_row(view, field, i, fx_before)
            for k in range(3):
                product[k, i] = out[k]
            return fx

        run_rows(parts, 1, EX - 1, row, x_flux(parts[0], field, 0))
        unit[0] = gather_wide(field, hot)
        unit[1] = gather_wide(product, hot)

    @pl.when(jnp.logical_not(flow))
    def _():
        complete(faces, rim, k_rim_in, k_rim, halos, None)
        late_terms(faces, rim, field, beside, halos)
        unit_surroundings(unit_old, halos, q)
        load_rows([q], [field], True)
        solid_image(row_parts(faces, rim), [field], [product], 3)


def early_kernel(field, product, faces, state, sums, acc):
    flow = lax.axis_index("group") == 0

    @pl.when(flow)
    def _():
        def dots(i, acc):
            acc = list(acc)
            inside, last = tile_rows(), lanes(EY) == Z - 1

            def add(n, v):
                acc[n] = acc[n] + fold(jnp.where(inside, v, 0.0))

            ws = [product[k, i] for k in range(3)]
            below = flow_below(ws, last)
            g = m1 = m2 = m3 = cr = cw = 0.0
            for k in range(3):
                r, w = field[k, i], ws[k]
                dx, dy, dz = w - product[k, i + 1], w - up_y(w), w - below[k]
                cf = faces[9 + k, i]
                g = g + r * r
                m1 = m1 + r * w
                m2 = m2 + w * w
                cr = cr + cf * r
                cw = cw + cf * w
                m3 = m3 + (
                    faces[k, i] * dx * dx
                    + faces[3 + k, i] * dy * dy
                    + faces[6 + k, i] * dz * dz
                    + cf * w * w
                )
            for n, v in enumerate((g, m1, m2, m3, cr, cw)):
                add(n, v)
            weight = jnp.where(last, faces[8, i], 0.0)
            add(6, weight * field[2, i])
            add(7, weight * ws[2])
            acc[8] = acc[8] + fold(to_tile(weight) * state[2, i - OX])
            return tuple(acc)

        zero = jnp.zeros((8, Z), F32)
        found = dict(enumerate(loop(OX, OX + X, dots, (zero,) * FIRST_SUM, 2)))
        sums[...] = spread_sums(found)

    @pl.when(jnp.logical_not(flow))
    def _():
        sums[...] = spread_sums(gram_sums(faces, [field], [product], PAIRS[:1], acc))


def sums_kernel(field, product, faces, rim, unit, sums_in, sums, field12, product12, acc):
    flow = lax.axis_index("group") == 0
    everyone = sums.shape[0]

    @pl.when(flow)
    def _():
        sums[...] = jnp.broadcast_to(sums_in[:1], (everyone, Z))

    @pl.when(jnp.logical_not(flow))
    def _():
        fields = [field] + [field12.at[a] for a in range(2)]
        products = [product] + [product12.at[a] for a in range(2)]
        load_rows([unit.at[a] for a in range(2)], fields[1:], False)
        solid_image(row_parts(faces, rim), fields[1:], products[1:], 2)
        found = gram_sums(faces, fields, products, PAIRS[1:], acc)
        own = sums_in[:1] + spread_sums(found)[:1]
        sums[...] = jnp.broadcast_to(own, (everyone, Z))


def two_sum(a, b):
    s = a + b
    t = s - a
    return s, (a - (s - t)) + (b - t)


def quick(a, b):
    s = a + b
    return s, b - (s - a)


def halves(a):
    t = 4097.0 * a
    high = t - (t - a)
    return high, a - high


def two_product(a, b):
    p = a * b
    ah, al = halves(a)
    bh, bl = halves(b)
    return p, ((ah * bh - p) + ah * bl + al * bh) + al * bl


def pair_add(a, b):
    s, e = two_sum(a[0], b[0])
    return quick(s, e + (a[1] + b[1]))


def pair_less(a, b):
    return pair_add(a, (-b[0], -b[1]))


def pair_times(a, b):
    p, e = two_product(a[0], b[0])
    return quick(p, e + (a[0] * b[1] + a[1] * b[0]))


def pair_over(a, b):
    q = a[0] / b[0]
    rest = pair_less(a, pair_times(b, (q, jnp.zeros_like(q))))
    return quick(q, rest[0] / b[0])


def krylov(g, m1, m2, m3):
    a0 = pair_over(g, m1)
    h = pair_times(a0, pair_over(m2, m1))
    one = (jnp.ones_like(a0[0]), jnp.zeros_like(a0[0]))
    rho = pair_less(h, one)[0]
    third = pair_times(pair_times(a0, a0), pair_over(m3, m1))
    sigma = pair_less(third, pair_times(h, h))[0]
    more = (rho > 1e-9) & (sigma > 1e-9)
    a1 = jnp.where(more, a0[0] * rho / jnp.where(more, sigma, 1.0), 0.0)
    return a0[0] + a1 * h[0], -a0[0] * a1


def final_kernel(sums, state, field, product, field12, product12, out, balance, *, cells):
    flow = lax.axis_index("group") == 0
    total = (sums[...], jnp.zeros(sums.shape, F32))
    while total[0].shape[0] > 8:
        half = total[0].shape[0] // 2
        total = pair_add([v[:half] for v in total], [v[half:] for v in total])
    for step in (4, 2, 1):
        total = pair_add(total, [pltpu.roll(v, step, 0) for v in total])

    def number(n):
        return tuple(jnp.broadcast_to(v[:1, n : n + 1], (8, Z)) for v in total)

    c0, c1 = krylov(number(0), number(1), number(2), number(3))
    columns = cells // (3 * Z)
    outflow = (number(8)[0] + c0 * number(6)[0] + c1 * number(7)[0]) / columns
    stored = (c0 * number(4)[0] + c1 * number(5)[0]) / cells
    balance[0] = outflow[0, 0]
    balance[1] = stored[0, 0]

    def tall(v):
        return jnp.concatenate([v] * (EY // 8), axis=0)

    @pl.when(flow)
    def _():
        s0, s1 = tall(c0), tall(c1)

        def row(x, carry):
            for k in range(3):
                step = s0 * field[k, OX + x] + s1 * product[k, OX + x]
                out[k, x] = state[k, x] + to_tile(step)
            return carry

        loop(0, X, row)

    @pl.when(jnp.logical_not(flow))
    def _():
        zero = jnp.zeros((8, Z), F32)
        weights = [
            (jnp.ones((8, Z), F32), zero),
            (2.0 * c0, zero),
            (2.0 * c1, zero),
            two_product(c0, c0),
            two_product(2.0 * c0, c1),
            two_product(c1, c1),
        ]
        moments = []
        for m in range(4):
            start = FIRST_SUM + 6 * m
            total = number(start)
            for n in range(1, 6):
                total = pair_add(total, pair_times(weights[n], number(start + n)))
            moments.append(total)
        d0, d1 = krylov(*moments)
        scale_r = [tall(d0), tall(d0 * c0), tall(d0 * c1)]
        scale_w = [tall(d1), tall(d1 * c0), tall(d1 * c1)]

        def row(x, carry):
            for c in range(3):
                step = scale_r[0] * field[c, OX + x] + scale_w[0] * product[c, OX + x]
                for a in range(2):
                    step = step + scale_r[a + 1] * field12[a, c, OX + x]
                    step = step + scale_w[a + 1] * product12[a, c, OX + x]
                out[c, x] = state[c, x] + to_tile(step)
            return carry

        loop(0, X, row)


def swaps(first, second, axis):
    groups, rows, columns = (lax.axis_size(a) for a in AXES)
    count, found = lax.axis_size(axis), []
    for value, start in ((first, 0), (second, 1)):
        pairs = []
        for g in range(groups):
            for i in range(rows):
                for j in range(columns):
                    place = i if axis == "gx" else j
                    step = 1 if place % 2 == start else -1
                    if 0 <= place + step < count:
                        here = (g * rows + i) * columns + j
                        pairs.append((here, here + step * (columns if axis == "gx" else 1)))
        found.append(lax.ppermute(value, AXES, pairs))
    return found


def core_swap(value):
    count = lax.axis_size("gx") * lax.axis_size("gy")
    pairs = [(n, (n + count) % (2 * count)) for n in range(2 * count)]
    return lax.ppermute(value, AXES, pairs)


def body(state, conduct, capacity, supply, flags, layer_map):
    state, conduct, capacity, supply = state[0], conduct[0], capacity[0], supply[0]
    layer_map = layer_map.reshape(1, 3 * Z)
    cells = X * Y * 3 * Z * lax.axis_size("gx") * lax.axis_size("gy")
    devices = lax.axis_size("group") * lax.axis_size("gx") * lax.axis_size("gy")
    tile = struct(3, X, Y, Z)
    brick = struct(X, Y, Z)
    wide = (EX, EY, Z)
    full = struct(3, *wide)

    y_face = struct(len(Y_ROWS), X, Z)
    xa, xb, ya, yb = call(
        pack_kernel,
        x_faces(X_ROWS) + [y_face] * 2,
        [
            pltpu.VMEM((X, Y), jnp.int32),
            pltpu.VMEM((3, X, Y, Z), F32),
            pltpu.VMEM((3, 3, X, Y, Z), F32),
            pltpu.VMEM((X, Y, Z), F32),
            pltpu.VMEM((X, Y, Z), F32),
            pltpu.VMEM((3, X, Y, Z), F32),
            pltpu.SemaphoreType.DMA((14,)),
        ],
        left=(0, 1, 2, 3),
        limit=58,
        count=4,
    )(flags, state, conduct, capacity)
    k_halos = lax.optimization_barrier(swaps(xa, xb, "gx") + swaps(ya, yb, "gy"))
    wide_faces = struct(12, *wide)
    tables = [pltpu.VMEM((6, *wide), F32), pltpu.VMEM(wide, F32)]
    inner, tz, unit0 = call(
        interior_kernel,
        [wide_faces, tile, brick],
        tables + [pltpu.VMEM((X, Y, Z), F32)],
        cost=30_000_000,
    )(state, conduct, capacity, flags, layer_map)
    cross = core_swap(call(strain_kernel, brick)(state, unit0, *k_halos))
    base, beside = call(
        first_kernel,
        [tile, struct(8, Z)],
        tables + [pltpu.VMEM((3, *wide), F32)],
        cost=20_000_000,
    )(state, conduct, capacity, supply, inner, *k_halos)
    faces, k_rim = call(
        halo_kernel, [wide_faces, struct(6, len(K_RIM), EY, Z)], tables, cost=30_000_000
    )(conduct, capacity, tz, layer_map, *k_halos)
    residual, xa, xb = call(residual_kernel, [tile] + x_faces(R_ROWS))(
        base, cross, cross, layer_map
    )
    halos = swaps(xa, xb, "gx")
    ya, yb = call(relay_kernel, [struct(Y_PACK, Z)] * 2)(
        residual, cross, *halos, k_halos[0], k_halos[1]
    )
    halos = halos + swaps(ya, yb, "gy")
    rim, field, product, unit12 = call(
        image_kernel,
        [struct(12, len(RIM), EY, Z), full, full, struct(2, EX - 2, EY, Z)],
        [pltpu.VMEM((6, len(K_RIM), EY, Z), F32), pltpu.VMEM((EX - 2, EY, Z), F32)],
    )(residual, cross, beside, layer_map, *halos, faces, k_rim)
    unit12 = core_swap(unit12)
    sums = call(early_kernel, struct(8, Z), [pltpu.VMEM((4, 8, Z), F32)], cost=20_000_000)(
        field, product, faces, state
    )
    sums, field12, product12 = call(
        sums_kernel,
        [struct(devices, Z), struct(2, 3, *wide), struct(2, 3, *wide)],
        [pltpu.VMEM((20, 8, Z), F32)],
    )(field, product, faces, rim, unit12, sums)
    sums = lax.all_to_all(sums, AXES, 0, 0, tiled=True)

    def finish(*refs):
        final_kernel(*refs, cells=cells)

    new_state, balance = call(finish, [tile, struct(2)], scalars=(1,))(
        sums, state, field, product, field12, product12
    )
    return new_state[None], balance


def solution(mesh):
    placed = (
        P("group", None, "gx", "gy", None),
        P("group", None, None, "gx", "gy", None),
        P("group", "gx", "gy", None),
        P("group", None, "gx", "gy", None),
        P("gx", "gy"),
        P(),
    )
    return jax.shard_map(
        body,
        mesh=mesh,
        in_specs=placed,
        out_specs=(P("group", None, "gx", "gy", None), P()),
        check_vma=False,
    )
```

```python
import jax
import jax.numpy as jnp
from jax import lax
from jax.experimental import pallas as pl
from jax.experimental.pallas import tpu as pltpu
from jax.sharding import PartitionSpec as P

AXES = ("group", "gx", "gy")
X, Y, Z = 16, 32, 128
OX, OY = 3, 4
EX, EY = X + 2 * OX, Y + 2 * OY
BETA = 0.5
BIOT = 0.8
F32 = jnp.float32

X_ROWS = [(f, r) for f in range(13) for r in range(1, (3 if f < 3 else 2 if f < 10 else 1) + 1)]
NEAR = [(f, r) for f, r in X_ROWS if r == 1 and not 3 <= f < 9]
X_ROWS = NEAR + [row for row in X_ROWS if row not in NEAR]
Y_ROWS = [
    (f, r) for f in range(13) for r in range(1, (3 if 3 <= f < 6 else 2 if f < 10 else 1) + 1)
]
CORNER = [(1, 1), (1, 2), (2, 1), (2, 2), (1, 3), (3, 1)]
K_CORNERS = (
    [(f, i, j) for f in range(3) for i, j in CORNER[:4] + [(3, 1)]]
    + [(f, i, j) for f in range(3, 6) for i, j in CORNER[:4] + [(1, 3)]]
    + [(f, i, j) for f in range(6, 10) for i, j in CORNER[:3]]
)
R_ROWS = [(f, r) for f in range(3) for r in range(1, 4)]
R_CORNERS = [(f, i, j) for f in range(3) for i, j in CORNER]
AT_R = [len(R_ROWS) * X, len(R_ROWS) * X + len(R_CORNERS)]
AT_K = [AT_R[1] + len(R_CORNERS), AT_R[1] + len(R_CORNERS) + len(K_CORNERS)]
AT_Q = [AT_K[1] + len(K_CORNERS), AT_K[1] + len(K_CORNERS) + 3]
AT_U = AT_Q[1] + 3
Y_PACK = -(-(AT_U + 4) // 8) * 8
Q_SLOT = [R_ROWS.index((0, 3)), R_ROWS.index((1, 3))]


def struct(*shape):
    return jax.ShapeDtypeStruct(shape, F32)


def call(kernel, outs, scratch=(), left=(), count=0, cost=None, limit=20, scalars=()):
    extra = {}
    if left:
        extra["in_specs"] = [
            pl.BlockSpec(memory_space=pltpu.HBM if n in left else pltpu.VMEM) for n in range(count)
        ]
    if scalars:
        extra["out_specs"] = [
            pl.BlockSpec(memory_space=pltpu.SMEM if n in scalars else pltpu.VMEM)
            for n in range(len(outs))
        ]
    if cost:
        extra["cost_estimate"] = pl.CostEstimate(
            flops=cost, bytes_accessed=cost, transcendentals=0
        )
    return pl.pallas_call(
        kernel,
        out_shape=outs,
        scratch_shapes=list(scratch),
        compiler_params=pltpu.CompilerParams(vmem_limit_bytes=limit << 20),
        **extra,
    )


def up_y(v):
    return pltpu.roll(v, v.shape[0] - 1, 0)


def down_y(v):
    return pltpu.roll(v, 1, 0)


def up_z(v):
    return pltpu.roll(v, Z - 1, 1)


def down_z(v):
    return pltpu.roll(v, 1, 1)


def lanes(rows):
    return lax.broadcasted_iota(jnp.int32, (rows, Z), 1)


def rows_of(rows):
    return lax.broadcasted_iota(jnp.int32, (rows, Z), 0)


def to_tile(v):
    return pltpu.roll(v, EY - OY, 0)[:Y]


def harmonic(a, b):
    return 2.0 * a * b / jnp.maximum(a + b, 1e-30)


def one_hot(map_ref):
    brick = lax.broadcasted_iota(jnp.int32, (Z, 3 * Z), 0)
    return jnp.where(brick == map_ref[...], 1.0, 0.0).astype(jnp.bfloat16)


def dot_split(v, hot, contract):
    high = v.astype(jnp.bfloat16)
    low = (v - high.astype(F32)).astype(jnp.bfloat16)
    dims = (((1,), (contract,)), ((), ()))
    return lax.dot_general(high, hot, dims, preferred_element_type=F32) + lax.dot_general(
        low, hot, dims, preferred_element_type=F32
    )


def spread(v, hot, k):
    return dot_split(v, hot[:, k * Z : (k + 1) * Z], 0)


def gather_up(parts, hot):
    total = None
    for k, v in enumerate(parts):
        part = dot_split(v, hot[:, k * Z : (k + 1) * Z], 1)
        total = part if total is None else total + part
    ones = jnp.ones((8, 3 * Z), jnp.bfloat16)
    counts = lax.dot_general(ones, hot, (((1,), (1,)), ((), ())), preferred_element_type=F32)
    return total * (1.0 / counts[:1])


def gather_wide(ref, hot):
    rows = EX - 2
    parts = [ref[k, 1 : EX - 1].reshape(rows * EY, Z) for k in range(3)]
    return gather_up(parts, hot).reshape(rows, EY, Z)


def fetch(pairs, sem, start=0):
    copies = [pltpu.make_async_copy(a, b, sem.at[start + n]) for n, (a, b) in enumerate(pairs)]
    for copy in copies:
        copy.start()
    return copies


class Joined:
    def __init__(self, near, far):
        self.near, self.far = near, far

    def place(self, at):
        n, rest = (at[0], at[1:]) if isinstance(at, tuple) else (at, ())
        ref, n = (self.near, n) if n < len(NEAR) else (self.far, n - len(NEAR))
        return ref, (n, *rest)

    def __getitem__(self, at):
        ref, at = self.place(at)
        return ref[at]

    def __setitem__(self, at, value):
        ref, at = self.place(at)
        ref[at] = value


class Either:
    def __init__(self, odd, at_odd, at_even):
        self.odd, self.at_odd, self.at_even = odd, at_odd, at_even

    def __getitem__(self, at):
        return jnp.where(self.odd, self.at_odd[at], self.at_even[at])


def parity(axis):
    return lax.rem(lax.axis_index(axis), 2) == 1


def lower_upper(axis, first, second):
    odd = parity(axis)
    return Either(odd, first, second), Either(odd, second, first)


def surroundings(xa, xb, ya, yb):
    return lower_upper("gx", xa, xb) + lower_upper("gy", ya, yb)


def put(first, second, at, odd, tail, head):
    first[at] = jnp.where(odd, head, tail)
    second[at] = jnp.where(odd, tail, head)


def pack_x(source, rows, first, second):
    odd = parity("gx")
    for n, (f, r) in enumerate(rows):
        put(first, second, n, odd, source(f)[X - r], source(f)[r - 1])


def unpack_x(target, rows, low, up):
    for n, (f, r) in enumerate(rows):
        target(f)[OX - r, OY : OY + Y] = low[n]
        target(f)[OX + X - 1 + r, OY : OY + Y] = up[n]


def corner_at(side, i, j):
    row = OX - i if side[0] == 0 else OX + X - 1 + i
    column = OY - j if side[1] == 0 else OY + Y - 1 + j
    return row, slice(column, column + 1)


def x_faces(rows):
    return [struct(len(rows), Y, Z)] * 2


def loop(first, last, body, init=0, unroll=4):
    steps = (last - first) // unroll

    def step(n, carry):
        for m in range(unroll):
            carry = body(first + n * unroll + m, carry)
        return carry

    init = lax.fori_loop(0, steps, step, init)
    for i in range(first + steps * unroll, last):
        init = body(i, init)
    return init


def vertical_faces(conduct, flags, bottom, store):
    flow = lax.axis_index("group") == 0
    last = lanes(Y) == Z - 1
    eye = jnp.where(
        lax.broadcasted_iota(jnp.int32, (Y, Y), 0) == lax.broadcasted_iota(jnp.int32, (Y, Y), 1),
        1.0,
        0.0,
    ).astype(jnp.bfloat16)
    columns = lax.dot_general(
        eye,
        flags[...].astype(F32).astype(jnp.bfloat16),
        (((1,), (1,)), ((), ())),
        preferred_element_type=F32,
    )
    for x in range(X):
        bottom[x] = jnp.broadcast_to(columns[:, x : x + 1], (Y, Z))

    def row(x, carry):
        kz = [conduct[2, k, x] for k in range(3)]
        rolled = [up_z(v) for v in kz]
        ends = [rolled[1], rolled[2], bottom[x] * kz[2]]
        for k in range(3):
            end = jnp.where(flow, ends[k], kz[k])
            store(x, k, harmonic(kz[k], jnp.where(last, end, rolled[k])))
        return carry

    loop(0, X, row)


def pack_kernel(flags_in, state_in, conduct_in, capacity_in, xa, xb, fa, fb, ya, yb, *scratch):
    flags, state, conduct, capacity, bottom, tz, sem = scratch
    early = [(flags_in, flags)] + [(conduct_in.at[2, k], conduct.at[2, k]) for k in range(3)]
    late = [(conduct_in.at[d, k], conduct.at[d, k]) for d in range(2) for k in range(3)]
    late += [(state_in.at[k], state.at[k]) for k in range(3)] + [(capacity_in, capacity)]
    early = fetch(early, sem)
    late = fetch(late, sem, len(early))
    for copy in early:
        copy.wait()
    def store(x, k, value):
        tz[k, x] = value

    vertical_faces(conduct, flags, bottom, store)
    for copy in late:
        copy.wait()

    def source(f):
        if f < 6:
            return conduct.at[f // 3, f % 3]
        if f < 9:
            return tz.at[f - 6]
        return capacity if f == 9 else state.at[f - 10]

    pack_x(source, X_ROWS, Joined(xa, fa), Joined(xb, fb))
    odd = parity("gy")
    for n, (f, r) in enumerate(Y_ROWS):
        put(ya, yb, n, odd, source(f)[:, Y - r, :], source(f)[:, r - 1, :])


class Faces:
    def __init__(self, x, y, z, own):
        self.x, self.y, self.z, self.own = x, y, z, own


def faces_in(ref, shift=0):
    return Faces(*[lambda c, i, d=d: ref[3 * d + c, i - shift] for d in range(4)])


def lateral(faces, v_ref, c, i, v, fx_before):
    fx = faces.x(c, i) * (v - v_ref[c, i + 1])
    fy = faces.y(c, i) * (v - up_y(v))
    return (fx - fx_before) + (fy - down_y(fy)), fx


def x_flux(faces, v_ref, i):
    return tuple(faces.x(c, i) * (v_ref[c, i] - v_ref[c, i + 1]) for c in range(3))


def flow_below(vs, last):
    rolled = [up_z(v) for v in vs]
    ends = [rolled[1], rolled[2], 0.0]
    return [jnp.where(last, ends[k], rolled[k]) for k in range(3)]


def flow_row(faces, v_ref, i, fx_before):
    last, first = lanes(EY) == Z - 1, lanes(EY) == 0
    vs = [v_ref[k, i] for k in range(3)]
    below = flow_below(vs, last)
    fz = [faces.z(k, i) * (vs[k] - below[k]) for k in range(3)]
    moved = [down_z(v) for v in fz]
    ends = [0.0, moved[0], moved[1]]
    out, fx_now = [], []
    for k in range(3):
        side, fx = lateral(faces, v_ref, k, i, vs[k], fx_before[k])
        above = jnp.where(first, ends[k], moved[k])
        out.append(faces.own(k, i) * vs[k] + side + (fz[k] - above))
        fx_now.append(fx)
    return out, tuple(fx_now)


def strain_row(v_ref, i):
    v0, v1, v2 = v_ref[0, i], v_ref[1, i], v_ref[2, i]
    low = jnp.where(lanes(EY) == Z - 1, 0.0, up_z(v2))
    return (v_ref[0, i + 1] - v0) + (up_y(v1) - v1) + (low - v2)


def solid_row(faces, v_ref, i, s_before, fx_before):
    last, first = lanes(EY) == Z - 1, lanes(EY) == 0
    e = strain_row(v_ref, i)
    s = faces.own(0, i) * e
    grad = [s_before - s, down_y(s) - s, jnp.where(first, 0.0, down_z(s)) - s]
    out, fx_now = [], []
    for c in range(3):
        v = v_ref[c, i]
        side, fx = lateral(faces, v_ref, c, i, v, fx_before[c])
        fz = faces.z(c, i) * (v - jnp.where(last, 0.0, up_z(v)))
        above = jnp.where(first, 0.0, down_z(fz))
        out.append((side + (fz - above)) + grad[c])
        fx_now.append(fx)
    return out, s, tuple(fx_now)


BESIDE = [(1, -1, Y), (1, X - 1, Y), (1, -1, 0), (1, X - 1, 0)]
BESIDE += [(0, X, -1), (0, 0, -1), (0, X, Y - 1), (0, 0, Y - 1)]


def place_tile(conduct, capacity, keep, caps):
    at = slice(OY, OY + Y)

    def row(x, carry):
        for f in range(6):
            keep[f, OX + x, at] = conduct[f // 3, f % 3, x]
        caps[OX + x, at] = capacity[x]
        return carry

    loop(0, X, row)


def interior_kernel(state, conduct, capacity, flags, layer_map, faces, tz, unit, keep, caps, bottom):
    flow = lax.axis_index("group") == 0
    place_tile(conduct, capacity, keep, caps)

    def store(x, k, value):
        tz[k, x] = value
        faces[6 + k, OX + x, OY : OY + Y] = value

    vertical_faces(conduct, flags, bottom, store)
    loop(OX, OX + X, lambda i, carry: lateral_faces(keep, faces, i))

    @pl.when(flow)
    def _():
        hot = one_hot(layer_map)
        bricks = caps[OX : OX + X].reshape(X * EY, Z)
        for k in range(3):
            faces[9 + k, OX : OX + X] = (spread(bricks, hot, k) + BETA).reshape(X, EY, Z)
        parts = [state[k].reshape(X * Y, Z) for k in range(3)]
        unit[...] = gather_up(parts, hot).reshape(X, Y, Z)


def lateral_faces(keep, faces, i):
    for c in range(3):
        faces[c, i] = harmonic(keep[c, i], keep[c, i + 1])
        here = keep[3 + c, i]
        faces[3 + c, i] = harmonic(here, up_y(here))
    return 0


def strain_kernel(state, unit, xa, xb, ya, yb, strain):
    flow = lax.axis_index("group") == 0
    _, xu, _, yu = surroundings(xa, xb, ya, yb)

    @pl.when(flow)
    def _():
        strain[...] = unit[...]

    @pl.when(jnp.logical_not(flow))
    def _():
        last = lanes(Y) == Z - 1
        edge = rows_of(Y) == Y - 1
        n_x, n_y = X_ROWS.index((10, 1)), Y_ROWS.index((11, 1))
        for x in range(X):
            v0, v1, v2 = (state[c, x] for c in range(3))
            east = state[0, x + 1] if x + 1 < X else xu[n_x]
            north = jnp.where(edge, yu[n_y, x : x + 1], up_y(v1))
            low = jnp.where(last, 0.0, up_z(v2))
            strain[x] = (east - v0) + (north - v1) + (low - v2)


def first_kernel(state, conduct, capacity, supply, faces_ref, xa, xb, ya, yb, *refs):
    xl, xu, yl, yu = surroundings(xa, xb, ya, yb)
    base, beside, sides, own, field = refs
    flow = lax.axis_index("group") == 0

    def place(x, carry):
        for c in range(3):
            field[c, OX + x, OY : OY + Y] = state[c, x]
        for f in range(6):
            sides[f, OX + x] = faces_ref[f, OX + x]
        return carry

    loop(0, X, place)
    for c in range(3):
        n = X_ROWS.index((10 + c, 1))
        field[c, OX - 1, OY : OY + Y] = xl[n]
        field[c, OX + X, OY : OY + Y] = xu[n]
        n = Y_ROWS.index((10 + c, 1))
        field[c, OX : OX + X, OY - 1, :] = yl[n]
        field[c, OX : OX + X, OY + Y, :] = yu[n]
        n = X_ROWS.index((c, 1))
        at = slice(OY, OY + Y)
        sides[c, OX - 1, at] = harmonic(xl[n], conduct[0, c, 0])
        sides[c, OX + X - 1, at] = harmonic(conduct[0, c, X - 1], xu[n])
        n = Y_ROWS.index((3 + c, 1))
        sides[3 + c, OX : OX + X, OY - 1, :] = harmonic(yl[n], conduct[1, c, :, 0, :])
        sides[3 + c, OX : OX + X, OY + Y - 1, :] = harmonic(conduct[1, c, :, Y - 1, :], yu[n])
    field[1, OX - 1, OY + Y : OY + Y + 1] = jnp.zeros((1, Z), F32)
    field[0, OX + X, OY - 1 : OY] = jnp.zeros((1, Z), F32)
    for n, (c, x, y) in enumerate(BESIDE):
        beside[n : n + 1] = field[c, OX + x, OY + y : OY + y + 1]
    inner = faces_in(faces_ref)
    outer = faces_in(sides)

    @pl.when(flow)
    def _():
        faces = Faces(outer.x, outer.y, inner.z, inner.own)

        def row(i, fx_before):
            image, fx = flow_row(faces, field, i, fx_before)
            for k in range(3):
                base[k, i - OX] = (
                    supply[k, i - OX] + BETA * state[k, i - OX] - to_tile(image[k])
                )
            return fx

        loop(OX, OX + X, row, x_flux(faces, field, OX - 1))

    @pl.when(jnp.logical_not(flow))
    def _():
        def place(x, carry):
            own[OX + x, OY : OY + Y] = capacity[x]
            return carry

        loop(0, X, place)
        own[OX - 1, OY : OY + Y] = xl[X_ROWS.index((9, 1))]
        own[OX : OX + X, OY - 1, :] = yl[Y_ROWS.index((9, 1))]
        faces = Faces(outer.x, outer.y, inner.z, lambda c, i: own[i])

        def row(i, carry):
            image, s, fx = solid_row(faces, field, i, carry[0], carry[1])
            for c in range(3):
                base[c, i - OX] = supply[c, i - OX] - to_tile(image[c])
            return s, fx

        before = faces.own(0, OX - 1) * strain_row(field, OX - 1)
        loop(OX, OX + X, row, (before, x_flux(faces, field, OX - 1)))


def halo_kernel(conduct, capacity, tz, layer_map, xa, xb, ya, yb, fa, fb, *refs):
    faces, rim, keep, caps = refs
    xl, xu, yl, yu = surroundings(Joined(xa, fa), Joined(xb, fb), ya, yb)
    flow = lax.axis_index("group") == 0

    def target(f):
        if f < 6:
            return keep.at[f]
        return faces.at[f] if f < 9 else caps

    place_tile(conduct, capacity, keep, caps)

    def place(x, carry):
        for k in range(3):
            faces[6 + k, OX + x, OY : OY + Y] = tz[k, x]
        return carry

    loop(0, X, place)
    for n, (f, r) in enumerate(X_ROWS):
        if f < 10:
            target(f)[OX - r, OY : OY + Y] = xl[n]
            target(f)[OX + X - 1 + r, OY : OY + Y] = xu[n]
    for n, (f, r) in enumerate(Y_ROWS):
        if f < 10:
            target(f)[OX : OX + X, OY - r, :] = yl[n]
            target(f)[OX : OX + X, OY + Y - 1 + r, :] = yu[n]
    loop(0, EX - 1, lambda i, carry: lateral_faces(keep, faces, i))
    for n, i in enumerate(K_RIM):
        for f in range(6):
            rim[f, n] = keep[f, i]

    @pl.when(flow)
    def _():
        hot = one_hot(layer_map)
        bricks = caps[1 : EX - 1].reshape((EX - 2) * EY, Z)
        for k in range(3):
            faces[9 + k, 1 : EX - 1] = (spread(bricks, hot, k) + BETA).reshape(EX - 2, EY, Z)

    @pl.when(jnp.logical_not(flow))
    def _():
        faces[9] = caps[...]


BESIDE = [(1, -1, Y), (1, X - 1, Y), (1, -1, 0), (1, X - 1, 0)]
BESIDE += [(0, X, -1), (0, 0, -1), (0, X, Y - 1), (0, 0, Y - 1)]
RIM = [0, 1, 2, EX - 4, EX - 3, EX - 2]
K_RIM = [0, 1, 2, 3, EX - 4, EX - 3, EX - 2, EX - 1]


def residual_kernel(base, strain, unit, layer_map, residual, xa, xb):
    flow = lax.axis_index("group") == 0

    @pl.when(flow)
    def _():
        hot = one_hot(layer_map)
        e = strain[...].reshape(X * Y, Z)
        for k in range(3):
            residual[k] = base[k] - BIOT * spread(e, hot, k).reshape(X, Y, Z)

    @pl.when(jnp.logical_not(flow))
    def _():
        residual[...] = base[...]

    pack_x(lambda f: residual.at[f], R_ROWS, xa, xb)

    @pl.when(jnp.logical_not(flow))
    def _():
        odd = parity("gx")
        for depth, n in enumerate(Q_SLOT):
            put(xa, xb, n, odd, unit[X - 1 - depth], unit[depth])


def relay_kernel(residual, unit, xa, xb, ka, kb, fa, fb, ya, yb):
    flow = lax.axis_index("group") == 0
    odd = parity("gy")
    r_halos, k_halos = lower_upper("gx", xa, xb), lower_upper("gx", Joined(ka, fa), Joined(kb, fb))

    def give(at, count, ref, index, j):
        put(ya, yb, slice(at, at + count), odd, ref[index(Y - j)], ref[index(j - 1)])

    for n, (f, r) in enumerate(R_ROWS):
        give(n * X, X, residual, lambda y: (f, slice(None), y), r)
    for side in range(2):
        r_halo, k_halo = r_halos[side], k_halos[side]
        for n, (f, i, j) in enumerate(R_CORNERS):
            row = R_ROWS.index((f, i))
            give(AT_R[side] + n, 1, r_halo, lambda y: (row, slice(y, y + 1)), j)
        for n, (f, i, j) in enumerate(K_CORNERS):
            row = X_ROWS.index((f, i))
            give(AT_K[side] + n, 1, k_halo, lambda y: (row, slice(y, y + 1)), j)
        for n, (i, j) in enumerate(CORNER[:3]):
            row = Q_SLOT[i - 1]
            give(AT_Q[side] + n, 1, r_halo, lambda y: (row, slice(y, y + 1)), j)
        for c in range(2):
            row = X_ROWS.index((10 + c, 1))
            give(AT_U + 2 * side + c, 1, k_halo, lambda y: (row, slice(y, y + 1)), 1)

    @pl.when(jnp.logical_not(flow))
    def _():
        for depth, n in enumerate(Q_SLOT):
            give(n * X, X, unit, lambda y: (slice(None), y), depth + 1)


def fold(v):
    return jnp.sum(v.reshape(v.shape[0] // 8, 8, Z), axis=0)


def spread_sums(found):
    lane = lanes(8)
    row = jnp.zeros((8, Z), F32)
    first = rows_of(8) == 0
    for n, total in found.items():
        row = jnp.where(first & (lane == n), jnp.sum(total), row)
    return row


def tile_rows():
    at = rows_of(EY)
    return (at >= OY) & (at < OY + Y)


def fill(residual, target, halos):
    xl, xu, yl, yu = halos

    def place(x, carry):
        for k in range(3):
            target[k, OX + x, OY : OY + Y] = residual[k, x]
        return carry

    loop(0, X, place)
    unpack_x(lambda f: target.at[f], R_ROWS, xl, xu)
    for n, (f, r) in enumerate(R_ROWS):
        target[f, OX : OX + X, OY - r, :] = yl[n * X : (n + 1) * X]
        target[f, OX : OX + X, OY + Y - 1 + r, :] = yu[n * X : (n + 1) * X]
    for v, pack in enumerate((yl, yu)):
        for h in range(2):
            for n, (f, i, j) in enumerate(R_CORNERS):
                row, column = corner_at((h, v), i, j)
                target[f, row, column] = pack[AT_R[h] + n : AT_R[h] + n + 1]


def complete(faces, rim, k_rim_in, k_rim, halos, hot):
    for n, i in enumerate(RIM):
        for f in range(6, 12):
            rim[f, n] = faces[f, i]
    k_rim[...] = k_rim_in[...]
    order = []
    for v, pack in enumerate(halos[2:]):
        for h in range(2):
            for n, (f, i, j) in enumerate(K_CORNERS):
                row, column = corner_at((h, v), i, j)
                value = pack[AT_K[h] + n : AT_K[h] + n + 1]
                if f < 6:
                    k_rim[f, K_RIM.index(row), column] = value
                elif f < 9:
                    rim[f, RIM.index(row), column] = value
                else:
                    order.append((RIM.index(row), column, value))
    for n, i in enumerate(RIM):
        m = K_RIM.index(i)
        for c in range(3):
            rim[c, n] = harmonic(k_rim[c, m], k_rim[c, m + 1])
            here = k_rim[3 + c, m]
            rim[3 + c, n] = harmonic(here, up_y(here))
    if hot is None:
        for row, column, value in order:
            rim[9, row, column] = value
    else:
        values = [value for _, _, value in order]
        values += [jnp.zeros((1, Z), F32)] * (16 - len(values))
        caps = jnp.concatenate(values, axis=0)
        for k in range(3):
            storage = spread(caps, hot, k) + BETA
            for n, (row, column, _) in enumerate(order):
                rim[9 + k, row, column] = storage[n : n + 1]


def row_parts(faces, rim):
    return faces_in(rim), faces_in(faces), faces_in(rim, EX - 7)


def run_rows(parts, first, last, body, init, unroll=3):
    low, middle, high = parts
    for i in range(first, OX):
        init = body(low, i, init)
    init = loop(max(first, OX), EX - 4, lambda i, carry: body(middle, i, carry), init, unroll)
    for i in range(EX - 4, last):
        init = body(high, i, init)
    return init


PAIRS = [(0, 0), (0, 1), (0, 2), (1, 1), (1, 2), (2, 2)]
FIRST_SUM = 9


def grid_mask(before, after):
    gx, gy = lax.axis_index("gx"), lax.axis_index("gy")
    gx_last, gy_last = lax.axis_size("gx") - 1, lax.axis_size("gy") - 1
    at = rows_of(EY)
    in_y = (at >= OY - jnp.where(gy > 0, before, 0)) & (
        at < OY + Y + jnp.where(gy < gy_last, after, 0)
    )

    def in_grid(i):
        in_x = ((i >= OX) | (gx > 0)) & ((i < OX + X) | (gx < gx_last))
        return in_y & in_x

    return in_grid


def load_rows(q_refs, targets, added):
    in_grid = grid_mask(1, 2)

    def row(i, carry):
        for q_ref, target in zip(q_refs, targets):
            load_row(q_ref, target, i, in_grid(i))
        return carry

    def load_row(q_ref, target, i, ok):
        first = lanes(EY) == 0
        q = q_ref[i - 1]
        push = [
            BIOT * (q_ref[i - 2] - q),
            BIOT * (down_y(q) - q),
            BIOT * (jnp.where(first, 0.0, down_z(q)) - q),
        ]
        for c in range(3):
            v = push[c] + target[c, i] if added else push[c]
            target[c, i] = jnp.where(ok, v, 0.0)

    loop(OX - 1, OX + X + 2, row)


def solid_image(parts, f_refs, p_refs, unroll):
    in_grid = grid_mask(0, 1)

    def row(faces, i, carry):
        ok, after = in_grid(i), []
        for f_ref, p_ref, (s, fx) in zip(f_refs, p_refs, carry):
            out, s, fx = solid_row(faces, f_ref, i, s, fx)
            for c in range(3):
                p_ref[c, i] = jnp.where(ok, out[c], 0.0)
            after.append((s, fx))
        return tuple(after)

    view = parts[0]
    start = [
        (view.own(0, OX - 1) * strain_row(f, OX - 1), x_flux(view, f, OX - 1)) for f in f_refs
    ]
    run_rows(parts, OX, OX + X + 1, row, tuple(start), unroll)


def gram_sums(faces, fields, products, pairs, acc):
    acc[...] = jnp.zeros(acc.shape, F32)
    vectors = range(len(fields))

    def row(i, carry):
        inside, last = tile_rows(), lanes(EY) == Z - 1

        def only(v):
            return jnp.where(inside, v, 0.0)

        def add(n, v):
            acc[n] = acc[n] + fold(v)

        strains = [strain_row(p, i) for p in products]
        modulus = only(faces[9, i])
        pushes = [modulus * e for e in strains]
        for n, (a, b) in enumerate(pairs):
            add(4 * n + 3, pushes[a] * strains[b])
        for c in range(3):
            ws = [p[c, i] for p in products]
            dx = [ws[a] - products[a][c, i + 1] for a in vectors]
            dy = [w - up_y(w) for w in ws]
            dz = [w - jnp.where(last, 0.0, up_z(w)) for w in ws]
            sx, sy, sz = (only(faces[3 * d + c, i]) for d in range(3))
            fx = [sx * d for d in dx]
            fy = [sy * d for d in dy]
            fz = [sz * d for d in dz]
            for n, (a, b) in enumerate(pairs):
                add(4 * n + 3, fx[a] * dx[b] + fy[a] * dy[b] + fz[a] * dz[b])
            rs = [only(f[c, i]) for f in fields]
            ws = [only(w) for w in ws]
            for n, (a, b) in enumerate(pairs):
                add(4 * n, rs[a] * rs[b])
                add(4 * n + 1, rs[a] * ws[b])
                add(4 * n + 2, ws[a] * ws[b])
        return carry

    loop(OX, OX + X, row, 0, 2)
    found = {}
    for n, pair in enumerate(pairs):
        for m in range(4):
            found[FIRST_SUM + 6 * m + PAIRS.index(pair)] = acc[4 * n + m]
    return found


def unit_surroundings(unit, halos, q):
    xl, xu, yl, yu = halos

    def place(x, carry):
        q[OX - 1 + x, OY : OY + Y] = unit[x]
        return carry

    loop(0, X, place)
    for depth, n in enumerate(Q_SLOT):
        q[OX - 2 - depth, OY : OY + Y] = xl[n]
        q[OX + X - 1 + depth, OY : OY + Y] = xu[n]
        rows = slice(n * X, (n + 1) * X)
        q[OX - 1 : OX - 1 + X, OY - 1 - depth, :] = yl[rows]
        q[OX - 1 : OX - 1 + X, OY + Y + depth, :] = yu[rows]
    for v, pack in enumerate((yl, yu)):
        for h in range(2):
            for n, (i, j) in enumerate(CORNER[:3]):
                row, column = corner_at((h, v), i, j)
                q[row - 1, column] = pack[AT_Q[h] + n : AT_Q[h] + n + 1]


def late_terms(faces, rim, field, beside, halos):
    yl, yu = halos[2:]

    def modulus(x, y):
        i, column = OX + x, slice(OY + y, OY + y + 1)
        return rim[9, RIM.index(i), column] if i in RIM else faces[9, i, column]

    u1 = [yu[AT_U + 1 : AT_U + 2]] + [beside[n : n + 1] for n in (1, 2, 3)]
    u0 = [yl[AT_U + 2 : AT_U + 3]] + [beside[n : n + 1] for n in (5, 6, 7)]
    for u, (x, y) in zip(u1, ((0, Y - 1), (X, Y - 1), (0, -1), (X, -1))):
        row, column = OX + x, slice(OY + y, OY + y + 1)
        field[0, row, column] = field[0, row, column] - modulus(x - 1, y) * u
    for u, (x, y) in zip(u0, ((X - 1, 0), (-1, 0), (X - 1, Y), (-1, Y))):
        row, column = OX + x, slice(OY + y, OY + y + 1)
        field[1, row, column] = field[1, row, column] - modulus(x, y - 1) * u


def image_kernel(residual, unit_old, beside, layer_map, *refs):
    halos, (faces, k_rim_in, rim, field, product, unit, k_rim, q) = refs[:4], refs[4:]
    halos = surroundings(*halos)
    flow = lax.axis_index("group") == 0
    fill(residual, field, halos)

    @pl.when(flow)
    def _():
        hot = one_hot(layer_map)
        complete(faces, rim, k_rim_in, k_rim, halos, hot)
        parts = row_parts(faces, rim)

        def row(view, i, fx_before):
            out, fx = flow_row(view, field, i, fx_before)
            for k in range(3):
                product[k, i] = out[k]
            return fx

        run_rows(parts, 1, EX - 1, row, x_flux(parts[0], field, 0))
        unit[0] = gather_wide(field, hot)
        unit[1] = gather_wide(product, hot)

    @pl.when(jnp.logical_not(flow))
    def _():
        complete(faces, rim, k_rim_in, k_rim, halos, None)
        late_terms(faces, rim, field, beside, halos)
        unit_surroundings(unit_old, halos, q)
        load_rows([q], [field], True)
        solid_image(row_parts(faces, rim), [field], [product], 3)


def early_kernel(field, product, faces, state, sums, acc):
    flow = lax.axis_index("group") == 0

    @pl.when(flow)
    def _():
        def dots(i, acc):
            acc = list(acc)
            inside, last = tile_rows(), lanes(EY) == Z - 1

            def add(n, v):
                acc[n] = acc[n] + fold(jnp.where(inside, v, 0.0))

            ws = [product[k, i] for k in range(3)]
            below = flow_below(ws, last)
            g = m1 = m2 = m3 = cr = cw = 0.0
            for k in range(3):
                r, w = field[k, i], ws[k]
                dx, dy, dz = w - product[k, i + 1], w - up_y(w), w - below[k]
                cf = faces[9 + k, i]
                g = g + r * r
                m1 = m1 + r * w
                m2 = m2 + w * w
                cr = cr + cf * r
                cw = cw + cf * w
                m3 = m3 + (
                    faces[k, i] * dx * dx
                    + faces[3 + k, i] * dy * dy
                    + faces[6 + k, i] * dz * dz
                    + cf * w * w
                )
            for n, v in enumerate((g, m1, m2, m3, cr, cw)):
                add(n, v)
            weight = jnp.where(last, faces[8, i], 0.0)
            add(6, weight * field[2, i])
            add(7, weight * ws[2])
            acc[8] = acc[8] + fold(to_tile(weight) * state[2, i - OX])
            return tuple(acc)

        zero = jnp.zeros((8, Z), F32)
        found = dict(enumerate(loop(OX, OX + X, dots, (zero,) * FIRST_SUM, 2)))
        sums[...] = spread_sums(found)

    @pl.when(jnp.logical_not(flow))
    def _():
        sums[...] = spread_sums(gram_sums(faces, [field], [product], PAIRS[:1], acc))


def sums_kernel(field, product, faces, rim, unit, sums_in, sums, field12, product12, acc):
    flow = lax.axis_index("group") == 0
    everyone = sums.shape[0]

    @pl.when(flow)
    def _():
        sums[...] = jnp.broadcast_to(sums_in[:1], (everyone, Z))

    @pl.when(jnp.logical_not(flow))
    def _():
        fields = [field] + [field12.at[a] for a in range(2)]
        products = [product] + [product12.at[a] for a in range(2)]
        load_rows([unit.at[a] for a in range(2)], fields[1:], False)
        solid_image(row_parts(faces, rim), fields[1:], products[1:], 2)
        found = gram_sums(faces, fields, products, PAIRS[1:], acc)
        own = sums_in[:1] + spread_sums(found)[:1]
        sums[...] = jnp.broadcast_to(own, (everyone, Z))


def two_sum(a, b):
    s = a + b
    t = s - a
    return s, (a - (s - t)) + (b - t)


def quick(a, b):
    s = a + b
    return s, b - (s - a)


def halves(a):
    t = 4097.0 * a
    high = t - (t - a)
    return high, a - high


def two_product(a, b):
    p = a * b
    ah, al = halves(a)
    bh, bl = halves(b)
    return p, ((ah * bh - p) + ah * bl + al * bh) + al * bl


def pair_add(a, b):
    s, e = two_sum(a[0], b[0])
    return quick(s, e + (a[1] + b[1]))


def pair_less(a, b):
    return pair_add(a, (-b[0], -b[1]))


def pair_times(a, b):
    p, e = two_product(a[0], b[0])
    return quick(p, e + (a[0] * b[1] + a[1] * b[0]))


def pair_over(a, b):
    q = a[0] / b[0]
    rest = pair_less(a, pair_times(b, (q, jnp.zeros_like(q))))
    return quick(q, rest[0] / b[0])


def krylov(g, m1, m2, m3):
    a0 = pair_over(g, m1)
    h = pair_times(a0, pair_over(m2, m1))
    one = (jnp.ones_like(a0[0]), jnp.zeros_like(a0[0]))
    rho = pair_less(h, one)[0]
    third = pair_times(pair_times(a0, a0), pair_over(m3, m1))
    sigma = pair_less(third, pair_times(h, h))[0]
    more = (rho > 1e-9) & (sigma > 1e-9)
    a1 = jnp.where(more, a0[0] * rho / jnp.where(more, sigma, 1.0), 0.0)
    return a0[0] + a1 * h[0], -a0[0] * a1


def final_kernel(sums, state, field, product, field12, product12, out, balance, *, cells):
    flow = lax.axis_index("group") == 0
    total = (sums[...], jnp.zeros(sums.shape, F32))
    while total[0].shape[0] > 8:
        half = total[0].shape[0] // 2
        total = pair_add([v[:half] for v in total], [v[half:] for v in total])
    for step in (4, 2, 1):
        total = pair_add(total, [pltpu.roll(v, step, 0) for v in total])

    def number(n):
        return tuple(jnp.broadcast_to(v[:1, n : n + 1], (8, Z)) for v in total)

    c0, c1 = krylov(number(0), number(1), number(2), number(3))
    columns = cells // (3 * Z)
    outflow = (number(8)[0] + c0 * number(6)[0] + c1 * number(7)[0]) / columns
    stored = (c0 * number(4)[0] + c1 * number(5)[0]) / cells
    balance[0] = outflow[0, 0]
    balance[1] = stored[0, 0]

    def tall(v):
        return jnp.concatenate([v] * (EY // 8), axis=0)

    @pl.when(flow)
    def _():
        s0, s1 = tall(c0), tall(c1)

        def row(x, carry):
            for k in range(3):
                step = s0 * field[k, OX + x] + s1 * product[k, OX + x]
                out[k, x] = state[k, x] + to_tile(step)
            return carry

        loop(0, X, row)

    @pl.when(jnp.logical_not(flow))
    def _():
        zero = jnp.zeros((8, Z), F32)
        weights = [
            (jnp.ones((8, Z), F32), zero),
            (2.0 * c0, zero),
            (2.0 * c1, zero),
            two_product(c0, c0),
            two_product(2.0 * c0, c1),
            two_product(c1, c1),
        ]
        moments = []
        for m in range(4):
            start = FIRST_SUM + 6 * m
            total = number(start)
            for n in range(1, 6):
                total = pair_add(total, pair_times(weights[n], number(start + n)))
            moments.append(total)
        d0, d1 = krylov(*moments)
        scale_r = [tall(d0), tall(d0 * c0), tall(d0 * c1)]
        scale_w = [tall(d1), tall(d1 * c0), tall(d1 * c1)]

        def row(x, carry):
            for c in range(3):
                step = scale_r[0] * field[c, OX + x] + scale_w[0] * product[c, OX + x]
                for a in range(2):
                    step = step + scale_r[a + 1] * field12[a, c, OX + x]
                    step = step + scale_w[a + 1] * product12[a, c, OX + x]
                out[c, x] = state[c, x] + to_tile(step)
            return carry

        loop(0, X, row)


def swaps(first, second, axis):
    groups, rows, columns = (lax.axis_size(a) for a in AXES)
    count, found = lax.axis_size(axis), []
    for value, start in ((first, 0), (second, 1)):
        pairs = []
        for g in range(groups):
            for i in range(rows):
                for j in range(columns):
                    place = i if axis == "gx" else j
                    step = 1 if place % 2 == start else -1
                    if 0 <= place + step < count:
                        here = (g * rows + i) * columns + j
                        pairs.append((here, here + step * (columns if axis == "gx" else 1)))
        found.append(lax.ppermute(value, AXES, pairs))
    return found


def core_swap(value):
    count = lax.axis_size("gx") * lax.axis_size("gy")
    pairs = [(n, (n + count) % (2 * count)) for n in range(2 * count)]
    return lax.ppermute(value, AXES, pairs)


def body(state, conduct, capacity, supply, flags, layer_map):
    state, conduct, capacity, supply = state[0], conduct[0], capacity[0], supply[0]
    layer_map = layer_map.reshape(1, 3 * Z)
    cells = X * Y * 3 * Z * lax.axis_size("gx") * lax.axis_size("gy")
    devices = lax.axis_size("group") * lax.axis_size("gx") * lax.axis_size("gy")
    tile = struct(3, X, Y, Z)
    brick = struct(X, Y, Z)
    wide = (EX, EY, Z)
    full = struct(3, *wide)

    y_face = struct(len(Y_ROWS), X, Z)
    xa, xb, fa, fb, ya, yb = call(
        pack_kernel,
        x_faces(NEAR) + x_faces(X_ROWS[len(NEAR) :]) + [y_face] * 2,
        [
            pltpu.VMEM((X, Y), jnp.int32),
            pltpu.VMEM((3, X, Y, Z), F32),
            pltpu.VMEM((3, 3, X, Y, Z), F32),
            pltpu.VMEM((X, Y, Z), F32),
            pltpu.VMEM((X, Y, Z), F32),
            pltpu.VMEM((3, X, Y, Z), F32),
            pltpu.SemaphoreType.DMA((14,)),
        ],
        left=(0, 1, 2, 3),
        limit=58,
        count=4,
    )(flags, state, conduct, capacity)
    k_halos = lax.optimization_barrier(swaps(xa, xb, "gx") + swaps(ya, yb, "gy"))
    far = swaps(fa, fb, "gx")
    wide_faces = struct(12, *wide)
    tables = [pltpu.VMEM((6, *wide), F32), pltpu.VMEM(wide, F32)]
    inner, tz, unit0 = call(
        interior_kernel,
        [wide_faces, tile, brick],
        tables + [pltpu.VMEM((X, Y, Z), F32)],
        cost=30_000_000,
    )(state, conduct, capacity, flags, layer_map)
    cross = core_swap(call(strain_kernel, brick)(state, unit0, *k_halos))
    base, beside = call(
        first_kernel,
        [tile, struct(8, Z)],
        tables + [pltpu.VMEM((3, *wide), F32)],
        cost=20_000_000,
    )(state, conduct, capacity, supply, inner, *k_halos)
    faces, k_rim = call(
        halo_kernel, [wide_faces, struct(6, len(K_RIM), EY, Z)], tables, cost=30_000_000
    )(conduct, capacity, tz, layer_map, *k_halos, *far)
    residual, xa, xb = call(residual_kernel, [tile] + x_faces(R_ROWS))(
        base, cross, cross, layer_map
    )
    halos = swaps(xa, xb, "gx")
    ya, yb = call(relay_kernel, [struct(Y_PACK, Z)] * 2)(
        residual, cross, *halos, k_halos[0], k_halos[1], *far
    )
    halos = halos + swaps(ya, yb, "gy")
    rim, field, product, unit12 = call(
        image_kernel,
        [struct(12, len(RIM), EY, Z), full, full, struct(2, EX - 2, EY, Z)],
        [pltpu.VMEM((6, len(K_RIM), EY, Z), F32), pltpu.VMEM((EX - 2, EY, Z), F32)],
    )(residual, cross, beside, layer_map, *halos, faces, k_rim)
    unit12 = core_swap(unit12)
    sums = call(early_kernel, struct(8, Z), [pltpu.VMEM((4, 8, Z), F32)], cost=20_000_000)(
        field, product, faces, state
    )
    sums, field12, product12 = call(
        sums_kernel,
        [struct(devices, Z), struct(2, 3, *wide), struct(2, 3, *wide)],
        [pltpu.VMEM((20, 8, Z), F32)],
    )(field, product, faces, rim, unit12, sums)
    sums = lax.all_to_all(sums, AXES, 0, 0, tiled=True)

    def finish(*refs):
        final_kernel(*refs, cells=cells)

    new_state, balance = call(finish, [tile, struct(2)], scalars=(1,))(
        sums, state, field, product, field12, product12
    )
    return new_state[None], balance


def solution(mesh):
    placed = (
        P("group", None, "gx", "gy", None),
        P("group", None, None, "gx", "gy", None),
        P("group", "gx", "gy", None),
        P("group", None, "gx", "gy", None),
        P("gx", "gy"),
        P(),
    )
    return jax.shard_map(
        body,
        mesh=mesh,
        in_specs=placed,
        out_specs=(P("group", None, "gx", "gy", None), P()),
        check_vma=False,
    )
```

```python
import jax
import jax.numpy as jnp
from jax import lax
from jax.experimental import pallas as pl
from jax.experimental.pallas import tpu as pltpu
from jax.sharding import PartitionSpec as P

AXES = ("group", "gx", "gy")
X, Y, Z = 16, 32, 128
OX, OY = 3, 4
EX, EY = X + 2 * OX, Y + 2 * OY
BETA = 0.5
BIOT = 0.8
F32 = jnp.float32

X_ROWS = [(f, r) for f in range(13) for r in range(1, (3 if f < 3 else 2 if f < 10 else 1) + 1)]
NEAR = [(f, r) for f, r in X_ROWS if r == 1 and not 3 <= f < 9]
X_ROWS = NEAR + [row for row in X_ROWS if row not in NEAR]
Y_ROWS = [
    (f, r) for f in range(13) for r in range(1, (3 if 3 <= f < 6 else 2 if f < 10 else 1) + 1)
]
CORNER = [(1, 1), (1, 2), (2, 1), (2, 2), (1, 3), (3, 1)]
K_CORNERS = (
    [(f, i, j) for f in range(3) for i, j in CORNER[:4] + [(3, 1)]]
    + [(f, i, j) for f in range(3, 6) for i, j in CORNER[:4] + [(1, 3)]]
    + [(f, i, j) for f in range(6, 10) for i, j in CORNER[:3]]
)
R_ROWS = [(f, r) for f in range(3) for r in range(1, 4)]
R_CORNERS = [(f, i, j) for f in range(3) for i, j in CORNER]
AT_R = [len(R_ROWS) * X, len(R_ROWS) * X + len(R_CORNERS)]
AT_K = [AT_R[1] + len(R_CORNERS), AT_R[1] + len(R_CORNERS) + len(K_CORNERS)]
AT_Q = [AT_K[1] + len(K_CORNERS), AT_K[1] + len(K_CORNERS) + 3]
AT_U = AT_Q[1] + 3
Y_PACK = -(-(AT_U + 4) // 8) * 8
Q_SLOT = [R_ROWS.index((0, 3)), R_ROWS.index((1, 3))]


def struct(*shape):
    return jax.ShapeDtypeStruct(shape, F32)


def call(kernel, outs, scratch=(), left=(), count=0, cost=None, limit=20, scalars=()):
    extra = {}
    if left:
        extra["in_specs"] = [
            pl.BlockSpec(memory_space=pltpu.HBM if n in left else pltpu.VMEM) for n in range(count)
        ]
    if scalars:
        extra["out_specs"] = [
            pl.BlockSpec(memory_space=pltpu.SMEM if n in scalars else pltpu.VMEM)
            for n in range(len(outs))
        ]
    if cost:
        extra["cost_estimate"] = pl.CostEstimate(
            flops=cost, bytes_accessed=cost, transcendentals=0
        )
    return pl.pallas_call(
        kernel,
        out_shape=outs,
        scratch_shapes=list(scratch),
        compiler_params=pltpu.CompilerParams(vmem_limit_bytes=limit << 20),
        **extra,
    )


def up_y(v):
    return pltpu.roll(v, v.shape[0] - 1, 0)


def down_y(v):
    return pltpu.roll(v, 1, 0)


def up_z(v):
    return pltpu.roll(v, Z - 1, 1)


def down_z(v):
    return pltpu.roll(v, 1, 1)


def lanes(rows):
    return lax.broadcasted_iota(jnp.int32, (rows, Z), 1)


def rows_of(rows):
    return lax.broadcasted_iota(jnp.int32, (rows, Z), 0)


def to_tile(v):
    return pltpu.roll(v, EY - OY, 0)[:Y]


def harmonic(a, b):
    return 2.0 * a * b / jnp.maximum(a + b, 1e-30)


def one_hot(map_ref):
    brick = lax.broadcasted_iota(jnp.int32, (Z, 3 * Z), 0)
    return jnp.where(brick == map_ref[...], 1.0, 0.0).astype(jnp.bfloat16)


def dot_split(v, hot, contract):
    high = v.astype(jnp.bfloat16)
    low = (v - high.astype(F32)).astype(jnp.bfloat16)
    dims = (((1,), (contract,)), ((), ()))
    return lax.dot_general(high, hot, dims, preferred_element_type=F32) + lax.dot_general(
        low, hot, dims, preferred_element_type=F32
    )


def spread(v, hot, k):
    return dot_split(v, hot[:, k * Z : (k + 1) * Z], 0)


def gather_up(parts, hot):
    total = None
    for k, v in enumerate(parts):
        part = dot_split(v, hot[:, k * Z : (k + 1) * Z], 1)
        total = part if total is None else total + part
    ones = jnp.ones((8, 3 * Z), jnp.bfloat16)
    counts = lax.dot_general(ones, hot, (((1,), (1,)), ((), ())), preferred_element_type=F32)
    return total * (1.0 / counts[:1])


def gather_wide(ref, hot):
    rows = EX - 2
    parts = [ref[k, 1 : EX - 1].reshape(rows * EY, Z) for k in range(3)]
    return gather_up(parts, hot).reshape(rows, EY, Z)


def fetch(pairs, sem, start=0):
    copies = [pltpu.make_async_copy(a, b, sem.at[start + n]) for n, (a, b) in enumerate(pairs)]
    for copy in copies:
        copy.start()
    return copies


class Joined:
    def __init__(self, near, far):
        self.near, self.far = near, far

    def place(self, at):
        n, rest = (at[0], at[1:]) if isinstance(at, tuple) else (at, ())
        ref, n = (self.near, n) if n < len(NEAR) else (self.far, n - len(NEAR))
        return ref, (n, *rest)

    def __getitem__(self, at):
        ref, at = self.place(at)
        return ref[at]

    def __setitem__(self, at, value):
        ref, at = self.place(at)
        ref[at] = value


class Either:
    def __init__(self, odd, at_odd, at_even):
        self.odd, self.at_odd, self.at_even = odd, at_odd, at_even

    def __getitem__(self, at):
        return jnp.where(self.odd, self.at_odd[at], self.at_even[at])


def parity(axis):
    return lax.rem(lax.axis_index(axis), 2) == 1


def lower_upper(axis, first, second):
    odd = parity(axis)
    return Either(odd, first, second), Either(odd, second, first)


def surroundings(xa, xb, ya, yb):
    return lower_upper("gx", xa, xb) + lower_upper("gy", ya, yb)


def put(first, second, at, odd, tail, head):
    first[at] = jnp.where(odd, head, tail)
    second[at] = jnp.where(odd, tail, head)


def pack_x(source, rows, first, second):
    odd = parity("gx")
    for n, (f, r) in enumerate(rows):
        put(first, second, n, odd, source(f)[X - r], source(f)[r - 1])


def unpack_x(target, rows, low, up):
    for n, (f, r) in enumerate(rows):
        target(f)[OX - r, OY : OY + Y] = low[n]
        target(f)[OX + X - 1 + r, OY : OY + Y] = up[n]


def corner_at(side, i, j):
    row = OX - i if side[0] == 0 else OX + X - 1 + i
    column = OY - j if side[1] == 0 else OY + Y - 1 + j
    return row, slice(column, column + 1)


def x_faces(rows):
    return [struct(len(rows), Y, Z)] * 2


def loop(first, last, body, init=0, unroll=4):
    steps = (last - first) // unroll

    def step(n, carry):
        for m in range(unroll):
            carry = body(first + n * unroll + m, carry)
        return carry

    init = lax.fori_loop(0, steps, step, init)
    for i in range(first + steps * unroll, last):
        init = body(i, init)
    return init


def vertical_faces(conduct, flags, bottom, store):
    flow = lax.axis_index("group") == 0
    last = lanes(Y) == Z - 1
    eye = jnp.where(
        lax.broadcasted_iota(jnp.int32, (Y, Y), 0) == lax.broadcasted_iota(jnp.int32, (Y, Y), 1),
        1.0,
        0.0,
    ).astype(jnp.bfloat16)
    columns = lax.dot_general(
        eye,
        flags[...].astype(F32).astype(jnp.bfloat16),
        (((1,), (1,)), ((), ())),
        preferred_element_type=F32,
    )
    for x in range(X):
        bottom[x] = jnp.broadcast_to(columns[:, x : x + 1], (Y, Z))

    def row(x, carry):
        kz = [conduct[2, k, x] for k in range(3)]
        rolled = [up_z(v) for v in kz]
        ends = [rolled[1], rolled[2], bottom[x] * kz[2]]
        for k in range(3):
            end = jnp.where(flow, ends[k], kz[k])
            store(x, k, harmonic(kz[k], jnp.where(last, end, rolled[k])))
        return carry

    loop(0, X, row)


def pack_kernel(flags_in, state_in, conduct_in, capacity_in, xa, xb, fb, ya, yb, *scratch):
    flags, state, conduct, capacity, bottom, tz, sem = scratch
    early = [(flags_in, flags)] + [(conduct_in.at[2, k], conduct.at[2, k]) for k in range(3)]
    late = [(conduct_in.at[d, k], conduct.at[d, k]) for d in range(2) for k in range(3)]
    late += [(state_in.at[k], state.at[k]) for k in range(3)] + [(capacity_in, capacity)]
    early = fetch(early, sem)
    late = fetch(late, sem, len(early))
    for copy in early:
        copy.wait()
    def store(x, k, value):
        tz[k, x] = value

    vertical_faces(conduct, flags, bottom, store)
    for copy in late:
        copy.wait()

    def source(f):
        if f < 6:
            return conduct.at[f // 3, f % 3]
        if f < 9:
            return tz.at[f - 6]
        return capacity if f == 9 else state.at[f - 10]

    pack_x(source, X_ROWS, xa, Joined(xb, fb))
    odd = parity("gy")
    for n, (f, r) in enumerate(Y_ROWS):
        put(ya, yb, n, odd, source(f)[:, Y - r, :], source(f)[:, r - 1, :])


class Faces:
    def __init__(self, x, y, z, own):
        self.x, self.y, self.z, self.own = x, y, z, own


def faces_in(ref, shift=0):
    return Faces(*[lambda c, i, d=d: ref[3 * d + c, i - shift] for d in range(4)])


def lateral(faces, v_ref, c, i, v, fx_before):
    fx = faces.x(c, i) * (v - v_ref[c, i + 1])
    fy = faces.y(c, i) * (v - up_y(v))
    return (fx - fx_before) + (fy - down_y(fy)), fx


def x_flux(faces, v_ref, i):
    return tuple(faces.x(c, i) * (v_ref[c, i] - v_ref[c, i + 1]) for c in range(3))


def flow_below(vs, last):
    rolled = [up_z(v) for v in vs]
    ends = [rolled[1], rolled[2], 0.0]
    return [jnp.where(last, ends[k], rolled[k]) for k in range(3)]


def flow_row(faces, v_ref, i, fx_before):
    last, first = lanes(EY) == Z - 1, lanes(EY) == 0
    vs = [v_ref[k, i] for k in range(3)]
    below = flow_below(vs, last)
    fz = [faces.z(k, i) * (vs[k] - below[k]) for k in range(3)]
    moved = [down_z(v) for v in fz]
    ends = [0.0, moved[0], moved[1]]
    out, fx_now = [], []
    for k in range(3):
        side, fx = lateral(faces, v_ref, k, i, vs[k], fx_before[k])
        above = jnp.where(first, ends[k], moved[k])
        out.append(faces.own(k, i) * vs[k] + side + (fz[k] - above))
        fx_now.append(fx)
    return out, tuple(fx_now)


def strain_row(v_ref, i):
    v0, v1, v2 = v_ref[0, i], v_ref[1, i], v_ref[2, i]
    low = jnp.where(lanes(EY) == Z - 1, 0.0, up_z(v2))
    return (v_ref[0, i + 1] - v0) + (up_y(v1) - v1) + (low - v2)


def solid_row(faces, v_ref, i, s_before, fx_before):
    last, first = lanes(EY) == Z - 1, lanes(EY) == 0
    e = strain_row(v_ref, i)
    s = faces.own(0, i) * e
    grad = [s_before - s, down_y(s) - s, jnp.where(first, 0.0, down_z(s)) - s]
    out, fx_now = [], []
    for c in range(3):
        v = v_ref[c, i]
        side, fx = lateral(faces, v_ref, c, i, v, fx_before[c])
        fz = faces.z(c, i) * (v - jnp.where(last, 0.0, up_z(v)))
        above = jnp.where(first, 0.0, down_z(fz))
        out.append((side + (fz - above)) + grad[c])
        fx_now.append(fx)
    return out, s, tuple(fx_now)


BESIDE = [(1, -1, Y), (1, X - 1, Y), (1, -1, 0), (1, X - 1, 0)]
BESIDE += [(0, X, -1), (0, 0, -1), (0, X, Y - 1), (0, 0, Y - 1)]


def place_tile(conduct, capacity, keep, caps):
    at = slice(OY, OY + Y)

    def row(x, carry):
        for f in range(6):
            keep[f, OX + x, at] = conduct[f // 3, f % 3, x]
        caps[OX + x, at] = capacity[x]
        return carry

    loop(0, X, row)


def interior_kernel(state, conduct, capacity, flags, layer_map, faces, tz, unit, keep, caps, bottom):
    flow = lax.axis_index("group") == 0
    place_tile(conduct, capacity, keep, caps)

    def store(x, k, value):
        tz[k, x] = value
        faces[6 + k, OX + x, OY : OY + Y] = value

    vertical_faces(conduct, flags, bottom, store)
    loop(OX, OX + X, lambda i, carry: lateral_faces(keep, faces, i))

    @pl.when(flow)
    def _():
        hot = one_hot(layer_map)
        bricks = caps[OX : OX + X].reshape(X * EY, Z)
        for k in range(3):
            faces[9 + k, OX : OX + X] = (spread(bricks, hot, k) + BETA).reshape(X, EY, Z)
        parts = [state[k].reshape(X * Y, Z) for k in range(3)]
        unit[...] = gather_up(parts, hot).reshape(X, Y, Z)


def lateral_faces(keep, faces, i):
    for c in range(3):
        faces[c, i] = harmonic(keep[c, i], keep[c, i + 1])
        here = keep[3 + c, i]
        faces[3 + c, i] = harmonic(here, up_y(here))
    return 0


def strain_kernel(state, unit, xa, xb, ya, yb, strain):
    flow = lax.axis_index("group") == 0
    _, xu, _, yu = surroundings(xa, xb, ya, yb)

    @pl.when(flow)
    def _():
        strain[...] = unit[...]

    @pl.when(jnp.logical_not(flow))
    def _():
        last = lanes(Y) == Z - 1
        edge = rows_of(Y) == Y - 1
        n_x, n_y = X_ROWS.index((10, 1)), Y_ROWS.index((11, 1))
        for x in range(X):
            v0, v1, v2 = (state[c, x] for c in range(3))
            east = state[0, x + 1] if x + 1 < X else xu[n_x]
            north = jnp.where(edge, yu[n_y, x : x + 1], up_y(v1))
            low = jnp.where(last, 0.0, up_z(v2))
            strain[x] = (east - v0) + (north - v1) + (low - v2)


def first_kernel(state, conduct, capacity, supply, faces_ref, xa, xb, ya, yb, *refs):
    xl, xu, yl, yu = surroundings(xa, xb, ya, yb)
    base, beside, sides, own, field = refs
    flow = lax.axis_index("group") == 0

    def place(x, carry):
        for c in range(3):
            field[c, OX + x, OY : OY + Y] = state[c, x]
        for f in range(6):
            sides[f, OX + x] = faces_ref[f, OX + x]
        return carry

    loop(0, X, place)
    for c in range(3):
        n = X_ROWS.index((10 + c, 1))
        field[c, OX - 1, OY : OY + Y] = xl[n]
        field[c, OX + X, OY : OY + Y] = xu[n]
        n = Y_ROWS.index((10 + c, 1))
        field[c, OX : OX + X, OY - 1, :] = yl[n]
        field[c, OX : OX + X, OY + Y, :] = yu[n]
        n = X_ROWS.index((c, 1))
        at = slice(OY, OY + Y)
        sides[c, OX - 1, at] = harmonic(xl[n], conduct[0, c, 0])
        sides[c, OX + X - 1, at] = harmonic(conduct[0, c, X - 1], xu[n])
        n = Y_ROWS.index((3 + c, 1))
        sides[3 + c, OX : OX + X, OY - 1, :] = harmonic(yl[n], conduct[1, c, :, 0, :])
        sides[3 + c, OX : OX + X, OY + Y - 1, :] = harmonic(conduct[1, c, :, Y - 1, :], yu[n])
    field[1, OX - 1, OY + Y : OY + Y + 1] = jnp.zeros((1, Z), F32)
    field[0, OX + X, OY - 1 : OY] = jnp.zeros((1, Z), F32)
    for n, (c, x, y) in enumerate(BESIDE):
        beside[n : n + 1] = field[c, OX + x, OY + y : OY + y + 1]
    inner = faces_in(faces_ref)
    outer = faces_in(sides)

    @pl.when(flow)
    def _():
        faces = Faces(outer.x, outer.y, inner.z, inner.own)

        def row(i, fx_before):
            image, fx = flow_row(faces, field, i, fx_before)
            for k in range(3):
                base[k, i - OX] = (
                    supply[k, i - OX] + BETA * state[k, i - OX] - to_tile(image[k])
                )
            return fx

        loop(OX, OX + X, row, x_flux(faces, field, OX - 1))

    @pl.when(jnp.logical_not(flow))
    def _():
        def place(x, carry):
            own[OX + x, OY : OY + Y] = capacity[x]
            return carry

        loop(0, X, place)
        own[OX - 1, OY : OY + Y] = xl[X_ROWS.index((9, 1))]
        own[OX : OX + X, OY - 1, :] = yl[Y_ROWS.index((9, 1))]
        faces = Faces(outer.x, outer.y, inner.z, lambda c, i: own[i])

        def row(i, carry):
            image, s, fx = solid_row(faces, field, i, carry[0], carry[1])
            for c in range(3):
                base[c, i - OX] = supply[c, i - OX] - to_tile(image[c])
            return s, fx

        before = faces.own(0, OX - 1) * strain_row(field, OX - 1)
        loop(OX, OX + X, row, (before, x_flux(faces, field, OX - 1)))


def halo_kernel(conduct, capacity, tz, layer_map, xa, xb, ya, yb, fb, *refs):
    faces, rim, keep, caps = refs
    xl, xu, yl, yu = surroundings(xa, Joined(xb, fb), ya, yb)
    flow = lax.axis_index("group") == 0

    def target(f):
        if f < 6:
            return keep.at[f]
        return faces.at[f] if f < 9 else caps

    place_tile(conduct, capacity, keep, caps)

    def place(x, carry):
        for k in range(3):
            faces[6 + k, OX + x, OY : OY + Y] = tz[k, x]
        return carry

    loop(0, X, place)
    for n, (f, r) in enumerate(X_ROWS):
        if f < 10:
            target(f)[OX - r, OY : OY + Y] = xl[n]
            target(f)[OX + X - 1 + r, OY : OY + Y] = xu[n]
    for n, (f, r) in enumerate(Y_ROWS):
        if f < 10:
            target(f)[OX : OX + X, OY - r, :] = yl[n]
            target(f)[OX : OX + X, OY + Y - 1 + r, :] = yu[n]
    loop(0, EX - 1, lambda i, carry: lateral_faces(keep, faces, i))
    for n, i in enumerate(K_RIM):
        for f in range(6):
            rim[f, n] = keep[f, i]

    @pl.when(flow)
    def _():
        hot = one_hot(layer_map)
        bricks = caps[1 : EX - 1].reshape((EX - 2) * EY, Z)
        for k in range(3):
            faces[9 + k, 1 : EX - 1] = (spread(bricks, hot, k) + BETA).reshape(EX - 2, EY, Z)

    @pl.when(jnp.logical_not(flow))
    def _():
        faces[9] = caps[...]


BESIDE = [(1, -1, Y), (1, X - 1, Y), (1, -1, 0), (1, X - 1, 0)]
BESIDE += [(0, X, -1), (0, 0, -1), (0, X, Y - 1), (0, 0, Y - 1)]
RIM = [0, 1, 2, EX - 4, EX - 3, EX - 2]
K_RIM = [0, 1, 2, 3, EX - 4, EX - 3, EX - 2, EX - 1]


def residual_kernel(base, strain, unit, layer_map, residual, xa, xb):
    flow = lax.axis_index("group") == 0

    @pl.when(flow)
    def _():
        hot = one_hot(layer_map)
        e = strain[...].reshape(X * Y, Z)
        for k in range(3):
            residual[k] = base[k] - BIOT * spread(e, hot, k).reshape(X, Y, Z)

    @pl.when(jnp.logical_not(flow))
    def _():
        residual[...] = base[...]

    pack_x(lambda f: residual.at[f], R_ROWS, xa, xb)

    @pl.when(jnp.logical_not(flow))
    def _():
        odd = parity("gx")
        for depth, n in enumerate(Q_SLOT):
            put(xa, xb, n, odd, unit[X - 1 - depth], unit[depth])


def relay_kernel(residual, unit, xa, xb, ka, kb, fb, ya, yb):
    flow = lax.axis_index("group") == 0
    odd = parity("gy")
    r_halos, k_halos = lower_upper("gx", xa, xb), lower_upper("gx", ka, Joined(kb, fb))

    def give(at, count, ref, index, j):
        put(ya, yb, slice(at, at + count), odd, ref[index(Y - j)], ref[index(j - 1)])

    for n, (f, r) in enumerate(R_ROWS):
        give(n * X, X, residual, lambda y: (f, slice(None), y), r)
    for side in range(2):
        r_halo, k_halo = r_halos[side], k_halos[side]
        for n, (f, i, j) in enumerate(R_CORNERS):
            row = R_ROWS.index((f, i))
            give(AT_R[side] + n, 1, r_halo, lambda y: (row, slice(y, y + 1)), j)
        for n, (f, i, j) in enumerate(K_CORNERS):
            row = X_ROWS.index((f, i))
            give(AT_K[side] + n, 1, k_halo, lambda y: (row, slice(y, y + 1)), j)
        for n, (i, j) in enumerate(CORNER[:3]):
            row = Q_SLOT[i - 1]
            give(AT_Q[side] + n, 1, r_halo, lambda y: (row, slice(y, y + 1)), j)
        for c in range(2):
            row = X_ROWS.index((10 + c, 1))
            give(AT_U + 2 * side + c, 1, k_halo, lambda y: (row, slice(y, y + 1)), 1)

    @pl.when(jnp.logical_not(flow))
    def _():
        for depth, n in enumerate(Q_SLOT):
            give(n * X, X, unit, lambda y: (slice(None), y), depth + 1)


def fold(v):
    return jnp.sum(v.reshape(v.shape[0] // 8, 8, Z), axis=0)


def spread_sums(found):
    lane = lanes(8)
    row = jnp.zeros((8, Z), F32)
    first = rows_of(8) == 0
    for n, total in found.items():
        row = jnp.where(first & (lane == n), jnp.sum(total), row)
    return row


def tile_rows():
    at = rows_of(EY)
    return (at >= OY) & (at < OY + Y)


def fill(residual, target, halos):
    xl, xu, yl, yu = halos

    def place(x, carry):
        for k in range(3):
            target[k, OX + x, OY : OY + Y] = residual[k, x]
        return carry

    loop(0, X, place)
    unpack_x(lambda f: target.at[f], R_ROWS, xl, xu)
    for n, (f, r) in enumerate(R_ROWS):
        target[f, OX : OX + X, OY - r, :] = yl[n * X : (n + 1) * X]
        target[f, OX : OX + X, OY + Y - 1 + r, :] = yu[n * X : (n + 1) * X]
    for v, pack in enumerate((yl, yu)):
        for h in range(2):
            for n, (f, i, j) in enumerate(R_CORNERS):
                row, column = corner_at((h, v), i, j)
                target[f, row, column] = pack[AT_R[h] + n : AT_R[h] + n + 1]


def complete(faces, rim, k_rim_in, k_rim, halos, hot):
    for n, i in enumerate(RIM):
        for f in range(6, 12):
            rim[f, n] = faces[f, i]
    k_rim[...] = k_rim_in[...]
    order = []
    for v, pack in enumerate(halos[2:]):
        for h in range(2):
            for n, (f, i, j) in enumerate(K_CORNERS):
                row, column = corner_at((h, v), i, j)
                value = pack[AT_K[h] + n : AT_K[h] + n + 1]
                if f < 6:
                    k_rim[f, K_RIM.index(row), column] = value
                elif f < 9:
                    rim[f, RIM.index(row), column] = value
                else:
                    order.append((RIM.index(row), column, value))
    for n, i in enumerate(RIM):
        m = K_RIM.index(i)
        for c in range(3):
            rim[c, n] = harmonic(k_rim[c, m], k_rim[c, m + 1])
            here = k_rim[3 + c, m]
            rim[3 + c, n] = harmonic(here, up_y(here))
    if hot is None:
        for row, column, value in order:
            rim[9, row, column] = value
    else:
        values = [value for _, _, value in order]
        values += [jnp.zeros((1, Z), F32)] * (16 - len(values))
        caps = jnp.concatenate(values, axis=0)
        for k in range(3):
            storage = spread(caps, hot, k) + BETA
            for n, (row, column, _) in enumerate(order):
                rim[9 + k, row, column] = storage[n : n + 1]


def row_parts(faces, rim):
    return faces_in(rim), faces_in(faces), faces_in(rim, EX - 7)


def run_rows(parts, first, last, body, init, unroll=3):
    low, middle, high = parts
    for i in range(first, OX):
        init = body(low, i, init)
    init = loop(max(first, OX), EX - 4, lambda i, carry: body(middle, i, carry), init, unroll)
    for i in range(EX - 4, last):
        init = body(high, i, init)
    return init


PAIRS = [(0, 0), (0, 1), (0, 2), (1, 1), (1, 2), (2, 2)]
FIRST_SUM = 9


def grid_mask(before, after):
    gx, gy = lax.axis_index("gx"), lax.axis_index("gy")
    gx_last, gy_last = lax.axis_size("gx") - 1, lax.axis_size("gy") - 1
    at = rows_of(EY)
    in_y = (at >= OY - jnp.where(gy > 0, before, 0)) & (
        at < OY + Y + jnp.where(gy < gy_last, after, 0)
    )

    def in_grid(i):
        in_x = ((i >= OX) | (gx > 0)) & ((i < OX + X) | (gx < gx_last))
        return in_y & in_x

    return in_grid


def load_rows(q_refs, targets, added):
    in_grid = grid_mask(1, 2)

    def row(i, carry):
        for q_ref, target in zip(q_refs, targets):
            load_row(q_ref, target, i, in_grid(i))
        return carry

    def load_row(q_ref, target, i, ok):
        first = lanes(EY) == 0
        q = q_ref[i - 1]
        push = [
            BIOT * (q_ref[i - 2] - q),
            BIOT * (down_y(q) - q),
            BIOT * (jnp.where(first, 0.0, down_z(q)) - q),
        ]
        for c in range(3):
            v = push[c] + target[c, i] if added else push[c]
            target[c, i] = jnp.where(ok, v, 0.0)

    loop(OX - 1, OX + X + 2, row)


def solid_image(parts, f_refs, p_refs, unroll):
    in_grid = grid_mask(0, 1)

    def row(faces, i, carry):
        ok, after = in_grid(i), []
        for f_ref, p_ref, (s, fx) in zip(f_refs, p_refs, carry):
            out, s, fx = solid_row(faces, f_ref, i, s, fx)
            for c in range(3):
                p_ref[c, i] = jnp.where(ok, out[c], 0.0)
            after.append((s, fx))
        return tuple(after)

    view = parts[0]
    start = [
        (view.own(0, OX - 1) * strain_row(f, OX - 1), x_flux(view, f, OX - 1)) for f in f_refs
    ]
    run_rows(parts, OX, OX + X + 1, row, tuple(start), unroll)


def gram_sums(faces, fields, products, pairs, acc):
    acc[...] = jnp.zeros(acc.shape, F32)
    vectors = range(len(fields))

    def row(i, carry):
        inside, last = tile_rows(), lanes(EY) == Z - 1

        def only(v):
            return jnp.where(inside, v, 0.0)

        def add(n, v):
            acc[n] = acc[n] + fold(v)

        strains = [strain_row(p, i) for p in products]
        modulus = only(faces[9, i])
        later = sorted({b for _, b in pairs})
        pushes = {b: modulus * strains[b] for b in later}
        for n, (a, b) in enumerate(pairs):
            add(4 * n + 3, pushes[b] * strains[a])
        for c in range(3):
            ws = [p[c, i] for p in products]
            dx = [ws[a] - products[a][c, i + 1] for a in vectors]
            dy = [w - up_y(w) for w in ws]
            dz = [w - jnp.where(last, 0.0, up_z(w)) for w in ws]
            sx, sy, sz = (only(faces[3 * d + c, i]) for d in range(3))
            fx = {b: sx * dx[b] for b in later}
            fy = {b: sy * dy[b] for b in later}
            fz = {b: sz * dz[b] for b in later}
            rs = [f[c, i] for f in fields]
            r_in = {b: only(rs[b]) for b in later}
            w_in = {b: only(ws[b]) for b in later}
            for n, (a, b) in enumerate(pairs):
                add(4 * n + 3, fx[b] * dx[a] + fy[b] * dy[a] + fz[b] * dz[a])
                add(4 * n, r_in[b] * rs[a])
                add(4 * n + 1, r_in[b] * ws[a])
                add(4 * n + 2, w_in[b] * ws[a])
        return carry

    loop(OX, OX + X, row, 0, 2)
    found = {}
    for n, pair in enumerate(pairs):
        for m in range(4):
            found[FIRST_SUM + 6 * m + PAIRS.index(pair)] = acc[4 * n + m]
    return found


def unit_surroundings(unit, halos, q):
    xl, xu, yl, yu = halos

    def place(x, carry):
        q[OX - 1 + x, OY : OY + Y] = unit[x]
        return carry

    loop(0, X, place)
    for depth, n in enumerate(Q_SLOT):
        q[OX - 2 - depth, OY : OY + Y] = xl[n]
        q[OX + X - 1 + depth, OY : OY + Y] = xu[n]
        rows = slice(n * X, (n + 1) * X)
        q[OX - 1 : OX - 1 + X, OY - 1 - depth, :] = yl[rows]
        q[OX - 1 : OX - 1 + X, OY + Y + depth, :] = yu[rows]
    for v, pack in enumerate((yl, yu)):
        for h in range(2):
            for n, (i, j) in enumerate(CORNER[:3]):
                row, column = corner_at((h, v), i, j)
                q[row - 1, column] = pack[AT_Q[h] + n : AT_Q[h] + n + 1]


def late_terms(faces, rim, field, beside, halos):
    yl, yu = halos[2:]

    def modulus(x, y):
        i, column = OX + x, slice(OY + y, OY + y + 1)
        return rim[9, RIM.index(i), column] if i in RIM else faces[9, i, column]

    u1 = [yu[AT_U + 1 : AT_U + 2]] + [beside[n : n + 1] for n in (1, 2, 3)]
    u0 = [yl[AT_U + 2 : AT_U + 3]] + [beside[n : n + 1] for n in (5, 6, 7)]
    for u, (x, y) in zip(u1, ((0, Y - 1), (X, Y - 1), (0, -1), (X, -1))):
        row, column = OX + x, slice(OY + y, OY + y + 1)
        field[0, row, column] = field[0, row, column] - modulus(x - 1, y) * u
    for u, (x, y) in zip(u0, ((X - 1, 0), (-1, 0), (X - 1, Y), (-1, Y))):
        row, column = OX + x, slice(OY + y, OY + y + 1)
        field[1, row, column] = field[1, row, column] - modulus(x, y - 1) * u


def image_kernel(residual, unit_old, beside, layer_map, *refs):
    halos, (faces, k_rim_in, rim, field, product, unit, k_rim, q) = refs[:4], refs[4:]
    halos = surroundings(*halos)
    flow = lax.axis_index("group") == 0
    fill(residual, field, halos)

    @pl.when(flow)
    def _():
        hot = one_hot(layer_map)
        complete(faces, rim, k_rim_in, k_rim, halos, hot)
        parts = row_parts(faces, rim)

        def row(view, i, fx_before):
            out, fx = flow_row(view, field, i, fx_before)
            for k in range(3):
                product[k, i] = out[k]
            return fx

        run_rows(parts, 1, EX - 1, row, x_flux(parts[0], field, 0))
        unit[0] = gather_wide(field, hot)
        unit[1] = gather_wide(product, hot)

    @pl.when(jnp.logical_not(flow))
    def _():
        complete(faces, rim, k_rim_in, k_rim, halos, None)
        late_terms(faces, rim, field, beside, halos)
        unit_surroundings(unit_old, halos, q)
        load_rows([q], [field], True)
        solid_image(row_parts(faces, rim), [field], [product], 3)


def early_kernel(field, product, faces, state, sums, acc):
    flow = lax.axis_index("group") == 0

    @pl.when(flow)
    def _():
        def dots(i, acc):
            acc = list(acc)
            inside, last = tile_rows(), lanes(EY) == Z - 1

            def add(n, v):
                acc[n] = acc[n] + fold(jnp.where(inside, v, 0.0))

            ws = [product[k, i] for k in range(3)]
            below = flow_below(ws, last)
            g = m1 = m2 = m3 = cr = cw = 0.0
            for k in range(3):
                r, w = field[k, i], ws[k]
                dx, dy, dz = w - product[k, i + 1], w - up_y(w), w - below[k]
                cf = faces[9 + k, i]
                g = g + r * r
                m1 = m1 + r * w
                m2 = m2 + w * w
                cr = cr + cf * r
                cw = cw + cf * w
                m3 = m3 + (
                    faces[k, i] * dx * dx
                    + faces[3 + k, i] * dy * dy
                    + faces[6 + k, i] * dz * dz
                    + cf * w * w
                )
            for n, v in enumerate((g, m1, m2, m3, cr, cw)):
                add(n, v)
            weight = jnp.where(last, faces[8, i], 0.0)
            add(6, weight * field[2, i])
            add(7, weight * ws[2])
            acc[8] = acc[8] + fold(to_tile(weight) * state[2, i - OX])
            return tuple(acc)

        zero = jnp.zeros((8, Z), F32)
        found = dict(enumerate(loop(OX, OX + X, dots, (zero,) * FIRST_SUM, 2)))
        sums[...] = spread_sums(found)

    @pl.when(jnp.logical_not(flow))
    def _():
        sums[...] = spread_sums(gram_sums(faces, [field], [product], PAIRS[:1], acc))


def sums_kernel(field, product, faces, rim, unit, sums_in, sums, field12, product12, acc):
    flow = lax.axis_index("group") == 0
    everyone = sums.shape[0]

    @pl.when(flow)
    def _():
        sums[...] = jnp.broadcast_to(sums_in[:1], (everyone, Z))

    @pl.when(jnp.logical_not(flow))
    def _():
        fields = [field] + [field12.at[a] for a in range(2)]
        products = [product] + [product12.at[a] for a in range(2)]
        load_rows([unit.at[a] for a in range(2)], fields[1:], False)
        solid_image(row_parts(faces, rim), fields[1:], products[1:], 2)
        found = gram_sums(faces, fields, products, PAIRS[1:], acc)
        own = sums_in[:1] + spread_sums(found)[:1]
        sums[...] = jnp.broadcast_to(own, (everyone, Z))


def two_sum(a, b):
    s = a + b
    t = s - a
    return s, (a - (s - t)) + (b - t)


def quick(a, b):
    s = a + b
    return s, b - (s - a)


def halves(a):
    t = 4097.0 * a
    high = t - (t - a)
    return high, a - high


def two_product(a, b):
    p = a * b
    ah, al = halves(a)
    bh, bl = halves(b)
    return p, ((ah * bh - p) + ah * bl + al * bh) + al * bl


def pair_add(a, b):
    s, e = two_sum(a[0], b[0])
    return quick(s, e + (a[1] + b[1]))


def pair_less(a, b):
    return pair_add(a, (-b[0], -b[1]))


def pair_times(a, b):
    p, e = two_product(a[0], b[0])
    return quick(p, e + (a[0] * b[1] + a[1] * b[0]))


def pair_over(a, b):
    q = a[0] / b[0]
    rest = pair_less(a, pair_times(b, (q, jnp.zeros_like(q))))
    return quick(q, rest[0] / b[0])


def krylov(g, m1, m2, m3):
    a0 = pair_over(g, m1)
    h = pair_times(a0, pair_over(m2, m1))
    one = (jnp.ones_like(a0[0]), jnp.zeros_like(a0[0]))
    rho = pair_less(h, one)[0]
    third = pair_times(pair_times(a0, a0), pair_over(m3, m1))
    sigma = pair_less(third, pair_times(h, h))[0]
    more = (rho > 1e-9) & (sigma > 1e-9)
    a1 = jnp.where(more, a0[0] * rho / jnp.where(more, sigma, 1.0), 0.0)
    return a0[0] + a1 * h[0], -a0[0] * a1


def final_kernel(sums, state, field, product, field12, product12, out, balance, *, cells):
    flow = lax.axis_index("group") == 0
    total = (sums[...], jnp.zeros(sums.shape, F32))
    while total[0].shape[0] > 8:
        half = total[0].shape[0] // 2
        total = pair_add([v[:half] for v in total], [v[half:] for v in total])
    for step in (4, 2, 1):
        total = pair_add(total, [pltpu.roll(v, step, 0) for v in total])

    def number(n):
        return tuple(jnp.broadcast_to(v[:1, n : n + 1], (8, Z)) for v in total)

    c0, c1 = krylov(number(0), number(1), number(2), number(3))
    columns = cells // (3 * Z)
    outflow = (number(8)[0] + c0 * number(6)[0] + c1 * number(7)[0]) / columns
    stored = (c0 * number(4)[0] + c1 * number(5)[0]) / cells
    balance[0] = outflow[0, 0]
    balance[1] = stored[0, 0]

    def tall(v):
        return jnp.concatenate([v] * (EY // 8), axis=0)

    @pl.when(flow)
    def _():
        s0, s1 = tall(c0), tall(c1)

        def row(x, carry):
            for k in range(3):
                step = s0 * field[k, OX + x] + s1 * product[k, OX + x]
                out[k, x] = state[k, x] + to_tile(step)
            return carry

        loop(0, X, row)

    @pl.when(jnp.logical_not(flow))
    def _():
        zero = jnp.zeros((8, Z), F32)
        weights = [
            (jnp.ones((8, Z), F32), zero),
            (2.0 * c0, zero),
            (2.0 * c1, zero),
            two_product(c0, c0),
            two_product(2.0 * c0, c1),
            two_product(c1, c1),
        ]
        moments = []
        for m in range(4):
            start = FIRST_SUM + 6 * m
            total = number(start)
            for n in range(1, 6):
                total = pair_add(total, pair_times(weights[n], number(start + n)))
            moments.append(total)
        d0, d1 = krylov(*moments)
        scale_r = [tall(d0), tall(d0 * c0), tall(d0 * c1)]
        scale_w = [tall(d1), tall(d1 * c0), tall(d1 * c1)]

        def row(x, carry):
            for c in range(3):
                step = scale_r[0] * field[c, OX + x] + scale_w[0] * product[c, OX + x]
                for a in range(2):
                    step = step + scale_r[a + 1] * field12[a, c, OX + x]
                    step = step + scale_w[a + 1] * product12[a, c, OX + x]
                out[c, x] = state[c, x] + to_tile(step)
            return carry

        loop(0, X, row)


def swap(value, start, axis):
    groups, rows, columns = (lax.axis_size(a) for a in AXES)
    pairs = []
    for g in range(groups):
        for i in range(rows):
            for j in range(columns):
                place = i if axis == "gx" else j
                step = 1 if place % 2 == start else -1
                if 0 <= place + step < lax.axis_size(axis):
                    here = (g * rows + i) * columns + j
                    pairs.append((here, here + step * (columns if axis == "gx" else 1)))
    return lax.ppermute(value, AXES, pairs)


def swaps(first, second, axis):
    return [swap(first, 0, axis), swap(second, 1, axis)]


def core_swap(value):
    count = lax.axis_size("gx") * lax.axis_size("gy")
    pairs = [(n, (n + count) % (2 * count)) for n in range(2 * count)]
    return lax.ppermute(value, AXES, pairs)


def body(state, conduct, capacity, supply, flags, layer_map):
    state, conduct, capacity, supply = state[0], conduct[0], capacity[0], supply[0]
    layer_map = layer_map.reshape(1, 3 * Z)
    cells = X * Y * 3 * Z * lax.axis_size("gx") * lax.axis_size("gy")
    devices = lax.axis_size("group") * lax.axis_size("gx") * lax.axis_size("gy")
    tile = struct(3, X, Y, Z)
    brick = struct(X, Y, Z)
    wide = (EX, EY, Z)
    full = struct(3, *wide)

    y_face = struct(len(Y_ROWS), X, Z)
    x_parts = [struct(n, Y, Z) for n in (len(X_ROWS), len(NEAR), len(X_ROWS) - len(NEAR))]
    xa, xb, fb, ya, yb = call(
        pack_kernel,
        x_parts + [y_face] * 2,
        [
            pltpu.VMEM((X, Y), jnp.int32),
            pltpu.VMEM((3, X, Y, Z), F32),
            pltpu.VMEM((3, 3, X, Y, Z), F32),
            pltpu.VMEM((X, Y, Z), F32),
            pltpu.VMEM((X, Y, Z), F32),
            pltpu.VMEM((3, X, Y, Z), F32),
            pltpu.SemaphoreType.DMA((14,)),
        ],
        left=(0, 1, 2, 3),
        limit=58,
        count=4,
    )(flags, state, conduct, capacity)
    k_halos = lax.optimization_barrier(swaps(xa, xb, "gx") + swaps(ya, yb, "gy"))
    far = swap(fb, 1, "gx")
    wide_faces = struct(12, *wide)
    tables = [pltpu.VMEM((6, *wide), F32), pltpu.VMEM(wide, F32)]
    inner, tz, unit0 = call(
        interior_kernel,
        [wide_faces, tile, brick],
        tables + [pltpu.VMEM((X, Y, Z), F32)],
        cost=30_000_000,
    )(state, conduct, capacity, flags, layer_map)
    cross = core_swap(call(strain_kernel, brick)(state, unit0, *k_halos))
    base, beside = call(
        first_kernel,
        [tile, struct(8, Z)],
        tables + [pltpu.VMEM((3, *wide), F32)],
        cost=20_000_000,
    )(state, conduct, capacity, supply, inner, *k_halos)
    faces, k_rim = call(
        halo_kernel, [wide_faces, struct(6, len(K_RIM), EY, Z)], tables, cost=30_000_000
    )(conduct, capacity, tz, layer_map, *k_halos, far)
    residual, xa, xb = call(residual_kernel, [tile] + x_faces(R_ROWS))(
        base, cross, cross, layer_map
    )
    halos = swaps(xa, xb, "gx")
    ya, yb = call(relay_kernel, [struct(Y_PACK, Z)] * 2)(
        residual, cross, *halos, k_halos[0], k_halos[1], far
    )
    halos = halos + swaps(ya, yb, "gy")
    rim, field, product, unit12 = call(
        image_kernel,
        [struct(12, len(RIM), EY, Z), full, full, struct(2, EX - 2, EY, Z)],
        [pltpu.VMEM((6, len(K_RIM), EY, Z), F32), pltpu.VMEM((EX - 2, EY, Z), F32)],
    )(residual, cross, beside, layer_map, *halos, faces, k_rim)
    unit12 = core_swap(unit12)
    sums = call(early_kernel, struct(8, Z), [pltpu.VMEM((4, 8, Z), F32)], cost=20_000_000)(
        field, product, faces, state
    )
    sums, field12, product12 = call(
        sums_kernel,
        [struct(devices, Z), struct(2, 3, *wide), struct(2, 3, *wide)],
        [pltpu.VMEM((20, 8, Z), F32)],
    )(field, product, faces, rim, unit12, sums)
    sums = lax.all_to_all(sums, AXES, 0, 0, tiled=True)

    def finish(*refs):
        final_kernel(*refs, cells=cells)

    new_state, balance = call(finish, [tile, struct(2)], scalars=(1,))(
        sums, state, field, product, field12, product12
    )
    return new_state[None], balance


def solution(mesh):
    placed = (
        P("group", None, "gx", "gy", None),
        P("group", None, None, "gx", "gy", None),
        P("group", "gx", "gy", None),
        P("group", None, "gx", "gy", None),
        P("gx", "gy"),
        P(),
    )
    return jax.shard_map(
        body,
        mesh=mesh,
        in_specs=placed,
        out_specs=(P("group", None, "gx", "gy", None), P()),
        check_vma=False,
    )
```

```python
import jax
import jax.numpy as jnp
from jax import lax
from jax.experimental import pallas as pl
from jax.experimental.pallas import tpu as pltpu
from jax.sharding import PartitionSpec as P

AXES = ("group", "gx", "gy")
X, Y, Z = 16, 32, 128
OX, OY = 3, 4
EX, EY = X + 2 * OX, Y + 2 * OY
BETA = 0.5
BIOT = 0.8
F32 = jnp.float32

X_ROWS = [(f, r) for f in range(13) for r in range(1, (3 if f < 3 else 2 if f < 10 else 1) + 1)]
NEAR = [(f, r) for f, r in X_ROWS if r == 1 and not 3 <= f < 9]
X_ROWS = NEAR + [row for row in X_ROWS if row not in NEAR]
Y_ROWS = [
    (f, r) for f in range(13) for r in range(1, (3 if 3 <= f < 6 else 2 if f < 10 else 1) + 1)
]
CORNER = [(1, 1), (1, 2), (2, 1), (2, 2), (1, 3), (3, 1)]
K_CORNERS = (
    [(f, i, j) for f in range(3) for i, j in CORNER[:4] + [(3, 1)]]
    + [(f, i, j) for f in range(3, 6) for i, j in CORNER[:4] + [(1, 3)]]
    + [(f, i, j) for f in range(6, 10) for i, j in CORNER[:3]]
)
R_ROWS = [(f, r) for f in range(3) for r in range(1, 4)]
R_CORNERS = [(f, i, j) for f in range(3) for i, j in CORNER]
AT_R = [len(R_ROWS) * X, len(R_ROWS) * X + len(R_CORNERS)]
AT_K = [AT_R[1] + len(R_CORNERS), AT_R[1] + len(R_CORNERS) + len(K_CORNERS)]
AT_Q = [AT_K[1] + len(K_CORNERS), AT_K[1] + len(K_CORNERS) + 3]
AT_U = AT_Q[1] + 3
Y_PACK = -(-(AT_U + 4) // 8) * 8
Q_SLOT = [R_ROWS.index((0, 3)), R_ROWS.index((1, 3))]


def struct(*shape):
    return jax.ShapeDtypeStruct(shape, F32)


def call(kernel, outs, scratch=(), left=(), count=0, cost=None, limit=20, scalars=()):
    extra = {}
    if left:
        extra["in_specs"] = [
            pl.BlockSpec(memory_space=pltpu.HBM if n in left else pltpu.VMEM) for n in range(count)
        ]
    if scalars:
        extra["out_specs"] = [
            pl.BlockSpec(memory_space=pltpu.SMEM if n in scalars else pltpu.VMEM)
            for n in range(len(outs))
        ]
    if cost:
        extra["cost_estimate"] = pl.CostEstimate(
            flops=cost, bytes_accessed=cost, transcendentals=0
        )
    return pl.pallas_call(
        kernel,
        out_shape=outs,
        scratch_shapes=list(scratch),
        compiler_params=pltpu.CompilerParams(vmem_limit_bytes=limit << 20),
        **extra,
    )


def up_y(v):
    return pltpu.roll(v, v.shape[0] - 1, 0)


def down_y(v):
    return pltpu.roll(v, 1, 0)


def up_z(v):
    return pltpu.roll(v, Z - 1, 1)


def down_z(v):
    return pltpu.roll(v, 1, 1)


def lanes(rows):
    return lax.broadcasted_iota(jnp.int32, (rows, Z), 1)


def rows_of(rows):
    return lax.broadcasted_iota(jnp.int32, (rows, Z), 0)


def to_tile(v):
    return pltpu.roll(v, EY - OY, 0)[:Y]


def harmonic(a, b):
    return 2.0 * a * b / jnp.maximum(a + b, 1e-30)


def one_hot(map_ref):
    brick = lax.broadcasted_iota(jnp.int32, (Z, 3 * Z), 0)
    return jnp.where(brick == map_ref[...], 1.0, 0.0).astype(jnp.bfloat16)


def dot_split(v, hot, contract):
    high = v.astype(jnp.bfloat16)
    low = (v - high.astype(F32)).astype(jnp.bfloat16)
    dims = (((1,), (contract,)), ((), ()))
    return lax.dot_general(high, hot, dims, preferred_element_type=F32) + lax.dot_general(
        low, hot, dims, preferred_element_type=F32
    )


def spread(v, hot, k):
    return dot_split(v, hot[:, k * Z : (k + 1) * Z], 0)


def gather_up(parts, hot):
    total = None
    for k, v in enumerate(parts):
        part = dot_split(v, hot[:, k * Z : (k + 1) * Z], 1)
        total = part if total is None else total + part
    ones = jnp.ones((8, 3 * Z), jnp.bfloat16)
    counts = lax.dot_general(ones, hot, (((1,), (1,)), ((), ())), preferred_element_type=F32)
    return total * (1.0 / counts[:1])


def gather_wide(ref, hot):
    rows = EX - 2
    parts = [ref[k, 1 : EX - 1].reshape(rows * EY, Z) for k in range(3)]
    return gather_up(parts, hot).reshape(rows, EY, Z)


def fetch(pairs, sem, start=0):
    copies = [pltpu.make_async_copy(a, b, sem.at[start + n]) for n, (a, b) in enumerate(pairs)]
    for copy in copies:
        copy.start()
    return copies


class Joined:
    def __init__(self, near, far):
        self.near, self.far = near, far

    def place(self, at):
        n, rest = (at[0], at[1:]) if isinstance(at, tuple) else (at, ())
        ref, n = (self.near, n) if n < len(NEAR) else (self.far, n - len(NEAR))
        return ref, (n, *rest)

    def __getitem__(self, at):
        ref, at = self.place(at)
        return ref[at]

    def __setitem__(self, at, value):
        ref, at = self.place(at)
        ref[at] = value


class Either:
    def __init__(self, odd, at_odd, at_even):
        self.odd, self.at_odd, self.at_even = odd, at_odd, at_even

    def __getitem__(self, at):
        return jnp.where(self.odd, self.at_odd[at], self.at_even[at])


def parity(axis):
    return lax.rem(lax.axis_index(axis), 2) == 1


def lower_upper(axis, first, second):
    odd = parity(axis)
    return Either(odd, first, second), Either(odd, second, first)


def surroundings(xa, xb, ya, yb):
    return lower_upper("gx", xa, xb) + lower_upper("gy", ya, yb)


def put(first, second, at, odd, tail, head):
    first[at] = jnp.where(odd, head, tail)
    second[at] = jnp.where(odd, tail, head)


def pack_x(source, rows, first, second):
    odd = parity("gx")
    for n, (f, r) in enumerate(rows):
        put(first, second, n, odd, source(f)[X - r], source(f)[r - 1])


def unpack_x(target, rows, low, up):
    for n, (f, r) in enumerate(rows):
        target(f)[OX - r, OY : OY + Y] = low[n]
        target(f)[OX + X - 1 + r, OY : OY + Y] = up[n]


def corner_at(side, i, j):
    row = OX - i if side[0] == 0 else OX + X - 1 + i
    column = OY - j if side[1] == 0 else OY + Y - 1 + j
    return row, slice(column, column + 1)


def x_faces(rows):
    return [struct(len(rows), Y, Z)] * 2


def loop(first, last, body, init=0, unroll=4):
    steps = (last - first) // unroll

    def step(n, carry):
        for m in range(unroll):
            carry = body(first + n * unroll + m, carry)
        return carry

    init = lax.fori_loop(0, steps, step, init)
    for i in range(first + steps * unroll, last):
        init = body(i, init)
    return init


def vertical_faces(conduct, flags, bottom, store):
    flow = lax.axis_index("group") == 0
    last = lanes(Y) == Z - 1
    eye = jnp.where(
        lax.broadcasted_iota(jnp.int32, (Y, Y), 0) == lax.broadcasted_iota(jnp.int32, (Y, Y), 1),
        1.0,
        0.0,
    ).astype(jnp.bfloat16)
    columns = lax.dot_general(
        eye,
        flags[...].astype(F32).astype(jnp.bfloat16),
        (((1,), (1,)), ((), ())),
        preferred_element_type=F32,
    )
    for x in range(X):
        bottom[x] = jnp.broadcast_to(columns[:, x : x + 1], (Y, Z))

    def row(x, carry):
        kz = [conduct[2, k, x] for k in range(3)]
        rolled = [up_z(v) for v in kz]
        ends = [rolled[1], rolled[2], bottom[x] * kz[2]]
        for k in range(3):
            end = jnp.where(flow, ends[k], kz[k])
            store(x, k, harmonic(kz[k], jnp.where(last, end, rolled[k])))
        return carry

    loop(0, X, row)


def pack_kernel(flags_in, state_in, conduct_in, capacity_in, xa, xb, fb, ya, yb, *scratch):
    flags, state, conduct, capacity, bottom, tz, sem = scratch
    early = [(flags_in, flags)] + [(conduct_in.at[2, k], conduct.at[2, k]) for k in range(3)]
    late = [(conduct_in.at[d, k], conduct.at[d, k]) for d in range(2) for k in range(3)]
    late += [(state_in.at[k], state.at[k]) for k in range(3)] + [(capacity_in, capacity)]
    early = fetch(early, sem)
    late = fetch(late, sem, len(early))
    for copy in early:
        copy.wait()
    def store(x, k, value):
        tz[k, x] = value

    vertical_faces(conduct, flags, bottom, store)
    for copy in late:
        copy.wait()

    def source(f):
        if f < 6:
            return conduct.at[f // 3, f % 3]
        if f < 9:
            return tz.at[f - 6]
        return capacity if f == 9 else state.at[f - 10]

    pack_x(source, X_ROWS, xa, Joined(xb, fb))
    odd = parity("gy")
    for n, (f, r) in enumerate(Y_ROWS):
        put(ya, yb, n, odd, source(f)[:, Y - r, :], source(f)[:, r - 1, :])


class Faces:
    def __init__(self, x, y, z, own):
        self.x, self.y, self.z, self.own = x, y, z, own


def faces_in(ref, shift=0):
    return Faces(*[lambda c, i, d=d: ref[3 * d + c, i - shift] for d in range(4)])


def lateral(faces, v_ref, c, i, v, fx_before):
    fx = faces.x(c, i) * (v - v_ref[c, i + 1])
    fy = faces.y(c, i) * (v - up_y(v))
    return (fx - fx_before) + (fy - down_y(fy)), fx


def x_flux(faces, v_ref, i):
    return tuple(faces.x(c, i) * (v_ref[c, i] - v_ref[c, i + 1]) for c in range(3))


def flow_below(vs, last):
    rolled = [up_z(v) for v in vs]
    ends = [rolled[1], rolled[2], 0.0]
    return [jnp.where(last, ends[k], rolled[k]) for k in range(3)]


def flow_row(faces, v_ref, i, fx_before):
    last, first = lanes(EY) == Z - 1, lanes(EY) == 0
    vs = [v_ref[k, i] for k in range(3)]
    below = flow_below(vs, last)
    fz = [faces.z(k, i) * (vs[k] - below[k]) for k in range(3)]
    moved = [down_z(v) for v in fz]
    ends = [0.0, moved[0], moved[1]]
    out, fx_now = [], []
    for k in range(3):
        side, fx = lateral(faces, v_ref, k, i, vs[k], fx_before[k])
        above = jnp.where(first, ends[k], moved[k])
        out.append(faces.own(k, i) * vs[k] + side + (fz[k] - above))
        fx_now.append(fx)
    return out, tuple(fx_now)


def strain_row(v_ref, i):
    v0, v1, v2 = v_ref[0, i], v_ref[1, i], v_ref[2, i]
    low = jnp.where(lanes(EY) == Z - 1, 0.0, up_z(v2))
    return (v_ref[0, i + 1] - v0) + (up_y(v1) - v1) + (low - v2)


def solid_row(faces, v_ref, i, s_before, fx_before):
    last, first = lanes(EY) == Z - 1, lanes(EY) == 0
    e = strain_row(v_ref, i)
    s = faces.own(0, i) * e
    grad = [s_before - s, down_y(s) - s, jnp.where(first, 0.0, down_z(s)) - s]
    out, fx_now = [], []
    for c in range(3):
        v = v_ref[c, i]
        side, fx = lateral(faces, v_ref, c, i, v, fx_before[c])
        fz = faces.z(c, i) * (v - jnp.where(last, 0.0, up_z(v)))
        above = jnp.where(first, 0.0, down_z(fz))
        out.append((side + (fz - above)) + grad[c])
        fx_now.append(fx)
    return out, s, tuple(fx_now)


BESIDE = [(1, -1, Y), (1, X - 1, Y), (1, -1, 0), (1, X - 1, 0)]
BESIDE += [(0, X, -1), (0, 0, -1), (0, X, Y - 1), (0, 0, Y - 1)]


def place_tile(conduct, capacity, keep, caps):
    at = slice(OY, OY + Y)

    def row(x, carry):
        for f in range(6):
            keep[f, OX + x, at] = conduct[f // 3, f % 3, x]
        caps[OX + x, at] = capacity[x]
        return carry

    loop(0, X, row)


def interior_kernel(state, conduct, capacity, flags, layer_map, faces, tz, unit, keep, caps, bottom):
    flow = lax.axis_index("group") == 0
    place_tile(conduct, capacity, keep, caps)

    def store(x, k, value):
        tz[k, x] = value
        faces[6 + k, OX + x, OY : OY + Y] = value

    vertical_faces(conduct, flags, bottom, store)
    loop(OX, OX + X, lambda i, carry: lateral_faces(keep, faces, i))

    @pl.when(flow)
    def _():
        hot = one_hot(layer_map)
        bricks = caps[OX : OX + X].reshape(X * EY, Z)
        for k in range(3):
            faces[9 + k, OX : OX + X] = (spread(bricks, hot, k) + BETA).reshape(X, EY, Z)
        parts = [state[k].reshape(X * Y, Z) for k in range(3)]
        unit[...] = gather_up(parts, hot).reshape(X, Y, Z)


def lateral_faces(keep, faces, i):
    for c in range(3):
        faces[c, i] = harmonic(keep[c, i], keep[c, i + 1])
        here = keep[3 + c, i]
        faces[3 + c, i] = harmonic(here, up_y(here))
    return 0


def strain_kernel(state, unit, xa, xb, ya, yb, strain):
    flow = lax.axis_index("group") == 0
    _, xu, _, yu = surroundings(xa, xb, ya, yb)

    @pl.when(flow)
    def _():
        strain[...] = unit[...]

    @pl.when(jnp.logical_not(flow))
    def _():
        last = lanes(Y) == Z - 1
        edge = rows_of(Y) == Y - 1
        n_x, n_y = X_ROWS.index((10, 1)), Y_ROWS.index((11, 1))
        for x in range(X):
            v0, v1, v2 = (state[c, x] for c in range(3))
            east = state[0, x + 1] if x + 1 < X else xu[n_x]
            north = jnp.where(edge, yu[n_y, x : x + 1], up_y(v1))
            low = jnp.where(last, 0.0, up_z(v2))
            strain[x] = (east - v0) + (north - v1) + (low - v2)


def first_kernel(state, conduct, capacity, supply, faces_ref, xa, xb, ya, yb, *refs):
    xl, xu, yl, yu = surroundings(xa, xb, ya, yb)
    base, beside, sides, own, field = refs
    flow = lax.axis_index("group") == 0

    def place(x, carry):
        for c in range(3):
            field[c, OX + x, OY : OY + Y] = state[c, x]
        for f in range(6):
            sides[f, OX + x] = faces_ref[f, OX + x]
        return carry

    loop(0, X, place)
    for c in range(3):
        n = X_ROWS.index((10 + c, 1))
        field[c, OX - 1, OY : OY + Y] = xl[n]
        field[c, OX + X, OY : OY + Y] = xu[n]
        n = Y_ROWS.index((10 + c, 1))
        field[c, OX : OX + X, OY - 1, :] = yl[n]
        field[c, OX : OX + X, OY + Y, :] = yu[n]
        n = X_ROWS.index((c, 1))
        at = slice(OY, OY + Y)
        sides[c, OX - 1, at] = harmonic(xl[n], conduct[0, c, 0])
        sides[c, OX + X - 1, at] = harmonic(conduct[0, c, X - 1], xu[n])
        n = Y_ROWS.index((3 + c, 1))
        sides[3 + c, OX : OX + X, OY - 1, :] = harmonic(yl[n], conduct[1, c, :, 0, :])
        sides[3 + c, OX : OX + X, OY + Y - 1, :] = harmonic(conduct[1, c, :, Y - 1, :], yu[n])
    field[1, OX - 1, OY + Y : OY + Y + 1] = jnp.zeros((1, Z), F32)
    field[0, OX + X, OY - 1 : OY] = jnp.zeros((1, Z), F32)
    for n, (c, x, y) in enumerate(BESIDE):
        beside[n : n + 1] = field[c, OX + x, OY + y : OY + y + 1]
    inner = faces_in(faces_ref)
    outer = faces_in(sides)

    @pl.when(flow)
    def _():
        faces = Faces(outer.x, outer.y, inner.z, inner.own)

        def row(i, fx_before):
            image, fx = flow_row(faces, field, i, fx_before)
            for k in range(3):
                base[k, i - OX] = (
                    supply[k, i - OX] + BETA * state[k, i - OX] - to_tile(image[k])
                )
            return fx

        loop(OX, OX + X, row, x_flux(faces, field, OX - 1))

    @pl.when(jnp.logical_not(flow))
    def _():
        def place(x, carry):
            own[OX + x, OY : OY + Y] = capacity[x]
            return carry

        loop(0, X, place)
        own[OX - 1, OY : OY + Y] = xl[X_ROWS.index((9, 1))]
        own[OX : OX + X, OY - 1, :] = yl[Y_ROWS.index((9, 1))]
        faces = Faces(outer.x, outer.y, inner.z, lambda c, i: own[i])

        def row(i, carry):
            image, s, fx = solid_row(faces, field, i, carry[0], carry[1])
            for c in range(3):
                base[c, i - OX] = supply[c, i - OX] - to_tile(image[c])
            return s, fx

        before = faces.own(0, OX - 1) * strain_row(field, OX - 1)
        loop(OX, OX + X, row, (before, x_flux(faces, field, OX - 1)))


def halo_kernel(conduct, capacity, tz, layer_map, xa, xb, ya, yb, fb, *refs):
    faces, rim, keep, caps = refs
    xl, xu, yl, yu = surroundings(xa, Joined(xb, fb), ya, yb)
    flow = lax.axis_index("group") == 0

    def target(f):
        if f < 6:
            return keep.at[f]
        return faces.at[f] if f < 9 else caps

    place_tile(conduct, capacity, keep, caps)

    def place(x, carry):
        for k in range(3):
            faces[6 + k, OX + x, OY : OY + Y] = tz[k, x]
        return carry

    loop(0, X, place)
    for n, (f, r) in enumerate(X_ROWS):
        if f < 10:
            target(f)[OX - r, OY : OY + Y] = xl[n]
            target(f)[OX + X - 1 + r, OY : OY + Y] = xu[n]
    for n, (f, r) in enumerate(Y_ROWS):
        if f < 10:
            target(f)[OX : OX + X, OY - r, :] = yl[n]
            target(f)[OX : OX + X, OY + Y - 1 + r, :] = yu[n]
    loop(0, EX - 1, lambda i, carry: lateral_faces(keep, faces, i))
    for n, i in enumerate(K_RIM):
        for f in range(6):
            rim[f, n] = keep[f, i]

    @pl.when(flow)
    def _():
        hot = one_hot(layer_map)
        bricks = caps[1 : EX - 1].reshape((EX - 2) * EY, Z)
        for k in range(3):
            faces[9 + k, 1 : EX - 1] = (spread(bricks, hot, k) + BETA).reshape(EX - 2, EY, Z)

    @pl.when(jnp.logical_not(flow))
    def _():
        faces[9] = caps[...]


BESIDE = [(1, -1, Y), (1, X - 1, Y), (1, -1, 0), (1, X - 1, 0)]
BESIDE += [(0, X, -1), (0, 0, -1), (0, X, Y - 1), (0, 0, Y - 1)]
RIM = [0, 1, 2, EX - 4, EX - 3, EX - 2]
K_RIM = [0, 1, 2, 3, EX - 4, EX - 3, EX - 2, EX - 1]


def residual_kernel(base, strain, unit, layer_map, residual, xa, xb):
    flow = lax.axis_index("group") == 0

    @pl.when(flow)
    def _():
        hot = one_hot(layer_map)
        e = strain[...].reshape(X * Y, Z)
        for k in range(3):
            residual[k] = base[k] - BIOT * spread(e, hot, k).reshape(X, Y, Z)

    @pl.when(jnp.logical_not(flow))
    def _():
        residual[...] = base[...]

    pack_x(lambda f: residual.at[f], R_ROWS, xa, xb)

    @pl.when(jnp.logical_not(flow))
    def _():
        odd = parity("gx")
        for depth, n in enumerate(Q_SLOT):
            put(xa, xb, n, odd, unit[X - 1 - depth], unit[depth])


def relay_kernel(residual, unit, xa, xb, ka, kb, fb, ya, yb):
    flow = lax.axis_index("group") == 0
    odd = parity("gy")
    r_halos, k_halos = lower_upper("gx", xa, xb), lower_upper("gx", ka, Joined(kb, fb))

    def give(at, count, ref, index, j):
        put(ya, yb, slice(at, at + count), odd, ref[index(Y - j)], ref[index(j - 1)])

    for n, (f, r) in enumerate(R_ROWS):
        give(n * X, X, residual, lambda y: (f, slice(None), y), r)
    for side in range(2):
        r_halo, k_halo = r_halos[side], k_halos[side]
        for n, (f, i, j) in enumerate(R_CORNERS):
            row = R_ROWS.index((f, i))
            give(AT_R[side] + n, 1, r_halo, lambda y: (row, slice(y, y + 1)), j)
        for n, (f, i, j) in enumerate(K_CORNERS):
            row = X_ROWS.index((f, i))
            give(AT_K[side] + n, 1, k_halo, lambda y: (row, slice(y, y + 1)), j)
        for n, (i, j) in enumerate(CORNER[:3]):
            row = Q_SLOT[i - 1]
            give(AT_Q[side] + n, 1, r_halo, lambda y: (row, slice(y, y + 1)), j)
        for c in range(2):
            row = X_ROWS.index((10 + c, 1))
            give(AT_U + 2 * side + c, 1, k_halo, lambda y: (row, slice(y, y + 1)), 1)

    @pl.when(jnp.logical_not(flow))
    def _():
        for depth, n in enumerate(Q_SLOT):
            give(n * X, X, unit, lambda y: (slice(None), y), depth + 1)


def fold(v):
    return jnp.sum(v.reshape(v.shape[0] // 8, 8, Z), axis=0)


def spread_sums(found):
    lane = lanes(8)
    row = jnp.zeros((8, Z), F32)
    first = rows_of(8) == 0
    for n, total in found.items():
        row = jnp.where(first & (lane == n), jnp.sum(total), row)
    return row


def tile_rows():
    at = rows_of(EY)
    return (at >= OY) & (at < OY + Y)


def fill(residual, target, halos):
    xl, xu, yl, yu = halos

    def place(x, carry):
        for k in range(3):
            target[k, OX + x, OY : OY + Y] = residual[k, x]
        return carry

    loop(0, X, place)
    unpack_x(lambda f: target.at[f], R_ROWS, xl, xu)
    for n, (f, r) in enumerate(R_ROWS):
        target[f, OX : OX + X, OY - r, :] = yl[n * X : (n + 1) * X]
        target[f, OX : OX + X, OY + Y - 1 + r, :] = yu[n * X : (n + 1) * X]
    for v, pack in enumerate((yl, yu)):
        for h in range(2):
            for n, (f, i, j) in enumerate(R_CORNERS):
                row, column = corner_at((h, v), i, j)
                target[f, row, column] = pack[AT_R[h] + n : AT_R[h] + n + 1]


def complete(faces, rim, k_rim_in, k_rim, halos, hot):
    for n, i in enumerate(RIM):
        for f in range(6, 12):
            rim[f, n] = faces[f, i]
    k_rim[...] = k_rim_in[...]
    order = []
    for v, pack in enumerate(halos[2:]):
        for h in range(2):
            for n, (f, i, j) in enumerate(K_CORNERS):
                row, column = corner_at((h, v), i, j)
                value = pack[AT_K[h] + n : AT_K[h] + n + 1]
                if f < 6:
                    k_rim[f, K_RIM.index(row), column] = value
                elif f < 9:
                    rim[f, RIM.index(row), column] = value
                else:
                    order.append((RIM.index(row), column, value))
    for n, i in enumerate(RIM):
        m = K_RIM.index(i)
        for c in range(3):
            rim[c, n] = harmonic(k_rim[c, m], k_rim[c, m + 1])
            here = k_rim[3 + c, m]
            rim[3 + c, n] = harmonic(here, up_y(here))
    if hot is None:
        for row, column, value in order:
            rim[9, row, column] = value
    else:
        values = [value for _, _, value in order]
        values += [jnp.zeros((1, Z), F32)] * (16 - len(values))
        caps = jnp.concatenate(values, axis=0)
        for k in range(3):
            storage = spread(caps, hot, k) + BETA
            for n, (row, column, _) in enumerate(order):
                rim[9 + k, row, column] = storage[n : n + 1]


def row_parts(faces, rim):
    return faces_in(rim), faces_in(faces), faces_in(rim, EX - 7)


def run_rows(parts, first, last, body, init, unroll=3):
    low, middle, high = parts
    for i in range(first, OX):
        init = body(low, i, init)
    init = loop(max(first, OX), EX - 4, lambda i, carry: body(middle, i, carry), init, unroll)
    for i in range(EX - 4, last):
        init = body(high, i, init)
    return init


PAIRS = [(0, 0), (0, 1), (0, 2), (1, 1), (1, 2), (2, 2)]
FIRST_SUM = 9


def grid_mask(before, after):
    gx, gy = lax.axis_index("gx"), lax.axis_index("gy")
    gx_last, gy_last = lax.axis_size("gx") - 1, lax.axis_size("gy") - 1
    at = rows_of(EY)
    in_y = (at >= OY - jnp.where(gy > 0, before, 0)) & (
        at < OY + Y + jnp.where(gy < gy_last, after, 0)
    )

    def in_grid(i):
        in_x = ((i >= OX) | (gx > 0)) & ((i < OX + X) | (gx < gx_last))
        return in_y & in_x

    return in_grid


def load_rows(q_refs, targets, added):
    in_grid = grid_mask(1, 2)

    def row(i, carry):
        for q_ref, target in zip(q_refs, targets):
            load_row(q_ref, target, i, in_grid(i))
        return carry

    def load_row(q_ref, target, i, ok):
        first = lanes(EY) == 0
        q = q_ref[i - 1]
        push = [
            BIOT * (q_ref[i - 2] - q),
            BIOT * (down_y(q) - q),
            BIOT * (jnp.where(first, 0.0, down_z(q)) - q),
        ]
        for c in range(3):
            v = push[c] + target[c, i] if added else push[c]
            target[c, i] = jnp.where(ok, v, 0.0)

    loop(OX - 1, OX + X + 2, row)


def solid_image(parts, f_refs, p_refs, unroll):
    in_grid = grid_mask(0, 1)

    def row(faces, i, carry):
        ok, after = in_grid(i), []
        for f_ref, p_ref, (s, fx) in zip(f_refs, p_refs, carry):
            out, s, fx = solid_row(faces, f_ref, i, s, fx)
            for c in range(3):
                p_ref[c, i] = jnp.where(ok, out[c], 0.0)
            after.append((s, fx))
        return tuple(after)

    view = parts[0]
    start = [
        (view.own(0, OX - 1) * strain_row(f, OX - 1), x_flux(view, f, OX - 1)) for f in f_refs
    ]
    run_rows(parts, OX, OX + X + 1, row, tuple(start), unroll)


def gram_sums(faces, fields, products, pairs, acc):
    acc[...] = jnp.zeros(acc.shape, F32)
    vectors = range(len(fields))

    def row(i, carry):
        inside, last = tile_rows(), lanes(EY) == Z - 1

        def only(v):
            return jnp.where(inside, v, 0.0)

        def add(n, v):
            acc[n] = acc[n] + fold(v)

        strains = [strain_row(p, i) for p in products]
        modulus = only(faces[9, i])
        later = sorted({b for _, b in pairs})
        pushes = {b: modulus * strains[b] for b in later}
        for n, (a, b) in enumerate(pairs):
            add(4 * n + 3, pushes[b] * strains[a])
        for c in range(3):
            ws = [p[c, i] for p in products]
            dx = [ws[a] - products[a][c, i + 1] for a in vectors]
            dy = [w - up_y(w) for w in ws]
            dz = [w - jnp.where(last, 0.0, up_z(w)) for w in ws]
            sx, sy, sz = (only(faces[3 * d + c, i]) for d in range(3))
            fx = {b: sx * dx[b] for b in later}
            fy = {b: sy * dy[b] for b in later}
            fz = {b: sz * dz[b] for b in later}
            rs = [f[c, i] for f in fields]
            r_in = {b: only(rs[b]) for b in later}
            w_in = {b: only(ws[b]) for b in later}
            for n, (a, b) in enumerate(pairs):
                add(4 * n + 3, fx[b] * dx[a] + fy[b] * dy[a] + fz[b] * dz[a])
                add(4 * n, r_in[b] * rs[a])
                add(4 * n + 1, r_in[b] * ws[a])
                add(4 * n + 2, w_in[b] * ws[a])
        return carry

    loop(OX, OX + X, row, 0, 2)
    found = {}
    for n, pair in enumerate(pairs):
        for m in range(4):
            found[FIRST_SUM + 6 * m + PAIRS.index(pair)] = acc[4 * n + m]
    return found


def unit_surroundings(unit, halos, q):
    xl, xu, yl, yu = halos

    def place(x, carry):
        q[OX - 1 + x, OY : OY + Y] = unit[x]
        return carry

    loop(0, X, place)
    for depth, n in enumerate(Q_SLOT):
        q[OX - 2 - depth, OY : OY + Y] = xl[n]
        q[OX + X - 1 + depth, OY : OY + Y] = xu[n]
        rows = slice(n * X, (n + 1) * X)
        q[OX - 1 : OX - 1 + X, OY - 1 - depth, :] = yl[rows]
        q[OX - 1 : OX - 1 + X, OY + Y + depth, :] = yu[rows]
    for v, pack in enumerate((yl, yu)):
        for h in range(2):
            for n, (i, j) in enumerate(CORNER[:3]):
                row, column = corner_at((h, v), i, j)
                q[row - 1, column] = pack[AT_Q[h] + n : AT_Q[h] + n + 1]


def late_terms(faces, rim, field, beside, halos):
    yl, yu = halos[2:]

    def modulus(x, y):
        i, column = OX + x, slice(OY + y, OY + y + 1)
        return rim[9, RIM.index(i), column] if i in RIM else faces[9, i, column]

    u1 = [yu[AT_U + 1 : AT_U + 2]] + [beside[n : n + 1] for n in (1, 2, 3)]
    u0 = [yl[AT_U + 2 : AT_U + 3]] + [beside[n : n + 1] for n in (5, 6, 7)]
    for u, (x, y) in zip(u1, ((0, Y - 1), (X, Y - 1), (0, -1), (X, -1))):
        row, column = OX + x, slice(OY + y, OY + y + 1)
        field[0, row, column] = field[0, row, column] - modulus(x - 1, y) * u
    for u, (x, y) in zip(u0, ((X - 1, 0), (-1, 0), (X - 1, Y), (-1, Y))):
        row, column = OX + x, slice(OY + y, OY + y + 1)
        field[1, row, column] = field[1, row, column] - modulus(x, y - 1) * u


def image_kernel(residual, unit_old, beside, layer_map, *refs):
    halos, (faces, k_rim_in, rim, field, product, unit, k_rim, q) = refs[:4], refs[4:]
    halos = surroundings(*halos)
    flow = lax.axis_index("group") == 0
    fill(residual, field, halos)

    @pl.when(flow)
    def _():
        hot = one_hot(layer_map)
        complete(faces, rim, k_rim_in, k_rim, halos, hot)
        parts = row_parts(faces, rim)

        def row(view, i, fx_before):
            out, fx = flow_row(view, field, i, fx_before)
            for k in range(3):
                product[k, i] = out[k]
            return fx

        run_rows(parts, 1, EX - 1, row, x_flux(parts[0], field, 0))
        unit[0] = gather_wide(field, hot)
        unit[1] = gather_wide(product, hot)

    @pl.when(jnp.logical_not(flow))
    def _():
        complete(faces, rim, k_rim_in, k_rim, halos, None)
        late_terms(faces, rim, field, beside, halos)
        unit_surroundings(unit_old, halos, q)
        load_rows([q], [field], True)
        solid_image(row_parts(faces, rim), [field], [product], 3)


def early_kernel(field, product, faces, state, sums, acc):
    flow = lax.axis_index("group") == 0

    @pl.when(flow)
    def _():
        def dots(i, acc):
            acc = list(acc)
            inside, last = tile_rows(), lanes(EY) == Z - 1

            def add(n, v):
                acc[n] = acc[n] + fold(jnp.where(inside, v, 0.0))

            ws = [product[k, i] for k in range(3)]
            below = flow_below(ws, last)
            g = m1 = m2 = m3 = cr = cw = 0.0
            for k in range(3):
                r, w = field[k, i], ws[k]
                dx, dy, dz = w - product[k, i + 1], w - up_y(w), w - below[k]
                cf = faces[9 + k, i]
                g = g + r * r
                m1 = m1 + r * w
                m2 = m2 + w * w
                cr = cr + cf * r
                cw = cw + cf * w
                m3 = m3 + (
                    faces[k, i] * dx * dx
                    + faces[3 + k, i] * dy * dy
                    + faces[6 + k, i] * dz * dz
                    + cf * w * w
                )
            for n, v in enumerate((g, m1, m2, m3, cr, cw)):
                add(n, v)
            weight = jnp.where(last, faces[8, i], 0.0)
            add(6, weight * field[2, i])
            add(7, weight * ws[2])
            acc[8] = acc[8] + fold(to_tile(weight) * state[2, i - OX])
            return tuple(acc)

        zero = jnp.zeros((8, Z), F32)
        found = dict(enumerate(loop(OX, OX + X, dots, (zero,) * FIRST_SUM, 2)))
        sums[...] = spread_sums(found)

    @pl.when(jnp.logical_not(flow))
    def _():
        sums[...] = spread_sums(gram_sums(faces, [field], [product], PAIRS[:1], acc))


def sums_kernel(field, product, faces, rim, unit, sums_in, sums, field12, product12, acc):
    flow = lax.axis_index("group") == 0
    everyone = sums.shape[0]

    @pl.when(flow)
    def _():
        sums[...] = jnp.broadcast_to(sums_in[:1], (everyone, Z))

    @pl.when(jnp.logical_not(flow))
    def _():
        fields = [field] + [field12.at[a] for a in range(2)]
        products = [product] + [product12.at[a] for a in range(2)]
        load_rows([unit.at[a] for a in range(2)], fields[1:], False)
        solid_image(row_parts(faces, rim), fields[1:], products[1:], 2)
        found = gram_sums(faces, fields, products, PAIRS[1:], acc)
        own = sums_in[:1] + spread_sums(found)[:1]
        sums[...] = jnp.broadcast_to(own, (everyone, Z))


def two_sum(a, b):
    s = a + b
    t = s - a
    return s, (a - (s - t)) + (b - t)


def quick(a, b):
    s = a + b
    return s, b - (s - a)


def halves(a):
    t = 4097.0 * a
    high = t - (t - a)
    return high, a - high


def two_product(a, b):
    p = a * b
    ah, al = halves(a)
    bh, bl = halves(b)
    return p, ((ah * bh - p) + ah * bl + al * bh) + al * bl


def pair_add(a, b):
    s, e = two_sum(a[0], b[0])
    return quick(s, e + (a[1] + b[1]))


def pair_less(a, b):
    return pair_add(a, (-b[0], -b[1]))


def pair_times(a, b):
    p, e = two_product(a[0], b[0])
    return quick(p, e + (a[0] * b[1] + a[1] * b[0]))


def pair_over(a, b):
    q = a[0] / b[0]
    rest = pair_less(a, pair_times(b, (q, jnp.zeros_like(q))))
    return quick(q, rest[0] / b[0])


def krylov(g, m1, m2, m3):
    a0 = pair_over(g, m1)
    h = pair_times(a0, pair_over(m2, m1))
    one = (jnp.ones_like(a0[0]), jnp.zeros_like(a0[0]))
    rho = pair_less(h, one)[0]
    third = pair_times(pair_times(a0, a0), pair_over(m3, m1))
    sigma = pair_less(third, pair_times(h, h))[0]
    more = (rho > 1e-9) & (sigma > 1e-9)
    a1 = jnp.where(more, a0[0] * rho / jnp.where(more, sigma, 1.0), 0.0)
    return a0[0] + a1 * h[0], -a0[0] * a1


def final_kernel(sums, state, field, product, field12, product12, out, balance, *, cells):
    flow = lax.axis_index("group") == 0
    total = (sums[...], jnp.zeros(sums.shape, F32))
    while total[0].shape[0] > 8:
        half = total[0].shape[0] // 2
        total = pair_add([v[:half] for v in total], [v[half:] for v in total])
    for step in (4, 2, 1):
        total = pair_add(total, [pltpu.roll(v, step, 0) for v in total])

    def number(n):
        return tuple(jnp.broadcast_to(v[:1, n : n + 1], (8, Z)) for v in total)

    c0, c1 = krylov(number(0), number(1), number(2), number(3))
    columns = cells // (3 * Z)
    outflow = (number(8)[0] + c0 * number(6)[0] + c1 * number(7)[0]) / columns
    stored = (c0 * number(4)[0] + c1 * number(5)[0]) / cells
    balance[0] = outflow[0, 0]
    balance[1] = stored[0, 0]

    def tall(v):
        return jnp.concatenate([v] * (EY // 8), axis=0)

    @pl.when(flow)
    def _():
        s0, s1 = tall(c0), tall(c1)

        def row(x, carry):
            for k in range(3):
                step = s0 * field[k, OX + x] + s1 * product[k, OX + x]
                out[k, x] = state[k, x] + to_tile(step)
            return carry

        loop(0, X, row)

    @pl.when(jnp.logical_not(flow))
    def _():
        zero = jnp.zeros((8, Z), F32)
        weights = [
            (jnp.ones((8, Z), F32), zero),
            (2.0 * c0, zero),
            (2.0 * c1, zero),
            two_product(c0, c0),
            two_product(2.0 * c0, c1),
            two_product(c1, c1),
        ]
        moments = []
        for m in range(4):
            start = FIRST_SUM + 6 * m
            total = number(start)
            for n in range(1, 6):
                total = pair_add(total, pair_times(weights[n], number(start + n)))
            moments.append(total)
        d0, d1 = krylov(*moments)
        scale_r = [tall(d0), tall(d0 * c0), tall(d0 * c1)]
        scale_w = [tall(d1), tall(d1 * c0), tall(d1 * c1)]

        def row(x, carry):
            for c in range(3):
                step = scale_r[0] * field[c, OX + x] + scale_w[0] * product[c, OX + x]
                for a in range(2):
                    step = step + scale_r[a + 1] * field12[a, c, OX + x]
                    step = step + scale_w[a + 1] * product12[a, c, OX + x]
                out[c, x] = state[c, x] + to_tile(step)
            return carry

        loop(0, X, row)


def swap(value, start, axis):
    groups, rows, columns = (lax.axis_size(a) for a in AXES)
    pairs = []
    for g in range(groups):
        for i in range(rows):
            for j in range(columns):
                place = i if axis == "gx" else j
                step = 1 if place % 2 == start else -1
                if 0 <= place + step < lax.axis_size(axis):
                    here = (g * rows + i) * columns + j
                    pairs.append((here, here + step * (columns if axis == "gx" else 1)))
    return lax.ppermute(value, AXES, pairs)


def swaps(first, second, axis):
    return [swap(first, 0, axis), swap(second, 1, axis)]


def core_swap(value):
    count = lax.axis_size("gx") * lax.axis_size("gy")
    pairs = [(n, (n + count) % (2 * count)) for n in range(2 * count)]
    return lax.ppermute(value, AXES, pairs)


def body(state, conduct, capacity, supply, flags, layer_map):
    state, conduct, capacity, supply = state[0], conduct[0], capacity[0], supply[0]
    layer_map = layer_map.reshape(1, 3 * Z)
    cells = X * Y * 3 * Z * lax.axis_size("gx") * lax.axis_size("gy")
    devices = lax.axis_size("group") * lax.axis_size("gx") * lax.axis_size("gy")
    tile = struct(3, X, Y, Z)
    brick = struct(X, Y, Z)
    wide = (EX, EY, Z)
    full = struct(3, *wide)

    y_face = struct(len(Y_ROWS), X, Z)
    x_parts = [struct(n, Y, Z) for n in (len(X_ROWS), len(NEAR), len(X_ROWS) - len(NEAR))]
    xa, xb, fb, ya, yb = call(
        pack_kernel,
        x_parts + [y_face] * 2,
        [
            pltpu.VMEM((X, Y), jnp.int32),
            pltpu.VMEM((3, X, Y, Z), F32),
            pltpu.VMEM((3, 3, X, Y, Z), F32),
            pltpu.VMEM((X, Y, Z), F32),
            pltpu.VMEM((X, Y, Z), F32),
            pltpu.VMEM((3, X, Y, Z), F32),
            pltpu.SemaphoreType.DMA((14,)),
        ],
        left=(0, 1, 2, 3),
        limit=58,
        count=4,
    )(flags, state, conduct, capacity)
    k_halos = lax.optimization_barrier(swaps(xa, xb, "gx") + swaps(ya, yb, "gy"))
    far = swap(fb, 1, "gx")
    wide_faces = struct(12, *wide)
    tables = [pltpu.VMEM((6, *wide), F32), pltpu.VMEM(wide, F32)]
    inner, tz, unit0 = call(
        interior_kernel,
        [wide_faces, tile, brick],
        tables + [pltpu.VMEM((X, Y, Z), F32)],
        cost=30_000_000,
    )(state, conduct, capacity, flags, layer_map)
    inner, far = lax.optimization_barrier((inner, far))
    cross = core_swap(call(strain_kernel, brick)(state, unit0, *k_halos))
    base, beside = call(
        first_kernel,
        [tile, struct(8, Z)],
        tables + [pltpu.VMEM((3, *wide), F32)],
        cost=20_000_000,
    )(state, conduct, capacity, supply, inner, *k_halos)
    faces, k_rim = call(
        halo_kernel, [wide_faces, struct(6, len(K_RIM), EY, Z)], tables, cost=30_000_000
    )(conduct, capacity, tz, layer_map, *k_halos, far)
    residual, xa, xb = call(residual_kernel, [tile] + x_faces(R_ROWS))(
        base, cross, cross, layer_map
    )
    halos = swaps(xa, xb, "gx")
    ya, yb = call(relay_kernel, [struct(Y_PACK, Z)] * 2)(
        residual, cross, *halos, k_halos[0], k_halos[1], far
    )
    halos = halos + swaps(ya, yb, "gy")
    rim, field, product, unit12 = call(
        image_kernel,
        [struct(12, len(RIM), EY, Z), full, full, struct(2, EX - 2, EY, Z)],
        [pltpu.VMEM((6, len(K_RIM), EY, Z), F32), pltpu.VMEM((EX - 2, EY, Z), F32)],
    )(residual, cross, beside, layer_map, *halos, faces, k_rim)
    unit12 = core_swap(unit12)
    sums = call(early_kernel, struct(8, Z), [pltpu.VMEM((4, 8, Z), F32)], cost=20_000_000)(
        field, product, faces, state
    )
    sums, field12, product12 = call(
        sums_kernel,
        [struct(devices, Z), struct(2, 3, *wide), struct(2, 3, *wide)],
        [pltpu.VMEM((20, 8, Z), F32)],
    )(field, product, faces, rim, unit12, sums)
    sums = lax.all_to_all(sums, AXES, 0, 0, tiled=True)

    def finish(*refs):
        final_kernel(*refs, cells=cells)

    new_state, balance = call(finish, [tile, struct(2)], scalars=(1,))(
        sums, state, field, product, field12, product12
    )
    return new_state[None], balance


def solution(mesh):
    placed = (
        P("group", None, "gx", "gy", None),
        P("group", None, None, "gx", "gy", None),
        P("group", "gx", "gy", None),
        P("group", None, "gx", "gy", None),
        P("gx", "gy"),
        P(),
    )
    return jax.shard_map(
        body,
        mesh=mesh,
        in_specs=placed,
        out_specs=(P("group", None, "gx", "gy", None), P()),
        check_vma=False,
    )
```

```python
import jax
import jax.numpy as jnp
from jax import lax
from jax.experimental import pallas as pl
from jax.experimental.pallas import tpu as pltpu
from jax.sharding import PartitionSpec as P

AXES = ("group", "gx", "gy")
X, Y, Z = 16, 32, 128
OX, OY = 3, 4
EX, EY = X + 2 * OX, Y + 2 * OY
BETA = 0.5
BIOT = 0.8
F32 = jnp.float32

X_ROWS = [(f, r) for f in range(13) for r in range(1, (3 if f < 3 else 2 if f < 10 else 1) + 1)]
NEAR = [(f, r) for f, r in X_ROWS if r == 1 and not 3 <= f < 9]
X_ROWS = NEAR + [row for row in X_ROWS if row not in NEAR]
Y_ROWS = [
    (f, r) for f in range(13) for r in range(1, (3 if 3 <= f < 6 else 2 if f < 10 else 1) + 1)
]
CORNER = [(1, 1), (1, 2), (2, 1), (2, 2), (1, 3), (3, 1)]
K_CORNERS = (
    [(f, i, j) for f in range(3) for i, j in CORNER[:4] + [(3, 1)]]
    + [(f, i, j) for f in range(3, 6) for i, j in CORNER[:4] + [(1, 3)]]
    + [(f, i, j) for f in range(6, 10) for i, j in CORNER[:3]]
)
R_ROWS = [(f, r) for f in range(3) for r in range(1, 4)]
R_CORNERS = [(f, i, j) for f in range(3) for i, j in CORNER]
AT_R = [len(R_ROWS) * X, len(R_ROWS) * X + len(R_CORNERS)]
AT_K = [AT_R[1] + len(R_CORNERS), AT_R[1] + len(R_CORNERS) + len(K_CORNERS)]
AT_Q = [AT_K[1] + len(K_CORNERS), AT_K[1] + len(K_CORNERS) + 3]
AT_U = AT_Q[1] + 3
Y_PACK = -(-(AT_U + 4) // 8) * 8
Q_SLOT = [R_ROWS.index((0, 3)), R_ROWS.index((1, 3))]


def struct(*shape):
    return jax.ShapeDtypeStruct(shape, F32)


def call(kernel, outs, scratch=(), left=(), count=0, cost=None, limit=20, scalars=()):
    extra = {}
    if left:
        extra["in_specs"] = [
            pl.BlockSpec(memory_space=pltpu.HBM if n in left else pltpu.VMEM) for n in range(count)
        ]
    if scalars:
        extra["out_specs"] = [
            pl.BlockSpec(memory_space=pltpu.SMEM if n in scalars else pltpu.VMEM)
            for n in range(len(outs))
        ]
    if cost:
        extra["cost_estimate"] = pl.CostEstimate(
            flops=cost, bytes_accessed=cost, transcendentals=0
        )
    return pl.pallas_call(
        kernel,
        out_shape=outs,
        scratch_shapes=list(scratch),
        compiler_params=pltpu.CompilerParams(vmem_limit_bytes=limit << 20),
        **extra,
    )


def up_y(v):
    return pltpu.roll(v, v.shape[0] - 1, 0)


def down_y(v):
    return pltpu.roll(v, 1, 0)


def up_z(v):
    return pltpu.roll(v, Z - 1, 1)


def down_z(v):
    return pltpu.roll(v, 1, 1)


def lanes(rows):
    return lax.broadcasted_iota(jnp.int32, (rows, Z), 1)


def rows_of(rows):
    return lax.broadcasted_iota(jnp.int32, (rows, Z), 0)


def to_tile(v):
    return pltpu.roll(v, EY - OY, 0)[:Y]


def harmonic(a, b):
    return 2.0 * a * b / jnp.maximum(a + b, 1e-30)


def one_hot(map_ref):
    brick = lax.broadcasted_iota(jnp.int32, (Z, 3 * Z), 0)
    return jnp.where(brick == map_ref[...], 1.0, 0.0).astype(jnp.bfloat16)


def dot_split(v, hot, contract):
    high = v.astype(jnp.bfloat16)
    low = (v - high.astype(F32)).astype(jnp.bfloat16)
    dims = (((1,), (contract,)), ((), ()))
    return lax.dot_general(high, hot, dims, preferred_element_type=F32) + lax.dot_general(
        low, hot, dims, preferred_element_type=F32
    )


def spread(v, hot, k):
    return dot_split(v, hot[:, k * Z : (k + 1) * Z], 0)


def gather_up(parts, hot):
    total = None
    for k, v in enumerate(parts):
        part = dot_split(v, hot[:, k * Z : (k + 1) * Z], 1)
        total = part if total is None else total + part
    ones = jnp.ones((8, 3 * Z), jnp.bfloat16)
    counts = lax.dot_general(ones, hot, (((1,), (1,)), ((), ())), preferred_element_type=F32)
    return total * (1.0 / counts[:1])


def gather_wide(ref, hot):
    rows = EX - 2
    parts = [ref[k, 1 : EX - 1].reshape(rows * EY, Z) for k in range(3)]
    return gather_up(parts, hot).reshape(rows, EY, Z)


def fetch(pairs, sem, start=0):
    copies = [pltpu.make_async_copy(a, b, sem.at[start + n]) for n, (a, b) in enumerate(pairs)]
    for copy in copies:
        copy.start()
    return copies


class Joined:
    def __init__(self, near, far):
        self.near, self.far = near, far

    def place(self, at):
        n, rest = (at[0], at[1:]) if isinstance(at, tuple) else (at, ())
        ref, n = (self.near, n) if n < len(NEAR) else (self.far, n - len(NEAR))
        return ref, (n, *rest)

    def __getitem__(self, at):
        ref, at = self.place(at)
        return ref[at]

    def __setitem__(self, at, value):
        ref, at = self.place(at)
        ref[at] = value


class Either:
    def __init__(self, odd, at_odd, at_even):
        self.odd, self.at_odd, self.at_even = odd, at_odd, at_even

    def __getitem__(self, at):
        return jnp.where(self.odd, self.at_odd[at], self.at_even[at])


def parity(axis):
    return lax.rem(lax.axis_index(axis), 2) == 1


def lower_upper(axis, first, second):
    odd = parity(axis)
    return Either(odd, first, second), Either(odd, second, first)


def surroundings(xa, xb, ya, yb):
    return lower_upper("gx", xa, xb) + lower_upper("gy", ya, yb)


def put(first, second, at, odd, tail, head):
    first[at] = jnp.where(odd, head, tail)
    second[at] = jnp.where(odd, tail, head)


def pack_x(source, rows, first, second):
    odd = parity("gx")
    for n, (f, r) in enumerate(rows):
        put(first, second, n, odd, source(f)[X - r], source(f)[r - 1])


def unpack_x(target, rows, low, up):
    for n, (f, r) in enumerate(rows):
        target(f)[OX - r, OY : OY + Y] = low[n]
        target(f)[OX + X - 1 + r, OY : OY + Y] = up[n]


def corner_at(side, i, j):
    row = OX - i if side[0] == 0 else OX + X - 1 + i
    column = OY - j if side[1] == 0 else OY + Y - 1 + j
    return row, slice(column, column + 1)


def x_faces(rows):
    return [struct(len(rows), Y, Z)] * 2


def loop(first, last, body, init=0, unroll=4):
    steps = (last - first) // unroll

    def step(n, carry):
        for m in range(unroll):
            carry = body(first + n * unroll + m, carry)
        return carry

    init = lax.fori_loop(0, steps, step, init)
    for i in range(first + steps * unroll, last):
        init = body(i, init)
    return init


def vertical_faces(conduct, flags, bottom, store):
    flow = lax.axis_index("group") == 0
    last = lanes(Y) == Z - 1
    eye = jnp.where(
        lax.broadcasted_iota(jnp.int32, (Y, Y), 0) == lax.broadcasted_iota(jnp.int32, (Y, Y), 1),
        1.0,
        0.0,
    ).astype(jnp.bfloat16)
    columns = lax.dot_general(
        eye,
        flags[...].astype(F32).astype(jnp.bfloat16),
        (((1,), (1,)), ((), ())),
        preferred_element_type=F32,
    )
    for x in range(X):
        bottom[x] = jnp.broadcast_to(columns[:, x : x + 1], (Y, Z))

    def row(x, carry):
        kz = [conduct[2, k, x] for k in range(3)]
        rolled = [up_z(v) for v in kz]
        ends = [rolled[1], rolled[2], bottom[x] * kz[2]]
        for k in range(3):
            end = jnp.where(flow, ends[k], kz[k])
            store(x, k, harmonic(kz[k], jnp.where(last, end, rolled[k])))
        return carry

    loop(0, X, row)


def pack_kernel(flags_in, state_in, conduct_in, capacity_in, xa, xb, fa, fb, ya, yb, *scratch):
    flags, state, conduct, capacity, bottom, tz, sem = scratch
    early = [(flags_in, flags)] + [(conduct_in.at[2, k], conduct.at[2, k]) for k in range(3)]
    late = [(conduct_in.at[d, k], conduct.at[d, k]) for d in range(2) for k in range(3)]
    late += [(state_in.at[k], state.at[k]) for k in range(3)] + [(capacity_in, capacity)]
    early = fetch(early, sem)
    late = fetch(late, sem, len(early))
    for copy in early:
        copy.wait()
    def store(x, k, value):
        tz[k, x] = value

    vertical_faces(conduct, flags, bottom, store)
    for copy in late:
        copy.wait()

    def source(f):
        if f < 6:
            return conduct.at[f // 3, f % 3]
        if f < 9:
            return tz.at[f - 6]
        return capacity if f == 9 else state.at[f - 10]

    pack_x(source, X_ROWS, Joined(xa, fa), Joined(xb, fb))
    odd = parity("gy")
    for n, (f, r) in enumerate(Y_ROWS):
        put(ya, yb, n, odd, source(f)[:, Y - r, :], source(f)[:, r - 1, :])


class Faces:
    def __init__(self, x, y, z, own):
        self.x, self.y, self.z, self.own = x, y, z, own


def faces_in(ref, shift=0):
    return Faces(*[lambda c, i, d=d: ref[3 * d + c, i - shift] for d in range(4)])


def lateral(faces, v_ref, c, i, v, fx_before):
    fx = faces.x(c, i) * (v - v_ref[c, i + 1])
    fy = faces.y(c, i) * (v - up_y(v))
    return (fx - fx_before) + (fy - down_y(fy)), fx


def x_flux(faces, v_ref, i):
    return tuple(faces.x(c, i) * (v_ref[c, i] - v_ref[c, i + 1]) for c in range(3))


def flow_below(vs, last):
    rolled = [up_z(v) for v in vs]
    ends = [rolled[1], rolled[2], 0.0]
    return [jnp.where(last, ends[k], rolled[k]) for k in range(3)]


def flow_row(faces, v_ref, i, fx_before):
    last, first = lanes(EY) == Z - 1, lanes(EY) == 0
    vs = [v_ref[k, i] for k in range(3)]
    below = flow_below(vs, last)
    fz = [faces.z(k, i) * (vs[k] - below[k]) for k in range(3)]
    moved = [down_z(v) for v in fz]
    ends = [0.0, moved[0], moved[1]]
    out, fx_now = [], []
    for k in range(3):
        side, fx = lateral(faces, v_ref, k, i, vs[k], fx_before[k])
        above = jnp.where(first, ends[k], moved[k])
        out.append(faces.own(k, i) * vs[k] + side + (fz[k] - above))
        fx_now.append(fx)
    return out, tuple(fx_now)


def strain_row(v_ref, i):
    v0, v1, v2 = v_ref[0, i], v_ref[1, i], v_ref[2, i]
    low = jnp.where(lanes(EY) == Z - 1, 0.0, up_z(v2))
    return (v_ref[0, i + 1] - v0) + (up_y(v1) - v1) + (low - v2)


def solid_row(faces, v_ref, i, s_before, fx_before):
    last, first = lanes(EY) == Z - 1, lanes(EY) == 0
    e = strain_row(v_ref, i)
    s = faces.own(0, i) * e
    grad = [s_before - s, down_y(s) - s, jnp.where(first, 0.0, down_z(s)) - s]
    out, fx_now = [], []
    for c in range(3):
        v = v_ref[c, i]
        side, fx = lateral(faces, v_ref, c, i, v, fx_before[c])
        fz = faces.z(c, i) * (v - jnp.where(last, 0.0, up_z(v)))
        above = jnp.where(first, 0.0, down_z(fz))
        out.append((side + (fz - above)) + grad[c])
        fx_now.append(fx)
    return out, s, tuple(fx_now)


BESIDE = [(1, -1, Y), (1, X - 1, Y), (1, -1, 0), (1, X - 1, 0)]
BESIDE += [(0, X, -1), (0, 0, -1), (0, X, Y - 1), (0, 0, Y - 1)]


def place_tile(conduct, capacity, keep, caps):
    at = slice(OY, OY + Y)

    def row(x, carry):
        for f in range(6):
            keep[f, OX + x, at] = conduct[f // 3, f % 3, x]
        caps[OX + x, at] = capacity[x]
        return carry

    loop(0, X, row)


def interior_kernel(state, conduct, capacity, flags, layer_map, faces, tz, unit, keep, caps, bottom):
    flow = lax.axis_index("group") == 0
    place_tile(conduct, capacity, keep, caps)

    def store(x, k, value):
        tz[k, x] = value
        faces[6 + k, OX + x, OY : OY + Y] = value

    vertical_faces(conduct, flags, bottom, store)
    loop(OX, OX + X, lambda i, carry: lateral_faces(keep, faces, i))

    @pl.when(flow)
    def _():
        hot = one_hot(layer_map)
        bricks = caps[OX : OX + X].reshape(X * EY, Z)
        for k in range(3):
            faces[9 + k, OX : OX + X] = (spread(bricks, hot, k) + BETA).reshape(X, EY, Z)
        parts = [state[k].reshape(X * Y, Z) for k in range(3)]
        unit[...] = gather_up(parts, hot).reshape(X, Y, Z)


def lateral_faces(keep, faces, i):
    for c in range(3):
        faces[c, i] = harmonic(keep[c, i], keep[c, i + 1])
        here = keep[3 + c, i]
        faces[3 + c, i] = harmonic(here, up_y(here))
    return 0


def strain_kernel(state, unit, xa, xb, ya, yb, strain):
    flow = lax.axis_index("group") == 0
    _, xu, _, yu = surroundings(xa, xb, ya, yb)

    @pl.when(flow)
    def _():
        strain[...] = unit[...]

    @pl.when(jnp.logical_not(flow))
    def _():
        last = lanes(Y) == Z - 1
        edge = rows_of(Y) == Y - 1
        n_x, n_y = X_ROWS.index((10, 1)), Y_ROWS.index((11, 1))
        for x in range(X):
            v0, v1, v2 = (state[c, x] for c in range(3))
            east = state[0, x + 1] if x + 1 < X else xu[n_x]
            north = jnp.where(edge, yu[n_y, x : x + 1], up_y(v1))
            low = jnp.where(last, 0.0, up_z(v2))
            strain[x] = (east - v0) + (north - v1) + (low - v2)


def first_kernel(state, conduct, capacity, supply, faces_ref, xa, xb, ya, yb, *refs):
    xl, xu, yl, yu = surroundings(xa, xb, ya, yb)
    base, beside, sides, own, field = refs
    flow = lax.axis_index("group") == 0

    def place(x, carry):
        for c in range(3):
            field[c, OX + x, OY : OY + Y] = state[c, x]
        for f in range(6):
            sides[f, OX + x] = faces_ref[f, OX + x]
        return carry

    loop(0, X, place)
    for c in range(3):
        n = X_ROWS.index((10 + c, 1))
        field[c, OX - 1, OY : OY + Y] = xl[n]
        field[c, OX + X, OY : OY + Y] = xu[n]
        n = Y_ROWS.index((10 + c, 1))
        field[c, OX : OX + X, OY - 1, :] = yl[n]
        field[c, OX : OX + X, OY + Y, :] = yu[n]
        n = X_ROWS.index((c, 1))
        at = slice(OY, OY + Y)
        sides[c, OX - 1, at] = harmonic(xl[n], conduct[0, c, 0])
        sides[c, OX + X - 1, at] = harmonic(conduct[0, c, X - 1], xu[n])
        n = Y_ROWS.index((3 + c, 1))
        sides[3 + c, OX : OX + X, OY - 1, :] = harmonic(yl[n], conduct[1, c, :, 0, :])
        sides[3 + c, OX : OX + X, OY + Y - 1, :] = harmonic(conduct[1, c, :, Y - 1, :], yu[n])
    field[1, OX - 1, OY + Y : OY + Y + 1] = jnp.zeros((1, Z), F32)
    field[0, OX + X, OY - 1 : OY] = jnp.zeros((1, Z), F32)
    for n, (c, x, y) in enumerate(BESIDE):
        beside[n : n + 1] = field[c, OX + x, OY + y : OY + y + 1]
    inner = faces_in(faces_ref)
    outer = faces_in(sides)

    @pl.when(flow)
    def _():
        faces = Faces(outer.x, outer.y, inner.z, inner.own)

        def row(i, fx_before):
            image, fx = flow_row(faces, field, i, fx_before)
            for k in range(3):
                base[k, i - OX] = (
                    supply[k, i - OX] + BETA * state[k, i - OX] - to_tile(image[k])
                )
            return fx

        loop(OX, OX + X, row, x_flux(faces, field, OX - 1))

    @pl.when(jnp.logical_not(flow))
    def _():
        def place(x, carry):
            own[OX + x, OY : OY + Y] = capacity[x]
            return carry

        loop(0, X, place)
        own[OX - 1, OY : OY + Y] = xl[X_ROWS.index((9, 1))]
        own[OX : OX + X, OY - 1, :] = yl[Y_ROWS.index((9, 1))]
        faces = Faces(outer.x, outer.y, inner.z, lambda c, i: own[i])

        def row(i, carry):
            image, s, fx = solid_row(faces, field, i, carry[0], carry[1])
            for c in range(3):
                base[c, i - OX] = supply[c, i - OX] - to_tile(image[c])
            return s, fx

        before = faces.own(0, OX - 1) * strain_row(field, OX - 1)
        loop(OX, OX + X, row, (before, x_flux(faces, field, OX - 1)))


def halo_kernel(conduct, capacity, tz, layer_map, xa, xb, ya, yb, fa, fb, *refs):
    faces, rim, keep, caps = refs
    xl, xu, yl, yu = surroundings(Joined(xa, fa), Joined(xb, fb), ya, yb)
    flow = lax.axis_index("group") == 0

    def target(f):
        if f < 6:
            return keep.at[f]
        return faces.at[f] if f < 9 else caps

    place_tile(conduct, capacity, keep, caps)

    def place(x, carry):
        for k in range(3):
            faces[6 + k, OX + x, OY : OY + Y] = tz[k, x]
        return carry

    loop(0, X, place)
    for n, (f, r) in enumerate(X_ROWS):
        if f < 10:
            target(f)[OX - r, OY : OY + Y] = xl[n]
            target(f)[OX + X - 1 + r, OY : OY + Y] = xu[n]
    for n, (f, r) in enumerate(Y_ROWS):
        if f < 10:
            target(f)[OX : OX + X, OY - r, :] = yl[n]
            target(f)[OX : OX + X, OY + Y - 1 + r, :] = yu[n]
    loop(0, EX - 1, lambda i, carry: lateral_faces(keep, faces, i))
    for n, i in enumerate(K_RIM):
        for f in range(6):
            rim[f, n] = keep[f, i]

    @pl.when(flow)
    def _():
        hot = one_hot(layer_map)
        bricks = caps[1 : EX - 1].reshape((EX - 2) * EY, Z)
        for k in range(3):
            faces[9 + k, 1 : EX - 1] = (spread(bricks, hot, k) + BETA).reshape(EX - 2, EY, Z)

    @pl.when(jnp.logical_not(flow))
    def _():
        faces[9] = caps[...]


BESIDE = [(1, -1, Y), (1, X - 1, Y), (1, -1, 0), (1, X - 1, 0)]
BESIDE += [(0, X, -1), (0, 0, -1), (0, X, Y - 1), (0, 0, Y - 1)]
RIM = [0, 1, 2, EX - 4, EX - 3, EX - 2]
K_RIM = [0, 1, 2, 3, EX - 4, EX - 3, EX - 2, EX - 1]


def residual_kernel(base, strain, unit, layer_map, residual, xa, xb):
    flow = lax.axis_index("group") == 0

    @pl.when(flow)
    def _():
        hot = one_hot(layer_map)
        e = strain[...].reshape(X * Y, Z)
        for k in range(3):
            residual[k] = base[k] - BIOT * spread(e, hot, k).reshape(X, Y, Z)

    @pl.when(jnp.logical_not(flow))
    def _():
        residual[...] = base[...]

    pack_x(lambda f: residual.at[f], R_ROWS, xa, xb)

    @pl.when(jnp.logical_not(flow))
    def _():
        odd = parity("gx")
        for depth, n in enumerate(Q_SLOT):
            put(xa, xb, n, odd, unit[X - 1 - depth], unit[depth])


def relay_kernel(residual, unit, xa, xb, ka, kb, fa, fb, ya, yb):
    flow = lax.axis_index("group") == 0
    odd = parity("gy")
    r_halos, k_halos = lower_upper("gx", xa, xb), lower_upper("gx", Joined(ka, fa), Joined(kb, fb))

    def give(at, count, ref, index, j):
        put(ya, yb, slice(at, at + count), odd, ref[index(Y - j)], ref[index(j - 1)])

    for n, (f, r) in enumerate(R_ROWS):
        give(n * X, X, residual, lambda y: (f, slice(None), y), r)
    for side in range(2):
        r_halo, k_halo = r_halos[side], k_halos[side]
        for n, (f, i, j) in enumerate(R_CORNERS):
            row = R_ROWS.index((f, i))
            give(AT_R[side] + n, 1, r_halo, lambda y: (row, slice(y, y + 1)), j)
        for n, (f, i, j) in enumerate(K_CORNERS):
            row = X_ROWS.index((f, i))
            give(AT_K[side] + n, 1, k_halo, lambda y: (row, slice(y, y + 1)), j)
        for n, (i, j) in enumerate(CORNER[:3]):
            row = Q_SLOT[i - 1]
            give(AT_Q[side] + n, 1, r_halo, lambda y: (row, slice(y, y + 1)), j)
        for c in range(2):
            row = X_ROWS.index((10 + c, 1))
            give(AT_U + 2 * side + c, 1, k_halo, lambda y: (row, slice(y, y + 1)), 1)

    @pl.when(jnp.logical_not(flow))
    def _():
        for depth, n in enumerate(Q_SLOT):
            give(n * X, X, unit, lambda y: (slice(None), y), depth + 1)


def fold(v):
    return jnp.sum(v.reshape(v.shape[0] // 8, 8, Z), axis=0)


def spread_sums(found):
    lane = lanes(8)
    row = jnp.zeros((8, Z), F32)
    first = rows_of(8) == 0
    for n, total in found.items():
        row = jnp.where(first & (lane == n), jnp.sum(total), row)
    return row


def tile_rows():
    at = rows_of(EY)
    return (at >= OY) & (at < OY + Y)


def fill(residual, target, halos):
    xl, xu, yl, yu = halos

    def place(x, carry):
        for k in range(3):
            target[k, OX + x, OY : OY + Y] = residual[k, x]
        return carry

    loop(0, X, place)
    unpack_x(lambda f: target.at[f], R_ROWS, xl, xu)
    for n, (f, r) in enumerate(R_ROWS):
        target[f, OX : OX + X, OY - r, :] = yl[n * X : (n + 1) * X]
        target[f, OX : OX + X, OY + Y - 1 + r, :] = yu[n * X : (n + 1) * X]
    for v, pack in enumerate((yl, yu)):
        for h in range(2):
            for n, (f, i, j) in enumerate(R_CORNERS):
                row, column = corner_at((h, v), i, j)
                target[f, row, column] = pack[AT_R[h] + n : AT_R[h] + n + 1]


def complete(faces, rim, k_rim_in, k_rim, halos, hot):
    for n, i in enumerate(RIM):
        for f in range(6, 12):
            rim[f, n] = faces[f, i]
    k_rim[...] = k_rim_in[...]
    order = []
    for v, pack in enumerate(halos[2:]):
        for h in range(2):
            for n, (f, i, j) in enumerate(K_CORNERS):
                row, column = corner_at((h, v), i, j)
                value = pack[AT_K[h] + n : AT_K[h] + n + 1]
                if f < 6:
                    k_rim[f, K_RIM.index(row), column] = value
                elif f < 9:
                    rim[f, RIM.index(row), column] = value
                else:
                    order.append((RIM.index(row), column, value))
    for n, i in enumerate(RIM):
        m = K_RIM.index(i)
        for c in range(3):
            rim[c, n] = harmonic(k_rim[c, m], k_rim[c, m + 1])
            here = k_rim[3 + c, m]
            rim[3 + c, n] = harmonic(here, up_y(here))
    if hot is None:
        for row, column, value in order:
            rim[9, row, column] = value
    else:
        values = [value for _, _, value in order]
        values += [jnp.zeros((1, Z), F32)] * (16 - len(values))
        caps = jnp.concatenate(values, axis=0)
        for k in range(3):
            storage = spread(caps, hot, k) + BETA
            for n, (row, column, _) in enumerate(order):
                rim[9 + k, row, column] = storage[n : n + 1]


def row_parts(faces, rim):
    return faces_in(rim), faces_in(faces), faces_in(rim, EX - 7)


def run_rows(parts, first, last, body, init, unroll=3):
    low, middle, high = parts
    for i in range(first, OX):
        init = body(low, i, init)
    init = loop(max(first, OX), EX - 4, lambda i, carry: body(middle, i, carry), init, unroll)
    for i in range(EX - 4, last):
        init = body(high, i, init)
    return init


PAIRS = [(0, 0), (0, 1), (0, 2), (1, 1), (1, 2), (2, 2)]
FIRST_SUM = 9


def grid_mask(before, after):
    gx, gy = lax.axis_index("gx"), lax.axis_index("gy")
    gx_last, gy_last = lax.axis_size("gx") - 1, lax.axis_size("gy") - 1
    at = rows_of(EY)
    in_y = (at >= OY - jnp.where(gy > 0, before, 0)) & (
        at < OY + Y + jnp.where(gy < gy_last, after, 0)
    )

    def in_grid(i):
        in_x = ((i >= OX) | (gx > 0)) & ((i < OX + X) | (gx < gx_last))
        return in_y & in_x

    return in_grid


def load_rows(q_refs, targets, added):
    in_grid = grid_mask(1, 2)

    def row(i, carry):
        for q_ref, target in zip(q_refs, targets):
            load_row(q_ref, target, i, in_grid(i))
        return carry

    def load_row(q_ref, target, i, ok):
        first = lanes(EY) == 0
        q = q_ref[i - 1]
        push = [
            BIOT * (q_ref[i - 2] - q),
            BIOT * (down_y(q) - q),
            BIOT * (jnp.where(first, 0.0, down_z(q)) - q),
        ]
        for c in range(3):
            v = push[c] + target[c, i] if added else push[c]
            target[c, i] = jnp.where(ok, v, 0.0)

    loop(OX - 1, OX + X + 2, row)


def solid_image(parts, f_refs, p_refs, unroll):
    in_grid = grid_mask(0, 1)

    def row(faces, i, carry):
        ok, after = in_grid(i), []
        for f_ref, p_ref, (s, fx) in zip(f_refs, p_refs, carry):
            out, s, fx = solid_row(faces, f_ref, i, s, fx)
            for c in range(3):
                p_ref[c, i] = jnp.where(ok, out[c], 0.0)
            after.append((s, fx))
        return tuple(after)

    view = parts[0]
    start = [
        (view.own(0, OX - 1) * strain_row(f, OX - 1), x_flux(view, f, OX - 1)) for f in f_refs
    ]
    run_rows(parts, OX, OX + X + 1, row, tuple(start), unroll)


def gram_sums(faces, fields, products, pairs, acc):
    acc[...] = jnp.zeros(acc.shape, F32)
    vectors = range(len(fields))

    def row(i, carry):
        inside, last = tile_rows(), lanes(EY) == Z - 1

        def only(v):
            return jnp.where(inside, v, 0.0)

        def add(n, v):
            acc[n] = acc[n] + fold(v)

        strains = [strain_row(p, i) for p in products]
        modulus = only(faces[9, i])
        later = sorted({b for _, b in pairs})
        pushes = {b: modulus * strains[b] for b in later}
        for n, (a, b) in enumerate(pairs):
            add(4 * n + 3, pushes[b] * strains[a])
        for c in range(3):
            ws = [p[c, i] for p in products]
            dx = [ws[a] - products[a][c, i + 1] for a in vectors]
            dy = [w - up_y(w) for w in ws]
            dz = [w - jnp.where(last, 0.0, up_z(w)) for w in ws]
            sx, sy, sz = (only(faces[3 * d + c, i]) for d in range(3))
            fx = {b: sx * dx[b] for b in later}
            fy = {b: sy * dy[b] for b in later}
            fz = {b: sz * dz[b] for b in later}
            rs = [f[c, i] for f in fields]
            r_in = {b: only(rs[b]) for b in later}
            w_in = {b: only(ws[b]) for b in later}
            for n, (a, b) in enumerate(pairs):
                add(4 * n + 3, fx[b] * dx[a] + fy[b] * dy[a] + fz[b] * dz[a])
                add(4 * n, r_in[b] * rs[a])
                add(4 * n + 1, r_in[b] * ws[a])
                add(4 * n + 2, w_in[b] * ws[a])
        return carry

    loop(OX, OX + X, row, 0, 2)
    found = {}
    for n, pair in enumerate(pairs):
        for m in range(4):
            found[FIRST_SUM + 6 * m + PAIRS.index(pair)] = acc[4 * n + m]
    return found


def unit_surroundings(unit, halos, q):
    xl, xu, yl, yu = halos

    def place(x, carry):
        q[OX - 1 + x, OY : OY + Y] = unit[x]
        return carry

    loop(0, X, place)
    for depth, n in enumerate(Q_SLOT):
        q[OX - 2 - depth, OY : OY + Y] = xl[n]
        q[OX + X - 1 + depth, OY : OY + Y] = xu[n]
        rows = slice(n * X, (n + 1) * X)
        q[OX - 1 : OX - 1 + X, OY - 1 - depth, :] = yl[rows]
        q[OX - 1 : OX - 1 + X, OY + Y + depth, :] = yu[rows]
    for v, pack in enumerate((yl, yu)):
        for h in range(2):
            for n, (i, j) in enumerate(CORNER[:3]):
                row, column = corner_at((h, v), i, j)
                q[row - 1, column] = pack[AT_Q[h] + n : AT_Q[h] + n + 1]


def late_terms(faces, rim, field, beside, halos):
    yl, yu = halos[2:]

    def modulus(x, y):
        i, column = OX + x, slice(OY + y, OY + y + 1)
        return rim[9, RIM.index(i), column] if i in RIM else faces[9, i, column]

    u1 = [yu[AT_U + 1 : AT_U + 2]] + [beside[n : n + 1] for n in (1, 2, 3)]
    u0 = [yl[AT_U + 2 : AT_U + 3]] + [beside[n : n + 1] for n in (5, 6, 7)]
    for u, (x, y) in zip(u1, ((0, Y - 1), (X, Y - 1), (0, -1), (X, -1))):
        row, column = OX + x, slice(OY + y, OY + y + 1)
        field[0, row, column] = field[0, row, column] - modulus(x - 1, y) * u
    for u, (x, y) in zip(u0, ((X - 1, 0), (-1, 0), (X - 1, Y), (-1, Y))):
        row, column = OX + x, slice(OY + y, OY + y + 1)
        field[1, row, column] = field[1, row, column] - modulus(x, y - 1) * u


def image_kernel(residual, unit_old, beside, layer_map, *refs):
    halos, (faces, k_rim_in, rim, field, product, unit, k_rim, q) = refs[:4], refs[4:]
    halos = surroundings(*halos)
    flow = lax.axis_index("group") == 0
    fill(residual, field, halos)

    @pl.when(flow)
    def _():
        hot = one_hot(layer_map)
        complete(faces, rim, k_rim_in, k_rim, halos, hot)
        parts = row_parts(faces, rim)

        def row(view, i, fx_before):
            out, fx = flow_row(view, field, i, fx_before)
            for k in range(3):
                product[k, i] = out[k]
            return fx

        run_rows(parts, 1, EX - 1, row, x_flux(parts[0], field, 0))
        unit[0] = gather_wide(field, hot)
        unit[1] = gather_wide(product, hot)

    @pl.when(jnp.logical_not(flow))
    def _():
        complete(faces, rim, k_rim_in, k_rim, halos, None)
        late_terms(faces, rim, field, beside, halos)
        unit_surroundings(unit_old, halos, q)
        load_rows([q], [field], True)
        solid_image(row_parts(faces, rim), [field], [product], 3)


def early_kernel(field, product, faces, state, sums, acc):
    flow = lax.axis_index("group") == 0

    @pl.when(flow)
    def _():
        def dots(i, acc):
            acc = list(acc)
            inside, last = tile_rows(), lanes(EY) == Z - 1

            def add(n, v):
                acc[n] = acc[n] + fold(jnp.where(inside, v, 0.0))

            ws = [product[k, i] for k in range(3)]
            below = flow_below(ws, last)
            g = m1 = m2 = m3 = cr = cw = 0.0
            for k in range(3):
                r, w = field[k, i], ws[k]
                dx, dy, dz = w - product[k, i + 1], w - up_y(w), w - below[k]
                cf = faces[9 + k, i]
                g = g + r * r
                m1 = m1 + r * w
                m2 = m2 + w * w
                cr = cr + cf * r
                cw = cw + cf * w
                m3 = m3 + (
                    faces[k, i] * dx * dx
                    + faces[3 + k, i] * dy * dy
                    + faces[6 + k, i] * dz * dz
                    + cf * w * w
                )
            for n, v in enumerate((g, m1, m2, m3, cr, cw)):
                add(n, v)
            weight = jnp.where(last, faces[8, i], 0.0)
            add(6, weight * field[2, i])
            add(7, weight * ws[2])
            acc[8] = acc[8] + fold(to_tile(weight) * state[2, i - OX])
            return tuple(acc)

        zero = jnp.zeros((8, Z), F32)
        found = dict(enumerate(loop(OX, OX + X, dots, (zero,) * FIRST_SUM, 2)))
        sums[...] = spread_sums(found)

    @pl.when(jnp.logical_not(flow))
    def _():
        sums[...] = spread_sums(gram_sums(faces, [field], [product], PAIRS[:1], acc))


def sums_kernel(field, product, faces, rim, unit, sums_in, sums, field12, product12, acc):
    flow = lax.axis_index("group") == 0
    everyone = sums.shape[0]

    @pl.when(flow)
    def _():
        sums[...] = jnp.broadcast_to(sums_in[:1], (everyone, Z))

    @pl.when(jnp.logical_not(flow))
    def _():
        fields = [field] + [field12.at[a] for a in range(2)]
        products = [product] + [product12.at[a] for a in range(2)]
        load_rows([unit.at[a] for a in range(2)], fields[1:], False)
        solid_image(row_parts(faces, rim), fields[1:], products[1:], 2)
        found = gram_sums(faces, fields, products, PAIRS[1:], acc)
        own = sums_in[:1] + spread_sums(found)[:1]
        sums[...] = jnp.broadcast_to(own, (everyone, Z))


def two_sum(a, b):
    s = a + b
    t = s - a
    return s, (a - (s - t)) + (b - t)


def quick(a, b):
    s = a + b
    return s, b - (s - a)


def halves(a):
    t = 4097.0 * a
    high = t - (t - a)
    return high, a - high


def two_product(a, b):
    p = a * b
    ah, al = halves(a)
    bh, bl = halves(b)
    return p, ((ah * bh - p) + ah * bl + al * bh) + al * bl


def pair_add(a, b):
    s, e = two_sum(a[0], b[0])
    return quick(s, e + (a[1] + b[1]))


def pair_less(a, b):
    return pair_add(a, (-b[0], -b[1]))


def pair_times(a, b):
    p, e = two_product(a[0], b[0])
    return quick(p, e + (a[0] * b[1] + a[1] * b[0]))


def pair_over(a, b):
    q = a[0] / b[0]
    rest = pair_less(a, pair_times(b, (q, jnp.zeros_like(q))))
    return quick(q, rest[0] / b[0])


def krylov(g, m1, m2, m3):
    a0 = pair_over(g, m1)
    h = pair_times(a0, pair_over(m2, m1))
    one = (jnp.ones_like(a0[0]), jnp.zeros_like(a0[0]))
    rho = pair_less(h, one)[0]
    third = pair_times(pair_times(a0, a0), pair_over(m3, m1))
    sigma = pair_less(third, pair_times(h, h))[0]
    more = (rho > 1e-9) & (sigma > 1e-9)
    a1 = jnp.where(more, a0[0] * rho / jnp.where(more, sigma, 1.0), 0.0)
    return a0[0] + a1 * h[0], -a0[0] * a1


def final_kernel(sums, state, field, product, field12, product12, out, balance, *, cells):
    flow = lax.axis_index("group") == 0
    total = (sums[...], jnp.zeros(sums.shape, F32))
    while total[0].shape[0] > 8:
        half = total[0].shape[0] // 2
        total = pair_add([v[:half] for v in total], [v[half:] for v in total])
    for step in (4, 2, 1):
        total = pair_add(total, [pltpu.roll(v, step, 0) for v in total])

    def number(n):
        return tuple(jnp.broadcast_to(v[:1, n : n + 1], (8, Z)) for v in total)

    c0, c1 = krylov(number(0), number(1), number(2), number(3))
    columns = cells // (3 * Z)
    outflow = (number(8)[0] + c0 * number(6)[0] + c1 * number(7)[0]) / columns
    stored = (c0 * number(4)[0] + c1 * number(5)[0]) / cells
    balance[0] = outflow[0, 0]
    balance[1] = stored[0, 0]

    def tall(v):
        return jnp.concatenate([v] * (EY // 8), axis=0)

    @pl.when(flow)
    def _():
        s0, s1 = tall(c0), tall(c1)

        def row(x, carry):
            for k in range(3):
                step = s0 * field[k, OX + x] + s1 * product[k, OX + x]
                out[k, x] = state[k, x] + to_tile(step)
            return carry

        loop(0, X, row)

    @pl.when(jnp.logical_not(flow))
    def _():
        zero = jnp.zeros((8, Z), F32)
        weights = [
            (jnp.ones((8, Z), F32), zero),
            (2.0 * c0, zero),
            (2.0 * c1, zero),
            two_product(c0, c0),
            two_product(2.0 * c0, c1),
            two_product(c1, c1),
        ]
        moments = []
        for m in range(4):
            start = FIRST_SUM + 6 * m
            total = number(start)
            for n in range(1, 6):
                total = pair_add(total, pair_times(weights[n], number(start + n)))
            moments.append(total)
        d0, d1 = krylov(*moments)
        scale_r = [tall(d0), tall(d0 * c0), tall(d0 * c1)]
        scale_w = [tall(d1), tall(d1 * c0), tall(d1 * c1)]

        def row(x, carry):
            for c in range(3):
                step = scale_r[0] * field[c, OX + x] + scale_w[0] * product[c, OX + x]
                for a in range(2):
                    step = step + scale_r[a + 1] * field12[a, c, OX + x]
                    step = step + scale_w[a + 1] * product12[a, c, OX + x]
                out[c, x] = state[c, x] + to_tile(step)
            return carry

        loop(0, X, row)


def swaps(first, second, axis):
    groups, rows, columns = (lax.axis_size(a) for a in AXES)
    count, found = lax.axis_size(axis), []
    for value, start in ((first, 0), (second, 1)):
        pairs = []
        for g in range(groups):
            for i in range(rows):
                for j in range(columns):
                    place = i if axis == "gx" else j
                    step = 1 if place % 2 == start else -1
                    if 0 <= place + step < count:
                        here = (g * rows + i) * columns + j
                        pairs.append((here, here + step * (columns if axis == "gx" else 1)))
        found.append(lax.ppermute(value, AXES, pairs))
    return found


def core_swap(value):
    count = lax.axis_size("gx") * lax.axis_size("gy")
    pairs = [(n, (n + count) % (2 * count)) for n in range(2 * count)]
    return lax.ppermute(value, AXES, pairs)


def body(state, conduct, capacity, supply, flags, layer_map):
    state, conduct, capacity, supply = state[0], conduct[0], capacity[0], supply[0]
    layer_map = layer_map.reshape(1, 3 * Z)
    cells = X * Y * 3 * Z * lax.axis_size("gx") * lax.axis_size("gy")
    devices = lax.axis_size("group") * lax.axis_size("gx") * lax.axis_size("gy")
    tile = struct(3, X, Y, Z)
    brick = struct(X, Y, Z)
    wide = (EX, EY, Z)
    full = struct(3, *wide)

    y_face = struct(len(Y_ROWS), X, Z)
    xa, xb, fa, fb, ya, yb = call(
        pack_kernel,
        x_faces(NEAR) + x_faces(X_ROWS[len(NEAR) :]) + [y_face] * 2,
        [
            pltpu.VMEM((X, Y), jnp.int32),
            pltpu.VMEM((3, X, Y, Z), F32),
            pltpu.VMEM((3, 3, X, Y, Z), F32),
            pltpu.VMEM((X, Y, Z), F32),
            pltpu.VMEM((X, Y, Z), F32),
            pltpu.VMEM((3, X, Y, Z), F32),
            pltpu.SemaphoreType.DMA((14,)),
        ],
        left=(0, 1, 2, 3),
        limit=58,
        count=4,
    )(flags, state, conduct, capacity)
    k_halos = lax.optimization_barrier(swaps(xa, xb, "gx") + swaps(ya, yb, "gy"))
    far = swaps(fa, fb, "gx")
    wide_faces = struct(12, *wide)
    tables = [pltpu.VMEM((6, *wide), F32), pltpu.VMEM(wide, F32)]
    inner, tz, unit0 = call(
        interior_kernel,
        [wide_faces, tile, brick],
        tables + [pltpu.VMEM((X, Y, Z), F32)],
        cost=30_000_000,
    )(state, conduct, capacity, flags, layer_map)
    cross = core_swap(call(strain_kernel, brick)(state, unit0, *k_halos))
    base, beside = call(
        first_kernel,
        [tile, struct(8, Z)],
        tables + [pltpu.VMEM((3, *wide), F32)],
        cost=20_000_000,
    )(state, conduct, capacity, supply, inner, *k_halos)
    faces, k_rim = call(
        halo_kernel, [wide_faces, struct(6, len(K_RIM), EY, Z)], tables, cost=30_000_000
    )(conduct, capacity, tz, layer_map, *k_halos, *far)
    residual, xa, xb = call(residual_kernel, [tile] + x_faces(R_ROWS))(
        base, cross, cross, layer_map
    )
    halos = swaps(xa, xb, "gx")
    ya, yb = call(relay_kernel, [struct(Y_PACK, Z)] * 2)(
        residual, cross, *halos, k_halos[0], k_halos[1], *far
    )
    halos = halos + swaps(ya, yb, "gy")
    rim, field, product, unit12 = call(
        image_kernel,
        [struct(12, len(RIM), EY, Z), full, full, struct(2, EX - 2, EY, Z)],
        [pltpu.VMEM((6, len(K_RIM), EY, Z), F32), pltpu.VMEM((EX - 2, EY, Z), F32)],
    )(residual, cross, beside, layer_map, *halos, faces, k_rim)
    unit12 = core_swap(unit12)
    sums = call(early_kernel, struct(8, Z), [pltpu.VMEM((4, 8, Z), F32)], cost=20_000_000)(
        field, product, faces, state
    )
    sums, field12, product12 = call(
        sums_kernel,
        [struct(devices, Z), struct(2, 3, *wide), struct(2, 3, *wide)],
        [pltpu.VMEM((20, 8, Z), F32)],
    )(field, product, faces, rim, unit12, sums)
    sums = lax.all_to_all(sums, AXES, 0, 0, tiled=True)

    def finish(*refs):
        final_kernel(*refs, cells=cells)

    new_state, balance = call(finish, [tile, struct(2)], scalars=(1,))(
        sums, state, field, product, field12, product12
    )
    return new_state[None], balance


def solution(mesh):
    placed = (
        P("group", None, "gx", "gy", None),
        P("group", None, None, "gx", "gy", None),
        P("group", "gx", "gy", None),
        P("group", None, "gx", "gy", None),
        P("gx", "gy"),
        P(),
    )
    return jax.shard_map(
        body,
        mesh=mesh,
        in_specs=placed,
        out_specs=(P("group", None, "gx", "gy", None), P()),
        check_vma=False,
    )
```

```python
import jax
import jax.numpy as jnp
from jax import lax
from jax.experimental import pallas as pl
from jax.experimental.pallas import tpu as pltpu
from jax.sharding import PartitionSpec as P

AXES = ("group", "gx", "gy")
X, Y, Z = 16, 32, 128
OX, OY = 3, 4
EX, EY = X + 2 * OX, Y + 2 * OY
BETA = 0.5
BIOT = 0.8
F32 = jnp.float32

X_ROWS = [(f, r) for f in range(13) for r in range(1, (3 if f < 3 else 2 if f < 10 else 1) + 1)]
NEAR = [(f, r) for f, r in X_ROWS if r == 1 and not 3 <= f < 9]
X_ROWS = NEAR + [row for row in X_ROWS if row not in NEAR]
Y_ROWS = [
    (f, r) for f in range(13) for r in range(1, (3 if 3 <= f < 6 else 2 if f < 10 else 1) + 1)
]
CORNER = [(1, 1), (1, 2), (2, 1), (2, 2), (1, 3), (3, 1)]
K_CORNERS = (
    [(f, i, j) for f in range(3) for i, j in CORNER[:4] + [(3, 1)]]
    + [(f, i, j) for f in range(3, 6) for i, j in CORNER[:4] + [(1, 3)]]
    + [(f, i, j) for f in range(6, 10) for i, j in CORNER[:3]]
)
R_ROWS = [(f, r) for f in range(3) for r in range(1, 4)]
R_CORNERS = [(f, i, j) for f in range(3) for i, j in CORNER]
AT_R = [len(R_ROWS) * X, len(R_ROWS) * X + len(R_CORNERS)]
AT_K = [AT_R[1] + len(R_CORNERS), AT_R[1] + len(R_CORNERS) + len(K_CORNERS)]
AT_Q = [AT_K[1] + len(K_CORNERS), AT_K[1] + len(K_CORNERS) + 3]
AT_U = AT_Q[1] + 3
Y_PACK = -(-(AT_U + 4) // 8) * 8
Q_SLOT = [R_ROWS.index((0, 3)), R_ROWS.index((1, 3))]


def struct(*shape):
    return jax.ShapeDtypeStruct(shape, F32)


def call(kernel, outs, scratch=(), left=(), count=0, cost=None, limit=20, scalars=()):
    extra = {}
    if left:
        extra["in_specs"] = [
            pl.BlockSpec(memory_space=pltpu.HBM if n in left else pltpu.VMEM) for n in range(count)
        ]
    if scalars:
        extra["out_specs"] = [
            pl.BlockSpec(memory_space=pltpu.SMEM if n in scalars else pltpu.VMEM)
            for n in range(len(outs))
        ]
    if cost:
        extra["cost_estimate"] = pl.CostEstimate(
            flops=cost, bytes_accessed=cost, transcendentals=0
        )
    return pl.pallas_call(
        kernel,
        out_shape=outs,
        scratch_shapes=list(scratch),
        compiler_params=pltpu.CompilerParams(vmem_limit_bytes=limit << 20),
        **extra,
    )


def up_y(v):
    return pltpu.roll(v, v.shape[0] - 1, 0)


def down_y(v):
    return pltpu.roll(v, 1, 0)


def up_z(v):
    return pltpu.roll(v, Z - 1, 1)


def down_z(v):
    return pltpu.roll(v, 1, 1)


def lanes(rows):
    return lax.broadcasted_iota(jnp.int32, (rows, Z), 1)


def rows_of(rows):
    return lax.broadcasted_iota(jnp.int32, (rows, Z), 0)


def to_tile(v):
    return pltpu.roll(v, EY - OY, 0)[:Y]


def harmonic(a, b):
    return 2.0 * a * b / jnp.maximum(a + b, 1e-30)


def one_hot(map_ref):
    brick = lax.broadcasted_iota(jnp.int32, (Z, 3 * Z), 0)
    return jnp.where(brick == map_ref[...], 1.0, 0.0).astype(jnp.bfloat16)


def dot_split(v, hot, contract):
    high = v.astype(jnp.bfloat16)
    low = (v - high.astype(F32)).astype(jnp.bfloat16)
    dims = (((1,), (contract,)), ((), ()))
    return lax.dot_general(high, hot, dims, preferred_element_type=F32) + lax.dot_general(
        low, hot, dims, preferred_element_type=F32
    )


def spread(v, hot, k):
    return dot_split(v, hot[:, k * Z : (k + 1) * Z], 0)


def gather_up(parts, hot):
    total = None
    for k, v in enumerate(parts):
        part = dot_split(v, hot[:, k * Z : (k + 1) * Z], 1)
        total = part if total is None else total + part
    ones = jnp.ones((8, 3 * Z), jnp.bfloat16)
    counts = lax.dot_general(ones, hot, (((1,), (1,)), ((), ())), preferred_element_type=F32)
    return total * (1.0 / counts[:1])


def gather_wide(ref, hot):
    rows = EX - 2
    parts = [ref[k, 1 : EX - 1].reshape(rows * EY, Z) for k in range(3)]
    return gather_up(parts, hot).reshape(rows, EY, Z)


def fetch(pairs, sem, start=0):
    copies = [pltpu.make_async_copy(a, b, sem.at[start + n]) for n, (a, b) in enumerate(pairs)]
    for copy in copies:
        copy.start()
    return copies


def corner_row(n, side):
    c = 2 * n + side
    return len(NEAR) + c // Y, slice(c % Y, c % Y + 1)


NEAR_ROWS = len(NEAR) + -(-2 * len(K_CORNERS) // Y)


class Joined:
    def __init__(self, near, far):
        self.near, self.far = near, far

    def place(self, at):
        n, rest = (at[0], at[1:]) if isinstance(at, tuple) else (at, ())
        ref, n = (self.near, n) if n < len(NEAR) else (self.far, n - len(NEAR))
        return ref, (n, *rest)

    def __getitem__(self, at):
        ref, at = self.place(at)
        return ref[at]

    def __setitem__(self, at, value):
        ref, at = self.place(at)
        ref[at] = value


class Either:
    def __init__(self, odd, at_odd, at_even):
        self.odd, self.at_odd, self.at_even = odd, at_odd, at_even

    def __getitem__(self, at):
        return jnp.where(self.odd, self.at_odd[at], self.at_even[at])


def parity(axis):
    return lax.rem(lax.axis_index(axis), 2) == 1


def lower_upper(axis, first, second):
    odd = parity(axis)
    return Either(odd, first, second), Either(odd, second, first)


def surroundings(xa, xb, ya, yb):
    return lower_upper("gx", xa, xb) + lower_upper("gy", ya, yb)


def put(first, second, at, odd, tail, head):
    first[at] = jnp.where(odd, head, tail)
    second[at] = jnp.where(odd, tail, head)


def pack_x(source, rows, first, second):
    odd = parity("gx")
    for n, (f, r) in enumerate(rows):
        put(first, second, n, odd, source(f)[X - r], source(f)[r - 1])


def unpack_x(target, rows, low, up):
    for n, (f, r) in enumerate(rows):
        target(f)[OX - r, OY : OY + Y] = low[n]
        target(f)[OX + X - 1 + r, OY : OY + Y] = up[n]


def corner_at(side, i, j):
    row = OX - i if side[0] == 0 else OX + X - 1 + i
    column = OY - j if side[1] == 0 else OY + Y - 1 + j
    return row, slice(column, column + 1)


def x_faces(rows):
    return [struct(len(rows), Y, Z)] * 2


def loop(first, last, body, init=0, unroll=4):
    steps = (last - first) // unroll

    def step(n, carry):
        for m in range(unroll):
            carry = body(first + n * unroll + m, carry)
        return carry

    init = lax.fori_loop(0, steps, step, init)
    for i in range(first + steps * unroll, last):
        init = body(i, init)
    return init


def vertical_faces(conduct, flags, bottom, store):
    flow = lax.axis_index("group") == 0
    last = lanes(Y) == Z - 1
    eye = jnp.where(
        lax.broadcasted_iota(jnp.int32, (Y, Y), 0) == lax.broadcasted_iota(jnp.int32, (Y, Y), 1),
        1.0,
        0.0,
    ).astype(jnp.bfloat16)
    columns = lax.dot_general(
        eye,
        flags[...].astype(F32).astype(jnp.bfloat16),
        (((1,), (1,)), ((), ())),
        preferred_element_type=F32,
    )
    for x in range(X):
        bottom[x] = jnp.broadcast_to(columns[:, x : x + 1], (Y, Z))

    def row(x, carry):
        kz = [conduct[2, k, x] for k in range(3)]
        rolled = [up_z(v) for v in kz]
        ends = [rolled[1], rolled[2], bottom[x] * kz[2]]
        for k in range(3):
            end = jnp.where(flow, ends[k], kz[k])
            store(x, k, harmonic(kz[k], jnp.where(last, end, rolled[k])))
        return carry

    loop(0, X, row)


def pack_kernel(flags_in, state_in, conduct_in, capacity_in, xa, xb, fa, fb, ya, yb, *scratch):
    flags, state, conduct, capacity, bottom, tz, sem = scratch
    early = [(flags_in, flags)] + [(conduct_in.at[2, k], conduct.at[2, k]) for k in range(3)]
    late = [(conduct_in.at[d, k], conduct.at[d, k]) for d in range(2) for k in range(3)]
    late += [(state_in.at[k], state.at[k]) for k in range(3)] + [(capacity_in, capacity)]
    early = fetch(early, sem)
    late = fetch(late, sem, len(early))
    for copy in early:
        copy.wait()
    def store(x, k, value):
        tz[k, x] = value

    vertical_faces(conduct, flags, bottom, store)
    for copy in late:
        copy.wait()

    def source(f):
        if f < 6:
            return conduct.at[f // 3, f % 3]
        if f < 9:
            return tz.at[f - 6]
        return capacity if f == 9 else state.at[f - 10]

    pack_x(source, X_ROWS, Joined(xa, fa), Joined(xb, fb))
    odd = parity("gx")
    for n, (f, i, j) in enumerate(K_CORNERS):
        for side, y in enumerate((Y - j, j - 1)):
            column = slice(y, y + 1)
            put(xa, xb, corner_row(n, side), odd, source(f)[X - i, column], source(f)[i - 1, column])
    odd = parity("gy")
    for n, (f, r) in enumerate(Y_ROWS):
        put(ya, yb, n, odd, source(f)[:, Y - r, :], source(f)[:, r - 1, :])


class Faces:
    def __init__(self, x, y, z, own):
        self.x, self.y, self.z, self.own = x, y, z, own


def faces_in(ref, shift=0):
    return Faces(*[lambda c, i, d=d: ref[3 * d + c, i - shift] for d in range(4)])


def lateral(faces, v_ref, c, i, v, fx_before):
    fx = faces.x(c, i) * (v - v_ref[c, i + 1])
    fy = faces.y(c, i) * (v - up_y(v))
    return (fx - fx_before) + (fy - down_y(fy)), fx


def x_flux(faces, v_ref, i):
    return tuple(faces.x(c, i) * (v_ref[c, i] - v_ref[c, i + 1]) for c in range(3))


def flow_below(vs, last):
    rolled = [up_z(v) for v in vs]
    ends = [rolled[1], rolled[2], 0.0]
    return [jnp.where(last, ends[k], rolled[k]) for k in range(3)]


def flow_row(faces, v_ref, i, fx_before):
    last, first = lanes(EY) == Z - 1, lanes(EY) == 0
    vs = [v_ref[k, i] for k in range(3)]
    below = flow_below(vs, last)
    fz = [faces.z(k, i) * (vs[k] - below[k]) for k in range(3)]
    moved = [down_z(v) for v in fz]
    ends = [0.0, moved[0], moved[1]]
    out, fx_now = [], []
    for k in range(3):
        side, fx = lateral(faces, v_ref, k, i, vs[k], fx_before[k])
        above = jnp.where(first, ends[k], moved[k])
        out.append(faces.own(k, i) * vs[k] + side + (fz[k] - above))
        fx_now.append(fx)
    return out, tuple(fx_now)


def strain_row(v_ref, i):
    v0, v1, v2 = v_ref[0, i], v_ref[1, i], v_ref[2, i]
    low = jnp.where(lanes(EY) == Z - 1, 0.0, up_z(v2))
    return (v_ref[0, i + 1] - v0) + (up_y(v1) - v1) + (low - v2)


def solid_row(faces, v_ref, i, s_before, fx_before):
    last, first = lanes(EY) == Z - 1, lanes(EY) == 0
    e = strain_row(v_ref, i)
    s = faces.own(0, i) * e
    grad = [s_before - s, down_y(s) - s, jnp.where(first, 0.0, down_z(s)) - s]
    out, fx_now = [], []
    for c in range(3):
        v = v_ref[c, i]
        side, fx = lateral(faces, v_ref, c, i, v, fx_before[c])
        fz = faces.z(c, i) * (v - jnp.where(last, 0.0, up_z(v)))
        above = jnp.where(first, 0.0, down_z(fz))
        out.append((side + (fz - above)) + grad[c])
        fx_now.append(fx)
    return out, s, tuple(fx_now)


BESIDE = [(1, -1, Y), (1, X - 1, Y), (1, -1, 0), (1, X - 1, 0)]
BESIDE += [(0, X, -1), (0, 0, -1), (0, X, Y - 1), (0, 0, Y - 1)]


def place_tile(conduct, capacity, keep, caps):
    at = slice(OY, OY + Y)

    def row(x, carry):
        for f in range(6):
            keep[f, OX + x, at] = conduct[f // 3, f % 3, x]
        caps[OX + x, at] = capacity[x]
        return carry

    loop(0, X, row)


def interior_kernel(state, conduct, capacity, flags, layer_map, faces, tz, unit, keep, caps, bottom):
    flow = lax.axis_index("group") == 0
    place_tile(conduct, capacity, keep, caps)

    def store(x, k, value):
        tz[k, x] = value
        faces[6 + k, OX + x, OY : OY + Y] = value

    vertical_faces(conduct, flags, bottom, store)
    loop(OX, OX + X, lambda i, carry: lateral_faces(keep, faces, i))

    @pl.when(flow)
    def _():
        hot = one_hot(layer_map)
        bricks = caps[OX : OX + X].reshape(X * EY, Z)
        for k in range(3):
            faces[9 + k, OX : OX + X] = (spread(bricks, hot, k) + BETA).reshape(X, EY, Z)
        parts = [state[k].reshape(X * Y, Z) for k in range(3)]
        unit[...] = gather_up(parts, hot).reshape(X, Y, Z)


def lateral_faces(keep, faces, i):
    for c in range(3):
        faces[c, i] = harmonic(keep[c, i], keep[c, i + 1])
        here = keep[3 + c, i]
        faces[3 + c, i] = harmonic(here, up_y(here))
    return 0


def strain_kernel(state, unit, xa, xb, ya, yb, strain):
    flow = lax.axis_index("group") == 0
    _, xu, _, yu = surroundings(xa, xb, ya, yb)

    @pl.when(flow)
    def _():
        strain[...] = unit[...]

    @pl.when(jnp.logical_not(flow))
    def _():
        last = lanes(Y) == Z - 1
        edge = rows_of(Y) == Y - 1
        n_x, n_y = X_ROWS.index((10, 1)), Y_ROWS.index((11, 1))
        for x in range(X):
            v0, v1, v2 = (state[c, x] for c in range(3))
            east = state[0, x + 1] if x + 1 < X else xu[n_x]
            north = jnp.where(edge, yu[n_y, x : x + 1], up_y(v1))
            low = jnp.where(last, 0.0, up_z(v2))
            strain[x] = (east - v0) + (north - v1) + (low - v2)


def first_kernel(state, conduct, capacity, supply, faces_ref, xa, xb, ya, yb, *refs):
    xl, xu, yl, yu = surroundings(xa, xb, ya, yb)
    base, beside, sides, own, field = refs
    flow = lax.axis_index("group") == 0

    def place(x, carry):
        for c in range(3):
            field[c, OX + x, OY : OY + Y] = state[c, x]
        for f in range(6):
            sides[f, OX + x] = faces_ref[f, OX + x]
        return carry

    loop(0, X, place)
    for c in range(3):
        n = X_ROWS.index((10 + c, 1))
        field[c, OX - 1, OY : OY + Y] = xl[n]
        field[c, OX + X, OY : OY + Y] = xu[n]
        n = Y_ROWS.index((10 + c, 1))
        field[c, OX : OX + X, OY - 1, :] = yl[n]
        field[c, OX : OX + X, OY + Y, :] = yu[n]
        n = X_ROWS.index((c, 1))
        at = slice(OY, OY + Y)
        sides[c, OX - 1, at] = harmonic(xl[n], conduct[0, c, 0])
        sides[c, OX + X - 1, at] = harmonic(conduct[0, c, X - 1], xu[n])
        n = Y_ROWS.index((3 + c, 1))
        sides[3 + c, OX : OX + X, OY - 1, :] = harmonic(yl[n], conduct[1, c, :, 0, :])
        sides[3 + c, OX : OX + X, OY + Y - 1, :] = harmonic(conduct[1, c, :, Y - 1, :], yu[n])
    field[1, OX - 1, OY + Y : OY + Y + 1] = jnp.zeros((1, Z), F32)
    field[0, OX + X, OY - 1 : OY] = jnp.zeros((1, Z), F32)
    for n, (c, x, y) in enumerate(BESIDE):
        beside[n : n + 1] = field[c, OX + x, OY + y : OY + y + 1]
    inner = faces_in(faces_ref)
    outer = faces_in(sides)

    @pl.when(flow)
    def _():
        faces = Faces(outer.x, outer.y, inner.z, inner.own)

        def row(i, fx_before):
            image, fx = flow_row(faces, field, i, fx_before)
            for k in range(3):
                base[k, i - OX] = (
                    supply[k, i - OX] + BETA * state[k, i - OX] - to_tile(image[k])
                )
            return fx

        loop(OX, OX + X, row, x_flux(faces, field, OX - 1))

    @pl.when(jnp.logical_not(flow))
    def _():
        def place(x, carry):
            own[OX + x, OY : OY + Y] = capacity[x]
            return carry

        loop(0, X, place)
        own[OX - 1, OY : OY + Y] = xl[X_ROWS.index((9, 1))]
        own[OX : OX + X, OY - 1, :] = yl[Y_ROWS.index((9, 1))]
        faces = Faces(outer.x, outer.y, inner.z, lambda c, i: own[i])

        def row(i, carry):
            image, s, fx = solid_row(faces, field, i, carry[0], carry[1])
            for c in range(3):
                base[c, i - OX] = supply[c, i - OX] - to_tile(image[c])
            return s, fx

        before = faces.own(0, OX - 1) * strain_row(field, OX - 1)
        loop(OX, OX + X, row, (before, x_flux(faces, field, OX - 1)))


def halo_kernel(conduct, capacity, tz, layer_map, xa, xb, ya, yb, fa, fb, *refs):
    faces, rim, keep, caps = refs
    xl, xu, yl, yu = surroundings(Joined(xa, fa), Joined(xb, fb), ya, yb)
    flow = lax.axis_index("group") == 0

    def target(f):
        if f < 6:
            return keep.at[f]
        return faces.at[f] if f < 9 else caps

    place_tile(conduct, capacity, keep, caps)

    def place(x, carry):
        for k in range(3):
            faces[6 + k, OX + x, OY : OY + Y] = tz[k, x]
        return carry

    loop(0, X, place)
    for n, (f, r) in enumerate(X_ROWS):
        if f < 10:
            target(f)[OX - r, OY : OY + Y] = xl[n]
            target(f)[OX + X - 1 + r, OY : OY + Y] = xu[n]
    for n, (f, r) in enumerate(Y_ROWS):
        if f < 10:
            target(f)[OX : OX + X, OY - r, :] = yl[n]
            target(f)[OX : OX + X, OY + Y - 1 + r, :] = yu[n]
    loop(0, EX - 1, lambda i, carry: lateral_faces(keep, faces, i))
    for n, i in enumerate(K_RIM):
        for f in range(6):
            rim[f, n] = keep[f, i]

    @pl.when(flow)
    def _():
        hot = one_hot(layer_map)
        bricks = caps[1 : EX - 1].reshape((EX - 2) * EY, Z)
        for k in range(3):
            faces[9 + k, 1 : EX - 1] = (spread(bricks, hot, k) + BETA).reshape(EX - 2, EY, Z)

    @pl.when(jnp.logical_not(flow))
    def _():
        faces[9] = caps[...]


BESIDE = [(1, -1, Y), (1, X - 1, Y), (1, -1, 0), (1, X - 1, 0)]
BESIDE += [(0, X, -1), (0, 0, -1), (0, X, Y - 1), (0, 0, Y - 1)]
RIM = [0, 1, 2, EX - 4, EX - 3, EX - 2]
K_RIM = [0, 1, 2, 3, EX - 4, EX - 3, EX - 2, EX - 1]


def residual_kernel(base, strain, unit, layer_map, residual, xa, xb):
    flow = lax.axis_index("group") == 0

    @pl.when(flow)
    def _():
        hot = one_hot(layer_map)
        e = strain[...].reshape(X * Y, Z)
        for k in range(3):
            residual[k] = base[k] - BIOT * spread(e, hot, k).reshape(X, Y, Z)

    @pl.when(jnp.logical_not(flow))
    def _():
        residual[...] = base[...]

    pack_x(lambda f: residual.at[f], R_ROWS, xa, xb)

    @pl.when(jnp.logical_not(flow))
    def _():
        odd = parity("gx")
        for depth, n in enumerate(Q_SLOT):
            put(xa, xb, n, odd, unit[X - 1 - depth], unit[depth])


def relay_kernel(residual, unit, xa, xb, ka, kb, ya, yb):
    flow = lax.axis_index("group") == 0
    odd = parity("gy")
    r_halos, k_halos = lower_upper("gx", xa, xb), lower_upper("gx", ka, kb)

    def give(at, count, ref, index, j):
        put(ya, yb, slice(at, at + count), odd, ref[index(Y - j)], ref[index(j - 1)])

    for n, (f, r) in enumerate(R_ROWS):
        give(n * X, X, residual, lambda y: (f, slice(None), y), r)
    for side in range(2):
        r_halo, k_halo = r_halos[side], k_halos[side]
        for n, (f, i, j) in enumerate(R_CORNERS):
            row = R_ROWS.index((f, i))
            give(AT_R[side] + n, 1, r_halo, lambda y: (row, slice(y, y + 1)), j)
        for n, (f, i, j) in enumerate(K_CORNERS):
            at = slice(AT_K[side] + n, AT_K[side] + n + 1)
            put(ya, yb, at, odd, k_halo[corner_row(n, 0)], k_halo[corner_row(n, 1)])
        for n, (i, j) in enumerate(CORNER[:3]):
            row = Q_SLOT[i - 1]
            give(AT_Q[side] + n, 1, r_halo, lambda y: (row, slice(y, y + 1)), j)
        for c in range(2):
            row = X_ROWS.index((10 + c, 1))
            give(AT_U + 2 * side + c, 1, k_halo, lambda y: (row, slice(y, y + 1)), 1)

    @pl.when(jnp.logical_not(flow))
    def _():
        for depth, n in enumerate(Q_SLOT):
            give(n * X, X, unit, lambda y: (slice(None), y), depth + 1)


def fold(v):
    return jnp.sum(v.reshape(v.shape[0] // 8, 8, Z), axis=0)


def spread_sums(found):
    lane = lanes(8)
    row = jnp.zeros((8, Z), F32)
    first = rows_of(8) == 0
    for n, total in found.items():
        row = jnp.where(first & (lane == n), jnp.sum(total), row)
    return row


def tile_rows():
    at = rows_of(EY)
    return (at >= OY) & (at < OY + Y)


def fill(residual, target, halos):
    xl, xu, yl, yu = halos

    def place(x, carry):
        for k in range(3):
            target[k, OX + x, OY : OY + Y] = residual[k, x]
        return carry

    loop(0, X, place)
    unpack_x(lambda f: target.at[f], R_ROWS, xl, xu)
    for n, (f, r) in enumerate(R_ROWS):
        target[f, OX : OX + X, OY - r, :] = yl[n * X : (n + 1) * X]
        target[f, OX : OX + X, OY + Y - 1 + r, :] = yu[n * X : (n + 1) * X]
    for v, pack in enumerate((yl, yu)):
        for h in range(2):
            for n, (f, i, j) in enumerate(R_CORNERS):
                row, column = corner_at((h, v), i, j)
                target[f, row, column] = pack[AT_R[h] + n : AT_R[h] + n + 1]


def complete(faces, rim, k_rim_in, k_rim, halos, hot):
    for n, i in enumerate(RIM):
        for f in range(6, 12):
            rim[f, n] = faces[f, i]
    k_rim[...] = k_rim_in[...]
    order = []
    for v, pack in enumerate(halos[2:]):
        for h in range(2):
            for n, (f, i, j) in enumerate(K_CORNERS):
                row, column = corner_at((h, v), i, j)
                value = pack[AT_K[h] + n : AT_K[h] + n + 1]
                if f < 6:
                    k_rim[f, K_RIM.index(row), column] = value
                elif f < 9:
                    rim[f, RIM.index(row), column] = value
                else:
                    order.append((RIM.index(row), column, value))
    for n, i in enumerate(RIM):
        m = K_RIM.index(i)
        for c in range(3):
            rim[c, n] = harmonic(k_rim[c, m], k_rim[c, m + 1])
            here = k_rim[3 + c, m]
            rim[3 + c, n] = harmonic(here, up_y(here))
    if hot is None:
        for row, column, value in order:
            rim[9, row, column] = value
    else:
        values = [value for _, _, value in order]
        values += [jnp.zeros((1, Z), F32)] * (16 - len(values))
        caps = jnp.concatenate(values, axis=0)
        for k in range(3):
            storage = spread(caps, hot, k) + BETA
            for n, (row, column, _) in enumerate(order):
                rim[9 + k, row, column] = storage[n : n + 1]


def row_parts(faces, rim):
    return faces_in(rim), faces_in(faces), faces_in(rim, EX - 7)


def run_rows(parts, first, last, body, init, unroll=3):
    low, middle, high = parts
    for i in range(first, OX):
        init = body(low, i, init)
    init = loop(max(first, OX), EX - 4, lambda i, carry: body(middle, i, carry), init, unroll)
    for i in range(EX - 4, last):
        init = body(high, i, init)
    return init


PAIRS = [(0, 0), (0, 1), (0, 2), (1, 1), (1, 2), (2, 2)]
FIRST_SUM = 9


def grid_mask(before, after):
    gx, gy = lax.axis_index("gx"), lax.axis_index("gy")
    gx_last, gy_last = lax.axis_size("gx") - 1, lax.axis_size("gy") - 1
    at = rows_of(EY)
    in_y = (at >= OY - jnp.where(gy > 0, before, 0)) & (
        at < OY + Y + jnp.where(gy < gy_last, after, 0)
    )

    def in_grid(i):
        in_x = ((i >= OX) | (gx > 0)) & ((i < OX + X) | (gx < gx_last))
        return in_y & in_x

    return in_grid


def load_rows(q_refs, targets, added):
    in_grid = grid_mask(1, 2)

    def row(i, carry):
        for q_ref, target in zip(q_refs, targets):
            load_row(q_ref, target, i, in_grid(i))
        return carry

    def load_row(q_ref, target, i, ok):
        first = lanes(EY) == 0
        q = q_ref[i - 1]
        push = [
            BIOT * (q_ref[i - 2] - q),
            BIOT * (down_y(q) - q),
            BIOT * (jnp.where(first, 0.0, down_z(q)) - q),
        ]
        for c in range(3):
            v = push[c] + target[c, i] if added else push[c]
            target[c, i] = jnp.where(ok, v, 0.0)

    loop(OX - 1, OX + X + 2, row)


def solid_image(parts, f_refs, p_refs, unroll):
    in_grid = grid_mask(0, 1)

    def row(faces, i, carry):
        ok, after = in_grid(i), []
        for f_ref, p_ref, (s, fx) in zip(f_refs, p_refs, carry):
            out, s, fx = solid_row(faces, f_ref, i, s, fx)
            for c in range(3):
                p_ref[c, i] = jnp.where(ok, out[c], 0.0)
            after.append((s, fx))
        return tuple(after)

    view = parts[0]
    start = [
        (view.own(0, OX - 1) * strain_row(f, OX - 1), x_flux(view, f, OX - 1)) for f in f_refs
    ]
    run_rows(parts, OX, OX + X + 1, row, tuple(start), unroll)


def gram_sums(faces, fields, products, pairs, acc):
    acc[...] = jnp.zeros(acc.shape, F32)
    vectors = range(len(fields))

    def row(i, carry):
        inside, last = tile_rows(), lanes(EY) == Z - 1

        def only(v):
            return jnp.where(inside, v, 0.0)

        def add(n, v):
            acc[n] = acc[n] + fold(v)

        strains = [strain_row(p, i) for p in products]
        modulus = only(faces[9, i])
        later = sorted({b for _, b in pairs})
        pushes = {b: modulus * strains[b] for b in later}
        for n, (a, b) in enumerate(pairs):
            add(4 * n + 3, pushes[b] * strains[a])
        for c in range(3):
            ws = [p[c, i] for p in products]
            dx = [ws[a] - products[a][c, i + 1] for a in vectors]
            dy = [w - up_y(w) for w in ws]
            dz = [w - jnp.where(last, 0.0, up_z(w)) for w in ws]
            sx, sy, sz = (only(faces[3 * d + c, i]) for d in range(3))
            fx = {b: sx * dx[b] for b in later}
            fy = {b: sy * dy[b] for b in later}
            fz = {b: sz * dz[b] for b in later}
            rs = [f[c, i] for f in fields]
            r_in = {b: only(rs[b]) for b in later}
            w_in = {b: only(ws[b]) for b in later}
            for n, (a, b) in enumerate(pairs):
                add(4 * n + 3, fx[b] * dx[a] + fy[b] * dy[a] + fz[b] * dz[a])
                add(4 * n, r_in[b] * rs[a])
                add(4 * n + 1, r_in[b] * ws[a])
                add(4 * n + 2, w_in[b] * ws[a])
        return carry

    loop(OX, OX + X, row, 0, 2)
    found = {}
    for n, pair in enumerate(pairs):
        for m in range(4):
            found[FIRST_SUM + 6 * m + PAIRS.index(pair)] = acc[4 * n + m]
    return found


def unit_surroundings(unit, halos, q):
    xl, xu, yl, yu = halos

    def place(x, carry):
        q[OX - 1 + x, OY : OY + Y] = unit[x]
        return carry

    loop(0, X, place)
    for depth, n in enumerate(Q_SLOT):
        q[OX - 2 - depth, OY : OY + Y] = xl[n]
        q[OX + X - 1 + depth, OY : OY + Y] = xu[n]
        rows = slice(n * X, (n + 1) * X)
        q[OX - 1 : OX - 1 + X, OY - 1 - depth, :] = yl[rows]
        q[OX - 1 : OX - 1 + X, OY + Y + depth, :] = yu[rows]
    for v, pack in enumerate((yl, yu)):
        for h in range(2):
            for n, (i, j) in enumerate(CORNER[:3]):
                row, column = corner_at((h, v), i, j)
                q[row - 1, column] = pack[AT_Q[h] + n : AT_Q[h] + n + 1]


def late_terms(faces, rim, field, beside, halos):
    yl, yu = halos[2:]

    def modulus(x, y):
        i, column = OX + x, slice(OY + y, OY + y + 1)
        return rim[9, RIM.index(i), column] if i in RIM else faces[9, i, column]

    u1 = [yu[AT_U + 1 : AT_U + 2]] + [beside[n : n + 1] for n in (1, 2, 3)]
    u0 = [yl[AT_U + 2 : AT_U + 3]] + [beside[n : n + 1] for n in (5, 6, 7)]
    for u, (x, y) in zip(u1, ((0, Y - 1), (X, Y - 1), (0, -1), (X, -1))):
        row, column = OX + x, slice(OY + y, OY + y + 1)
        field[0, row, column] = field[0, row, column] - modulus(x - 1, y) * u
    for u, (x, y) in zip(u0, ((X - 1, 0), (-1, 0), (X - 1, Y), (-1, Y))):
        row, column = OX + x, slice(OY + y, OY + y + 1)
        field[1, row, column] = field[1, row, column] - modulus(x, y - 1) * u


def image_kernel(residual, unit_old, beside, layer_map, *refs):
    halos, (faces, k_rim_in, rim, field, product, unit, k_rim, q) = refs[:4], refs[4:]
    halos = surroundings(*halos)
    flow = lax.axis_index("group") == 0
    fill(residual, field, halos)

    @pl.when(flow)
    def _():
        hot = one_hot(layer_map)
        complete(faces, rim, k_rim_in, k_rim, halos, hot)
        parts = row_parts(faces, rim)

        def row(view, i, fx_before):
            out, fx = flow_row(view, field, i, fx_before)
            for k in range(3):
                product[k, i] = out[k]
            return fx

        run_rows(parts, 1, EX - 1, row, x_flux(parts[0], field, 0))
        unit[0] = gather_wide(field, hot)
        unit[1] = gather_wide(product, hot)

    @pl.when(jnp.logical_not(flow))
    def _():
        complete(faces, rim, k_rim_in, k_rim, halos, None)
        late_terms(faces, rim, field, beside, halos)
        unit_surroundings(unit_old, halos, q)
        load_rows([q], [field], True)
        solid_image(row_parts(faces, rim), [field], [product], 3)


def early_kernel(field, product, faces, state, sums, acc):
    flow = lax.axis_index("group") == 0

    @pl.when(flow)
    def _():
        def dots(i, acc):
            acc = list(acc)
            inside, last = tile_rows(), lanes(EY) == Z - 1

            def add(n, v):
                acc[n] = acc[n] + fold(jnp.where(inside, v, 0.0))

            ws = [product[k, i] for k in range(3)]
            below = flow_below(ws, last)
            g = m1 = m2 = m3 = cr = cw = 0.0
            for k in range(3):
                r, w = field[k, i], ws[k]
                dx, dy, dz = w - product[k, i + 1], w - up_y(w), w - below[k]
                cf = faces[9 + k, i]
                g = g + r * r
                m1 = m1 + r * w
                m2 = m2 + w * w
                cr = cr + cf * r
                cw = cw + cf * w
                m3 = m3 + (
                    faces[k, i] * dx * dx
                    + faces[3 + k, i] * dy * dy
                    + faces[6 + k, i] * dz * dz
                    + cf * w * w
                )
            for n, v in enumerate((g, m1, m2, m3, cr, cw)):
                add(n, v)
            weight = jnp.where(last, faces[8, i], 0.0)
            add(6, weight * field[2, i])
            add(7, weight * ws[2])
            acc[8] = acc[8] + fold(to_tile(weight) * state[2, i - OX])
            return tuple(acc)

        zero = jnp.zeros((8, Z), F32)
        found = dict(enumerate(loop(OX, OX + X, dots, (zero,) * FIRST_SUM, 2)))
        sums[...] = spread_sums(found)

    @pl.when(jnp.logical_not(flow))
    def _():
        sums[...] = spread_sums(gram_sums(faces, [field], [product], PAIRS[:1], acc))


def sums_kernel(field, product, faces, rim, unit, sums_in, sums, field12, product12, acc):
    flow = lax.axis_index("group") == 0
    everyone = sums.shape[0]

    @pl.when(flow)
    def _():
        sums[...] = jnp.broadcast_to(sums_in[:1], (everyone, Z))

    @pl.when(jnp.logical_not(flow))
    def _():
        fields = [field] + [field12.at[a] for a in range(2)]
        products = [product] + [product12.at[a] for a in range(2)]
        load_rows([unit.at[a] for a in range(2)], fields[1:], False)
        solid_image(row_parts(faces, rim), fields[1:], products[1:], 2)
        found = gram_sums(faces, fields, products, PAIRS[1:], acc)
        own = sums_in[:1] + spread_sums(found)[:1]
        sums[...] = jnp.broadcast_to(own, (everyone, Z))


def two_sum(a, b):
    s = a + b
    t = s - a
    return s, (a - (s - t)) + (b - t)


def quick(a, b):
    s = a + b
    return s, b - (s - a)


def halves(a):
    t = 4097.0 * a
    high = t - (t - a)
    return high, a - high


def two_product(a, b):
    p = a * b
    ah, al = halves(a)
    bh, bl = halves(b)
    return p, ((ah * bh - p) + ah * bl + al * bh) + al * bl


def pair_add(a, b):
    s, e = two_sum(a[0], b[0])
    return quick(s, e + (a[1] + b[1]))


def pair_less(a, b):
    return pair_add(a, (-b[0], -b[1]))


def pair_times(a, b):
    p, e = two_product(a[0], b[0])
    return quick(p, e + (a[0] * b[1] + a[1] * b[0]))


def pair_over(a, b):
    q = a[0] / b[0]
    rest = pair_less(a, pair_times(b, (q, jnp.zeros_like(q))))
    return quick(q, rest[0] / b[0])


def krylov(g, m1, m2, m3):
    a0 = pair_over(g, m1)
    h = pair_times(a0, pair_over(m2, m1))
    one = (jnp.ones_like(a0[0]), jnp.zeros_like(a0[0]))
    rho = pair_less(h, one)[0]
    third = pair_times(pair_times(a0, a0), pair_over(m3, m1))
    sigma = pair_less(third, pair_times(h, h))[0]
    more = (rho > 1e-9) & (sigma > 1e-9)
    a1 = jnp.where(more, a0[0] * rho / jnp.where(more, sigma, 1.0), 0.0)
    return a0[0] + a1 * h[0], -a0[0] * a1


def final_kernel(sums, state, field, product, field12, product12, out, balance, *, cells):
    flow = lax.axis_index("group") == 0
    total = (sums[...], jnp.zeros(sums.shape, F32))
    while total[0].shape[0] > 8:
        half = total[0].shape[0] // 2
        total = pair_add([v[:half] for v in total], [v[half:] for v in total])
    for step in (4, 2, 1):
        total = pair_add(total, [pltpu.roll(v, step, 0) for v in total])

    def number(n):
        return tuple(jnp.broadcast_to(v[:1, n : n + 1], (8, Z)) for v in total)

    c0, c1 = krylov(number(0), number(1), number(2), number(3))
    columns = cells // (3 * Z)
    outflow = (number(8)[0] + c0 * number(6)[0] + c1 * number(7)[0]) / columns
    stored = (c0 * number(4)[0] + c1 * number(5)[0]) / cells
    balance[0] = outflow[0, 0]
    balance[1] = stored[0, 0]

    def tall(v):
        return jnp.concatenate([v] * (EY // 8), axis=0)

    @pl.when(flow)
    def _():
        s0, s1 = tall(c0), tall(c1)

        def row(x, carry):
            for k in range(3):
                step = s0 * field[k, OX + x] + s1 * product[k, OX + x]
                out[k, x] = state[k, x] + to_tile(step)
            return carry

        loop(0, X, row)

    @pl.when(jnp.logical_not(flow))
    def _():
        zero = jnp.zeros((8, Z), F32)
        weights = [
            (jnp.ones((8, Z), F32), zero),
            (2.0 * c0, zero),
            (2.0 * c1, zero),
            two_product(c0, c0),
            two_product(2.0 * c0, c1),
            two_product(c1, c1),
        ]
        moments = []
        for m in range(4):
            start = FIRST_SUM + 6 * m
            total = number(start)
            for n in range(1, 6):
                total = pair_add(total, pair_times(weights[n], number(start + n)))
            moments.append(total)
        d0, d1 = krylov(*moments)
        scale_r = [tall(d0), tall(d0 * c0), tall(d0 * c1)]
        scale_w = [tall(d1), tall(d1 * c0), tall(d1 * c1)]

        def row(x, carry):
            for c in range(3):
                step = scale_r[0] * field[c, OX + x] + scale_w[0] * product[c, OX + x]
                for a in range(2):
                    step = step + scale_r[a + 1] * field12[a, c, OX + x]
                    step = step + scale_w[a + 1] * product12[a, c, OX + x]
                out[c, x] = state[c, x] + to_tile(step)
            return carry

        loop(0, X, row)


def swaps(first, second, axis):
    groups, rows, columns = (lax.axis_size(a) for a in AXES)
    count, found = lax.axis_size(axis), []
    for value, start in ((first, 0), (second, 1)):
        pairs = []
        for g in range(groups):
            for i in range(rows):
                for j in range(columns):
                    place = i if axis == "gx" else j
                    step = 1 if place % 2 == start else -1
                    if 0 <= place + step < count:
                        here = (g * rows + i) * columns + j
                        pairs.append((here, here + step * (columns if axis == "gx" else 1)))
        found.append(lax.ppermute(value, AXES, pairs))
    return found


def core_swap(value):
    count = lax.axis_size("gx") * lax.axis_size("gy")
    pairs = [(n, (n + count) % (2 * count)) for n in range(2 * count)]
    return lax.ppermute(value, AXES, pairs)


def body(state, conduct, capacity, supply, flags, layer_map):
    state, conduct, capacity, supply = state[0], conduct[0], capacity[0], supply[0]
    layer_map = layer_map.reshape(1, 3 * Z)
    cells = X * Y * 3 * Z * lax.axis_size("gx") * lax.axis_size("gy")
    devices = lax.axis_size("group") * lax.axis_size("gx") * lax.axis_size("gy")
    tile = struct(3, X, Y, Z)
    brick = struct(X, Y, Z)
    wide = (EX, EY, Z)
    full = struct(3, *wide)

    y_face = struct(len(Y_ROWS), X, Z)
    xa, xb, fa, fb, ya, yb = call(
        pack_kernel,
        [struct(NEAR_ROWS, Y, Z)] * 2 + x_faces(X_ROWS[len(NEAR) :]) + [y_face] * 2,
        [
            pltpu.VMEM((X, Y), jnp.int32),
            pltpu.VMEM((3, X, Y, Z), F32),
            pltpu.VMEM((3, 3, X, Y, Z), F32),
            pltpu.VMEM((X, Y, Z), F32),
            pltpu.VMEM((X, Y, Z), F32),
            pltpu.VMEM((3, X, Y, Z), F32),
            pltpu.SemaphoreType.DMA((14,)),
        ],
        left=(0, 1, 2, 3),
        limit=58,
        count=4,
    )(flags, state, conduct, capacity)
    k_halos = lax.optimization_barrier(swaps(xa, xb, "gx") + swaps(ya, yb, "gy"))
    wide_faces = struct(12, *wide)
    tables = [pltpu.VMEM((6, *wide), F32), pltpu.VMEM(wide, F32)]
    inner, tz, unit0 = call(
        interior_kernel,
        [wide_faces, tile, brick],
        tables + [pltpu.VMEM((X, Y, Z), F32)],
        cost=30_000_000,
    )(state, conduct, capacity, flags, layer_map)
    cross = core_swap(call(strain_kernel, brick)(state, unit0, *k_halos))
    base, beside = call(
        first_kernel,
        [tile, struct(8, Z)],
        tables + [pltpu.VMEM((3, *wide), F32)],
        cost=20_000_000,
    )(state, conduct, capacity, supply, inner, *k_halos)
    residual, xa, xb = call(residual_kernel, [tile] + x_faces(R_ROWS))(
        base, cross, cross, layer_map
    )
    *halos, fa, fb = lax.optimization_barrier((*swaps(xa, xb, "gx"), fa, fb))
    far = swaps(fa, fb, "gx")
    faces, k_rim = call(
        halo_kernel, [wide_faces, struct(6, len(K_RIM), EY, Z)], tables, cost=30_000_000
    )(conduct, capacity, tz, layer_map, *k_halos, *far)
    ya, yb = call(relay_kernel, [struct(Y_PACK, Z)] * 2)(
        residual, cross, *halos, k_halos[0], k_halos[1]
    )
    halos = halos + swaps(ya, yb, "gy")
    rim, field, product, unit12 = call(
        image_kernel,
        [struct(12, len(RIM), EY, Z), full, full, struct(2, EX - 2, EY, Z)],
        [pltpu.VMEM((6, len(K_RIM), EY, Z), F32), pltpu.VMEM((EX - 2, EY, Z), F32)],
    )(residual, cross, beside, layer_map, *halos, faces, k_rim)
    unit12 = core_swap(unit12)
    sums = call(early_kernel, struct(8, Z), [pltpu.VMEM((4, 8, Z), F32)], cost=20_000_000)(
        field, product, faces, state
    )
    sums, field12, product12 = call(
        sums_kernel,
        [struct(devices, Z), struct(2, 3, *wide), struct(2, 3, *wide)],
        [pltpu.VMEM((20, 8, Z), F32)],
    )(field, product, faces, rim, unit12, sums)
    sums = lax.all_to_all(sums, AXES, 0, 0, tiled=True)

    def finish(*refs):
        final_kernel(*refs, cells=cells)

    new_state, balance = call(finish, [tile, struct(2)], scalars=(1,))(
        sums, state, field, product, field12, product12
    )
    return new_state[None], balance


def solution(mesh):
    placed = (
        P("group", None, "gx", "gy", None),
        P("group", None, None, "gx", "gy", None),
        P("group", "gx", "gy", None),
        P("group", None, "gx", "gy", None),
        P("gx", "gy"),
        P(),
    )
    return jax.shard_map(
        body,
        mesh=mesh,
        in_specs=placed,
        out_specs=(P("group", None, "gx", "gy", None), P()),
        check_vma=False,
    )
```

```python
import jax
import jax.numpy as jnp
from jax import lax
from jax.experimental import pallas as pl
from jax.experimental.pallas import tpu as pltpu
from jax.sharding import PartitionSpec as P

AXES = ("group", "gx", "gy")
X, Y, Z = 16, 32, 128
OX, OY = 3, 4
EX, EY = X + 2 * OX, Y + 2 * OY
BETA = 0.5
BIOT = 0.8
F32 = jnp.float32

X_ROWS = [(f, r) for f in range(13) for r in range(1, (3 if f < 3 else 2 if f < 10 else 1) + 1)]
NEAR = [(f, r) for f, r in X_ROWS if r == 1 and not 3 <= f < 9]
X_ROWS = NEAR + [row for row in X_ROWS if row not in NEAR]
Y_ROWS = [
    (f, r) for f in range(13) for r in range(1, (3 if 3 <= f < 6 else 2 if f < 10 else 1) + 1)
]
CORNER = [(1, 1), (1, 2), (2, 1), (2, 2), (1, 3), (3, 1)]
K_CORNERS = (
    [(f, i, j) for f in range(3) for i, j in CORNER[:4] + [(3, 1)]]
    + [(f, i, j) for f in range(3, 6) for i, j in CORNER[:4] + [(1, 3)]]
    + [(f, i, j) for f in range(6, 10) for i, j in CORNER[:3]]
)
R_ROWS = [(f, r) for f in range(3) for r in range(1, 4)]
R_CORNERS = [(f, i, j) for f in range(3) for i, j in CORNER]
AT_R = [len(R_ROWS) * X, len(R_ROWS) * X + len(R_CORNERS)]
AT_K = [AT_R[1] + len(R_CORNERS), AT_R[1] + len(R_CORNERS) + len(K_CORNERS)]
AT_Q = [AT_K[1] + len(K_CORNERS), AT_K[1] + len(K_CORNERS) + 3]
AT_U = AT_Q[1] + 3
Y_PACK = -(-(AT_U + 4) // 8) * 8
Q_SLOT = [R_ROWS.index((0, 3)), R_ROWS.index((1, 3))]


def struct(*shape):
    return jax.ShapeDtypeStruct(shape, F32)


def call(kernel, outs, scratch=(), left=(), count=0, cost=None, limit=20, scalars=()):
    extra = {}
    if left:
        extra["in_specs"] = [
            pl.BlockSpec(memory_space=pltpu.HBM if n in left else pltpu.VMEM) for n in range(count)
        ]
    if scalars:
        extra["out_specs"] = [
            pl.BlockSpec(memory_space=pltpu.SMEM if n in scalars else pltpu.VMEM)
            for n in range(len(outs))
        ]
    if cost:
        extra["cost_estimate"] = pl.CostEstimate(
            flops=cost, bytes_accessed=cost, transcendentals=0
        )
    return pl.pallas_call(
        kernel,
        out_shape=outs,
        scratch_shapes=list(scratch),
        compiler_params=pltpu.CompilerParams(vmem_limit_bytes=limit << 20),
        **extra,
    )


def up_y(v):
    return pltpu.roll(v, v.shape[0] - 1, 0)


def down_y(v):
    return pltpu.roll(v, 1, 0)


def up_z(v):
    return pltpu.roll(v, Z - 1, 1)


def down_z(v):
    return pltpu.roll(v, 1, 1)


def lanes(rows):
    return lax.broadcasted_iota(jnp.int32, (rows, Z), 1)


def rows_of(rows):
    return lax.broadcasted_iota(jnp.int32, (rows, Z), 0)


def to_tile(v):
    return pltpu.roll(v, EY - OY, 0)[:Y]


def harmonic(a, b):
    return 2.0 * a * b / jnp.maximum(a + b, 1e-30)


def one_hot(map_ref):
    brick = lax.broadcasted_iota(jnp.int32, (Z, 3 * Z), 0)
    return jnp.where(brick == map_ref[...], 1.0, 0.0).astype(jnp.bfloat16)


def dot_split(v, hot, contract):
    high = v.astype(jnp.bfloat16)
    low = (v - high.astype(F32)).astype(jnp.bfloat16)
    dims = (((1,), (contract,)), ((), ()))
    return lax.dot_general(high, hot, dims, preferred_element_type=F32) + lax.dot_general(
        low, hot, dims, preferred_element_type=F32
    )


def spread(v, hot, k):
    return dot_split(v, hot[:, k * Z : (k + 1) * Z], 0)


def gather_up(parts, hot):
    total = None
    for k, v in enumerate(parts):
        part = dot_split(v, hot[:, k * Z : (k + 1) * Z], 1)
        total = part if total is None else total + part
    ones = jnp.ones((8, 3 * Z), jnp.bfloat16)
    counts = lax.dot_general(ones, hot, (((1,), (1,)), ((), ())), preferred_element_type=F32)
    return total * (1.0 / counts[:1])


def gather_wide(ref, hot):
    rows = EX - 2
    parts = [ref[k, 1 : EX - 1].reshape(rows * EY, Z) for k in range(3)]
    return gather_up(parts, hot).reshape(rows, EY, Z)


def fetch(pairs, sem, start=0):
    copies = [pltpu.make_async_copy(a, b, sem.at[start + n]) for n, (a, b) in enumerate(pairs)]
    for copy in copies:
        copy.start()
    return copies


def corner_row(n, side):
    c = 2 * n + side
    return len(NEAR) + c // Y, slice(c % Y, c % Y + 1)


NEAR_ROWS = len(NEAR) + -(-2 * len(K_CORNERS) // Y)


class Joined:
    def __init__(self, near, far):
        self.near, self.far = near, far

    def place(self, at):
        n, rest = (at[0], at[1:]) if isinstance(at, tuple) else (at, ())
        ref, n = (self.near, n) if n < len(NEAR) else (self.far, n - len(NEAR))
        return ref, (n, *rest)

    def __getitem__(self, at):
        ref, at = self.place(at)
        return ref[at]

    def __setitem__(self, at, value):
        ref, at = self.place(at)
        ref[at] = value


class Either:
    def __init__(self, odd, at_odd, at_even):
        self.odd, self.at_odd, self.at_even = odd, at_odd, at_even

    def __getitem__(self, at):
        return jnp.where(self.odd, self.at_odd[at], self.at_even[at])


def parity(axis):
    return lax.rem(lax.axis_index(axis), 2) == 1


def lower_upper(axis, first, second):
    odd = parity(axis)
    return Either(odd, first, second), Either(odd, second, first)


def surroundings(xa, xb, ya, yb):
    return lower_upper("gx", xa, xb) + lower_upper("gy", ya, yb)


def put(first, second, at, odd, tail, head):
    first[at] = jnp.where(odd, head, tail)
    second[at] = jnp.where(odd, tail, head)


def pack_x(source, rows, first, second):
    odd = parity("gx")
    for n, (f, r) in enumerate(rows):
        put(first, second, n, odd, source(f)[X - r], source(f)[r - 1])


def unpack_x(target, rows, low, up):
    for n, (f, r) in enumerate(rows):
        target(f)[OX - r, OY : OY + Y] = low[n]
        target(f)[OX + X - 1 + r, OY : OY + Y] = up[n]


def corner_at(side, i, j):
    row = OX - i if side[0] == 0 else OX + X - 1 + i
    column = OY - j if side[1] == 0 else OY + Y - 1 + j
    return row, slice(column, column + 1)


def x_faces(rows):
    return [struct(len(rows), Y, Z)] * 2


def loop(first, last, body, init=0, unroll=4):
    steps = (last - first) // unroll

    def step(n, carry):
        for m in range(unroll):
            carry = body(first + n * unroll + m, carry)
        return carry

    init = lax.fori_loop(0, steps, step, init)
    for i in range(first + steps * unroll, last):
        init = body(i, init)
    return init


def vertical_faces(conduct, flags, bottom, store):
    flow = lax.axis_index("group") == 0
    last = lanes(Y) == Z - 1
    eye = jnp.where(
        lax.broadcasted_iota(jnp.int32, (Y, Y), 0) == lax.broadcasted_iota(jnp.int32, (Y, Y), 1),
        1.0,
        0.0,
    ).astype(jnp.bfloat16)
    columns = lax.dot_general(
        eye,
        flags[...].astype(F32).astype(jnp.bfloat16),
        (((1,), (1,)), ((), ())),
        preferred_element_type=F32,
    )
    for x in range(X):
        bottom[x] = jnp.broadcast_to(columns[:, x : x + 1], (Y, Z))

    def row(x, carry):
        kz = [conduct[2, k, x] for k in range(3)]
        rolled = [up_z(v) for v in kz]
        ends = [rolled[1], rolled[2], bottom[x] * kz[2]]
        for k in range(3):
            end = jnp.where(flow, ends[k], kz[k])
            store(x, k, harmonic(kz[k], jnp.where(last, end, rolled[k])))
        return carry

    loop(0, X, row)


def pack_kernel(flags_in, state_in, conduct_in, capacity_in, xa, xb, fa, fb, ya, yb, *scratch):
    flags, state, conduct, capacity, bottom, tz, sem = scratch
    early = [(flags_in, flags)] + [(conduct_in.at[2, k], conduct.at[2, k]) for k in range(3)]
    late = [(conduct_in.at[d, k], conduct.at[d, k]) for d in range(2) for k in range(3)]
    late += [(state_in.at[k], state.at[k]) for k in range(3)] + [(capacity_in, capacity)]
    early = fetch(early, sem)
    late = fetch(late, sem, len(early))
    for copy in early:
        copy.wait()
    def store(x, k, value):
        tz[k, x] = value

    vertical_faces(conduct, flags, bottom, store)
    for copy in late:
        copy.wait()

    def source(f):
        if f < 6:
            return conduct.at[f // 3, f % 3]
        if f < 9:
            return tz.at[f - 6]
        return capacity if f == 9 else state.at[f - 10]

    pack_x(source, X_ROWS, Joined(xa, fa), Joined(xb, fb))
    odd = parity("gx")
    for n, (f, i, j) in enumerate(K_CORNERS):
        for side, y in enumerate((Y - j, j - 1)):
            column = slice(y, y + 1)
            put(xa, xb, corner_row(n, side), odd, source(f)[X - i, column], source(f)[i - 1, column])
    odd = parity("gy")
    for n, (f, r) in enumerate(Y_ROWS):
        put(ya, yb, n, odd, source(f)[:, Y - r, :], source(f)[:, r - 1, :])


class Faces:
    def __init__(self, x, y, z, own):
        self.x, self.y, self.z, self.own = x, y, z, own


def faces_in(ref, shift=0):
    return Faces(*[lambda c, i, d=d: ref[3 * d + c, i - shift] for d in range(4)])


def lateral(faces, v_ref, c, i, v, fx_before):
    fx = faces.x(c, i) * (v - v_ref[c, i + 1])
    fy = faces.y(c, i) * (v - up_y(v))
    return (fx - fx_before) + (fy - down_y(fy)), fx


def x_flux(faces, v_ref, i):
    return tuple(faces.x(c, i) * (v_ref[c, i] - v_ref[c, i + 1]) for c in range(3))


def flow_below(vs, last):
    rolled = [up_z(v) for v in vs]
    ends = [rolled[1], rolled[2], 0.0]
    return [jnp.where(last, ends[k], rolled[k]) for k in range(3)]


def flow_row(faces, v_ref, i, fx_before):
    last, first = lanes(EY) == Z - 1, lanes(EY) == 0
    vs = [v_ref[k, i] for k in range(3)]
    below = flow_below(vs, last)
    fz = [faces.z(k, i) * (vs[k] - below[k]) for k in range(3)]
    moved = [down_z(v) for v in fz]
    ends = [0.0, moved[0], moved[1]]
    out, fx_now = [], []
    for k in range(3):
        side, fx = lateral(faces, v_ref, k, i, vs[k], fx_before[k])
        above = jnp.where(first, ends[k], moved[k])
        out.append(faces.own(k, i) * vs[k] + side + (fz[k] - above))
        fx_now.append(fx)
    return out, tuple(fx_now)


def strain_row(v_ref, i):
    v0, v1, v2 = v_ref[0, i], v_ref[1, i], v_ref[2, i]
    low = jnp.where(lanes(EY) == Z - 1, 0.0, up_z(v2))
    return (v_ref[0, i + 1] - v0) + (up_y(v1) - v1) + (low - v2)


def solid_row(faces, v_ref, i, s_before, fx_before):
    last, first = lanes(EY) == Z - 1, lanes(EY) == 0
    e = strain_row(v_ref, i)
    s = faces.own(0, i) * e
    grad = [s_before - s, down_y(s) - s, jnp.where(first, 0.0, down_z(s)) - s]
    out, fx_now = [], []
    for c in range(3):
        v = v_ref[c, i]
        side, fx = lateral(faces, v_ref, c, i, v, fx_before[c])
        fz = faces.z(c, i) * (v - jnp.where(last, 0.0, up_z(v)))
        above = jnp.where(first, 0.0, down_z(fz))
        out.append((side + (fz - above)) + grad[c])
        fx_now.append(fx)
    return out, s, tuple(fx_now)


BESIDE = [(1, -1, Y), (1, X - 1, Y), (1, -1, 0), (1, X - 1, 0)]
BESIDE += [(0, X, -1), (0, 0, -1), (0, X, Y - 1), (0, 0, Y - 1)]


def place_tile(conduct, capacity, keep, caps):
    at = slice(OY, OY + Y)

    def row(x, carry):
        for f in range(6):
            keep[f, OX + x, at] = conduct[f // 3, f % 3, x]
        caps[OX + x, at] = capacity[x]
        return carry

    loop(0, X, row)


def interior_kernel(state, conduct, capacity, flags, layer_map, faces, tz, unit, keep, caps, bottom):
    flow = lax.axis_index("group") == 0
    place_tile(conduct, capacity, keep, caps)

    def store(x, k, value):
        tz[k, x] = value
        faces[6 + k, OX + x, OY : OY + Y] = value

    vertical_faces(conduct, flags, bottom, store)
    loop(OX, OX + X, lambda i, carry: lateral_faces(keep, faces, i))

    @pl.when(flow)
    def _():
        hot = one_hot(layer_map)
        bricks = caps[OX : OX + X].reshape(X * EY, Z)
        for k in range(3):
            faces[9 + k, OX : OX + X] = (spread(bricks, hot, k) + BETA).reshape(X, EY, Z)
        parts = [state[k].reshape(X * Y, Z) for k in range(3)]
        unit[...] = gather_up(parts, hot).reshape(X, Y, Z)


def lateral_faces(keep, faces, i):
    for c in range(3):
        faces[c, i] = harmonic(keep[c, i], keep[c, i + 1])
        here = keep[3 + c, i]
        faces[3 + c, i] = harmonic(here, up_y(here))
    return 0


def strain_kernel(state, unit, xa, xb, ya, yb, strain):
    flow = lax.axis_index("group") == 0
    _, xu, _, yu = surroundings(xa, xb, ya, yb)

    @pl.when(flow)
    def _():
        strain[...] = unit[...]

    @pl.when(jnp.logical_not(flow))
    def _():
        last = lanes(Y) == Z - 1
        edge = rows_of(Y) == Y - 1
        n_x, n_y = X_ROWS.index((10, 1)), Y_ROWS.index((11, 1))
        for x in range(X):
            v0, v1, v2 = (state[c, x] for c in range(3))
            east = state[0, x + 1] if x + 1 < X else xu[n_x]
            north = jnp.where(edge, yu[n_y, x : x + 1], up_y(v1))
            low = jnp.where(last, 0.0, up_z(v2))
            strain[x] = (east - v0) + (north - v1) + (low - v2)


def first_kernel(state, conduct, capacity, supply, faces_ref, xa, xb, ya, yb, *refs):
    xl, xu, yl, yu = surroundings(xa, xb, ya, yb)
    base, beside, sides, own, field = refs
    flow = lax.axis_index("group") == 0

    def place(x, carry):
        for c in range(3):
            field[c, OX + x, OY : OY + Y] = state[c, x]
        for f in range(6):
            sides[f, OX + x] = faces_ref[f, OX + x]
        return carry

    loop(0, X, place)
    for c in range(3):
        n = X_ROWS.index((10 + c, 1))
        field[c, OX - 1, OY : OY + Y] = xl[n]
        field[c, OX + X, OY : OY + Y] = xu[n]
        n = Y_ROWS.index((10 + c, 1))
        field[c, OX : OX + X, OY - 1, :] = yl[n]
        field[c, OX : OX + X, OY + Y, :] = yu[n]
        n = X_ROWS.index((c, 1))
        at = slice(OY, OY + Y)
        sides[c, OX - 1, at] = harmonic(xl[n], conduct[0, c, 0])
        sides[c, OX + X - 1, at] = harmonic(conduct[0, c, X - 1], xu[n])
        n = Y_ROWS.index((3 + c, 1))
        sides[3 + c, OX : OX + X, OY - 1, :] = harmonic(yl[n], conduct[1, c, :, 0, :])
        sides[3 + c, OX : OX + X, OY + Y - 1, :] = harmonic(conduct[1, c, :, Y - 1, :], yu[n])
    field[1, OX - 1, OY + Y : OY + Y + 1] = jnp.zeros((1, Z), F32)
    field[0, OX + X, OY - 1 : OY] = jnp.zeros((1, Z), F32)
    for n, (c, x, y) in enumerate(BESIDE):
        beside[n : n + 1] = field[c, OX + x, OY + y : OY + y + 1]
    inner = faces_in(faces_ref)
    outer = faces_in(sides)

    @pl.when(flow)
    def _():
        faces = Faces(outer.x, outer.y, inner.z, inner.own)

        def row(i, fx_before):
            image, fx = flow_row(faces, field, i, fx_before)
            for k in range(3):
                base[k, i - OX] = (
                    supply[k, i - OX] + BETA * state[k, i - OX] - to_tile(image[k])
                )
            return fx

        loop(OX, OX + X, row, x_flux(faces, field, OX - 1))

    @pl.when(jnp.logical_not(flow))
    def _():
        def place(x, carry):
            own[OX + x, OY : OY + Y] = capacity[x]
            return carry

        loop(0, X, place)
        own[OX - 1, OY : OY + Y] = xl[X_ROWS.index((9, 1))]
        own[OX : OX + X, OY - 1, :] = yl[Y_ROWS.index((9, 1))]
        faces = Faces(outer.x, outer.y, inner.z, lambda c, i: own[i])

        def row(i, carry):
            image, s, fx = solid_row(faces, field, i, carry[0], carry[1])
            for c in range(3):
                base[c, i - OX] = supply[c, i - OX] - to_tile(image[c])
            return s, fx

        before = faces.own(0, OX - 1) * strain_row(field, OX - 1)
        loop(OX, OX + X, row, (before, x_flux(faces, field, OX - 1)))


def halo_kernel(conduct, capacity, tz, layer_map, xa, xb, ya, yb, fa, fb, *refs):
    faces, rim, keep, caps = refs
    xl, xu, yl, yu = surroundings(Joined(xa, fa), Joined(xb, fb), ya, yb)
    flow = lax.axis_index("group") == 0

    def target(f):
        if f < 6:
            return keep.at[f]
        return faces.at[f] if f < 9 else caps

    place_tile(conduct, capacity, keep, caps)

    def place(x, carry):
        for k in range(3):
            faces[6 + k, OX + x, OY : OY + Y] = tz[k, x]
        return carry

    loop(0, X, place)
    for n, (f, r) in enumerate(X_ROWS):
        if f < 10:
            target(f)[OX - r, OY : OY + Y] = xl[n]
            target(f)[OX + X - 1 + r, OY : OY + Y] = xu[n]
    for n, (f, r) in enumerate(Y_ROWS):
        if f < 10:
            target(f)[OX : OX + X, OY - r, :] = yl[n]
            target(f)[OX : OX + X, OY + Y - 1 + r, :] = yu[n]
    loop(0, EX - 1, lambda i, carry: lateral_faces(keep, faces, i))
    for n, i in enumerate(K_RIM):
        for f in range(6):
            rim[f, n] = keep[f, i]

    @pl.when(flow)
    def _():
        hot = one_hot(layer_map)
        bricks = caps[1 : EX - 1].reshape((EX - 2) * EY, Z)
        for k in range(3):
            faces[9 + k, 1 : EX - 1] = (spread(bricks, hot, k) + BETA).reshape(EX - 2, EY, Z)

    @pl.when(jnp.logical_not(flow))
    def _():
        faces[9] = caps[...]


BESIDE = [(1, -1, Y), (1, X - 1, Y), (1, -1, 0), (1, X - 1, 0)]
BESIDE += [(0, X, -1), (0, 0, -1), (0, X, Y - 1), (0, 0, Y - 1)]
RIM = [0, 1, 2, EX - 4, EX - 3, EX - 2]
K_RIM = [0, 1, 2, 3, EX - 4, EX - 3, EX - 2, EX - 1]


def residual_kernel(base, strain, unit, layer_map, residual, xa, xb):
    flow = lax.axis_index("group") == 0

    @pl.when(flow)
    def _():
        hot = one_hot(layer_map)
        e = strain[...].reshape(X * Y, Z)
        for k in range(3):
            residual[k] = base[k] - BIOT * spread(e, hot, k).reshape(X, Y, Z)

    @pl.when(jnp.logical_not(flow))
    def _():
        residual[...] = base[...]

    pack_x(lambda f: residual.at[f], R_ROWS, xa, xb)

    @pl.when(jnp.logical_not(flow))
    def _():
        odd = parity("gx")
        for depth, n in enumerate(Q_SLOT):
            put(xa, xb, n, odd, unit[X - 1 - depth], unit[depth])


def relay_kernel(residual, unit, xa, xb, ka, kb, ya, yb):
    flow = lax.axis_index("group") == 0
    odd = parity("gy")
    r_halos, k_halos = lower_upper("gx", xa, xb), lower_upper("gx", ka, kb)

    def give(at, count, ref, index, j):
        put(ya, yb, slice(at, at + count), odd, ref[index(Y - j)], ref[index(j - 1)])

    for n, (f, r) in enumerate(R_ROWS):
        give(n * X, X, residual, lambda y: (f, slice(None), y), r)
    for side in range(2):
        r_halo, k_halo = r_halos[side], k_halos[side]
        for n, (f, i, j) in enumerate(R_CORNERS):
            row = R_ROWS.index((f, i))
            give(AT_R[side] + n, 1, r_halo, lambda y: (row, slice(y, y + 1)), j)
        for n, (f, i, j) in enumerate(K_CORNERS):
            at = slice(AT_K[side] + n, AT_K[side] + n + 1)
            put(ya, yb, at, odd, k_halo[corner_row(n, 0)], k_halo[corner_row(n, 1)])
        for n, (i, j) in enumerate(CORNER[:3]):
            row = Q_SLOT[i - 1]
            give(AT_Q[side] + n, 1, r_halo, lambda y: (row, slice(y, y + 1)), j)
        for c in range(2):
            row = X_ROWS.index((10 + c, 1))
            give(AT_U + 2 * side + c, 1, k_halo, lambda y: (row, slice(y, y + 1)), 1)

    @pl.when(jnp.logical_not(flow))
    def _():
        for depth, n in enumerate(Q_SLOT):
            give(n * X, X, unit, lambda y: (slice(None), y), depth + 1)


def fold(v):
    return jnp.sum(v.reshape(v.shape[0] // 8, 8, Z), axis=0)


def spread_sums(found):
    lane = lanes(8)
    row = jnp.zeros((8, Z), F32)
    first = rows_of(8) == 0
    for n, total in found.items():
        row = jnp.where(first & (lane == n), jnp.sum(total), row)
    return row


def tile_rows():
    at = rows_of(EY)
    return (at >= OY) & (at < OY + Y)


def fill(residual, target, halos):
    xl, xu, yl, yu = halos

    def place(x, carry):
        for k in range(3):
            target[k, OX + x, OY : OY + Y] = residual[k, x]
        return carry

    loop(0, X, place)
    unpack_x(lambda f: target.at[f], R_ROWS, xl, xu)
    for n, (f, r) in enumerate(R_ROWS):
        target[f, OX : OX + X, OY - r, :] = yl[n * X : (n + 1) * X]
        target[f, OX : OX + X, OY + Y - 1 + r, :] = yu[n * X : (n + 1) * X]
    for v, pack in enumerate((yl, yu)):
        for h in range(2):
            for n, (f, i, j) in enumerate(R_CORNERS):
                row, column = corner_at((h, v), i, j)
                target[f, row, column] = pack[AT_R[h] + n : AT_R[h] + n + 1]


def complete(faces, rim, k_rim_in, k_rim, halos, hot):
    for n, i in enumerate(RIM):
        for f in range(6, 12):
            rim[f, n] = faces[f, i]
    k_rim[...] = k_rim_in[...]
    order = []
    for v, pack in enumerate(halos[2:]):
        for h in range(2):
            for n, (f, i, j) in enumerate(K_CORNERS):
                row, column = corner_at((h, v), i, j)
                value = pack[AT_K[h] + n : AT_K[h] + n + 1]
                if f < 6:
                    k_rim[f, K_RIM.index(row), column] = value
                elif f < 9:
                    rim[f, RIM.index(row), column] = value
                else:
                    order.append((RIM.index(row), column, value))
    for n, i in enumerate(RIM):
        m = K_RIM.index(i)
        for c in range(3):
            rim[c, n] = harmonic(k_rim[c, m], k_rim[c, m + 1])
            here = k_rim[3 + c, m]
            rim[3 + c, n] = harmonic(here, up_y(here))
    if hot is None:
        for row, column, value in order:
            rim[9, row, column] = value
    else:
        values = [value for _, _, value in order]
        values += [jnp.zeros((1, Z), F32)] * (16 - len(values))
        caps = jnp.concatenate(values, axis=0)
        for k in range(3):
            storage = spread(caps, hot, k) + BETA
            for n, (row, column, _) in enumerate(order):
                rim[9 + k, row, column] = storage[n : n + 1]


def row_parts(faces, rim):
    return faces_in(rim), faces_in(faces), faces_in(rim, EX - 7)


def run_rows(parts, first, last, body, init, unroll=3):
    low, middle, high = parts
    for i in range(first, OX):
        init = body(low, i, init)
    init = loop(max(first, OX), EX - 4, lambda i, carry: body(middle, i, carry), init, unroll)
    for i in range(EX - 4, last):
        init = body(high, i, init)
    return init


PAIRS = [(0, 0), (0, 1), (0, 2), (1, 1), (1, 2), (2, 2)]
FIRST_SUM = 9


def grid_mask(before, after):
    gx, gy = lax.axis_index("gx"), lax.axis_index("gy")
    gx_last, gy_last = lax.axis_size("gx") - 1, lax.axis_size("gy") - 1
    at = rows_of(EY)
    in_y = (at >= OY - jnp.where(gy > 0, before, 0)) & (
        at < OY + Y + jnp.where(gy < gy_last, after, 0)
    )

    def in_grid(i):
        in_x = ((i >= OX) | (gx > 0)) & ((i < OX + X) | (gx < gx_last))
        return in_y & in_x

    return in_grid


def load_rows(q_refs, targets, added):
    in_grid = grid_mask(1, 2)

    def row(i, carry):
        for q_ref, target in zip(q_refs, targets):
            load_row(q_ref, target, i, in_grid(i))
        return carry

    def load_row(q_ref, target, i, ok):
        first = lanes(EY) == 0
        q = q_ref[i - 1]
        push = [
            BIOT * (q_ref[i - 2] - q),
            BIOT * (down_y(q) - q),
            BIOT * (jnp.where(first, 0.0, down_z(q)) - q),
        ]
        for c in range(3):
            v = push[c] + target[c, i] if added else push[c]
            target[c, i] = jnp.where(ok, v, 0.0)

    loop(OX - 1, OX + X + 2, row)


def solid_image(parts, f_refs, p_refs, unroll):
    in_grid = grid_mask(0, 1)

    def row(faces, i, carry):
        ok, after = in_grid(i), []
        for f_ref, p_ref, (s, fx) in zip(f_refs, p_refs, carry):
            out, s, fx = solid_row(faces, f_ref, i, s, fx)
            for c in range(3):
                p_ref[c, i] = jnp.where(ok, out[c], 0.0)
            after.append((s, fx))
        return tuple(after)

    view = parts[0]
    start = [
        (view.own(0, OX - 1) * strain_row(f, OX - 1), x_flux(view, f, OX - 1)) for f in f_refs
    ]
    run_rows(parts, OX, OX + X + 1, row, tuple(start), unroll)


def gram_sums(faces, fields, products, pairs, acc):
    acc[...] = jnp.zeros(acc.shape, F32)
    vectors = range(len(fields))

    def row(i, carry):
        inside, last = tile_rows(), lanes(EY) == Z - 1

        def only(v):
            return jnp.where(inside, v, 0.0)

        def add(n, v):
            acc[n] = acc[n] + fold(v)

        strains = [strain_row(p, i) for p in products]
        modulus = only(faces[9, i])
        later = sorted({b for _, b in pairs})
        pushes = {b: modulus * strains[b] for b in later}
        for n, (a, b) in enumerate(pairs):
            add(4 * n + 3, pushes[b] * strains[a])
        for c in range(3):
            ws = [p[c, i] for p in products]
            dx = [ws[a] - products[a][c, i + 1] for a in vectors]
            dy = [w - up_y(w) for w in ws]
            dz = [w - jnp.where(last, 0.0, up_z(w)) for w in ws]
            sx, sy, sz = (only(faces[3 * d + c, i]) for d in range(3))
            fx = {b: sx * dx[b] for b in later}
            fy = {b: sy * dy[b] for b in later}
            fz = {b: sz * dz[b] for b in later}
            rs = [f[c, i] for f in fields]
            r_in = {b: only(rs[b]) for b in later}
            w_in = {b: only(ws[b]) for b in later}
            for n, (a, b) in enumerate(pairs):
                add(4 * n + 3, fx[b] * dx[a] + fy[b] * dy[a] + fz[b] * dz[a])
                add(4 * n, r_in[b] * rs[a])
                add(4 * n + 1, r_in[b] * ws[a])
                add(4 * n + 2, w_in[b] * ws[a])
        return carry

    loop(OX, OX + X, row, 0, 2)
    found = {}
    for n, pair in enumerate(pairs):
        for m in range(4):
            found[FIRST_SUM + 6 * m + PAIRS.index(pair)] = acc[4 * n + m]
    return found


def unit_surroundings(unit, halos, q):
    xl, xu, yl, yu = halos

    def place(x, carry):
        q[OX - 1 + x, OY : OY + Y] = unit[x]
        return carry

    loop(0, X, place)
    for depth, n in enumerate(Q_SLOT):
        q[OX - 2 - depth, OY : OY + Y] = xl[n]
        q[OX + X - 1 + depth, OY : OY + Y] = xu[n]
        rows = slice(n * X, (n + 1) * X)
        q[OX - 1 : OX - 1 + X, OY - 1 - depth, :] = yl[rows]
        q[OX - 1 : OX - 1 + X, OY + Y + depth, :] = yu[rows]
    for v, pack in enumerate((yl, yu)):
        for h in range(2):
            for n, (i, j) in enumerate(CORNER[:3]):
                row, column = corner_at((h, v), i, j)
                q[row - 1, column] = pack[AT_Q[h] + n : AT_Q[h] + n + 1]


def late_terms(faces, rim, field, beside, halos):
    yl, yu = halos[2:]

    def modulus(x, y):
        i, column = OX + x, slice(OY + y, OY + y + 1)
        return rim[9, RIM.index(i), column] if i in RIM else faces[9, i, column]

    u1 = [yu[AT_U + 1 : AT_U + 2]] + [beside[n : n + 1] for n in (1, 2, 3)]
    u0 = [yl[AT_U + 2 : AT_U + 3]] + [beside[n : n + 1] for n in (5, 6, 7)]
    for u, (x, y) in zip(u1, ((0, Y - 1), (X, Y - 1), (0, -1), (X, -1))):
        row, column = OX + x, slice(OY + y, OY + y + 1)
        field[0, row, column] = field[0, row, column] - modulus(x - 1, y) * u
    for u, (x, y) in zip(u0, ((X - 1, 0), (-1, 0), (X - 1, Y), (-1, Y))):
        row, column = OX + x, slice(OY + y, OY + y + 1)
        field[1, row, column] = field[1, row, column] - modulus(x, y - 1) * u


def image_kernel(residual, unit_old, beside, layer_map, *refs):
    halos, (faces, k_rim_in, rim, field, product, unit, k_rim, q) = refs[:4], refs[4:]
    halos = surroundings(*halos)
    flow = lax.axis_index("group") == 0
    fill(residual, field, halos)

    @pl.when(flow)
    def _():
        hot = one_hot(layer_map)
        complete(faces, rim, k_rim_in, k_rim, halos, hot)
        parts = row_parts(faces, rim)

        def row(view, i, fx_before):
            out, fx = flow_row(view, field, i, fx_before)
            for k in range(3):
                product[k, i] = out[k]
            return fx

        run_rows(parts, 1, EX - 1, row, x_flux(parts[0], field, 0))
        unit[0] = gather_wide(field, hot)
        unit[1] = gather_wide(product, hot)

    @pl.when(jnp.logical_not(flow))
    def _():
        complete(faces, rim, k_rim_in, k_rim, halos, None)
        late_terms(faces, rim, field, beside, halos)
        unit_surroundings(unit_old, halos, q)
        load_rows([q], [field], True)
        solid_image(row_parts(faces, rim), [field], [product], 3)


def early_kernel(field, product, faces, state, sums, acc):
    flow = lax.axis_index("group") == 0

    @pl.when(flow)
    def _():
        def dots(i, acc):
            acc = list(acc)
            inside, last = tile_rows(), lanes(EY) == Z - 1

            def add(n, v):
                acc[n] = acc[n] + fold(jnp.where(inside, v, 0.0))

            ws = [product[k, i] for k in range(3)]
            below = flow_below(ws, last)
            g = m1 = m2 = m3 = cr = cw = 0.0
            for k in range(3):
                r, w = field[k, i], ws[k]
                dx, dy, dz = w - product[k, i + 1], w - up_y(w), w - below[k]
                cf = faces[9 + k, i]
                g = g + r * r
                m1 = m1 + r * w
                m2 = m2 + w * w
                cr = cr + cf * r
                cw = cw + cf * w
                m3 = m3 + (
                    faces[k, i] * dx * dx
                    + faces[3 + k, i] * dy * dy
                    + faces[6 + k, i] * dz * dz
                    + cf * w * w
                )
            for n, v in enumerate((g, m1, m2, m3, cr, cw)):
                add(n, v)
            weight = jnp.where(last, faces[8, i], 0.0)
            add(6, weight * field[2, i])
            add(7, weight * ws[2])
            acc[8] = acc[8] + fold(to_tile(weight) * state[2, i - OX])
            return tuple(acc)

        zero = jnp.zeros((8, Z), F32)
        found = dict(enumerate(loop(OX, OX + X, dots, (zero,) * FIRST_SUM, 2)))
        sums[...] = spread_sums(found)

    @pl.when(jnp.logical_not(flow))
    def _():
        sums[...] = spread_sums(gram_sums(faces, [field], [product], PAIRS[:1], acc))


def sums_kernel(field, product, faces, rim, unit, sums_in, sums, field12, product12, acc):
    flow = lax.axis_index("group") == 0
    everyone = sums.shape[0]

    @pl.when(flow)
    def _():
        sums[...] = jnp.broadcast_to(sums_in[:1], (everyone, Z))

    @pl.when(jnp.logical_not(flow))
    def _():
        fields = [field] + [field12.at[a] for a in range(2)]
        products = [product] + [product12.at[a] for a in range(2)]
        load_rows([unit.at[a] for a in range(2)], fields[1:], False)
        solid_image(row_parts(faces, rim), fields[1:], products[1:], 2)
        found = gram_sums(faces, fields, products, PAIRS[1:], acc)
        own = sums_in[:1] + spread_sums(found)[:1]
        sums[...] = jnp.broadcast_to(own, (everyone, Z))


def two_sum(a, b):
    s = a + b
    t = s - a
    return s, (a - (s - t)) + (b - t)


def quick(a, b):
    s = a + b
    return s, b - (s - a)


def halves(a):
    t = 4097.0 * a
    high = t - (t - a)
    return high, a - high


def two_product(a, b):
    p = a * b
    ah, al = halves(a)
    bh, bl = halves(b)
    return p, ((ah * bh - p) + ah * bl + al * bh) + al * bl


def pair_add(a, b):
    s, e = two_sum(a[0], b[0])
    return quick(s, e + (a[1] + b[1]))


def pair_less(a, b):
    return pair_add(a, (-b[0], -b[1]))


def pair_times(a, b):
    p, e = two_product(a[0], b[0])
    return quick(p, e + (a[0] * b[1] + a[1] * b[0]))


def pair_over(a, b):
    q = a[0] / b[0]
    rest = pair_less(a, pair_times(b, (q, jnp.zeros_like(q))))
    return quick(q, rest[0] / b[0])


def krylov(g, m1, m2, m3):
    a0 = pair_over(g, m1)
    h = pair_times(a0, pair_over(m2, m1))
    one = (jnp.ones_like(a0[0]), jnp.zeros_like(a0[0]))
    rho = pair_less(h, one)[0]
    third = pair_times(pair_times(a0, a0), pair_over(m3, m1))
    sigma = pair_less(third, pair_times(h, h))[0]
    more = (rho > 1e-9) & (sigma > 1e-9)
    a1 = jnp.where(more, a0[0] * rho / jnp.where(more, sigma, 1.0), 0.0)
    return a0[0] + a1 * h[0], -a0[0] * a1


def final_kernel(sums, state, field, product, field12, product12, out, balance, *, cells):
    flow = lax.axis_index("group") == 0
    total = (sums[...], jnp.zeros(sums.shape, F32))
    while total[0].shape[0] > 8:
        half = total[0].shape[0] // 2
        total = pair_add([v[:half] for v in total], [v[half:] for v in total])
    for step in (4, 2, 1):
        total = pair_add(total, [pltpu.roll(v, step, 0) for v in total])

    def number(n):
        return tuple(jnp.broadcast_to(v[:1, n : n + 1], (8, Z)) for v in total)

    c0, c1 = krylov(number(0), number(1), number(2), number(3))
    columns = cells // (3 * Z)
    outflow = (number(8)[0] + c0 * number(6)[0] + c1 * number(7)[0]) / columns
    stored = (c0 * number(4)[0] + c1 * number(5)[0]) / cells
    balance[0] = outflow[0, 0]
    balance[1] = stored[0, 0]

    def tall(v):
        return jnp.concatenate([v] * (EY // 8), axis=0)

    @pl.when(flow)
    def _():
        s0, s1 = tall(c0), tall(c1)

        def row(x, carry):
            for k in range(3):
                step = s0 * field[k, OX + x] + s1 * product[k, OX + x]
                out[k, x] = state[k, x] + to_tile(step)
            return carry

        loop(0, X, row)

    @pl.when(jnp.logical_not(flow))
    def _():
        zero = jnp.zeros((8, Z), F32)
        weights = [
            (jnp.ones((8, Z), F32), zero),
            (2.0 * c0, zero),
            (2.0 * c1, zero),
            two_product(c0, c0),
            two_product(2.0 * c0, c1),
            two_product(c1, c1),
        ]
        moments = []
        for m in range(4):
            start = FIRST_SUM + 6 * m
            total = number(start)
            for n in range(1, 6):
                total = pair_add(total, pair_times(weights[n], number(start + n)))
            moments.append(total)
        d0, d1 = krylov(*moments)
        scale_r = [tall(d0), tall(d0 * c0), tall(d0 * c1)]
        scale_w = [tall(d1), tall(d1 * c0), tall(d1 * c1)]

        def row(x, carry):
            for c in range(3):
                step = scale_r[0] * field[c, OX + x] + scale_w[0] * product[c, OX + x]
                for a in range(2):
                    step = step + scale_r[a + 1] * field12[a, c, OX + x]
                    step = step + scale_w[a + 1] * product12[a, c, OX + x]
                out[c, x] = state[c, x] + to_tile(step)
            return carry

        loop(0, X, row)


def swaps(first, second, axis):
    groups, rows, columns = (lax.axis_size(a) for a in AXES)
    count, found = lax.axis_size(axis), []
    for value, start in ((first, 0), (second, 1)):
        pairs = []
        for g in range(groups):
            for i in range(rows):
                for j in range(columns):
                    place = i if axis == "gx" else j
                    step = 1 if place % 2 == start else -1
                    if 0 <= place + step < count:
                        here = (g * rows + i) * columns + j
                        pairs.append((here, here + step * (columns if axis == "gx" else 1)))
        found.append(lax.ppermute(value, AXES, pairs))
    return found


def core_swap(value):
    count = lax.axis_size("gx") * lax.axis_size("gy")
    pairs = [(n, (n + count) % (2 * count)) for n in range(2 * count)]
    return lax.ppermute(value, AXES, pairs)


def body(state, conduct, capacity, supply, flags, layer_map):
    state, conduct, capacity, supply = state[0], conduct[0], capacity[0], supply[0]
    layer_map = layer_map.reshape(1, 3 * Z)
    cells = X * Y * 3 * Z * lax.axis_size("gx") * lax.axis_size("gy")
    devices = lax.axis_size("group") * lax.axis_size("gx") * lax.axis_size("gy")
    tile = struct(3, X, Y, Z)
    brick = struct(X, Y, Z)
    wide = (EX, EY, Z)
    full = struct(3, *wide)

    y_face = struct(len(Y_ROWS), X, Z)
    xa, xb, fa, fb, ya, yb = call(
        pack_kernel,
        [struct(NEAR_ROWS, Y, Z)] * 2 + x_faces(X_ROWS[len(NEAR) :]) + [y_face] * 2,
        [
            pltpu.VMEM((X, Y), jnp.int32),
            pltpu.VMEM((3, X, Y, Z), F32),
            pltpu.VMEM((3, 3, X, Y, Z), F32),
            pltpu.VMEM((X, Y, Z), F32),
            pltpu.VMEM((X, Y, Z), F32),
            pltpu.VMEM((3, X, Y, Z), F32),
            pltpu.SemaphoreType.DMA((14,)),
        ],
        left=(0, 1, 2, 3),
        limit=58,
        count=4,
    )(flags, state, conduct, capacity)
    k_halos = lax.optimization_barrier(swaps(xa, xb, "gx") + swaps(ya, yb, "gy"))
    wide_faces = struct(12, *wide)
    tables = [pltpu.VMEM((6, *wide), F32), pltpu.VMEM(wide, F32)]
    inner, tz, unit0 = call(
        interior_kernel,
        [wide_faces, tile, brick],
        tables + [pltpu.VMEM((X, Y, Z), F32)],
        cost=30_000_000,
    )(state, conduct, capacity, flags, layer_map)
    cross = core_swap(call(strain_kernel, brick)(state, unit0, *k_halos))
    base, beside = call(
        first_kernel,
        [tile, struct(8, Z)],
        tables + [pltpu.VMEM((3, *wide), F32)],
        cost=20_000_000,
    )(state, conduct, capacity, supply, inner, *k_halos)
    residual, xa, xb = call(residual_kernel, [tile] + x_faces(R_ROWS))(
        base, cross, cross, layer_map
    )
    halos = swaps(xa, xb, "gx")
    far = swaps(fa, fb, "gx")
    faces, k_rim = call(
        halo_kernel, [wide_faces, struct(6, len(K_RIM), EY, Z)], tables, cost=30_000_000
    )(conduct, capacity, tz, layer_map, *k_halos, *far)
    ya, yb = call(relay_kernel, [struct(Y_PACK, Z)] * 2)(
        residual, cross, *halos, k_halos[0], k_halos[1]
    )
    halos = halos + swaps(ya, yb, "gy")
    rim, field, product, unit12 = call(
        image_kernel,
        [struct(12, len(RIM), EY, Z), full, full, struct(2, EX - 2, EY, Z)],
        [pltpu.VMEM((6, len(K_RIM), EY, Z), F32), pltpu.VMEM((EX - 2, EY, Z), F32)],
    )(residual, cross, beside, layer_map, *halos, faces, k_rim)
    unit12 = core_swap(unit12)
    sums = call(early_kernel, struct(8, Z), [pltpu.VMEM((4, 8, Z), F32)], cost=20_000_000)(
        field, product, faces, state
    )
    sums, field12, product12 = call(
        sums_kernel,
        [struct(devices, Z), struct(2, 3, *wide), struct(2, 3, *wide)],
        [pltpu.VMEM((20, 8, Z), F32)],
    )(field, product, faces, rim, unit12, sums)
    sums = lax.all_to_all(sums, AXES, 0, 0, tiled=True)

    def finish(*refs):
        final_kernel(*refs, cells=cells)

    new_state, balance = call(finish, [tile, struct(2)], scalars=(1,))(
        sums, state, field, product, field12, product12
    )
    return new_state[None], balance


def solution(mesh):
    placed = (
        P("group", None, "gx", "gy", None),
        P("group", None, None, "gx", "gy", None),
        P("group", "gx", "gy", None),
        P("group", None, "gx", "gy", None),
        P("gx", "gy"),
        P(),
    )
    return jax.shard_map(
        body,
        mesh=mesh,
        in_specs=placed,
        out_specs=(P("group", None, "gx", "gy", None), P()),
        check_vma=False,
    )
```
